32 devices in a mesh: experts: 4 (over z), context: 4 (over x, core), dp: 2 (over y).
Axes of the slice: x: 2, y: 2, z: 4, core: 2. Of those that a mesh axis runs over, the one named last changes fastest.
Arguments:
- tokens: bfloat16 [8, 1024, 1024], P(('experts', 'dp'), 'context'), may hold values from -6 to 6
- doc_starts: int32 [8, 8], P(('experts', 'dp')), may hold values from 0 to 1023, as said below
- expert_ids: int32 [8, 1024, 2], P(('experts', 'dp'), 'context'), may hold values from 0 to 3, all different within a row; in each aligned block of 256 rows (0 to 255, 256 to 511, ..., all dimensions but the last counted through in order) at most 160 rows name the same one
- attn_in: bfloat16 [2, 1024, 3072], P(None, ('experts', 'context', 'dp')), may hold values from -0.1875 to 0.1875
- attn_out: bfloat16 [2, 1024, 1024], P(None, ('experts', 'context', 'dp')), may hold values from -1 to 1
- router: bfloat16 [2, 1024, 4], P(None, ('experts', 'context', 'dp')), may hold values from -0.09375 to 0.09375
- gains: bfloat16 [2, 1024, 2], P(None, ('experts', 'context', 'dp')), may hold values from 0.099609375 to 1.8984375
- rel_table: bfloat16 [2, 512], P(None, ('experts', 'context', 'dp')), may hold values from -4 to 4
- expert_in: bfloat16 [2, 4, 1024, 5632], P(None, 'experts'), may hold values from -0.1875 to 0.1875
- expert_out: bfloat16 [2, 4, 1024, 2816], P(None, 'experts'), may hold values from -0.109375 to 0.109375
- out_grad: bfloat16 [8, 1024, 1024], P(('experts', 'dp'), 'context'), may hold values from -6 to 6
Outputs:
- result: bfloat16 [8, 1024, 1024], P(('experts', 'dp'), 'context')
- tokens_grad: float32 [8, 1024, 1024], P(('experts', 'dp'), 'context')
- attn_in_grad: float32 [2, 1024, 3072], P(None, ('experts', 'context', 'dp'))
- attn_out_grad: float32 [2, 1024, 1024], P(None, ('experts', 'context', 'dp'))
- router_grad: float32 [2, 1024, 4], P(None, ('experts', 'context', 'dp'))
- gains_grad: float32 [2, 1024, 2], P(None, ('experts', 'context', 'dp'))
- rel_table_grad: float32 [2, 512], P(None, ('experts', 'context', 'dp'))
- expert_in_grad: float32 [2, 4, 1024, 5632], P(None, 'experts', ('context', 'dp'))
- expert_out_grad: float32 [2, 4, 1024, 2816], P(None, 'experts', ('context', 'dp'))
The draws below stay inside these ranges and needn't reach their ends.
Inputs may be any that keep to these rules, and one draw needn't show every extreme that they name: `doc_starts`: each row holds the document starts of one sequence, not falling, the first 0; equal values mark empty documents. `expert_ids`: the two experts of a token differ; within each aligned block of 256 tokens no expert is named more than 160 times.
All inputs are finite; a program needn't handle non-finite values.
Results may differ from the reference program's by a relative error of at most 0.023.
Values may be sent and summed in bfloat16 or wider, within the bound.
No kernel may reach another device: no remote copies, remote signals or barrier semaphores. Data moves between devices by JAX's collectives and lax.ppermute only.
A program may use at most 384 MiB of HBM per device.

```python
import math
import jax
import jax.numpy as jnp
import numpy as np
from jax import lax

D = 1024
HEADS = 16
HEAD_DIM = 64
FF = 2816
BUCKETS = 32
MAX_DISTANCE = 128
LAYERS = 2
TOK_DEV = 256
EXPERTS = 4
SEQ = 1024
SEQS = 8
CAPACITY = 160


def draw_doc_starts(key, part):
    key = jax.random.fold_in(key, 7)
    subkeys = jax.random.split(key, 4)
    first_end = jax.random.randint(subkeys[0], (SEQS, 1), 1, TOK_DEV // 2)
    last_start = jax.random.randint(subkeys[1], (SEQS, 1), SEQ - TOK_DEV // 2, SEQ)
    early_starts = jax.random.randint(subkeys[2], (SEQS, 2), 0, first_end)
    late_starts = jax.random.randint(subkeys[3], (SEQS, 3), last_start, SEQ)
    joined = jnp.concatenate([jnp.zeros((SEQS, 1), jnp.int32), early_starts, first_end, last_start, late_starts], 1)
    return jnp.sort(joined, 1).astype(jnp.int32)


def level_of(own_key, extent, shards, smallest, top_value):
    level = 1.0
    for position, shards_of in shards:
        heights = jax.random.uniform(jax.random.fold_in(jax.random.fold_in(own_key, 6), position), (shards_of,), jnp.float32, smallest / len(shards), top_value / len(shards))
        level = level * jnp.repeat(jnp.exp(heights), extent[position] // shards_of).reshape((-1,) + (1,) * (len(extent) - 1 - position))
    return level


def deal_out(stream_key, own, number, rows, count, top, reach, skew):
    sequence = jax.random.permutation(stream_key, count)
    heavy_load, ordinary = shares(count, rows * top, reach, skew, True), shares(count, rows * top, reach, skew, False)
    places = jnp.arange(count)

    def named(sizes, offset_by):
        used = int((sizes > 0).sum())
        fixed = max(1, used // 4)
        moved = fixed + (places - fixed + offset_by * (used - fixed)) % max(1, count - fixed)
        return jnp.zeros((count,), jnp.int32).at[sequence[jnp.where(places < fixed, places, moved)]].set(jnp.asarray(sizes, jnp.int32))

    sizes = jnp.where(number % 4 == 0, named(heavy_load, number // 4), named(ordinary, number - number // 4 - 1))
    mixed = jax.random.permutation(jax.random.fold_in(own, 3), count)
    donor, receiver = mixed[0:count // 2 * 2:2], mixed[1:count // 2 * 2:2]
    margin = jnp.minimum(sizes[donor] - 1, reach - sizes[receiver]) // 2
    margin = jnp.where((donor == sequence[0]) | (receiver == sequence[0]) | (sizes[receiver] == 0), 0, jnp.maximum(margin, 0))
    moved = jax.random.randint(jax.random.fold_in(own, 4), (count // 2,), 0, 1 << 20) % (margin + 1)
    sizes = sizes.at[donor].add(-moved).at[receiver].add(moved)
    items = jnp.searchsorted(jnp.cumsum(sizes), jnp.arange(rows * top), side="right").astype(jnp.int32)
    grid = items.reshape(top, rows).T
    grid = grid[jax.random.permutation(jax.random.fold_in(own, 1), rows)]
    offset_by = jax.random.randint(jax.random.fold_in(own, 2), (rows, 1), 0, top)
    return jnp.take_along_axis(grid, (jnp.arange(top)[None, :] + offset_by) % top, axis=1)


def shares(count, total, bound, lean, full):
    loads = [(1 << 20) // math.isqrt(grade ** lean) + 1 for grade in range(1, count + 1)]
    largest = bound if full else min(bound, max(-(-total // count), total * loads[0] // sum(loads)))
    least = 1 if total - largest >= count - 1 else 0
    given, spare = [largest] + [least] * (count - 1), total - largest - least * (count - 1)
    while spare > 0:
        candidates = [i for i in range(1, count) if given[i] < largest] or [i for i in range(1, count) if given[i] < bound]
        pool, remaining = sum([loads[i] for i in candidates]), spare
        for i in candidates:
            more = min(bound - given[i], max(1, remaining * loads[i] // pool), spare)
            given[i] = given[i] + more
            spare = spare - more
    return np.array(given)


def noise(key, dims, deviation, most, shards=(), kind=jnp.bfloat16):
    drawn = deviation * jax.random.normal(key, dims, jnp.float32)
    if shards:
        drawn = drawn * level_of(key, dims, shards, -0.22, 0.18)
    return jnp.clip(drawn, -most, most).astype(kind)


def setup_inputs(seed: int = 0) -> dict:
    keys = jax.random.split(jax.random.key(seed), 12)
    tokens = noise(keys[0], (SEQS, SEQ, D), 1.0, 6.0, ((0, 8), (1, 4)))
    doc_starts = draw_doc_starts(jax.random.fold_in(keys[11], 71), 0)
    expert_ids_keys = jax.random.split(jax.random.fold_in(keys[2], 1), SEQS * SEQ // TOK_DEV)
    expert_ids_turns = jax.random.permutation(jax.random.fold_in(keys[2], 3), SEQS * SEQ // TOK_DEV)
    expert_ids = jax.vmap(lambda own, number: deal_out(jax.random.fold_in(keys[2], 2), own, number, TOK_DEV, EXPERTS, 2, CAPACITY, 1))(expert_ids_keys, expert_ids_turns).reshape((SEQS, SEQ, 2))
    attn_in = noise(keys[3], (LAYERS, D, 3 * D), D ** -0.5, 0.1875, ((1, 32),))
    attn_out = noise(keys[4], (LAYERS, D, D), (D // 32) ** -0.5, 1.0, ((1, 32),))
    router = noise(keys[5], (LAYERS, D, EXPERTS), (4 * D) ** -0.5, 0.09375, ((1, 32),))
    gains = jnp.clip(1.0 + 0.18 * jax.random.normal(keys[6], (LAYERS, D, 2), jnp.float32), 0.099609375, 1.8984375).astype(jnp.bfloat16)
    rel_table = noise(keys[7], (LAYERS, BUCKETS * HEADS), 1.0, 4.0, ((1, 32),))
    expert_in = noise(keys[8], (LAYERS, EXPERTS, D, 2 * FF), D ** -0.5, 0.1875, ((1, 4),))
    expert_out = noise(keys[9], (LAYERS, EXPERTS, D, FF), FF ** -0.5, 0.109375, ((1, 4),))
    out_grad = noise(keys[10], (SEQS, SEQ, D), 1.0, 6.0, ((0, 8), (1, 4)))
    return dict(tokens=tokens, doc_starts=doc_starts, expert_ids=expert_ids, attn_in=attn_in, attn_out=attn_out, router=router, gains=gains, rel_table=rel_table, expert_in=expert_in, expert_out=expert_out, out_grad=out_grad)


EPSILON = 1e-06
NEGATIVE = -1e+30
SCORE_SCALE = 0.125

@jax.custom_vjp
def low(v):
    return lax.optimization_barrier(v.astype(jnp.bfloat16)).astype(jnp.float32)

@jax.custom_vjp
def low_back(v):
    return v

def low_keep(v):
    return (low(v), None)

def low_pass(kept, grad):
    return (grad,)

def back_keep(v):
    return (v, None)

def back_low(kept, grad):
    return (low(grad),)
low.defvjp(low_keep, low_pass)
low_back.defvjp(back_keep, back_low)

def bucket_bounds(bucket_count, far_reach):
    half_count = bucket_count // 2
    bounds = list(range(1, half_count + 1))
    for section_index in range(1, half_count):
        bounds.append(int(math.ceil(half_count * (far_reach / half_count) ** (section_index / half_count))))
    return np.array(bounds, np.int32)

def bucket_of(distance):
    bounds = jnp.asarray(bucket_bounds(BUCKETS, MAX_DISTANCE))
    return lax.optimization_barrier(jnp.sum((distance[..., None] >= bounds).astype(jnp.int32), -1))

def distance_bias(bias_table, length):
    places = jnp.arange(length, dtype=jnp.int32)
    onehot_rows = (bucket_of(places)[:, None] == jnp.arange(BUCKETS, dtype=jnp.int32)[None, :]).astype(jnp.float32)
    return jnp.dot(onehot_rows, bias_table, precision=lax.Precision.HIGHEST)

def rms_norm(inputs, gain_row):
    return inputs * lax.rsqrt(lax.optimization_barrier(jnp.mean(inputs * inputs, -1, keepdims=True)) + EPSILON) * gain_row

def sequence_attention(normed, starts, w_attn_in, bias_table):
    length = normed.shape[0]
    packed = low(low_back(jnp.dot(normed, w_attn_in, precision=lax.Precision.HIGHEST)))
    queries = packed[:, :D].reshape(length, HEADS, HEAD_DIM)
    keys_all = packed[:, D:2 * D].reshape(length, HEADS, HEAD_DIM)
    values_all = packed[:, 2 * D:].reshape(length, HEADS, HEAD_DIM)
    places = jnp.arange(length, dtype=jnp.int32)
    owners = lax.optimization_barrier(jnp.sum((starts[None, :] <= places[:, None]).astype(jnp.int32), 1))
    allowed = (owners[:, None] == owners[None, :]) & (places[None, :] <= places[:, None])
    distance = jnp.maximum(places[:, None] - places[None, :], 0)
    bias_grid = jnp.take(distance_bias(bias_table, length).T, distance, axis=1)
    scores = jnp.einsum('qhd,khd->hqk', queries, keys_all, precision=lax.Precision.HIGHEST) * SCORE_SCALE + bias_grid
    scores = low_back(jnp.where(allowed[None], scores, NEGATIVE))
    row_peak = lax.optimization_barrier(jnp.max(scores, -1, keepdims=True))
    exponent = jnp.exp(scores - row_peak)
    softmax_p = exponent / lax.optimization_barrier(jnp.sum(exponent, -1, keepdims=True))
    weights = low(softmax_p)
    mixed_rows = jnp.einsum('hqk,khd->qhd', weights, values_all, precision=lax.Precision.HIGHEST).reshape(length, D)
    return low(low_back(mixed_rows))

def mixture(normed, w_router, w_expert_in, w_expert_out, expert_ids):
    experts_total = w_router.shape[1]
    blocks = normed.shape[0] * normed.shape[1] // TOK_DEV
    logits = jnp.dot(normed, w_router, precision=lax.Precision.HIGHEST)
    softmax_p = jax.nn.softmax(logits, -1)
    pick_table = (expert_ids[..., None] == jnp.arange(experts_total, dtype=jnp.int32)).astype(jnp.float32)
    picked = lax.optimization_barrier(jnp.sum(softmax_p[..., None, :] * pick_table, -1))
    gate_values = (picked / lax.optimization_barrier(jnp.sum(picked, -1, keepdims=True))).reshape(blocks, TOK_DEV, 2)
    chosen = expert_ids.reshape(blocks, TOK_DEV, 2)
    flat_hits = (chosen.reshape(blocks, TOK_DEV * 2)[..., None] == jnp.arange(experts_total, dtype=jnp.int32)).astype(jnp.int32)
    slot_index = (lax.optimization_barrier(jnp.sum(flat_hits * jnp.cumsum(flat_hits, 1), -1)) - 1).reshape(blocks, TOK_DEV, 2)
    block_index = jnp.broadcast_to(jnp.arange(blocks, dtype=jnp.int32)[:, None], (blocks, TOK_DEV))
    rows_low = low(normed).reshape(blocks, TOK_DEV, D)
    buffer = jnp.zeros((experts_total, blocks, CAPACITY, D), rows_low.dtype)
    for route_index in range(2):
        buffer = buffer.at[chosen[..., route_index], block_index, slot_index[..., route_index]].add(low_back(rows_low))

    def expert_rows(expert_item):
        row_block, w_in, w_out = expert_item
        inner_rows = low_back(jnp.dot(row_block, w_in, precision=lax.Precision.HIGHEST))
        hidden = low(jax.nn.gelu(inner_rows[:, :FF], approximate=True) * inner_rows[:, FF:])
        return low(low_back(jnp.dot(hidden, w_out.T, precision=lax.Precision.HIGHEST)))
    produced = lax.map(jax.checkpoint(expert_rows), (buffer.reshape(experts_total, blocks * CAPACITY, D), w_expert_in, w_expert_out))
    produced = produced.reshape(experts_total, blocks, CAPACITY, D)
    combined = jnp.zeros(rows_low.shape, rows_low.dtype)
    for route_index in range(2):
        combined = combined + gate_values[..., route_index, None] * produced[chosen[..., route_index], block_index, slot_index[..., route_index]]
    return combined.reshape(normed.shape)

def one_layer(stream, layer_weights, doc_starts, expert_ids):
    w_attn_in, w_attn_out, w_router, w_gains, w_table, w_expert_in, w_expert_out = layer_weights
    bias_table = w_table.reshape(BUCKETS, HEADS)
    normed = low(rms_norm(stream, w_gains[:, 0]))

    def per_sequence(pair_item):
        return sequence_attention(pair_item[0], pair_item[1], w_attn_in, bias_table)
    mixed_rows = lax.map(jax.checkpoint(per_sequence), (normed, doc_starts))
    middle = stream + low_back(jnp.dot(mixed_rows, w_attn_out, precision=lax.Precision.HIGHEST))
    return middle + mixture(rms_norm(middle, w_gains[:, 1]), w_router, w_expert_in, w_expert_out, expert_ids)

def reference(tokens, doc_starts, expert_ids, attn_in, attn_out, router, gains, rel_table, expert_in, expert_out, out_grad):

    def forward(stream, w_attn_in, w_attn_out, w_router, w_gains, w_table, w_expert_in, w_expert_out):
        for layer_index in range(LAYERS):
            layer_weights = (w_attn_in[layer_index], w_attn_out[layer_index], w_router[layer_index], w_gains[layer_index], w_table[layer_index], w_expert_in[layer_index], w_expert_out[layer_index])
            stream = one_layer(stream, layer_weights, doc_starts, expert_ids)
        return stream
    result, pull_back = jax.vjp(forward, tokens.astype(jnp.float32), attn_in.astype(jnp.float32), attn_out.astype(jnp.float32), router.astype(jnp.float32), gains.astype(jnp.float32), rel_table.astype(jnp.float32), expert_in.astype(jnp.float32), expert_out.astype(jnp.float32))
    gradients = pull_back(out_grad.astype(jnp.float32))
    return (result.astype(jnp.bfloat16), gradients[0], gradients[1], gradients[2], gradients[3], gradients[4], gradients[5], gradients[6], gradients[7])
```

```python
import math

import jax
import jax.numpy as jnp
import numpy as np
from jax import lax
from jax.experimental import pallas as pl
from jax.experimental.pallas import tpu as pltpu
from jax.sharding import PartitionSpec as P

D = 1024
HEADS = 16
HEAD_DIM = 64
FF = 2816
BUCKETS = 32
MAX_DISTANCE = 128
LAYERS = 2
EPSILON = 1e-06
NEGATIVE = -1e30
SCORE_SCALE = 0.125
ALL = ("experts", "context", "dp")
GROUP = 4
OWN = HEADS // GROUP
OWN_COLS = OWN * HEAD_DIM
PACKED = 3 * OWN_COLS
LANES = 128
REACH = 512
FF_TILE = 256
FF_STEPS = FF // FF_TILE
MIB = 1 << 20

bf16 = jnp.bfloat16
f32 = jnp.float32


def bucket_bounds(bucket_count, far_reach):
    half_count = bucket_count // 2
    bounds = list(range(1, half_count + 1))
    for section_index in range(1, half_count):
        bounds.append(
            int(math.ceil(half_count * (far_reach / half_count) ** (section_index / half_count)))
        )
    return np.array(bounds, np.int32)


def bucket_hits():
    distance = np.arange(REACH)
    bucket = (distance[:, None] >= bucket_bounds(BUCKETS, MAX_DISTANCE)).sum(-1)
    return (np.arange(BUCKETS)[:, None] == bucket[None, :]).astype(np.float32)


def dot(a, b, ca, cb, precision=None):
    return lax.dot_general(
        a, b, (((ca,), (cb,)), ((), ())), precision=precision, preferred_element_type=f32
    )


def whole_call(body, out_shape, args, *, flops=0, limit=48, scratch=(), smem=0, name=None):
    specs = [pl.BlockSpec(memory_space=pltpu.SMEM)] * smem + [
        pl.BlockSpec(memory_space=pltpu.VMEM)
    ] * (len(args) - smem)
    outs = tuple(out_shape)
    moved = sum(a.size * a.dtype.itemsize for a in list(args) + list(outs))
    return pl.pallas_call(
        body,
        out_shape=outs,
        in_specs=specs,
        out_specs=tuple(pl.BlockSpec(memory_space=pltpu.VMEM) for _ in outs),
        scratch_shapes=list(scratch),
        compiler_params=pltpu.CompilerParams(vmem_limit_bytes=limit * MIB),
        cost_estimate=pl.CostEstimate(
            flops=int(flops), bytes_accessed=int(moved), transcendentals=0
        ),
        name=name,
    )(*args)


def shape(dims, dtype):
    return jax.ShapeDtypeStruct(dims, dtype)


def rms_scale(inputs):
    return lax.rsqrt(jnp.mean(inputs * inputs, -1, keepdims=True) + EPSILON)


def norm_back(inputs, gain_row, upstream):
    inverse = rms_scale(inputs)
    scaled = upstream * gain_row
    inner_mean = jnp.mean(inputs * scaled, -1, keepdims=True)
    grad_inputs = inverse * scaled - inputs * (inverse * inverse * inverse) * inner_mean
    grad_gain = jnp.sum(upstream * inputs * inverse, 0, keepdims=True)
    return grad_inputs, grad_gain


def near_bias(bias_ref, head, rows):
    row = bias_ref[head : head + 1, :]
    return pltpu.roll(jnp.broadcast_to(row, (rows, REACH)), 0, 1, stride=1, stride_axis=0)


def masked_scores(keys, queries, near, low, key_block, query_block, rows):
    scores = dot(keys, queries, 1, 1)
    key_place = lax.broadcasted_iota(jnp.int32, (rows, rows), 0)
    seen = key_place >= low - key_block * rows
    if key_block == query_block:
        scores = scores + near[:, :rows]
        seen = seen & (key_place <= lax.broadcasted_iota(jnp.int32, (rows, rows), 1))
    elif key_block == query_block - 1:
        scores = scores + near[:, rows:]
    return jnp.where(seen, scores, NEGATIVE)


def attention_forward_body(
    place_ref, n0, n1, n2, n3, w_ref, bias_ref, low_ref, wo_ref,
    packed_ref, log_ref, mixed_ref, keep_ref, send_ref,
):
    me = place_ref[0]
    rows = n0.shape[0]
    for r, piece in enumerate((n0, n1, n2, n3)):
        packed_ref[r * rows : (r + 1) * rows, :] = dot(piece[...], w_ref[...], 1, 0).astype(bf16)
    lane = lax.broadcasted_iota(jnp.int32, (rows, LANES), 1)
    starts = [pl.multiple_of((b ^ me) * rows, rows) for b in range(GROUP)]
    for pair in range(OWN // 2):
        at = pair * LANES

        def part(b, which):
            column = which * OWN_COLS + at
            return packed_ref[pl.ds(starts[b], rows), column : column + LANES]

        sides = [(lane // HEAD_DIM) == side for side in range(2)]
        nears = [near_bias(bias_ref, pair * 2 + side, rows) for side in range(2)]
        for qb in range(GROUP):
            low = low_ref[:, qb * rows : (qb + 1) * rows]
            queries = part(qb, 0) * SCORE_SCALE
            total = None
            for side in range(2):
                mine = jnp.where(sides[side], queries, 0).astype(bf16)
                tiles = [
                    masked_scores(part(kb, 1), mine, nears[side], low, kb, qb, rows)
                    for kb in range(qb + 1)
                ]
                peak = jnp.max(tiles[0], 0, keepdims=True)
                for tile in tiles[1:]:
                    peak = jnp.maximum(peak, jnp.max(tile, 0, keepdims=True))
                weight_sum = jnp.zeros((1, rows), f32)
                out = jnp.zeros((LANES, rows), f32)
                for kb, tile in enumerate(tiles):
                    power = jnp.exp(tile - peak)
                    weight_sum = weight_sum + jnp.sum(power, 0, keepdims=True)
                    values = jnp.where(sides[side], part(kb, 2), 0).astype(bf16)
                    out = out + dot(values, power.astype(bf16), 0, 0)
                out = out / weight_sum
                total = out if total is None else total + out
                head = pair * 2 + side
                log_ref[head : head + 1, qb * rows : (qb + 1) * rows] = peak + jnp.log(weight_sum)
            mixed_ref[pl.ds(starts[qb], rows), at : at + LANES] = total.T.astype(bf16)
    width = wo_ref.shape[2]
    for r, (target, offset) in enumerate(
        ((keep_ref, 0), (send_ref, 0), (keep_ref, rows), (send_ref, rows))
    ):
        mixed = mixed_ref[r * rows : (r + 1) * rows, :]
        for q in range(wo_ref.shape[0]):
            target[offset : offset + rows, q * width : (q + 1) * width] = dot(
                mixed, wo_ref[q], 1, 0
            ).astype(target.dtype)


def attention_forward(place, pieces, w_in, bias_rows, low, w_out):
    rows = pieces[0].shape[0]
    total = GROUP * rows
    return whole_call(
        attention_forward_body,
        (
            shape((total, PACKED), bf16),
            shape((8, total), f32),
            shape((total, OWN_COLS), bf16),
            shape((2 * rows, D), f32),
            shape((2 * rows, D), bf16),
        ),
        [place, *pieces, w_in, bias_rows, low, w_out],
        smem=1,
        flops=2 * total * D * (PACKED + OWN_COLS) + 2 * total * total * OWN_COLS * 2,
        name="attention_forward",
    )


def attention_backward_body(
    place_ref, d0, d1, d2, d3, w_ref, bias_ref, low_ref, wo_ref, packed_ref, log_ref,
    grad_packed_ref, keep_ref, send_ref, table_ref, grad_mixed_ref, dk_ref, dv_ref,
):
    me = place_ref[0]
    rows = d0.shape[0]
    width = wo_ref.shape[2]
    for r, piece in enumerate((d0, d1, d2, d3)):
        got = jnp.zeros((rows, OWN_COLS), f32)
        for q in range(wo_ref.shape[0]):
            got = got + dot(piece[:, q * width : (q + 1) * width], wo_ref[q], 1, 1)
        grad_mixed_ref[r * rows : (r + 1) * rows, :] = got.astype(bf16)
    lane = lax.broadcasted_iota(jnp.int32, (rows, LANES), 1)
    starts = [pl.multiple_of((b ^ me) * rows, rows) for b in range(GROUP)]
    table_ref[...] = jnp.zeros(table_ref.shape, f32)
    for pair in range(OWN // 2):
        at = pair * LANES

        def part(b, which):
            column = which * OWN_COLS + at
            return packed_ref[pl.ds(starts[b], rows), column : column + LANES]

        sides = [(lane // HEAD_DIM) == side for side in range(2)]
        nears = [near_bias(bias_ref, pair * 2 + side, rows) for side in range(2)]
        diag = [jnp.zeros((rows, rows), f32) for _ in range(2)]
        before = [jnp.zeros((rows, rows), f32) for _ in range(2)]
        far = [jnp.zeros((1, rows), f32) for _ in range(2)]
        dk_ref[...] = jnp.zeros(dk_ref.shape, f32)
        dv_ref[...] = jnp.zeros(dv_ref.shape, f32)
        for qb in range(GROUP):
            low = low_ref[:, qb * rows : (qb + 1) * rows]
            queries = part(qb, 0) * SCORE_SCALE
            upstream = grad_mixed_ref[pl.ds(starts[qb], rows), at : at + LANES]
            grad_queries = jnp.zeros((LANES, rows), f32)
            for side in range(2):
                head = pair * 2 + side
                mine = jnp.where(sides[side], queries, 0).astype(bf16)
                above = jnp.where(sides[side], upstream, 0).astype(bf16)
                log_total = log_ref[head : head + 1, qb * rows : (qb + 1) * rows]
                probs, grads = [], []
                row_dot = jnp.zeros((1, rows), f32)
                for kb in range(qb + 1):
                    scores = masked_scores(part(kb, 1), mine, nears[side], low, kb, qb, rows)
                    prob = jnp.exp(scores - log_total)
                    grad = dot(part(kb, 2), above, 1, 1)
                    row_dot = row_dot + jnp.sum(prob * grad, 0, keepdims=True)
                    probs.append(prob)
                    grads.append(grad)
                for kb in range(qb + 1):
                    grad_score = probs[kb] * (grads[kb] - row_dot)
                    if kb == qb:
                        diag[side] = diag[side] + grad_score
                    elif kb == qb - 1:
                        before[side] = before[side] + grad_score
                    else:
                        far[side] = far[side] + jnp.sum(grad_score, 0, keepdims=True)
                    grad_low = grad_score.astype(bf16)
                    keys = jnp.where(sides[side], part(kb, 1), 0).astype(bf16)
                    grad_queries = grad_queries + dot(keys, grad_low, 0, 0)
                    span = slice(kb * rows, (kb + 1) * rows)
                    dk_ref[span, :] += dot(grad_low, mine, 1, 0)
                    dv_ref[span, :] += dot(probs[kb].astype(bf16), above, 1, 0)
            grad_packed_ref[pl.ds(starts[qb], rows), at : at + LANES] = (
                grad_queries.T * SCORE_SCALE
            ).astype(bf16)
        for kb in range(GROUP):
            span = slice(kb * rows, (kb + 1) * rows)
            for which, source in ((1, dk_ref), (2, dv_ref)):
                column = which * OWN_COLS + at
                grad_packed_ref[pl.ds(starts[kb], rows), column : column + LANES] = source[
                    span, :
                ].astype(bf16)
        distance = lax.broadcasted_iota(jnp.int32, (1, REACH), 1)
        for side in range(2):
            head = pair * 2 + side
            skewed = jnp.concatenate([diag[side], before[side]], 1)
            row_index = lax.broadcasted_iota(jnp.int32, (rows, REACH), 0)
            step = 1
            while step < rows:
                skewed = jnp.where(
                    (row_index & step) != 0, pltpu.roll(skewed, REACH - step, 1), skewed
                )
                step *= 2
            by_distance = jnp.sum(skewed, 0, keepdims=True)
            far_sum = jnp.sum(far[side], 1, keepdims=True)
            table_ref[head : head + 1, :] = by_distance + jnp.where(
                distance == REACH - 1, far_sum, 0.0
            )
    for r, (target, offset) in enumerate(
        ((keep_ref, 0), (send_ref, 0), (keep_ref, rows), (send_ref, rows))
    ):
        target[offset : offset + rows, :] = dot(
            grad_packed_ref[r * rows : (r + 1) * rows, :], w_ref[...], 1, 1
        ).astype(target.dtype)


def attention_backward(place, pieces, w_in, bias_rows, low, w_out, packed, log_total):
    rows = pieces[0].shape[0]
    total = GROUP * rows
    return whole_call(
        attention_backward_body,
        (
            shape((total, PACKED), bf16),
            shape((2 * rows, D), f32),
            shape((2 * rows, D), bf16),
            shape((8, REACH), f32),
        ),
        [place, *pieces, w_in, bias_rows, low, w_out, packed, log_total],
        smem=1,
        scratch=[
            pltpu.VMEM((total, OWN_COLS), bf16),
            pltpu.VMEM((total, LANES), f32),
            pltpu.VMEM((total, LANES), f32),
        ],
        flops=2 * total * D * (PACKED + OWN_COLS) + 2 * total * total * OWN_COLS * 5,
        name="attention_backward",
    )


def dense_grad_body(n0, n1, n2, n3, d0, d1, d2, d3, grad_packed_ref, mixed_ref, out_in, out_out):
    rows = n0.shape[0]
    total_in = None
    total_out = None
    for r, (normed, upstream) in enumerate(zip((n0, n1, n2, n3), (d0, d1, d2, d3))):
        span = slice(r * rows, (r + 1) * rows)
        one = dot(normed[...], grad_packed_ref[span, :], 0, 0)
        two = dot(mixed_ref[span, :], upstream[...], 0, 0)
        total_in = one if total_in is None else total_in + one
        total_out = two if total_out is None else total_out + two
    out_in[...] = total_in.astype(out_in.dtype)
    out_out[...] = total_out.astype(out_out.dtype)


def dense_grads(normed, upstream, grad_packed, mixed):
    rows = normed[0].shape[0]
    return whole_call(
        dense_grad_body,
        (shape((D, PACKED), bf16), shape((OWN_COLS, D), bf16)),
        [*normed, *upstream, grad_packed, mixed],
        flops=2 * GROUP * rows * D * (PACKED + OWN_COLS),
        name="dense_grads",
    )


def dispatch_grid(dest_rows, slots, tokens):
    place = lax.broadcasted_iota(jnp.int32, (slots, tokens), 0)
    first = place == dest_rows[0:1, :]
    second = place == dest_rows[1:2, :]
    return first, second


def one_hot(flags):
    return jnp.where(flags, 1.0, 0.0).astype(bf16)


def collect_grid(meta, slots):
    tokens = meta.shape[0]
    place = lax.broadcasted_iota(jnp.int32, (tokens, slots), 1)
    first = place == meta[:, 0:1].astype(jnp.int32)
    second = place == meta[:, 1:2].astype(jnp.int32)
    return first, second


def scatter_grads(upstream, meta, dest_rows, slots):
    tokens = upstream.shape[0]
    first, second = dispatch_grid(dest_rows, slots, tokens)
    return (
        dot(one_hot(first), (meta[:, 2:3] * upstream).astype(bf16), 1, 0)
        + dot(one_hot(second), (meta[:, 3:4] * upstream).astype(bf16), 1, 0)
    ).astype(bf16)


def route_body(experts, capacity, last, *refs):
    if last:
        (x_ref, keep_ref, recv_ref, far_ref, gain_ref, router_ref, ids_ref, idst_ref, grad_ref,
         middle_ref, rows_ref, soft_ref, meta_ref, dest_ref, sent_ref) = refs
    else:
        (x_ref, keep_ref, recv_ref, far_ref, gain_ref, router_ref, ids_ref, idst_ref,
         middle_ref, rows_ref, soft_ref, meta_ref, dest_ref) = refs
    tokens = x_ref.shape[0]
    slots = experts * capacity
    middle = (
        x_ref[...].astype(f32)
        + keep_ref[:tokens, :]
        + recv_ref[:tokens, :].astype(f32)
        + far_ref[...].astype(f32)
    )
    middle_ref[...] = middle
    normed = middle * rms_scale(middle) * gain_ref[...]
    lane = lax.broadcasted_iota(jnp.int32, (tokens, LANES), 1)
    logits = dot(normed, router_ref[...], 1, 1, lax.Precision.HIGHEST)
    logits = jnp.where(lane < experts, logits, NEGATIVE)
    power = jnp.exp(logits - jnp.max(logits, -1, keepdims=True))
    soft = power / jnp.sum(power, -1, keepdims=True)
    soft_ref[...] = soft
    ids = ids_ref[...]
    hit0 = lane == ids[:, 0:1]
    hit1 = lane == ids[:, 1:2]
    picked0 = jnp.sum(jnp.where(hit0, soft, 0.0), -1, keepdims=True)
    picked1 = jnp.sum(jnp.where(hit1, soft, 0.0), -1, keepdims=True)
    pick_total = picked0 + picked1
    down = lax.broadcasted_iota(jnp.int32, (tokens, tokens), 0)
    across = lax.broadcasted_iota(jnp.int32, (tokens, tokens), 1)
    counts = dot(one_hot(across < down), one_hot(hit0 | hit1), 1, 0)
    dest0 = ids[:, 0:1].astype(f32) * capacity + jnp.sum(
        jnp.where(hit0, counts, 0.0), -1, keepdims=True
    )
    dest1 = ids[:, 1:2].astype(f32) * capacity + jnp.sum(
        jnp.where(hit1, counts, 0.0), -1, keepdims=True
    )
    fields = (dest0, dest1, picked0 / pick_total, picked1 / pick_total, pick_total)
    meta = jnp.zeros((tokens, LANES), f32)
    for index, field in enumerate(fields):
        meta = jnp.where(lane == index, field, meta)
    meta_ref[...] = meta
    idst = idst_ref[...]
    sub = lax.broadcasted_iota(jnp.int32, (16, tokens), 0)
    row0 = sub == idst[0:1, :]
    row1 = sub == idst[1:2, :]
    row_counts = dot(one_hot(row0 | row1), one_hot(down < across), 1, 0)
    destr0 = idst[0:1, :] * capacity + jnp.sum(
        jnp.where(row0, row_counts, 0.0), 0, keepdims=True
    ).astype(jnp.int32)
    destr1 = idst[1:2, :] * capacity + jnp.sum(
        jnp.where(row1, row_counts, 0.0), 0, keepdims=True
    ).astype(jnp.int32)
    dest_rows = jnp.where(
        lax.broadcasted_iota(jnp.int32, (8, tokens), 0) == 0, destr0, destr1
    )
    dest_ref[...] = dest_rows
    first, second = dispatch_grid(dest_rows, slots, tokens)
    rows_ref[...] = dot(one_hot(first | second), normed.astype(bf16), 1, 0).astype(bf16)
    if last:
        sent_ref[...] = scatter_grads(grad_ref[...].astype(f32), meta, dest_rows, slots)


def route(experts, capacity, x, keep, recv, far, gain, router, ids, idst, grad=None):
    tokens = x.shape[0]
    slots = experts * capacity
    outs = [
        shape((tokens, D), f32),
        shape((slots, D), bf16),
        shape((tokens, LANES), f32),
        shape((tokens, LANES), f32),
        shape((8, tokens), jnp.int32),
    ]
    args = [x, keep, recv, far, gain, router, ids, idst]
    if grad is not None:
        outs.append(shape((slots, D), bf16))
        args.append(grad)

    def body(*refs):
        route_body(experts, capacity, grad is not None, *refs)

    return whole_call(body, outs, args, flops=2 * slots * tokens * D, name="route")


def combine_body(last, *refs):
    if last:
        middle_ref, back_ref, meta_ref, out_ref = refs
    else:
        middle_ref, back_ref, meta_ref, gain_ref, out_ref, normed_ref = refs
    meta = meta_ref[...]
    first, second = collect_grid(meta, back_ref.shape[0])
    x = (
        middle_ref[...]
        + meta[:, 2:3] * dot(one_hot(first), back_ref[...], 1, 0)
        + meta[:, 3:4] * dot(one_hot(second), back_ref[...], 1, 0)
    )
    out_ref[...] = x.astype(out_ref.dtype)
    if not last:
        normed_ref[...] = (x * rms_scale(x) * gain_ref[...]).astype(bf16)


def combine(middle, back, meta, gain=None):
    tokens = middle.shape[0]
    args = [middle, back, meta]
    outs = [shape((tokens, D), bf16 if gain is None else f32)]
    if gain is not None:
        args.append(gain)
        outs.append(shape((tokens, D), bf16))

    def body(*refs):
        combine_body(gain is None, *refs)

    return whole_call(
        body, outs, args, flops=4 * tokens * D * back.shape[0], name="combine"
    )


def expert_token_back_body(
    experts, back_ref, came_ref, g_ref, middle_ref, soft_ref, meta_ref, ids_ref, gain_ref,
    router_ref, dmiddle_ref, dattn_ref, small_ref,
):
    meta = meta_ref[...]
    g = g_ref[...].astype(f32)
    slots = back_ref.shape[0]
    first, second = collect_grid(meta, slots)
    grad_gate0 = jnp.sum(g * dot(one_hot(first), back_ref[...], 1, 0), -1, keepdims=True)
    grad_gate1 = jnp.sum(g * dot(one_hot(second), back_ref[...], 1, 0), -1, keepdims=True)
    grad_normed = dot(one_hot(first | second), came_ref[...], 1, 0)
    gap = (grad_gate0 - grad_gate1) / meta[:, 4:5]
    ids = ids_ref[...]
    lane = lax.broadcasted_iota(jnp.int32, meta.shape, 1)
    grad_soft = jnp.where(lane == ids[:, 0:1], meta[:, 3:4] * gap, 0.0) + jnp.where(
        lane == ids[:, 1:2], -meta[:, 2:3] * gap, 0.0
    )
    soft = soft_ref[...]
    grad_logits = soft * (grad_soft - jnp.sum(soft * grad_soft, -1, keepdims=True))
    middle = middle_ref[...]
    normed = middle * rms_scale(middle) * gain_ref[...]
    grad_router = dot(grad_logits.T, normed, 1, 0, lax.Precision.HIGHEST)
    grad_normed = grad_normed + dot(
        grad_logits, router_ref[...], 1, 0, lax.Precision.HIGHEST
    )
    grad_branch, grad_gain = norm_back(middle, gain_ref[...], grad_normed)
    dmiddle = g + grad_branch
    dmiddle_ref[...] = dmiddle
    dattn_ref[...] = dmiddle.astype(bf16)
    small_ref[:16, :] = grad_router[:16, :]
    small_ref[16:24, :] = jnp.broadcast_to(grad_gain, (8, D))


def expert_token_back(experts, back, came, g, middle, soft, meta, ids, gain, router):
    tokens = middle.shape[0]

    def body(*refs):
        expert_token_back_body(experts, *refs)

    return whole_call(
        body,
        (shape((tokens, D), f32), shape((tokens, D), bf16), shape((24, D), f32)),
        [back, came, g, middle, soft, meta, ids, gain, router],
        flops=6 * tokens * D * back.shape[0],
        name="expert_token_back",
    )


def attention_token_back_body(first_layer, *refs):
    if first_layer:
        x_ref, dmiddle_ref, keep_ref, recv_ref, far_ref, gain_ref, out_ref, small_ref = refs
    else:
        (x_ref, dmiddle_ref, keep_ref, recv_ref, far_ref, gain_ref, meta_ref, dest_ref,
         out_ref, small_ref, sent_ref) = refs
    tokens = x_ref.shape[0]
    grad_normed = (
        keep_ref[:tokens, :] + recv_ref[:tokens, :].astype(f32) + far_ref[...].astype(f32)
    )
    grad_branch, grad_gain = norm_back(x_ref[...].astype(f32), gain_ref[...], grad_normed)
    g = dmiddle_ref[...] + grad_branch
    out_ref[...] = g
    small_ref[...] = jnp.broadcast_to(grad_gain, (8, D))
    if not first_layer:
        sent_ref[...] = scatter_grads(g, meta_ref[...], dest_ref[...], sent_ref.shape[0])


def attention_token_back(x, dmiddle, keep, recv, far, gain, meta=None, dest=None, slots=0):
    tokens = x.shape[0]
    outs = [shape((tokens, D), f32), shape((8, D), f32)]
    args = [x, dmiddle, keep, recv, far, gain]
    if meta is not None:
        outs.append(shape((slots, D), bf16))
        args += [meta, dest]

    def body(*refs):
        attention_token_back_body(meta is None, *refs)

    return whole_call(
        body, outs, args, flops=4 * tokens * D * slots, name="attention_token_back"
    )


def gelu_parts(gate):
    inner = math.sqrt(2.0 / math.pi) * (gate + 0.044715 * gate * gate * gate)
    return jnp.tanh(inner)


def expert_forward_body(rows_ref, wg_ref, wu_ref, wo_ref, produced_ref, acts_ref, total_ref):
    step = pl.program_id(0)
    rows = rows_ref[...]
    gate = dot(rows, wg_ref[0, 0], 1, 0)
    up = dot(rows, wu_ref[0, 0], 1, 0)
    acts_ref[0] = gate.astype(bf16)
    acts_ref[1] = up.astype(bf16)
    hidden = (0.5 * gate * (1.0 + gelu_parts(gate)) * up).astype(bf16)
    out = dot(hidden, wo_ref[0, 0], 1, 1)

    @pl.when(step == 0)
    def _():
        total_ref[...] = out

    @pl.when(step > 0)
    def _():
        total_ref[...] += out

    @pl.when(step == FF_STEPS - 1)
    def _():
        produced_ref[...] = total_ref[...].astype(bf16)


def weight_specs(layer):
    return [
        pl.BlockSpec((1, 1, D, FF_TILE), lambda s: (layer, 0, 0, s)),
        pl.BlockSpec((1, 1, D, FF_TILE), lambda s: (layer, 0, 0, FF_STEPS + s)),
        pl.BlockSpec((1, 1, D, FF_TILE), lambda s: (layer, 0, 0, s)),
    ]


def expert_forward(layer, rows, w_in, w_out):
    count = rows.shape[0]
    return pl.pallas_call(
        expert_forward_body,
        grid=(FF_STEPS,),
        out_shape=(shape((count, D), bf16), shape((2, count, FF), bf16)),
        in_specs=[pl.BlockSpec((count, D), lambda s: (0, 0))] + weight_specs(layer),
        out_specs=(
            pl.BlockSpec((count, D), lambda s: (0, 0)),
            pl.BlockSpec((2, count, FF_TILE), lambda s: (0, 0, s)),
        ),
        scratch_shapes=[pltpu.VMEM((count, D), f32)],
        compiler_params=pltpu.CompilerParams(vmem_limit_bytes=40 * MIB),
        cost_estimate=pl.CostEstimate(
            flops=6 * count * D * FF, bytes_accessed=6 * D * FF, transcendentals=count * FF
        ),
        name="expert_forward",
    )(rows, w_in, w_in, w_out)


def expert_backward_body(
    grad_ref, acts_ref, wg_ref, wu_ref, wo_ref, drows_ref, grads_ref, total_ref
):
    step = pl.program_id(0)
    grad_hidden = dot(grad_ref[...], wo_ref[0, 0], 1, 0)
    gate = acts_ref[0].astype(f32)
    up = acts_ref[1].astype(f32)
    curve = gelu_parts(gate)
    value = 0.5 * gate * (1.0 + curve)
    slope = 0.5 * (1.0 + curve) + 0.5 * gate * (1.0 - curve * curve) * math.sqrt(
        2.0 / math.pi
    ) * (1.0 + 3.0 * 0.044715 * gate * gate)
    grad_gate = (grad_hidden * up * slope).astype(bf16)
    grad_up = (grad_hidden * value).astype(bf16)
    grads_ref[0] = grad_gate
    grads_ref[1] = grad_up
    grads_ref[2] = (value * up).astype(bf16)
    out = dot(grad_gate, wg_ref[0, 0], 1, 1) + dot(grad_up, wu_ref[0, 0], 1, 1)

    @pl.when(step == 0)
    def _():
        total_ref[...] = out

    @pl.when(step > 0)
    def _():
        total_ref[...] += out

    @pl.when(step == FF_STEPS - 1)
    def _():
        drows_ref[...] = total_ref[...].astype(bf16)


def expert_backward(layer, grad, acts, w_in, w_out):
    count = grad.shape[0]
    return pl.pallas_call(
        expert_backward_body,
        grid=(FF_STEPS,),
        out_shape=(shape((count, D), bf16), shape((3, count, FF), bf16)),
        in_specs=[
            pl.BlockSpec((count, D), lambda s: (0, 0)),
            pl.BlockSpec((2, count, FF_TILE), lambda s: (0, 0, s)),
        ]
        + weight_specs(layer),
        out_specs=(
            pl.BlockSpec((count, D), lambda s: (0, 0)),
            pl.BlockSpec((3, count, FF_TILE), lambda s: (0, 0, s)),
        ),
        scratch_shapes=[pltpu.VMEM((count, D), f32)],
        compiler_params=pltpu.CompilerParams(vmem_limit_bytes=48 * MIB),
        cost_estimate=pl.CostEstimate(
            flops=6 * count * D * FF, bytes_accessed=6 * D * FF, transcendentals=count * FF
        ),
        name="expert_backward",
    )(grad, acts, w_in, w_in, w_out)


def expert_grads_body(shares, rows_ref, grad_ref, parts_ref, out_ref, rows_t, grad_t):
    @pl.when(pl.program_id(0) == 0)
    def _():
        rows_t[...] = rows_ref[...].T
        grad_t[...] = grad_ref[...].T

    tall = D // shares
    for which in range(3):
        left = rows_t if which < 2 else grad_t
        got = dot(left[...], parts_ref[which], 1, 0).astype(bf16)
        for share in range(shares):
            out_ref[share, which] = got[share * tall : (share + 1) * tall, :]


def expert_grads(shares, rows, grad, parts):
    count = rows.shape[0]
    tall = D // shares

    def body(*refs):
        expert_grads_body(shares, *refs)

    return pl.pallas_call(
        body,
        grid=(FF_STEPS,),
        out_shape=shape((shares, 3, tall, FF), bf16),
        in_specs=[
            pl.BlockSpec((count, D), lambda s: (0, 0)),
            pl.BlockSpec((count, D), lambda s: (0, 0)),
            pl.BlockSpec((3, count, FF_TILE), lambda s: (0, 0, s)),
        ],
        out_specs=pl.BlockSpec((shares, 3, tall, FF_TILE), lambda s: (0, 0, 0, s)),
        scratch_shapes=[pltpu.VMEM((D, count), bf16), pltpu.VMEM((D, count), bf16)],
        compiler_params=pltpu.CompilerParams(vmem_limit_bytes=40 * MIB),
        cost_estimate=pl.CostEstimate(
            flops=6 * count * D * FF, bytes_accessed=6 * D * FF, transcendentals=0
        ),
        name="expert_grads",
    )(rows, grad, parts)


TWIN = [(i, i ^ 1) for i in range(GROUP)]
ACROSS = [(i, i ^ 2) for i in range(GROUP)]


def share_pieces(piece):
    across = lax.ppermute(piece, "context", ACROSS)
    twin = lax.ppermute(piece, "context", TWIN)
    return [piece, twin, across, lax.ppermute(across, "context", TWIN)]


def sum_pieces(keep, send):
    rows = keep.shape[0] // 2
    recv = lax.ppermute(send, "context", TWIN)
    other = (keep[rows:] + recv[rows:].astype(f32)).astype(bf16)
    return keep, recv, lax.ppermute(other, "context", ACROSS)


def exchange(rows):
    return lax.all_to_all(rows, "experts", split_axis=0, concat_axis=0, tiled=True)


def on_device(
    tokens, doc_starts, expert_ids, attn_in, attn_out, router, gains, rel_table,
    expert_in, expert_out, out_grad,
):
    experts = lax.axis_size("experts")
    pairs = lax.axis_size("dp")
    share = attn_in.shape[1]
    table_share = rel_table.shape[1]
    direct = share * pairs == HEAD_DIM and experts * GROUP == HEADS
    place = lax.axis_index("context").astype(jnp.int32).reshape(1)
    start_tokens = tokens[0]
    ids = expert_ids[0]
    idst = ids.T
    rows = start_tokens.shape[0]
    capacity = (10 * rows + 4 * experts - 1) // (4 * experts)
    slots = experts * capacity
    grad_in = out_grad[0]
    places = jnp.arange(GROUP * rows, dtype=jnp.int32)
    starts = doc_starts[0]
    low = jnp.max(
        jnp.where(starts[:, None] <= places[None, :], starts[:, None], 0), 0, keepdims=True
    )

    small = jnp.zeros((share, LANES), bf16)
    for layer in range(LAYERS):
        small = small.at[:, 32 * layer : 32 * layer + experts].set(router[layer])
        small = small.at[:, 32 * layer + 16 : 32 * layer + 18].set(gains[layer])
        small = small.at[0, 64 + 32 * layer : 64 + 32 * layer + table_share].set(rel_table[layer])
    split_in = attn_in.reshape(LAYERS, share, 3, OWN, GROUP, HEAD_DIM).transpose(4, 0, 1, 2, 3, 5)
    split_in = split_in.reshape(GROUP, LAYERS, share, PACKED)
    packet = jnp.concatenate(
        [split_in[:, 0], split_in[:, 1], jnp.broadcast_to(small, (GROUP, share, LANES))], -1
    )
    packet = lax.all_to_all(packet, "context", split_axis=0, concat_axis=0)
    packet = packet.reshape(GROUP * share, 2 * PACKED + LANES)

    def out_rows(layer):
        width = D // GROUP
        return jnp.concatenate(
            [attn_out[layer][:, q * width : (q + 1) * width] for q in range(GROUP)], 0
        )

    def gather(part):
        got = lax.all_gather(part, ("experts", "dp"), axis=0, tiled=False)
        return got.reshape(experts, pairs, GROUP, share, part.shape[-1])

    w_in, w_out = [], []
    small_all = None
    for layer in range(LAYERS):
        columns = [packet[:, layer * PACKED : (layer + 1) * PACKED]]
        if layer == 0:
            columns.append(packet[:, 2 * PACKED :])
        if direct:
            columns.append(out_rows(layer))
        got = gather(jnp.concatenate(columns, 1))
        w_in.append(got[..., :PACKED].transpose(0, 2, 1, 3, 4).reshape(D, PACKED))
        if layer == 0:
            small_all = got[..., PACKED : PACKED + LANES].transpose(0, 2, 1, 3, 4)
        if direct:
            w_out.append(
                got[..., -D // GROUP :].transpose(2, 0, 1, 3, 4).reshape(GROUP, OWN_COLS, D // GROUP)
            )
        else:
            full = lax.all_gather(attn_out[layer], ALL, axis=0, tiled=True)
            mine = lax.dynamic_index_in_dim(
                full.reshape(OWN, GROUP, HEAD_DIM, D), place[0], 1, keepdims=False
            )
            w_out.append(mine.reshape(OWN_COLS, GROUP, D // GROUP).transpose(1, 0, 2))
    by_feature = small_all.reshape(D, LANES).T
    hits = jnp.asarray(bucket_hits())
    gain_a, gain_b, routers, bias_rows = [], [], [], []
    for layer in range(LAYERS):
        top = 32 * layer
        gain_a.append(by_feature[top + 16 : top + 17].astype(f32))
        gain_b.append(by_feature[top + 17 : top + 18].astype(f32))
        routers.append(
            jnp.pad(by_feature[top : top + experts].astype(f32), ((0, LANES - experts), (0, 0)))
        )
        table = small_all[:, :, :, 0, 64 + top : 64 + top + table_share].reshape(
            BUCKETS, OWN, GROUP
        )
        table = lax.dynamic_index_in_dim(table, place[0], 2, keepdims=False).astype(f32)
        row = jnp.dot((table - table[-1:]).T, hits, precision=lax.Precision.HIGHEST)
        bias_rows.append(jnp.pad(row, ((0, 8 - OWN), (0, 0))))

    def first_norm(piece):
        wide = piece.astype(f32)
        return (wide * rms_scale(wide) * gain_a[0]).astype(bf16)

    pieces = [first_norm(piece) for piece in share_pieces(start_tokens)]
    x = start_tokens
    kept = []
    for layer in range(LAYERS):
        packed, log_total, mixed, keep, send = attention_forward(
            place, pieces, w_in[layer], bias_rows[layer], low, w_out[layer]
        )
        keep, recv, far = sum_pieces(keep, send)
        last = layer == LAYERS - 1
        routed = route(
            experts, capacity, x, keep, recv, far, gain_b[layer], routers[layer], ids, idst,
            grad_in if last else None,
        )
        middle, sent_rows, soft, meta, dest = routed[:5]
        arrived = exchange(sent_rows)
        if last:
            arrived_grad = exchange(routed[5])
        produced, acts = expert_forward(layer, arrived, expert_in, expert_out)
        back = exchange(produced)
        kept.append(
            (x, pieces, packed, log_total, mixed, middle, soft, meta, dest, arrived, acts, back)
        )
        if last:
            (result,) = combine(middle, back, meta)
        else:
            x, normed = combine(middle, back, meta, gain_a[layer + 1])
            pieces = share_pieces(normed)

    g = grad_in
    dense_out, expert_out_grads = [], []
    for layer in range(LAYERS - 1, -1, -1):
        x, pieces, packed, log_total, mixed, middle, soft, meta, dest, arrived, acts, back = kept[
            layer
        ]
        drows, parts = expert_backward(layer, arrived_grad, acts, expert_in, expert_out)
        came = exchange(drows)
        weight_grads = expert_grads(GROUP * pairs, arrived, arrived_grad, parts)
        expert_out_grads.insert(
            0, lax.psum_scatter(weight_grads, ("context", "dp"), scatter_dimension=0, tiled=False)
        )
        dmiddle, dattn, small_b = expert_token_back(
            experts, back, came, g, middle, soft, meta, ids, gain_b[layer], routers[layer]
        )
        grad_pieces = share_pieces(dattn)
        grad_packed, keep, send, by_distance = attention_backward(
            place, grad_pieces, w_in[layer], bias_rows[layer], low, w_out[layer], packed, log_total
        )
        keep, recv, far = sum_pieces(keep, send)
        grad_w_in, grad_w_out = dense_grads(pieces, grad_pieces, grad_packed, mixed)
        if layer > 0:
            below = kept[layer - 1]
            g, small_a, sent = attention_token_back(
                x, dmiddle, keep, recv, far, gain_a[layer], below[7], below[8], slots
            )
            arrived_grad = exchange(sent)
        else:
            g, small_a = attention_token_back(x, dmiddle, keep, recv, far, gain_a[layer])

        by_bucket = jnp.dot(hits, by_distance[:OWN].T, precision=lax.Precision.HIGHEST)
        spread = jnp.where(
            jnp.arange(GROUP)[None, None, :] == place[0], by_bucket[:, :, None], 0.0
        ).reshape(experts, GROUP, pairs, 1, table_share)
        features = jnp.concatenate([small_b[:experts], small_a[:1], small_b[16:17]], 0).T
        features = features.reshape(experts, GROUP, pairs, share, experts + 2)
        small_grad = jnp.zeros((experts, GROUP, pairs, share, LANES), f32)
        small_grad = small_grad.at[..., : experts + 2].set(features)
        small_grad = small_grad.at[..., :1, 64 : 64 + table_share].set(spread)
        pack = jnp.concatenate(
            [
                grad_w_in.reshape(experts, GROUP, pairs, share, PACKED),
                small_grad.astype(bf16),
            ],
            -1,
        ).transpose(0, 2, 1, 3, 4)
        pack = pack.reshape(experts * pairs, GROUP * share, PACKED + LANES)
        if direct:
            width = D // GROUP
            outer = grad_w_out.reshape(experts * pairs, share, GROUP, width).transpose(0, 2, 1, 3)
            pack = jnp.concatenate(
                [pack, outer.reshape(experts * pairs, GROUP * share, width)], -1
            )
        mine = lax.psum_scatter(pack, ("experts", "dp"), scatter_dimension=0, tiled=False)
        inner = mine[:, : PACKED + LANES].reshape(GROUP, share, PACKED + LANES)
        inner = lax.all_to_all(inner, "context", split_axis=0, concat_axis=0)
        g_in = inner[..., :PACKED].astype(f32).reshape(GROUP, share, 3, OWN, HEAD_DIM)
        g_in = g_in.transpose(1, 2, 3, 0, 4).reshape(share, 3 * D)
        g_small = jnp.sum(inner[..., PACKED:].astype(f32), 0)
        if direct:
            width = D // GROUP
            g_out = mine[:, -width:].astype(f32).reshape(GROUP, share, width)
            g_out = g_out.transpose(1, 0, 2).reshape(share, D)
        else:
            placed = jnp.where(
                jnp.arange(GROUP)[None, :, None, None] == place[0],
                grad_w_out.reshape(OWN, 1, HEAD_DIM, D),
                jnp.zeros((), bf16),
            ).reshape(D, D)
            g_out = lax.psum_scatter(placed, ALL, scatter_dimension=0, tiled=True).astype(f32)
        dense_out.insert(
            0,
            (
                g_in,
                g_out,
                g_small[:, :experts],
                g_small[:, experts : experts + 2],
                g_small[0, 64 : 64 + table_share],
            ),
        )
    dense = tuple(jnp.stack([entry[k] for entry in dense_out]) for k in range(5))
    tall = expert_out_grads[0].shape[1]
    wide = [entry.astype(f32) for entry in expert_out_grads]
    grad_expert_in = jnp.stack(
        [entry[:2].transpose(1, 0, 2).reshape(1, tall, 2 * FF) for entry in wide]
    )
    grad_expert_out = jnp.stack([entry[2:3] for entry in wide])
    return (result[None], g[None], *dense, grad_expert_in, grad_expert_out)


def solution(mesh):
    return jax.shard_map(
        on_device,
        mesh=mesh,
        in_specs=(
            P(("experts", "dp"), "context", None),
            P(("experts", "dp"), None),
            P(("experts", "dp"), "context", None),
            P(None, ("experts", "context", "dp"), None),
            P(None, ("experts", "context", "dp"), None),
            P(None, ("experts", "context", "dp"), None),
            P(None, ("experts", "context", "dp"), None),
            P(None, ("experts", "context", "dp")),
            P(None, "experts", None, None),
            P(None, "experts", None, None),
            P(("experts", "dp"), "context", None),
        ),
        out_specs=(
            P(("experts", "dp"), "context", None),
            P(("experts", "dp"), "context", None),
            P(None, ("experts", "context", "dp"), None),
            P(None, ("experts", "context", "dp"), None),
            P(None, ("experts", "context", "dp"), None),
            P(None, ("experts", "context", "dp"), None),
            P(None, ("experts", "context", "dp")),
            P(None, "experts", ("context", "dp"), None),
            P(None, "experts", ("context", "dp"), None),
        ),
        check_vma=False,
    )
```

```python
import math

import jax
import jax.numpy as jnp
import numpy as np
from jax import lax
from jax.experimental import pallas as pl
from jax.experimental.pallas import tpu as pltpu
from jax.sharding import PartitionSpec as P

D = 1024
HEADS = 16
HEAD_DIM = 64
FF = 2816
BUCKETS = 32
MAX_DISTANCE = 128
LAYERS = 2
EPSILON = 1e-06
NEGATIVE = -1e30
SCORE_SCALE = 0.125
ALL = ("experts", "context", "dp")
GROUP = 4
OWN = HEADS // GROUP
OWN_COLS = OWN * HEAD_DIM
PACKED = 3 * OWN_COLS
LANES = 128
REACH = 512
FF_TILE = 256
FF_STEPS = FF // FF_TILE
BACK_TILE = 1408
BACK_STEPS = FF // BACK_TILE
MIB = 1 << 20

bf16 = jnp.bfloat16
f32 = jnp.float32


def bucket_bounds(bucket_count, far_reach):
    half_count = bucket_count // 2
    bounds = list(range(1, half_count + 1))
    for section_index in range(1, half_count):
        bounds.append(
            int(math.ceil(half_count * (far_reach / half_count) ** (section_index / half_count)))
        )
    return np.array(bounds, np.int32)


def bucket_hits():
    distance = np.arange(REACH)
    bucket = (distance[:, None] >= bucket_bounds(BUCKETS, MAX_DISTANCE)).sum(-1)
    return (np.arange(BUCKETS)[:, None] == bucket[None, :]).astype(np.float32)


def dot(a, b, ca, cb, precision=None):
    return lax.dot_general(
        a, b, (((ca,), (cb,)), ((), ())), precision=precision, preferred_element_type=f32
    )


def whole_call(
    body, out_shape, args, *, flops=0, limit=16, scratch=(), smem=0, name=None, after=()
):
    specs = [pl.BlockSpec(memory_space=pltpu.SMEM)] * smem + [
        pl.BlockSpec(memory_space=pltpu.VMEM)
    ] * (len(args) - smem)
    outs = tuple(out_shape)
    moved = sum(a.size * a.dtype.itemsize for a in list(args) + list(outs))
    specs += [pl.BlockSpec(memory_space=pltpu.HBM)] * len(after)
    used = len(args)
    args = list(args) + [far_away(a) for a in after]

    def ordered(*refs):
        body(*refs[:used], *refs[used + len(after) :])

    return pl.pallas_call(
        ordered,
        out_shape=outs,
        in_specs=specs,
        out_specs=tuple(pl.BlockSpec(memory_space=pltpu.VMEM) for _ in outs),
        scratch_shapes=list(scratch),
        compiler_params=pltpu.CompilerParams(vmem_limit_bytes=limit * MIB),
        cost_estimate=pl.CostEstimate(
            flops=int(flops), bytes_accessed=int(moved), transcendentals=0
        ),
        name=name,
    )(*args)


def far_away(x):
    return pltpu.with_memory_space_constraint(x, pltpu.HBM)


def hold(x, after):
    def body(*refs):
        pass

    return pl.pallas_call(
        body,
        out_shape=pltpu.HBM(x.shape, x.dtype),
        in_specs=[pl.BlockSpec(memory_space=pltpu.HBM)] * (1 + len(after)),
        out_specs=pl.BlockSpec(memory_space=pltpu.HBM),
        input_output_aliases={0: 0},
        compiler_params=pltpu.CompilerParams(vmem_limit_bytes=MIB),
        cost_estimate=pl.CostEstimate(flops=0, bytes_accessed=0, transcendentals=0),
        name="hold",
    )(far_away(x), *[far_away(a) for a in after])


def shape(dims, dtype):
    return jax.ShapeDtypeStruct(dims, dtype)


def rms_scale(inputs):
    return lax.rsqrt(jnp.mean(inputs * inputs, -1, keepdims=True) + EPSILON)


def norm_back(inputs, gain_row, upstream):
    inverse = rms_scale(inputs)
    scaled = upstream * gain_row
    inner_mean = jnp.mean(inputs * scaled, -1, keepdims=True)
    grad_inputs = inverse * scaled - inputs * (inverse * inverse * inverse) * inner_mean
    grad_gain = jnp.sum(upstream * inputs * inverse, 0, keepdims=True)
    return grad_inputs, grad_gain


def placed(count, offset):
    index = lax.broadcasted_iota(jnp.int32, (count, LANES), 0)
    lane = lax.broadcasted_iota(jnp.int32, (count, LANES), 1)
    return one_hot(lane == index + offset)


def prepare_body(direct, in_ref, out_ref, router_ref, gains_ref, table_ref, *packets):
    share = in_ref.shape[1]
    for layer in range(LAYERS):
        for which in range(3):
            for head in range(OWN):
                for c in range(GROUP):
                    source = which * D + (head * GROUP + c) * HEAD_DIM
                    target = which * OWN_COLS + head * HEAD_DIM
                    packets[layer][c, :, target : target + HEAD_DIM] = in_ref[
                        layer, :, source : source + HEAD_DIM
                    ]
        if direct:
            width = D // GROUP
            for q in range(GROUP):
                packets[LAYERS + layer][q] = out_ref[layer, :, q * width : (q + 1) * width]
    small = jnp.zeros((share, LANES), f32)
    row = lax.broadcasted_iota(jnp.int32, (share, LANES), 0)
    for layer in range(LAYERS):
        top = 32 * layer
        small = small + dot(router_ref[layer], placed(router_ref.shape[2], top), 1, 0)
        small = small + dot(gains_ref[layer], placed(2, top + 16), 1, 0)
        bucket = dot(table_ref[layer : layer + 1, :], placed(table_ref.shape[1], top + 64), 1, 0)
        small = small + jnp.where(row == 0, bucket, 0.0)
    for c in range(GROUP):
        packets[0][c, :, PACKED:] = small.astype(bf16)


def prepare(direct, attn_in, attn_out, router, gains, rel_table):
    share = attn_in.shape[1]
    outs = [shape((GROUP, share, PACKED + LANES), bf16), shape((GROUP, share, PACKED), bf16)]
    if direct:
        outs += [shape((GROUP, share, D // GROUP), bf16)] * LAYERS

    def body(*refs):
        prepare_body(direct, *refs)

    return whole_call(
        body, outs, [attn_in, attn_out, router, gains, rel_table], name="prepare"
    )


def unpack_body(place_ref, got_ref, hits_ref, w_in_ref, w_out_ref, *rest):
    experts, pairs, _, share, total = got_ref.shape
    width = D // GROUP
    for e in range(experts):
        for d in range(pairs):
            for c in range(GROUP):
                row = ((e * GROUP + c) * pairs + d) * share
                w_in_ref[row : row + share, :] = got_ref[e, d, c, :, :PACKED]
                row = (e * pairs + d) * share
                w_out_ref[c, row : row + share, :] = got_ref[e, d, c, :, total - width :]
    if not rest:
        return
    feature_ref, bias_ref, flat_ref, bucket_ref = rest
    for e in range(experts):
        for d in range(pairs):
            for c in range(GROUP):
                index = (e * GROUP + c) * pairs + d
                block = got_ref[e, d, c, :, PACKED : PACKED + LANES].astype(f32)
                flat_ref[index * share : (index + 1) * share, :] = block
                bucket_ref[index : index + 1, :] = block[:1, :]
    feature_ref[...] = flat_ref[...].T
    head = lax.broadcasted_iota(jnp.int32, (8, LANES), 0)
    lane = lax.broadcasted_iota(jnp.int32, (8, LANES), 1)
    for layer in range(LAYERS):
        mine = jnp.where(
            (lane == 64 + 32 * layer + head * GROUP + place_ref[0]) & (head < OWN), 1.0, 0.0
        )
        table = dot(mine, bucket_ref[...], 1, 1, lax.Precision.HIGHEST)
        bias_ref[layer] = dot(
            table - table[:, BUCKETS - 1 :], hits_ref[...], 1, 0, lax.Precision.HIGHEST
        )


def unpack(place, got, hits, first):
    outs = [shape((D, PACKED), bf16), shape((GROUP, OWN_COLS, D // GROUP), bf16)]
    scratch = []
    if first:
        outs += [shape((LANES, D), f32), shape((LAYERS, 8, REACH), f32)]
        scratch = [pltpu.VMEM((D, LANES), f32), pltpu.VMEM((BUCKETS, LANES), f32)]
    return whole_call(
        unpack_body, outs, [place, got, hits], smem=1, scratch=scratch, name="unpack"
    )


def near_bias(bias_ref, layer, head, rows):
    row = bias_ref[layer, head : head + 1, :]
    return pltpu.roll(jnp.broadcast_to(row, (rows, REACH)), 0, 1, stride=1, stride_axis=0)


def masked_scores(keys, queries, near, low, key_block, query_block, rows):
    scores = dot(keys, queries, 1, 1)
    key_place = lax.broadcasted_iota(jnp.int32, (rows, rows), 0)
    seen = key_place >= low - key_block * rows
    if key_block == query_block:
        scores = scores + near[:, :rows]
        seen = seen & (key_place <= lax.broadcasted_iota(jnp.int32, (rows, rows), 1))
    elif key_block == query_block - 1:
        scores = scores + near[:, rows:]
    return jnp.where(seen, scores, NEGATIVE)


def attention_forward_body(
    layer, place_ref, n0, n1, n2, n3, w_ref, feature_ref, bias_ref, low_ref, wo_ref,
    packed_ref, log_ref, mixed_ref, keep_ref, send_ref, *normed_ref,
):
    me = place_ref[0]
    rows = n0.shape[0]
    for r, piece in enumerate((n0, n1, n2, n3)):
        normed = piece[...]
        if layer == 0:
            wide = normed.astype(f32)
            normed = (wide * rms_scale(wide) * feature_ref[16:17, :]).astype(bf16)
            normed_ref[0][r * rows : (r + 1) * rows, :] = normed
        packed_ref[r * rows : (r + 1) * rows, :] = dot(normed, w_ref[...], 1, 0).astype(bf16)
    lane = lax.broadcasted_iota(jnp.int32, (rows, LANES), 1)
    starts = [pl.multiple_of((b ^ me) * rows, rows) for b in range(GROUP)]
    for pair in range(OWN // 2):
        at = pair * LANES

        def part(b, which):
            column = which * OWN_COLS + at
            return packed_ref[pl.ds(starts[b], rows), column : column + LANES]

        sides = [(lane // HEAD_DIM) == side for side in range(2)]
        nears = [near_bias(bias_ref, layer, pair * 2 + side, rows) for side in range(2)]
        for qb in range(GROUP):
            low = low_ref[:, qb * rows : (qb + 1) * rows]
            queries = part(qb, 0) * SCORE_SCALE
            total = None
            for side in range(2):
                mine = jnp.where(sides[side], queries, 0).astype(bf16)
                tiles = [
                    masked_scores(part(kb, 1), mine, nears[side], low, kb, qb, rows)
                    for kb in range(qb + 1)
                ]
                peak = jnp.max(tiles[0], 0, keepdims=True)
                for tile in tiles[1:]:
                    peak = jnp.maximum(peak, jnp.max(tile, 0, keepdims=True))
                weight_sum = jnp.zeros((1, rows), f32)
                out = jnp.zeros((LANES, rows), f32)
                for kb, tile in enumerate(tiles):
                    power = jnp.exp(tile - peak)
                    weight_sum = weight_sum + jnp.sum(power, 0, keepdims=True)
                    values = jnp.where(sides[side], part(kb, 2), 0).astype(bf16)
                    out = out + dot(values, power.astype(bf16), 0, 0)
                out = out / weight_sum
                total = out if total is None else total + out
                head = pair * 2 + side
                log_ref[head : head + 1, qb * rows : (qb + 1) * rows] = peak + jnp.log(weight_sum)
            mixed_ref[pl.ds(starts[qb], rows), at : at + LANES] = total.T.astype(bf16)
    width = wo_ref.shape[2]
    for r, (target, offset) in enumerate(
        ((keep_ref, 0), (send_ref, 0), (keep_ref, rows), (send_ref, rows))
    ):
        mixed = mixed_ref[r * rows : (r + 1) * rows, :]
        for q in range(wo_ref.shape[0]):
            target[offset : offset + rows, q * width : (q + 1) * width] = dot(
                mixed, wo_ref[q], 1, 0
            ).astype(target.dtype)


def attention_forward(layer, place, pieces, w_in, feature, bias, low, w_out):
    rows = pieces[0].shape[0]
    total = GROUP * rows
    outs = [
        shape((total, PACKED), bf16),
        shape((8, total), f32),
        shape((total, OWN_COLS), bf16),
        shape((2 * rows, D), f32),
        shape((2 * rows, D), bf16),
    ]
    if layer == 0:
        outs.append(shape((total, D), bf16))

    def body(*refs):
        attention_forward_body(layer, *refs)

    return whole_call(
        body,
        outs,
        [place, *pieces, w_in, feature, bias, low, w_out],
        smem=1,
        flops=2 * total * D * (PACKED + OWN_COLS) + 2 * total * total * OWN_COLS * 2,
        limit=24,
        name="attention_forward",
    )


def attention_backward_body(
    layer, place_ref, d0, d1, d2, d3, w_ref, feature_ref, bias_ref, low_ref, wo_ref, packed_ref,
    log_ref, *refs,
):
    normed_refs = refs[:-8]
    (grad_packed_ref, keep_ref, send_ref, table_ref, gain_ref, grad_mixed_ref, dk_ref,
     dv_ref) = refs[-8:]
    me = place_ref[0]
    rows = d0.shape[0]
    width = wo_ref.shape[2]
    for r, piece in enumerate((d0, d1, d2, d3)):
        got = jnp.zeros((rows, OWN_COLS), f32)
        for q in range(wo_ref.shape[0]):
            got = got + dot(piece[:, q * width : (q + 1) * width], wo_ref[q], 1, 1)
        grad_mixed_ref[r * rows : (r + 1) * rows, :] = got.astype(bf16)
    lane = lax.broadcasted_iota(jnp.int32, (rows, LANES), 1)
    starts = [pl.multiple_of((b ^ me) * rows, rows) for b in range(GROUP)]
    table_ref[...] = jnp.zeros(table_ref.shape, f32)
    for pair in range(OWN // 2):
        at = pair * LANES

        def part(b, which):
            column = which * OWN_COLS + at
            return packed_ref[pl.ds(starts[b], rows), column : column + LANES]

        sides = [(lane // HEAD_DIM) == side for side in range(2)]
        nears = [near_bias(bias_ref, layer, pair * 2 + side, rows) for side in range(2)]
        diag = [jnp.zeros((rows, rows), f32) for _ in range(2)]
        before = [jnp.zeros((rows, rows), f32) for _ in range(2)]
        far = [jnp.zeros((1, rows), f32) for _ in range(2)]
        dk_ref[...] = jnp.zeros(dk_ref.shape, f32)
        dv_ref[...] = jnp.zeros(dv_ref.shape, f32)
        for qb in range(GROUP):
            low = low_ref[:, qb * rows : (qb + 1) * rows]
            queries = part(qb, 0) * SCORE_SCALE
            upstream = grad_mixed_ref[pl.ds(starts[qb], rows), at : at + LANES]
            grad_queries = jnp.zeros((LANES, rows), f32)
            for side in range(2):
                head = pair * 2 + side
                mine = jnp.where(sides[side], queries, 0).astype(bf16)
                above = jnp.where(sides[side], upstream, 0).astype(bf16)
                log_total = log_ref[head : head + 1, qb * rows : (qb + 1) * rows]
                probs, grads = [], []
                row_dot = jnp.zeros((1, rows), f32)
                for kb in range(qb + 1):
                    scores = masked_scores(part(kb, 1), mine, nears[side], low, kb, qb, rows)
                    prob = jnp.exp(scores - log_total)
                    grad = dot(part(kb, 2), above, 1, 1)
                    row_dot = row_dot + jnp.sum(prob * grad, 0, keepdims=True)
                    probs.append(prob)
                    grads.append(grad)
                for kb in range(qb + 1):
                    grad_score = probs[kb] * (grads[kb] - row_dot)
                    if kb == qb:
                        diag[side] = diag[side] + grad_score
                    elif kb == qb - 1:
                        before[side] = before[side] + grad_score
                    else:
                        far[side] = far[side] + jnp.sum(grad_score, 0, keepdims=True)
                    grad_low = grad_score.astype(bf16)
                    keys = jnp.where(sides[side], part(kb, 1), 0).astype(bf16)
                    grad_queries = grad_queries + dot(keys, grad_low, 0, 0)
                    span = slice(kb * rows, (kb + 1) * rows)
                    dk_ref[span, :] += dot(grad_low, mine, 1, 0)
                    dv_ref[span, :] += dot(probs[kb].astype(bf16), above, 1, 0)
            grad_packed_ref[pl.ds(starts[qb], rows), at : at + LANES] = (
                grad_queries.T * SCORE_SCALE
            ).astype(bf16)
        for kb in range(GROUP):
            span = slice(kb * rows, (kb + 1) * rows)
            for which, source in ((1, dk_ref), (2, dv_ref)):
                column = which * OWN_COLS + at
                grad_packed_ref[pl.ds(starts[kb], rows), column : column + LANES] = source[
                    span, :
                ].astype(bf16)
        distance = lax.broadcasted_iota(jnp.int32, (1, REACH), 1)
        for side in range(2):
            head = pair * 2 + side
            skewed = jnp.concatenate([diag[side], before[side]], 1)
            row_index = lax.broadcasted_iota(jnp.int32, (rows, REACH), 0)
            step = 1
            while step < rows:
                skewed = jnp.where(
                    (row_index & step) != 0, pltpu.roll(skewed, REACH - step, 1), skewed
                )
                step *= 2
            by_distance = jnp.sum(skewed, 0, keepdims=True)
            far_sum = jnp.sum(far[side], 1, keepdims=True)
            table_ref[head : head + 1, :] = by_distance + jnp.where(
                distance == REACH - 1, far_sum, 0.0
            )
    for r, (target, offset) in enumerate(
        ((keep_ref, 0), (send_ref, 0), (keep_ref, rows), (send_ref, rows))
    ):
        grad_normed = dot(grad_packed_ref[r * rows : (r + 1) * rows, :], w_ref[...], 1, 1)
        target[offset : offset + rows, :] = grad_normed.astype(target.dtype)
        part_gain = jnp.sum(grad_normed * block_of(normed_refs, r, rows).astype(f32), 0, keepdims=True)
        gain_sum = part_gain if r == 0 else gain_sum + part_gain
    gain_row = feature_ref[32 * layer + 16 : 32 * layer + 17, :]
    gain_ref[...] = jnp.broadcast_to(gain_sum / gain_row, gain_ref.shape)


def block_of(refs, r, rows):
    return refs[r][...] if len(refs) > 1 else refs[0][r * rows : (r + 1) * rows, :]


def attention_backward(
    layer, place, pieces, w_in, feature, bias, low, w_out, packed, log_total, normed, after=()
):
    rows = pieces[0].shape[0]
    total = GROUP * rows

    def body(*refs):
        attention_backward_body(layer, *refs)

    return whole_call(
        body,
        (
            shape((total, PACKED), bf16),
            shape((2 * rows, D), f32),
            shape((2 * rows, D), bf16),
            shape((8, REACH), f32),
            shape((8, D), f32),
        ),
        [place, *pieces, w_in, feature, bias, low, w_out, packed, log_total, *normed],
        smem=1,
        after=after,
        scratch=[
            pltpu.VMEM((total, OWN_COLS), bf16),
            pltpu.VMEM((total, LANES), f32),
            pltpu.VMEM((total, LANES), f32),
        ],
        flops=2 * total * D * (PACKED + OWN_COLS) + 2 * total * total * OWN_COLS * 5,
        limit=24,
        name="attention_backward",
    )


def dense_products(normed, upstream, grad_packed_ref, mixed_ref):
    rows = upstream[0].shape[0]
    total_in = None
    total_out = None
    for r in range(GROUP):
        span = slice(r * rows, (r + 1) * rows)
        one = dot(block_of(normed, r, rows), grad_packed_ref[span, :], 0, 0)
        two = dot(mixed_ref[span, :], upstream[r][...], 0, 0)
        total_in = one if total_in is None else total_in + one
        total_out = two if total_out is None else total_out + two
    return total_in, total_out


def dense_grads(normed, upstream, grad_packed, mixed):
    rows = upstream[0].shape[0]
    count = len(normed)

    def body(*refs):
        total_in, total_out = dense_products(
            refs[:count], refs[count : count + GROUP], refs[-4], refs[-3]
        )
        refs[-2][...] = total_in.astype(bf16)
        refs[-1][...] = total_out.astype(bf16)

    return whole_call(
        body,
        (shape((D, PACKED), bf16), shape((OWN_COLS, D), bf16)),
        [*normed, *upstream, grad_packed, mixed],
        flops=2 * GROUP * rows * D * (PACKED + OWN_COLS),
        name="dense_grads",
    )


def dense_pack(experts, pairs, share, place, normed, upstream, grad_packed, mixed, small, gain_a,
               by_distance, hits, after=()):
    rows = upstream[0].shape[0]
    count = len(normed)
    width = D // GROUP
    total = PACKED + LANES + width

    def body(place_ref, *refs):
        grad_packed_ref, mixed_ref, small_ref, gain_ref, distance_ref, hits_ref = refs[
            count + GROUP : count + GROUP + 6
        ]
        keep_ref, send_ref, in_ref, out_ref, flat_ref = refs[count + GROUP + 6 :]
        total_in, total_out = dense_products(
            refs[:count], refs[count : count + GROUP], grad_packed_ref, mixed_ref
        )
        in_ref[...] = total_in
        out_ref[...] = total_out
        row = lax.broadcasted_iota(jnp.int32, (8, D), 0)
        gains = jnp.where(
            row == 0, gain_ref[...], jnp.where(row == 1, small_ref[16:24, :], 0.0)
        )
        features = jnp.concatenate(
            [small_ref[:16, :], gains, jnp.zeros((LANES - 24, D), f32)], 0
        )
        flat_ref[...] = features.T
        by_bucket = dot(hits_ref[...], distance_ref[...], 1, 1, lax.Precision.HIGHEST)
        head = lax.broadcasted_iota(jnp.int32, (8, LANES), 0)
        lane = lax.broadcasted_iota(jnp.int32, (8, LANES), 1)
        mine = jnp.where((lane == 64 + head * GROUP + place_ref[0]) & (head < OWN), 1.0, 0.0)
        buckets = dot(by_bucket, mine, 1, 0, lax.Precision.HIGHEST)
        for index in range(BUCKETS):
            at = index * share
            flat_ref[at : at + 1, :] = flat_ref[at : at + 1, :] + buckets[index : index + 1, :]
        for target, d in ((keep_ref, place_ref[1]), (send_ref, 1 - place_ref[1])):
            for e in range(experts):
                for c in range(GROUP):
                    span = pl.ds(pl.multiple_of(((e * GROUP + c) * pairs + d) * share, share), share)
                    to = slice(c * share, (c + 1) * share)
                    target[e, to, :PACKED] = in_ref[span, :].astype(target.dtype)
                    target[e, to, PACKED : PACKED + LANES] = flat_ref[span, :].astype(target.dtype)
                    span = pl.ds(pl.multiple_of((e * pairs + d) * share, share), share)
                    target[e, to, PACKED + LANES :] = out_ref[
                        span, c * width : (c + 1) * width
                    ].astype(target.dtype)

    return whole_call(
        body,
        (
            shape((experts, GROUP * share, total), f32),
            shape((experts, GROUP * share, total), bf16),
        ),
        [place, *normed, *upstream, grad_packed, mixed, small, gain_a, by_distance, hits],
        smem=1,
        scratch=[
            pltpu.VMEM((D, PACKED), f32),
            pltpu.VMEM((OWN_COLS, D), f32),
            pltpu.VMEM((D, LANES), f32),
        ],
        flops=2 * GROUP * rows * D * (PACKED + OWN_COLS),
        after=after,
        name="dense_pack",
    )


def finish_dense(experts, share, inner, outer):
    width = D // GROUP

    def body(*refs):
        in_ref, out_ref, small_ref = refs[2 * LAYERS :]
        for layer in range(LAYERS):
            got, zone = refs[layer], refs[LAYERS + layer]
            for c in range(GROUP):
                for which in range(3):
                    for head in range(OWN):
                        source = which * OWN_COLS + head * HEAD_DIM
                        target = which * D + (head * GROUP + c) * HEAD_DIM
                        in_ref[layer, :, target : target + HEAD_DIM] = got[
                            c, :, source : source + HEAD_DIM
                        ].astype(f32)
                rows = slice(c * share, (c + 1) * share)
                part = zone[0, rows, PACKED + LANES :].astype(f32)
                for e in range(1, experts):
                    part = part + zone[e, rows, PACKED + LANES :].astype(f32)
                out_ref[layer, :, c * width : (c + 1) * width] = part
            total = got[0, :, PACKED:].astype(f32)
            for c in range(1, GROUP):
                total = total + got[c, :, PACKED:].astype(f32)
            small_ref[layer] = total

    return whole_call(
        body,
        (
            shape((LAYERS, share, 3 * D), f32),
            shape((LAYERS, share, D), f32),
            shape((LAYERS, share, LANES), f32),
        ),
        [*inner, *outer],
        name="finish_dense",
    )


def dispatch_grid(dest_rows, slots, tokens):
    place = lax.broadcasted_iota(jnp.int32, (slots, tokens), 0)
    first = place == dest_rows[0:1, :]
    second = place == dest_rows[1:2, :]
    return first, second


def one_hot(flags):
    return jnp.where(flags, 1.0, 0.0).astype(bf16)


def collect_grid(meta, slots):
    tokens = meta.shape[0]
    place = lax.broadcasted_iota(jnp.int32, (tokens, slots), 1)
    first = place == meta[:, 0:1].astype(jnp.int32)
    second = place == meta[:, 1:2].astype(jnp.int32)
    return first, second


def scatter_grads(upstream, meta, dest_rows, slots):
    tokens = upstream.shape[0]
    first, second = dispatch_grid(dest_rows, slots, tokens)
    return (
        dot(one_hot(first), (meta[:, 2:3] * upstream).astype(bf16), 1, 0)
        + dot(one_hot(second), (meta[:, 3:4] * upstream).astype(bf16), 1, 0)
    ).astype(bf16)


def route_body(layer, experts, capacity, last, *refs):
    top = 32 * layer
    if last:
        (x_ref, keep_ref, recv_ref, far_ref, feature_ref, ids_ref, idst_ref, grad_ref,
         middle_ref, rows_ref, soft_ref, meta_ref, dest_ref, sent_ref) = refs
    else:
        (x_ref, keep_ref, recv_ref, far_ref, feature_ref, ids_ref, idst_ref,
         middle_ref, rows_ref, soft_ref, meta_ref, dest_ref) = refs
    tokens = x_ref.shape[0]
    slots = experts * capacity
    middle = (
        x_ref[...].astype(f32)
        + keep_ref[:tokens, :]
        + recv_ref[:tokens, :].astype(f32)
        + far_ref[...].astype(f32)
    )
    middle_ref[...] = middle
    normed = middle * rms_scale(middle) * feature_ref[top + 17 : top + 18, :]
    lane = lax.broadcasted_iota(jnp.int32, (tokens, LANES), 1)
    logits = dot(normed, feature_ref[...], 1, 1, lax.Precision.HIGHEST)
    logits = jnp.where((lane >= top) & (lane < top + experts), logits, NEGATIVE)
    power = jnp.exp(logits - jnp.max(logits, -1, keepdims=True))
    soft = power / jnp.sum(power, -1, keepdims=True)
    soft_ref[...] = soft
    ids = ids_ref[...]
    hit0 = lane == ids[:, 0:1] + top
    hit1 = lane == ids[:, 1:2] + top
    picked0 = jnp.sum(jnp.where(hit0, soft, 0.0), -1, keepdims=True)
    picked1 = jnp.sum(jnp.where(hit1, soft, 0.0), -1, keepdims=True)
    pick_total = picked0 + picked1
    down = lax.broadcasted_iota(jnp.int32, (tokens, tokens), 0)
    across = lax.broadcasted_iota(jnp.int32, (tokens, tokens), 1)
    counts = dot(one_hot(across < down), one_hot(hit0 | hit1), 1, 0)
    dest0 = ids[:, 0:1].astype(f32) * capacity + jnp.sum(
        jnp.where(hit0, counts, 0.0), -1, keepdims=True
    )
    dest1 = ids[:, 1:2].astype(f32) * capacity + jnp.sum(
        jnp.where(hit1, counts, 0.0), -1, keepdims=True
    )
    fields = (dest0, dest1, picked0 / pick_total, picked1 / pick_total, pick_total)
    meta = jnp.zeros((tokens, LANES), f32)
    for index, field in enumerate(fields):
        meta = jnp.where(lane == index, field, meta)
    meta_ref[...] = meta
    idst = idst_ref[...]
    sub = lax.broadcasted_iota(jnp.int32, (16, tokens), 0)
    row0 = sub == idst[0:1, :]
    row1 = sub == idst[1:2, :]
    row_counts = dot(one_hot(row0 | row1), one_hot(down < across), 1, 0)
    destr0 = idst[0:1, :] * capacity + jnp.sum(
        jnp.where(row0, row_counts, 0.0), 0, keepdims=True
    ).astype(jnp.int32)
    destr1 = idst[1:2, :] * capacity + jnp.sum(
        jnp.where(row1, row_counts, 0.0), 0, keepdims=True
    ).astype(jnp.int32)
    dest_rows = jnp.where(
        lax.broadcasted_iota(jnp.int32, (8, tokens), 0) == 0, destr0, destr1
    )
    dest_ref[...] = dest_rows
    first, second = dispatch_grid(dest_rows, slots, tokens)
    rows_ref[...] = dot(one_hot(first | second), normed.astype(bf16), 1, 0).astype(bf16)
    if last:
        sent_ref[...] = scatter_grads(grad_ref[...].astype(f32), meta, dest_rows, slots)


def route(layer, experts, capacity, x, keep, recv, far, feature, ids, idst, grad=None):
    tokens = x.shape[0]
    slots = experts * capacity
    outs = [
        shape((tokens, D), f32),
        shape((slots, D), bf16),
        shape((tokens, LANES), f32),
        shape((tokens, LANES), f32),
        shape((8, tokens), jnp.int32),
    ]
    args = [x, keep, recv, far, feature, ids, idst]
    if grad is not None:
        outs.append(shape((slots, D), bf16))
        args.append(grad)

    def body(*refs):
        route_body(layer, experts, capacity, grad is not None, *refs)

    return whole_call(body, outs, args, flops=2 * slots * tokens * D, name="route")


def combine_body(last, *refs):
    if last:
        middle_ref, back_ref, meta_ref, out_ref = refs
    else:
        middle_ref, back_ref, meta_ref, gain_ref, out_ref, normed_ref = refs
    meta = meta_ref[...]
    first, second = collect_grid(meta, back_ref.shape[0])
    x = (
        middle_ref[...]
        + meta[:, 2:3] * dot(one_hot(first), back_ref[...], 1, 0)
        + meta[:, 3:4] * dot(one_hot(second), back_ref[...], 1, 0)
    )
    out_ref[...] = x.astype(out_ref.dtype)
    if not last:
        normed_ref[...] = (x * rms_scale(x) * gain_ref[48:49, :]).astype(bf16)


def combine(middle, back, meta, gain=None):
    tokens = middle.shape[0]
    args = [middle, back, meta]
    outs = [shape((tokens, D), bf16 if gain is None else f32)]
    if gain is not None:
        args.append(gain)
        outs.append(shape((tokens, D), bf16))

    def body(*refs):
        combine_body(gain is None, *refs)

    return whole_call(
        body, outs, args, flops=4 * tokens * D * back.shape[0], name="combine"
    )


def expert_token_back_body(
    layer, back_ref, came_ref, g_ref, middle_ref, soft_ref, meta_ref, ids_ref, feature_ref,
    dmiddle_ref, dattn_ref, small_ref,
):
    top = 32 * layer
    gain_row = feature_ref[top + 17 : top + 18, :]
    meta = meta_ref[...]
    g = g_ref[...].astype(f32)
    slots = back_ref.shape[0]
    first, second = collect_grid(meta, slots)
    grad_gate0 = jnp.sum(g * dot(one_hot(first), back_ref[...], 1, 0), -1, keepdims=True)
    grad_gate1 = jnp.sum(g * dot(one_hot(second), back_ref[...], 1, 0), -1, keepdims=True)
    grad_normed = dot(one_hot(first | second), came_ref[...], 1, 0)
    gap = (grad_gate0 - grad_gate1) / meta[:, 4:5]
    ids = ids_ref[...]
    lane = lax.broadcasted_iota(jnp.int32, meta.shape, 1)
    grad_soft = jnp.where(lane == ids[:, 0:1] + top, meta[:, 3:4] * gap, 0.0) + jnp.where(
        lane == ids[:, 1:2] + top, -meta[:, 2:3] * gap, 0.0
    )
    soft = soft_ref[...]
    grad_logits = soft * (grad_soft - jnp.sum(soft * grad_soft, -1, keepdims=True))
    middle = middle_ref[...]
    normed = middle * rms_scale(middle) * gain_row
    grad_router = dot(grad_logits.T, normed, 1, 0, lax.Precision.HIGHEST)
    grad_normed = grad_normed + dot(
        grad_logits, feature_ref[...], 1, 0, lax.Precision.HIGHEST
    )
    grad_branch, grad_gain = norm_back(middle, gain_row, grad_normed)
    dmiddle = g + grad_branch
    dmiddle_ref[...] = dmiddle
    dattn_ref[...] = dmiddle.astype(bf16)
    small_ref[:16, :] = grad_router[top : top + 16, :]
    small_ref[16:24, :] = jnp.broadcast_to(grad_gain, (8, D))


def expert_token_back(layer, back, came, g, middle, soft, meta, ids, feature, after=()):
    tokens = middle.shape[0]

    def body(*refs):
        expert_token_back_body(layer, *refs)

    return whole_call(
        body,
        (shape((tokens, D), f32), shape((tokens, D), bf16), shape((24, D), f32)),
        [back, came, g, middle, soft, meta, ids, feature],
        after=after,
        flops=6 * tokens * D * back.shape[0],
        name="expert_token_back",
    )


def attention_token_back_body(layer, *refs):
    if layer == 0:
        x_ref, dmiddle_ref, keep_ref, recv_ref, far_ref, feature_ref, out_ref = refs
    else:
        (x_ref, dmiddle_ref, keep_ref, recv_ref, far_ref, feature_ref, meta_ref, dest_ref,
         out_ref, sent_ref) = refs
    tokens = x_ref.shape[0]
    grad_normed = (
        keep_ref[:tokens, :] + recv_ref[:tokens, :].astype(f32) + far_ref[...].astype(f32)
    )
    gain_row = feature_ref[32 * layer + 16 : 32 * layer + 17, :]
    grad_branch, _ = norm_back(x_ref[...].astype(f32), gain_row, grad_normed)
    g = dmiddle_ref[...] + grad_branch
    out_ref[...] = g
    if layer > 0:
        sent_ref[...] = scatter_grads(g, meta_ref[...], dest_ref[...], sent_ref.shape[0])


def attention_token_back(layer, x, dmiddle, keep, recv, far, feature, meta=None, dest=None, slots=0):
    tokens = x.shape[0]
    outs = [shape((tokens, D), f32)]
    args = [x, dmiddle, keep, recv, far, feature]
    if meta is not None:
        outs.append(shape((slots, D), bf16))
        args += [meta, dest]

    def body(*refs):
        attention_token_back_body(layer, *refs)

    return whole_call(
        body, outs, args, flops=4 * tokens * D * slots, name="attention_token_back"
    )


def gelu_parts(gate):
    inner = math.sqrt(2.0 / math.pi) * (gate + 0.044715 * gate * gate * gate)
    return jnp.tanh(inner)


def expert_forward_body(rows_ref, wg_ref, wu_ref, wo_ref, produced_ref, acts_ref, total_ref):
    step = pl.program_id(0)
    rows = rows_ref[...]
    gate = dot(rows, wg_ref[0, 0], 1, 0)
    up = dot(rows, wu_ref[0, 0], 1, 0)
    acts_ref[0] = gate.astype(bf16)
    acts_ref[1] = up.astype(bf16)
    hidden = (0.5 * gate * (1.0 + gelu_parts(gate)) * up).astype(bf16)
    out = dot(hidden, wo_ref[0, 0], 1, 1)

    @pl.when(step == 0)
    def _():
        total_ref[...] = out

    @pl.when(step > 0)
    def _():
        total_ref[...] += out

    @pl.when(step == FF_STEPS - 1)
    def _():
        produced_ref[...] = total_ref[...].astype(bf16)


def weight_specs(layer, tile):
    return [
        pl.BlockSpec((1, 1, D, tile), lambda s: (layer, 0, 0, s)),
        pl.BlockSpec((1, 1, D, tile), lambda s: (layer, 0, 0, FF // tile + s)),
        pl.BlockSpec((1, 1, D, tile), lambda s: (layer, 0, 0, s)),
    ]


def expert_forward(layer, rows, w_in, w_out):
    count = rows.shape[0]
    return pl.pallas_call(
        expert_forward_body,
        grid=(FF_STEPS,),
        out_shape=(shape((count, D), bf16), pltpu.HBM((2, count, FF), bf16)),
        in_specs=[pl.BlockSpec((count, D), lambda s: (0, 0))] + weight_specs(layer, FF_TILE),
        out_specs=(
            pl.BlockSpec((count, D), lambda s: (0, 0)),
            pl.BlockSpec((2, count, FF_TILE), lambda s: (0, 0, s)),
        ),
        scratch_shapes=[pltpu.VMEM((count, D), f32)],
        compiler_params=pltpu.CompilerParams(vmem_limit_bytes=28 * MIB),
        cost_estimate=pl.CostEstimate(
            flops=6 * count * D * FF, bytes_accessed=6 * D * FF, transcendentals=count * FF
        ),
        name="expert_forward",
    )(rows, far_away(w_in), far_away(w_in), far_away(w_out))


def expert_backward_body(
    grad_ref, acts_ref, wg_ref, wu_ref, wo_ref, drows_ref, grads_ref, total_ref
):
    step = pl.program_id(0)
    grad_hidden = dot(grad_ref[...], wo_ref[0, 0], 1, 0)
    gate = acts_ref[0].astype(f32)
    up = acts_ref[1].astype(f32)
    curve = gelu_parts(gate)
    value = 0.5 * gate * (1.0 + curve)
    slope = 0.5 * (1.0 + curve) + 0.5 * gate * (1.0 - curve * curve) * math.sqrt(
        2.0 / math.pi
    ) * (1.0 + 3.0 * 0.044715 * gate * gate)
    grad_gate = (grad_hidden * up * slope).astype(bf16)
    grad_up = (grad_hidden * value).astype(bf16)
    grads_ref[0] = grad_gate
    grads_ref[1] = grad_up
    grads_ref[2] = (value * up).astype(bf16)
    out = dot(grad_gate, wg_ref[0, 0], 1, 1) + dot(grad_up, wu_ref[0, 0], 1, 1)

    @pl.when(step == 0)
    def _():
        total_ref[...] = out

    @pl.when(step > 0)
    def _():
        total_ref[...] += out

    @pl.when(step == BACK_STEPS - 1)
    def _():
        drows_ref[...] = total_ref[...].astype(bf16)


def expert_backward(layer, grad, acts, w_in, w_out, after=()):
    count = grad.shape[0]

    def body(*refs):
        expert_backward_body(*refs[:5], *refs[5 + len(after) :])

    return pl.pallas_call(
        body,
        grid=(BACK_STEPS,),
        out_shape=(shape((count, D), bf16), pltpu.HBM((3, count, FF), bf16)),
        in_specs=[
            pl.BlockSpec((count, D), lambda s: (0, 0)),
            pl.BlockSpec((2, count, BACK_TILE), lambda s: (0, 0, s)),
        ]
        + weight_specs(layer, BACK_TILE)
        + [pl.BlockSpec(memory_space=pltpu.HBM)] * len(after),
        out_specs=(
            pl.BlockSpec((count, D), lambda s: (0, 0)),
            pl.BlockSpec((3, count, BACK_TILE), lambda s: (0, 0, s)),
        ),
        scratch_shapes=[pltpu.VMEM((count, D), f32)],
        compiler_params=pltpu.CompilerParams(vmem_limit_bytes=56 * MIB),
        cost_estimate=pl.CostEstimate(
            flops=6 * count * D * FF, bytes_accessed=6 * D * FF, transcendentals=count * FF
        ),
        name="expert_backward",
    )(
        grad,
        far_away(acts),
        far_away(w_in),
        far_away(w_in),
        far_away(w_out),
        *[far_away(a) for a in after],
    )


def expert_grads_body(shares, rows_ref, grad_ref, parts_ref, out_ref, rows_t, grad_t):
    @pl.when(pl.program_id(0) == 0)
    def _():
        rows_t[...] = rows_ref[...].T
        grad_t[...] = grad_ref[...].T

    tall = D // shares
    for which in range(3):
        left = rows_t if which < 2 else grad_t
        got = dot(left[...], parts_ref[which], 1, 0).astype(bf16)
        for share in range(shares):
            out_ref[share, which] = got[share * tall : (share + 1) * tall, :]


def expert_grads(shares, rows, grad, parts, after=()):
    count = rows.shape[0]
    tall = D // shares

    def body(*refs):
        expert_grads_body(shares, *refs[:3], *refs[3 + len(after) :])

    return pl.pallas_call(
        body,
        grid=(FF_STEPS,),
        out_shape=pltpu.HBM((shares, 3, tall, FF), bf16),
        in_specs=[
            pl.BlockSpec((count, D), lambda s: (0, 0)),
            pl.BlockSpec((count, D), lambda s: (0, 0)),
            pl.BlockSpec((3, count, FF_TILE), lambda s: (0, 0, s)),
        ]
        + [pl.BlockSpec(memory_space=pltpu.HBM)] * len(after),
        out_specs=pl.BlockSpec((shares, 3, tall, FF_TILE), lambda s: (0, 0, 0, s)),
        scratch_shapes=[pltpu.VMEM((D, count), bf16), pltpu.VMEM((D, count), bf16)],
        compiler_params=pltpu.CompilerParams(vmem_limit_bytes=28 * MIB),
        cost_estimate=pl.CostEstimate(
            flops=6 * count * D * FF, bytes_accessed=6 * D * FF, transcendentals=0
        ),
        name="expert_grads",
    )(rows, grad, far_away(parts), *[far_away(a) for a in after])


def place_expert_grads(layer, summed, before=None, after=()):
    tall = summed.shape[1]
    outs = (
        pltpu.HBM((LAYERS, 1, tall, 2 * FF), f32),
        pltpu.HBM((LAYERS, 1, tall, FF), f32),
    )
    held = [] if before is None else list(before)

    def body(part_ref, out_part_ref, *refs):
        in_ref, out_ref = refs[-2:]
        in_ref[0, 0] = part_ref[0].astype(f32)
        out_ref[0, 0] = out_part_ref[0].astype(f32)

    return pl.pallas_call(
        body,
        grid=(2,),
        out_shape=outs,
        in_specs=[
            pl.BlockSpec((1, tall, FF), lambda s: (s, 0, 0)),
            pl.BlockSpec((1, tall, FF), lambda s: (2, 0, 0)),
        ]
        + [pl.BlockSpec(memory_space=pl.ANY)] * (len(held) + len(after)),
        out_specs=(
            pl.BlockSpec((1, 1, tall, FF), lambda s: (layer, 0, 0, s)),
            pl.BlockSpec((1, 1, tall, FF), lambda s: (layer, 0, 0, 0)),
        ),
        input_output_aliases={2: 0, 3: 1} if held else {},
        compiler_params=pltpu.CompilerParams(vmem_limit_bytes=32 * MIB),
        name="place_expert_grads",
    )(far_away(summed), far_away(summed), *[far_away(h) for h in [*held, *after]])


TWIN = [(i, i ^ 1) for i in range(GROUP)]
ACROSS = [(i, i ^ 2) for i in range(GROUP)]


def share_pieces(piece):
    across = lax.ppermute(piece, "context", ACROSS)
    twin = lax.ppermute(piece, "context", TWIN)
    return [piece, twin, across, lax.ppermute(across, "context", TWIN)]


def sum_pieces(keep, send):
    rows = keep.shape[0] // 2
    recv = lax.ppermute(send, "context", TWIN)
    other = (keep[rows:] + recv[rows:].astype(f32)).astype(bf16)
    return keep, recv, lax.ppermute(other, "context", ACROSS)


def sum_zone(zone):
    return jnp.sum(zone.astype(f32), 0)


def dense_sum(
    experts, pairs, share, table_share, place, grad_w_in, grad_w_out, small, gain_a, by_distance,
    hits,
):
    by_bucket = jnp.dot(hits, by_distance[:OWN].T, precision=lax.Precision.HIGHEST)
    buckets = jnp.where(
        jnp.arange(GROUP)[None, None, :] == place[0], by_bucket[:, :, None], 0.0
    ).reshape(experts, GROUP, pairs, 1, table_share)
    features = jnp.concatenate([small[:16], gain_a[:1], small[16:17]], 0).T
    features = features.reshape(experts, GROUP, pairs, share, 18)
    flat = jnp.zeros((experts, GROUP, pairs, share, LANES), f32)
    flat = flat.at[..., :18].set(features).at[..., :1, 64 : 64 + table_share].set(buckets)
    pack = jnp.concatenate(
        [grad_w_in.reshape(experts, GROUP, pairs, share, PACKED), flat.astype(bf16)], -1
    ).transpose(0, 2, 1, 3, 4)
    pack = pack.reshape(experts * pairs, GROUP * share, PACKED + LANES)
    mine = lax.psum_scatter(pack, ("experts", "dp"), scatter_dimension=0, tiled=False)
    inner = lax.all_to_all(
        mine.reshape(GROUP, share, PACKED + LANES), "context", split_axis=0, concat_axis=0
    ).astype(f32)
    g_in = inner[..., :PACKED].reshape(GROUP, share, 3, OWN, HEAD_DIM)
    g_in = g_in.transpose(1, 2, 3, 0, 4).reshape(share, 3 * D)
    placed_rows = jnp.where(
        jnp.arange(GROUP)[None, :, None, None] == place[0],
        grad_w_out.reshape(OWN, 1, HEAD_DIM, D),
        jnp.zeros((), bf16),
    ).reshape(D, D)
    g_out = lax.psum_scatter(placed_rows, ALL, scatter_dimension=0, tiled=True).astype(f32)
    return g_in, g_out, jnp.sum(inner[..., PACKED:], 0)


def exchange(rows):
    return lax.all_to_all(rows, "experts", split_axis=0, concat_axis=0, tiled=True)


def on_device(
    tokens, doc_starts, expert_ids, attn_in, attn_out, router, gains, rel_table,
    expert_in, expert_out, out_grad,
):
    experts = lax.axis_size("experts")
    pairs = lax.axis_size("dp")
    share = attn_in.shape[1]
    table_share = rel_table.shape[1]
    direct = share * pairs == HEAD_DIM and experts * GROUP == HEADS and pairs == 2
    place = jnp.stack([lax.axis_index("context"), lax.axis_index("dp")]).astype(jnp.int32)
    start_tokens = tokens[0]
    ids = expert_ids[0]
    idst = ids.T
    rows = start_tokens.shape[0]
    capacity = (10 * rows + 4 * experts - 1) // (4 * experts)
    slots = experts * capacity
    grad_in = out_grad[0]
    hits = jnp.asarray(bucket_hits())

    packets = prepare(direct, attn_in, attn_out, router, gains, rel_table)

    def spread(packet):
        return lax.all_to_all(packet, "context", split_axis=0, concat_axis=0)

    def gather(part):
        return lax.all_gather(part, ("experts", "dp"), axis=0, tiled=False).reshape(
            experts, pairs, *part.shape
        )

    if direct:
        first = gather(jnp.concatenate([spread(packets[0]), packets[2]], -1))
        second = gather(jnp.concatenate([spread(packets[1]), packets[3]], -1))
        w_in0, w_out0, feature, bias = unpack(place, first, hits, True)
        w_in1, w_out1 = unpack(place, second, hits, False)
        w_in, w_out = [w_in0, w_in1], [w_out0, w_out1]
    else:
        w_in, w_out = [], []
        for layer in range(LAYERS):
            got = gather(spread(packets[layer])).transpose(0, 2, 1, 3, 4)
            w_in.append(got[..., :PACKED].reshape(D, PACKED))
            if layer == 0:
                small_all = got[..., PACKED:]
            full = lax.all_gather(attn_out[layer], ALL, axis=0, tiled=True)
            mine = lax.dynamic_index_in_dim(
                full.reshape(OWN, GROUP, HEAD_DIM, D), place[0], 1, keepdims=False
            )
            w_out.append(mine.reshape(OWN_COLS, GROUP, D // GROUP).transpose(1, 0, 2))
        feature = small_all.reshape(D, LANES).astype(f32).T
        bias_rows = []
        for layer in range(LAYERS):
            at = 64 + 32 * layer
            table = small_all[:, :, :, 0, at : at + table_share].reshape(BUCKETS, OWN, GROUP)
            table = lax.dynamic_index_in_dim(table, place[0], 2, keepdims=False).astype(f32)
            row = jnp.dot((table - table[-1:]).T, hits, precision=lax.Precision.HIGHEST)
            bias_rows.append(jnp.pad(row, ((0, 8 - OWN), (0, 0))))
        bias = jnp.stack(bias_rows)
    places = jnp.arange(GROUP * rows, dtype=jnp.int32)
    starts = doc_starts[0]
    low = jnp.max(
        jnp.where(starts[:, None] <= places[None, :], starts[:, None], 0), 0, keepdims=True
    )

    pieces = share_pieces(start_tokens)
    x = start_tokens
    kept = []
    for layer in range(LAYERS):
        packed, log_total, mixed, keep, send, *normed_all = attention_forward(
            layer, place, pieces, w_in[layer], feature, bias, low, w_out[layer]
        )
        normed_rows = normed_all if layer == 0 else pieces
        keep, recv, far = sum_pieces(keep, send)
        last = layer == LAYERS - 1
        routed = route(
            layer, experts, capacity, x, keep, recv, far, feature, ids, idst,
            grad_in if last else None,
        )
        middle, sent_rows, soft, meta, dest = routed[:5]
        arrived = exchange(sent_rows)
        if last:
            arrived_grad = exchange(routed[5])
        produced, acts = expert_forward(layer, arrived, expert_in, expert_out)
        back = exchange(produced)
        kept.append(
            (x, normed_rows, packed, log_total, mixed, middle, soft, meta, dest, arrived, acts, back)
        )
        if last:
            (result,) = combine(middle, back, meta)
        else:
            x, normed = combine(middle, back, meta, feature)
            pieces = share_pieces(normed)

    g = grad_in
    inner, outer, expert_totals = [], [], []
    other = None
    placed_grads = None
    for layer in range(LAYERS - 1, -1, -1):
        (x, normed_rows, packed, log_total, mixed, middle, soft, meta, dest, arrived, acts,
         back) = kept[layer]
        drows, parts = expert_backward(layer, arrived_grad, acts, expert_in, expert_out)
        came = exchange(drows)
        early = [] if other is None else [other]
        weight_grads = expert_grads(
            GROUP * pairs, arrived, arrived_grad, parts, after=[back] + early
        )
        weight_grads = hold(weight_grads, [came])
        total = lax.psum_scatter(
            weight_grads, ("context", "dp"), scatter_dimension=0, tiled=False
        )
        dmiddle, dattn, small_b = expert_token_back(
            layer, back, came, g, middle, soft, meta, ids, feature,
            after=[weight_grads] + expert_totals,
        )
        early = []
        if expert_totals:
            early.append(place_expert_grads(layer + 1, expert_totals[0]))
            placed_grads = early.pop()
            early.append(placed_grads[0])
        expert_totals.append(total)
        if direct and other is not None:
            zone = exchange((keep_dense + other.astype(f32)).astype(bf16))
            outer.append(zone)
            early.append(zone)
        grad_pieces = share_pieces(dattn)
        grad_packed, keep, send, by_distance, gain_a = attention_backward(
            layer, place, grad_pieces, w_in[layer], feature, bias, low, w_out[layer], packed,
            log_total, normed_rows, after=early,
        )
        if direct and other is not None:
            inner.append(
                spread(sum_zone(zone)[:, : PACKED + LANES].astype(bf16).reshape(GROUP, share, -1))
            )
        keep, recv, far = sum_pieces(keep, send)
        if layer > 0:
            below = kept[layer - 1]
            g, sent = attention_token_back(
                layer, x, dmiddle, keep, recv, far, feature, below[7], below[8], slots
            )
            arrived_grad = exchange(sent)
        else:
            (g,) = attention_token_back(layer, x, dmiddle, keep, recv, far, feature)
        if direct:
            keep_dense, send_dense = dense_pack(
                experts, pairs, share, place, normed_rows, grad_pieces, grad_packed, mixed,
                small_b, gain_a, by_distance, hits, after=inner,
            )
            other = lax.ppermute(send_dense, "dp", [(0, 1), (1, 0)])
        else:
            grad_w_in, grad_w_out = dense_grads(normed_rows, grad_pieces, grad_packed, mixed)
            inner.append(
                dense_sum(
                    experts, pairs, share, table_share, place, grad_w_in, grad_w_out, small_b,
                    gain_a, by_distance, hits,
                )
            )
    expert_grads_all = place_expert_grads(0, expert_totals[1], placed_grads)
    if direct:
        zone = exchange((keep_dense + other.astype(f32)).astype(bf16))
        outer.append(zone)
        inner.append(
            spread(sum_zone(zone)[:, : PACKED + LANES].astype(bf16).reshape(GROUP, share, -1))
        )
        grad_attn_in, grad_attn_out, small_grad = finish_dense(
            experts, share, inner[::-1], outer[::-1]
        )
    else:
        grad_attn_in, grad_attn_out, small_grad = (
            jnp.stack([entry[k] for entry in inner[::-1]]) for k in range(3)
        )
    return (
        result[None],
        g[None],
        grad_attn_in,
        grad_attn_out,
        small_grad[..., :experts],
        small_grad[..., 16:18],
        small_grad[:, 0, 64 : 64 + table_share],
        *expert_grads_all,
    )


def solution(mesh):
    return jax.shard_map(
        on_device,
        mesh=mesh,
        in_specs=(
            P(("experts", "dp"), "context", None),
            P(("experts", "dp"), None),
            P(("experts", "dp"), "context", None),
            P(None, ("experts", "context", "dp"), None),
            P(None, ("experts", "context", "dp"), None),
            P(None, ("experts", "context", "dp"), None),
            P(None, ("experts", "context", "dp"), None),
            P(None, ("experts", "context", "dp")),
            P(None, "experts", None, None),
            P(None, "experts", None, None),
            P(("experts", "dp"), "context", None),
        ),
        out_specs=(
            P(("experts", "dp"), "context", None),
            P(("experts", "dp"), "context", None),
            P(None, ("experts", "context", "dp"), None),
            P(None, ("experts", "context", "dp"), None),
            P(None, ("experts", "context", "dp"), None),
            P(None, ("experts", "context", "dp"), None),
            P(None, ("experts", "context", "dp")),
            P(None, "experts", ("context", "dp"), None),
            P(None, "experts", ("context", "dp"), None),
        ),
        check_vma=False,
    )
```

```python
import math

import jax
import jax.numpy as jnp
import numpy as np
from jax import lax
from jax.experimental import pallas as pl
from jax.experimental.pallas import tpu as pltpu
from jax.sharding import PartitionSpec as P

D = 1024
HEADS = 16
HEAD_DIM = 64
FF = 2816
BUCKETS = 32
MAX_DISTANCE = 128
LAYERS = 2
EPSILON = 1e-06
NEGATIVE = -1e30
SCORE_SCALE = 0.125
ALL = ("experts", "context", "dp")
GROUP = 4
OWN = HEADS // GROUP
OWN_COLS = OWN * HEAD_DIM
PACKED = 3 * OWN_COLS
LANES = 128
REACH = 512
FF_TILE = 256
FF_STEPS = FF // FF_TILE
BACK_TILE = 1408
BACK_STEPS = FF // BACK_TILE
MIB = 1 << 20

bf16 = jnp.bfloat16
f32 = jnp.float32


def bucket_bounds(bucket_count, far_reach):
    half_count = bucket_count // 2
    bounds = list(range(1, half_count + 1))
    for section_index in range(1, half_count):
        bounds.append(
            int(math.ceil(half_count * (far_reach / half_count) ** (section_index / half_count)))
        )
    return np.array(bounds, np.int32)


def bucket_hits():
    distance = np.arange(REACH)
    bucket = (distance[:, None] >= bucket_bounds(BUCKETS, MAX_DISTANCE)).sum(-1)
    return (np.arange(BUCKETS)[:, None] == bucket[None, :]).astype(np.float32)


def dot(a, b, ca, cb, precision=None):
    return lax.dot_general(
        a, b, (((ca,), (cb,)), ((), ())), precision=precision, preferred_element_type=f32
    )


def whole_call(
    body, out_shape, args, *, flops=0, limit=16, scratch=(), smem=0, name=None, after=(),
    streamed=False,
):
    specs = [pl.BlockSpec(memory_space=pltpu.SMEM)] * smem + [
        pl.BlockSpec(memory_space=pltpu.VMEM)
    ] * (len(args) - smem)
    outs = tuple(out_shape)
    moved = sum(a.size * a.dtype.itemsize for a in list(args) + list(outs))
    specs += [pl.BlockSpec(memory_space=pltpu.HBM)] * len(after)
    used = len(args)
    args = list(args) + [far_away(a) for a in after]

    def ordered(*refs):
        body(*refs[:used], *refs[used + len(after) :])

    if streamed:
        args = args[:smem] + [far_away(a) for a in args[smem:]]

        def full(a):
            return pl.BlockSpec(a.shape, lambda i: (0,) * len(a.shape))

        return pl.pallas_call(
            ordered,
            grid=(1,),
            out_shape=outs,
            in_specs=specs[:smem] + [full(a) for a in args[smem:used]] + specs[used:],
            out_specs=tuple(full(o) for o in outs),
            scratch_shapes=list(scratch),
            compiler_params=pltpu.CompilerParams(vmem_limit_bytes=limit * MIB),
            cost_estimate=pl.CostEstimate(
                flops=int(flops), bytes_accessed=int(moved), transcendentals=0
            ),
            name=name,
        )(*args)
    return pl.pallas_call(
        ordered,
        out_shape=outs,
        in_specs=specs,
        out_specs=tuple(pl.BlockSpec(memory_space=pltpu.VMEM) for _ in outs),
        scratch_shapes=list(scratch),
        compiler_params=pltpu.CompilerParams(vmem_limit_bytes=limit * MIB),
        cost_estimate=pl.CostEstimate(
            flops=int(flops), bytes_accessed=int(moved), transcendentals=0
        ),
        name=name,
    )(*args)


def far_away(x):
    return pltpu.with_memory_space_constraint(x, pltpu.HBM)


def hold(x, after):
    def body(*refs):
        pass

    return pl.pallas_call(
        body,
        out_shape=pltpu.HBM(x.shape, x.dtype),
        in_specs=[pl.BlockSpec(memory_space=pltpu.HBM)] * (1 + len(after)),
        out_specs=pl.BlockSpec(memory_space=pltpu.HBM),
        input_output_aliases={0: 0},
        compiler_params=pltpu.CompilerParams(vmem_limit_bytes=MIB),
        cost_estimate=pl.CostEstimate(flops=0, bytes_accessed=0, transcendentals=0),
        name="hold",
    )(far_away(x), *[far_away(a) for a in after])


def shape(dims, dtype):
    return jax.ShapeDtypeStruct(dims, dtype)


def rms_scale(inputs):
    return lax.rsqrt(jnp.mean(inputs * inputs, -1, keepdims=True) + EPSILON)


def norm_back(inputs, gain_row, upstream):
    inverse = rms_scale(inputs)
    scaled = upstream * gain_row
    inner_mean = jnp.mean(inputs * scaled, -1, keepdims=True)
    grad_inputs = inverse * scaled - inputs * (inverse * inverse * inverse) * inner_mean
    grad_gain = jnp.sum(upstream * inputs * inverse, 0, keepdims=True)
    return grad_inputs, grad_gain


def placed(count, offset):
    index = lax.broadcasted_iota(jnp.int32, (count, LANES), 0)
    lane = lax.broadcasted_iota(jnp.int32, (count, LANES), 1)
    return one_hot(lane == index + offset)


def prepare_body(direct, in_ref, out_ref, router_ref, gains_ref, table_ref, *packets):
    share = in_ref.shape[1]
    for layer in range(LAYERS):
        for which in range(3):
            for head in range(OWN):
                for c in range(GROUP):
                    source = which * D + (head * GROUP + c) * HEAD_DIM
                    target = which * OWN_COLS + head * HEAD_DIM
                    target += layer * (PACKED + LANES)
                    packets[0][c, :, target : target + HEAD_DIM] = in_ref[
                        layer, :, source : source + HEAD_DIM
                    ]
        if direct:
            width = D // GROUP
            for q in range(GROUP):
                packets[1 + layer][q] = out_ref[layer, :, q * width : (q + 1) * width]
    small = jnp.zeros((share, LANES), f32)
    row = lax.broadcasted_iota(jnp.int32, (share, LANES), 0)
    for layer in range(LAYERS):
        top = 32 * layer
        small = small + dot(router_ref[layer], placed(router_ref.shape[2], top), 1, 0)
        small = small + dot(gains_ref[layer], placed(2, top + 16), 1, 0)
        bucket = dot(table_ref[layer : layer + 1, :], placed(table_ref.shape[1], top + 64), 1, 0)
        small = small + jnp.where(row == 0, bucket, 0.0)
    for c in range(GROUP):
        packets[0][c, :, PACKED : PACKED + LANES] = small.astype(bf16)


def prepare(direct, attn_in, attn_out, router, gains, rel_table):
    share = attn_in.shape[1]
    outs = [shape((GROUP, share, 2 * PACKED + LANES), bf16)]
    if direct:
        outs += [shape((GROUP, share, D // GROUP), bf16)] * LAYERS

    def body(*refs):
        prepare_body(direct, *refs)

    return whole_call(
        body, outs, [attn_in, attn_out, router, gains, rel_table], streamed=True, name="prepare"
    )


def unpack(place, hits, experts, pairs, layer, got):
    share = got.shape[-2]
    width = D // GROUP
    first = layer == 0

    def body(place_ref, hits_ref, got_ref, w_in_ref, w_out_ref, *rest):
        for index in range(experts * pairs):
            e, d = index // pairs, index % pairs
            for c in range(GROUP):
                owner = (e * GROUP + c) * pairs + d
                at = owner * share
                w_in_ref[at : at + share, :] = got_ref[index, c, :, :PACKED]
                w_out_ref[c, index * share : (index + 1) * share, :] = got_ref[
                    index, c, :, got_ref.shape[-1] - width :
                ]
                if first:
                    flags = got_ref[index, c, :, PACKED : PACKED + LANES].astype(f32)
                    rest[2][at : at + share, :] = flags
                    rest[3][owner : owner + 1, :] = flags[:1, :]
        if not first:
            return
        feature_ref, bias_ref, flat_ref, bucket_ref = rest
        feature_ref[...] = flat_ref[...].T
        head = lax.broadcasted_iota(jnp.int32, (8, LANES), 0)
        lane = lax.broadcasted_iota(jnp.int32, (8, LANES), 1)
        for other in range(LAYERS):
            mine = jnp.where(
                (lane == 64 + 32 * other + head * GROUP + place_ref[0]) & (head < OWN), 1.0, 0.0
            )
            table = dot(mine, bucket_ref[...], 1, 1, lax.Precision.HIGHEST)
            bias_ref[other] = dot(
                table - table[:, BUCKETS - 1 :], hits_ref[...], 1, 0, lax.Precision.HIGHEST
            )

    outs = [shape((D, PACKED), bf16), shape((GROUP, OWN_COLS, D // GROUP), bf16)]
    scratch = []
    if first:
        outs += [shape((LANES, D), f32), shape((LAYERS, 8, REACH), f32)]
        scratch = [pltpu.VMEM((D, LANES), f32), pltpu.VMEM((BUCKETS, LANES), f32)]
    return whole_call(
        body, outs, [place, hits, got], smem=1, scratch=scratch, name="unpack"
    )


def near_bias(bias_ref, layer, head, rows):
    row = bias_ref[layer, head : head + 1, :]
    return pltpu.roll(jnp.broadcast_to(row, (rows, REACH)), 0, 1, stride=1, stride_axis=0)


def masked_scores(keys, queries, near, low, key_block, query_block, rows):
    scores = dot(keys, queries, 1, 1)
    key_place = lax.broadcasted_iota(jnp.int32, (rows, rows), 0)
    seen = key_place >= low - key_block * rows
    if key_block == query_block:
        scores = scores + near[:, :rows]
        seen = seen & (key_place <= lax.broadcasted_iota(jnp.int32, (rows, rows), 1))
    elif key_block == query_block - 1:
        scores = scores + near[:, rows:]
    return jnp.where(seen, scores, NEGATIVE)


def attention_forward_body(
    layer, place_ref, n0, n1, n2, n3, w_ref, feature_ref, bias_ref, low_ref, wo_ref,
    packed_ref, log_ref, mixed_ref, keep_ref, send_ref, *normed_ref,
):
    me = place_ref[0]
    rows = n0.shape[0]
    for r, piece in enumerate((n0, n1, n2, n3)):
        normed = piece[...]
        if layer == 0:
            wide = normed.astype(f32)
            normed = (wide * rms_scale(wide) * feature_ref[16:17, :]).astype(bf16)
            normed_ref[0][r * rows : (r + 1) * rows, :] = normed
        packed_ref[r * rows : (r + 1) * rows, :] = dot(normed, w_ref[...], 1, 0).astype(bf16)
    lane = lax.broadcasted_iota(jnp.int32, (rows, LANES), 1)
    starts = [pl.multiple_of((b ^ me) * rows, rows) for b in range(GROUP)]
    for pair in range(OWN // 2):
        at = pair * LANES

        def part(b, which):
            column = which * OWN_COLS + at
            return packed_ref[pl.ds(starts[b], rows), column : column + LANES]

        sides = [(lane // HEAD_DIM) == side for side in range(2)]
        nears = [near_bias(bias_ref, layer, pair * 2 + side, rows) for side in range(2)]
        for qb in range(GROUP):
            low = low_ref[:, qb * rows : (qb + 1) * rows]
            queries = part(qb, 0) * SCORE_SCALE
            total = None
            for side in range(2):
                mine = jnp.where(sides[side], queries, 0).astype(bf16)
                tiles = [
                    masked_scores(part(kb, 1), mine, nears[side], low, kb, qb, rows)
                    for kb in range(qb + 1)
                ]
                peak = jnp.max(tiles[0], 0, keepdims=True)
                for tile in tiles[1:]:
                    peak = jnp.maximum(peak, jnp.max(tile, 0, keepdims=True))
                weight_sum = jnp.zeros((1, rows), f32)
                out = jnp.zeros((LANES, rows), f32)
                for kb, tile in enumerate(tiles):
                    power = jnp.exp(tile - peak)
                    weight_sum = weight_sum + jnp.sum(power, 0, keepdims=True)
                    values = jnp.where(sides[side], part(kb, 2), 0).astype(bf16)
                    out = out + dot(values, power.astype(bf16), 0, 0)
                out = out / weight_sum
                total = out if total is None else total + out
                head = pair * 2 + side
                log_ref[head : head + 1, qb * rows : (qb + 1) * rows] = peak + jnp.log(weight_sum)
            mixed_ref[pl.ds(starts[qb], rows), at : at + LANES] = total.T.astype(bf16)
    width = wo_ref.shape[2]
    for r, (target, offset) in enumerate(
        ((keep_ref, 0), (send_ref, 0), (keep_ref, rows), (send_ref, rows))
    ):
        mixed = mixed_ref[r * rows : (r + 1) * rows, :]
        for q in range(wo_ref.shape[0]):
            target[offset : offset + rows, q * width : (q + 1) * width] = dot(
                mixed, wo_ref[q], 1, 0
            ).astype(target.dtype)


def attention_forward(layer, place, pieces, w_in, feature, bias, low, w_out):
    rows = pieces[0].shape[0]
    total = GROUP * rows
    outs = [
        shape((total, PACKED), bf16),
        shape((8, total), f32),
        shape((total, OWN_COLS), bf16),
        shape((2 * rows, D), f32),
        shape((2 * rows, D), bf16),
    ]
    if layer == 0:
        outs.append(shape((total, D), bf16))

    def body(*refs):
        attention_forward_body(layer, *refs)

    return whole_call(
        body,
        outs,
        [place, *pieces, w_in, feature, bias, low, w_out],
        smem=1,
        flops=2 * total * D * (PACKED + OWN_COLS) + 2 * total * total * OWN_COLS * 2,
        limit=24,
        name="attention_forward",
    )


def attention_backward_body(
    layer, place_ref, d0, d1, d2, d3, w_ref, feature_ref, bias_ref, low_ref, wo_ref, packed_ref,
    log_ref, *refs,
):
    normed_refs = refs[:-8]
    (grad_packed_ref, keep_ref, send_ref, table_ref, gain_ref, grad_mixed_ref, dk_ref,
     dv_ref) = refs[-8:]
    me = place_ref[0]
    rows = d0.shape[0]
    width = wo_ref.shape[2]
    for r, piece in enumerate((d0, d1, d2, d3)):
        got = jnp.zeros((rows, OWN_COLS), f32)
        for q in range(wo_ref.shape[0]):
            got = got + dot(piece[:, q * width : (q + 1) * width], wo_ref[q], 1, 1)
        grad_mixed_ref[r * rows : (r + 1) * rows, :] = got.astype(bf16)
    lane = lax.broadcasted_iota(jnp.int32, (rows, LANES), 1)
    starts = [pl.multiple_of((b ^ me) * rows, rows) for b in range(GROUP)]
    table_ref[...] = jnp.zeros(table_ref.shape, f32)
    for pair in range(OWN // 2):
        at = pair * LANES

        def part(b, which):
            column = which * OWN_COLS + at
            return packed_ref[pl.ds(starts[b], rows), column : column + LANES]

        sides = [(lane // HEAD_DIM) == side for side in range(2)]
        nears = [near_bias(bias_ref, layer, pair * 2 + side, rows) for side in range(2)]
        diag = [jnp.zeros((rows, rows), f32) for _ in range(2)]
        before = [jnp.zeros((rows, rows), f32) for _ in range(2)]
        far = [jnp.zeros((1, rows), f32) for _ in range(2)]
        dk_ref[...] = jnp.zeros(dk_ref.shape, f32)
        dv_ref[...] = jnp.zeros(dv_ref.shape, f32)
        for qb in range(GROUP):
            low = low_ref[:, qb * rows : (qb + 1) * rows]
            queries = part(qb, 0) * SCORE_SCALE
            upstream = grad_mixed_ref[pl.ds(starts[qb], rows), at : at + LANES]
            grad_queries = jnp.zeros((LANES, rows), f32)
            for side in range(2):
                head = pair * 2 + side
                mine = jnp.where(sides[side], queries, 0).astype(bf16)
                above = jnp.where(sides[side], upstream, 0).astype(bf16)
                log_total = log_ref[head : head + 1, qb * rows : (qb + 1) * rows]
                probs, grads = [], []
                row_dot = jnp.zeros((1, rows), f32)
                for kb in range(qb + 1):
                    scores = masked_scores(part(kb, 1), mine, nears[side], low, kb, qb, rows)
                    prob = jnp.exp(scores - log_total)
                    grad = dot(part(kb, 2), above, 1, 1)
                    row_dot = row_dot + jnp.sum(prob * grad, 0, keepdims=True)
                    probs.append(prob)
                    grads.append(grad)
                for kb in range(qb + 1):
                    grad_score = probs[kb] * (grads[kb] - row_dot)
                    if kb == qb:
                        diag[side] = diag[side] + grad_score
                    elif kb == qb - 1:
                        before[side] = before[side] + grad_score
                    else:
                        far[side] = far[side] + jnp.sum(grad_score, 0, keepdims=True)
                    grad_low = grad_score.astype(bf16)
                    keys = jnp.where(sides[side], part(kb, 1), 0).astype(bf16)
                    grad_queries = grad_queries + dot(keys, grad_low, 0, 0)
                    span = slice(kb * rows, (kb + 1) * rows)
                    dk_ref[span, :] += dot(grad_low, mine, 1, 0)
                    dv_ref[span, :] += dot(probs[kb].astype(bf16), above, 1, 0)
            grad_packed_ref[pl.ds(starts[qb], rows), at : at + LANES] = (
                grad_queries.T * SCORE_SCALE
            ).astype(bf16)
        for kb in range(GROUP):
            span = slice(kb * rows, (kb + 1) * rows)
            for which, source in ((1, dk_ref), (2, dv_ref)):
                column = which * OWN_COLS + at
                grad_packed_ref[pl.ds(starts[kb], rows), column : column + LANES] = source[
                    span, :
                ].astype(bf16)
        distance = lax.broadcasted_iota(jnp.int32, (1, REACH), 1)
        for side in range(2):
            head = pair * 2 + side
            skewed = jnp.concatenate([diag[side], before[side]], 1)
            row_index = lax.broadcasted_iota(jnp.int32, (rows, REACH), 0)
            step = 1
            while step < rows:
                skewed = jnp.where(
                    (row_index & step) != 0, pltpu.roll(skewed, REACH - step, 1), skewed
                )
                step *= 2
            by_distance = jnp.sum(skewed, 0, keepdims=True)
            far_sum = jnp.sum(far[side], 1, keepdims=True)
            table_ref[head : head + 1, :] = by_distance + jnp.where(
                distance == REACH - 1, far_sum, 0.0
            )
    for r, (target, offset) in enumerate(
        ((keep_ref, 0), (send_ref, 0), (keep_ref, rows), (send_ref, rows))
    ):
        grad_normed = dot(grad_packed_ref[r * rows : (r + 1) * rows, :], w_ref[...], 1, 1)
        target[offset : offset + rows, :] = grad_normed.astype(target.dtype)
        part_gain = jnp.sum(grad_normed * block_of(normed_refs, r, rows).astype(f32), 0, keepdims=True)
        gain_sum = part_gain if r == 0 else gain_sum + part_gain
    gain_row = feature_ref[32 * layer + 16 : 32 * layer + 17, :]
    gain_ref[...] = jnp.broadcast_to(gain_sum / gain_row, gain_ref.shape)


def block_of(refs, r, rows):
    return refs[r][...] if len(refs) > 1 else refs[0][r * rows : (r + 1) * rows, :]


def attention_backward(
    layer, place, pieces, w_in, feature, bias, low, w_out, packed, log_total, normed, after=()
):
    rows = pieces[0].shape[0]
    total = GROUP * rows

    def body(*refs):
        attention_backward_body(layer, *refs)

    return whole_call(
        body,
        (
            shape((total, PACKED), bf16),
            shape((2 * rows, D), f32),
            shape((2 * rows, D), bf16),
            shape((8, REACH), f32),
            shape((8, D), f32),
        ),
        [place, *pieces, w_in, feature, bias, low, w_out, packed, log_total, *normed],
        smem=1,
        after=after,
        scratch=[
            pltpu.VMEM((total, OWN_COLS), bf16),
            pltpu.VMEM((total, LANES), f32),
            pltpu.VMEM((total, LANES), f32),
        ],
        flops=2 * total * D * (PACKED + OWN_COLS) + 2 * total * total * OWN_COLS * 5,
        limit=24,
        name="attention_backward",
    )


def dense_products(normed, upstream, grad_packed_ref, mixed_ref):
    rows = upstream[0].shape[0]
    total_in = None
    total_out = None
    for r in range(GROUP):
        span = slice(r * rows, (r + 1) * rows)
        one = dot(block_of(normed, r, rows), grad_packed_ref[span, :], 0, 0)
        two = dot(mixed_ref[span, :], upstream[r][...], 0, 0)
        total_in = one if total_in is None else total_in + one
        total_out = two if total_out is None else total_out + two
    return total_in, total_out


def dense_grads(normed, upstream, grad_packed, mixed):
    rows = upstream[0].shape[0]
    count = len(normed)

    def body(*refs):
        total_in, total_out = dense_products(
            refs[:count], refs[count : count + GROUP], refs[-4], refs[-3]
        )
        refs[-2][...] = total_in.astype(bf16)
        refs[-1][...] = total_out.astype(bf16)

    return whole_call(
        body,
        (shape((D, PACKED), bf16), shape((OWN_COLS, D), bf16)),
        [*normed, *upstream, grad_packed, mixed],
        flops=2 * GROUP * rows * D * (PACKED + OWN_COLS),
        name="dense_grads",
    )


def dense_pack(experts, pairs, share, place, normed, upstream, grad_packed, mixed, small, gain_a,
               by_distance, hits, split, after=()):
    rows = upstream[0].shape[0]
    count = len(normed)
    width = D // GROUP
    rest = LANES + width
    total = PACKED if split else PACKED + rest

    def body(place_ref, *refs):
        grad_packed_ref, mixed_ref, small_ref, gain_ref, distance_ref, hits_ref = refs[
            count + GROUP : count + GROUP + 6
        ]
        outs = refs[count + GROUP + 6 : -3]
        in_ref, out_ref, flat_ref = refs[-3:]
        total_in, total_out = dense_products(
            refs[:count], refs[count : count + GROUP], grad_packed_ref, mixed_ref
        )
        in_ref[...] = total_in
        out_ref[...] = total_out
        row = lax.broadcasted_iota(jnp.int32, (8, D), 0)
        gains = jnp.where(
            row == 0, gain_ref[...], jnp.where(row == 1, small_ref[16:24, :], 0.0)
        )
        features = jnp.concatenate(
            [small_ref[:16, :], gains, jnp.zeros((LANES - 24, D), f32)], 0
        )
        flat_ref[...] = features.T
        by_bucket = dot(hits_ref[...], distance_ref[...], 1, 1, lax.Precision.HIGHEST)
        head = lax.broadcasted_iota(jnp.int32, (8, LANES), 0)
        lane = lax.broadcasted_iota(jnp.int32, (8, LANES), 1)
        mine = jnp.where((lane == 64 + head * GROUP + place_ref[0]) & (head < OWN), 1.0, 0.0)
        buckets = dot(by_bucket, mine, 1, 0, lax.Precision.HIGHEST)
        for index in range(BUCKETS):
            at = index * share
            flat_ref[at : at + 1, :] = flat_ref[at : at + 1, :] + buckets[index : index + 1, :]
        for side, d in enumerate((place_ref[1], 1 - place_ref[1])):
            for e in range(experts):
                for c in range(GROUP):
                    at = ((e * GROUP + c) * pairs + d) * share
                    span = pl.ds(pl.multiple_of(at, share), share)
                    to = slice(c * share, (c + 1) * share)
                    target = outs[side]
                    target[e, to, :PACKED] = in_ref[span, :].astype(target.dtype)
                    out_span = pl.ds(pl.multiple_of((e * pairs + d) * share, share), share)
                    outer = out_ref[out_span, c * width : (c + 1) * width]
                    if split:
                        outs[2][e, side, to, :LANES] = flat_ref[span, :].astype(bf16)
                        outs[2][e, side, to, LANES:] = outer.astype(bf16)
                    else:
                        target[e, to, PACKED : PACKED + LANES] = flat_ref[span, :].astype(
                            target.dtype
                        )
                        target[e, to, PACKED + LANES :] = outer.astype(target.dtype)

    outs = [
        shape((experts, GROUP * share, total), f32),
        shape((experts, GROUP * share, total), bf16),
    ]
    if split:
        outs.append(shape((experts, pairs, GROUP * share, rest), bf16))
    return whole_call(
        body,
        outs,
        [place, *normed, *upstream, grad_packed, mixed, small, gain_a, by_distance, hits],
        smem=1,
        scratch=[
            pltpu.VMEM((D, PACKED), f32),
            pltpu.VMEM((OWN_COLS, D), f32),
            pltpu.VMEM((D, LANES), f32),
        ],
        flops=2 * GROUP * rows * D * (PACKED + OWN_COLS),
        after=after,
        streamed=True,
        limit=32,
        name="dense_pack",
    )


def finish_dense(share, inner, outer):
    width = D // GROUP

    def body(*refs):
        in_ref, out_ref, small_ref = refs[1 + LAYERS :]
        for layer in range(LAYERS):
            got, rows_out = refs[0], refs[1 + layer]
            for c in range(GROUP):
                for which in range(3):
                    for head in range(OWN):
                        source = which * OWN_COLS + head * HEAD_DIM
                        target = which * D + (head * GROUP + c) * HEAD_DIM
                        in_ref[layer, :, target : target + HEAD_DIM] = got[
                            c, layer, :, source : source + HEAD_DIM
                        ].astype(f32)
                out_ref[layer, :, c * width : (c + 1) * width] = rows_out[
                    c * share : (c + 1) * share, :
                ]
            total = got[0, layer, :, PACKED:].astype(f32)
            for c in range(1, GROUP):
                total = total + got[c, layer, :, PACKED:].astype(f32)
            small_ref[layer] = total

    return whole_call(
        body,
        (
            shape((LAYERS, share, 3 * D), f32),
            shape((LAYERS, share, D), f32),
            shape((LAYERS, share, LANES), f32),
        ),
        [inner, *outer],
        name="finish_dense",
    )


def dispatch_grid(dest_rows, slots, tokens):
    place = lax.broadcasted_iota(jnp.int32, (slots, tokens), 0)
    first = place == dest_rows[0:1, :]
    second = place == dest_rows[1:2, :]
    return first, second


def one_hot(flags):
    return jnp.where(flags, 1.0, 0.0).astype(bf16)


def collect_grid(meta, slots):
    tokens = meta.shape[0]
    place = lax.broadcasted_iota(jnp.int32, (tokens, slots), 1)
    first = place == meta[:, 0:1].astype(jnp.int32)
    second = place == meta[:, 1:2].astype(jnp.int32)
    return first, second


def scatter_grads(upstream, meta, dest_rows, slots):
    tokens = upstream.shape[0]
    first, second = dispatch_grid(dest_rows, slots, tokens)
    return (
        dot(one_hot(first), (meta[:, 2:3] * upstream).astype(bf16), 1, 0)
        + dot(one_hot(second), (meta[:, 3:4] * upstream).astype(bf16), 1, 0)
    ).astype(bf16)


def slot_rows(idst, capacity):
    tokens = idst.shape[1]
    down = lax.broadcasted_iota(jnp.int32, (tokens, tokens), 0)
    across = lax.broadcasted_iota(jnp.int32, (tokens, tokens), 1)
    sub = lax.broadcasted_iota(jnp.int32, (16, tokens), 0)
    row0 = sub == idst[0:1, :]
    row1 = sub == idst[1:2, :]
    counts = dot(one_hot(row0 | row1), one_hot(down < across), 1, 0)
    found = []
    for index, row in enumerate((row0, row1)):
        slot = jnp.sum(jnp.where(row, counts, 0.0), 0, keepdims=True).astype(jnp.int32)
        found.append(idst[index : index + 1, :] * capacity + slot)
    return jnp.where(lax.broadcasted_iota(jnp.int32, (8, tokens), 0) == 0, found[0], found[1])


def send_grads(experts, capacity, idst, grad, after):
    tokens = grad.shape[0]
    slots = experts * capacity

    def body(idst_ref, grad_ref, out_ref):
        first, second = dispatch_grid(slot_rows(idst_ref[...], capacity), slots, tokens)
        out_ref[...] = dot(one_hot(first | second), grad_ref[...], 1, 0).astype(bf16)

    (out,) = whole_call(
        body, [shape((slots, D), bf16)], [idst, grad], after=after, name="send_grads"
    )
    return out


def apply_gates(rows, gates):
    def body(rows_ref, gates_ref, out_ref):
        gate = jnp.sum(gates_ref[...].astype(f32), -1, keepdims=True)
        out_ref[...] = (gate * rows_ref[...].astype(f32)).astype(bf16)

    (out,) = whole_call(
        body, [shape(rows.shape, bf16)], [rows, gates], streamed=True, name="apply_gates"
    )
    return out


def route_body(layer, experts, capacity, last, *refs):
    top = 32 * layer
    if last:
        (x_ref, keep_ref, recv_ref, far_ref, feature_ref, ids_ref, idst_ref,
         middle_ref, rows_ref, soft_ref, meta_ref, dest_ref, sent_ref) = refs
    else:
        (x_ref, keep_ref, recv_ref, far_ref, feature_ref, ids_ref, idst_ref,
         middle_ref, rows_ref, soft_ref, meta_ref, dest_ref) = refs
    tokens = x_ref.shape[0]
    slots = experts * capacity
    middle = (
        x_ref[...].astype(f32)
        + keep_ref[:tokens, :]
        + recv_ref[:tokens, :].astype(f32)
        + far_ref[...].astype(f32)
    )
    middle_ref[...] = middle
    normed = middle * rms_scale(middle) * feature_ref[top + 17 : top + 18, :]
    lane = lax.broadcasted_iota(jnp.int32, (tokens, LANES), 1)
    logits = dot(normed, feature_ref[...], 1, 1, lax.Precision.HIGHEST)
    logits = jnp.where((lane >= top) & (lane < top + experts), logits, NEGATIVE)
    power = jnp.exp(logits - jnp.max(logits, -1, keepdims=True))
    soft = power / jnp.sum(power, -1, keepdims=True)
    soft_ref[...] = soft
    ids = ids_ref[...]
    hit0 = lane == ids[:, 0:1] + top
    hit1 = lane == ids[:, 1:2] + top
    picked0 = jnp.sum(jnp.where(hit0, soft, 0.0), -1, keepdims=True)
    picked1 = jnp.sum(jnp.where(hit1, soft, 0.0), -1, keepdims=True)
    pick_total = picked0 + picked1
    down = lax.broadcasted_iota(jnp.int32, (tokens, tokens), 0)
    across = lax.broadcasted_iota(jnp.int32, (tokens, tokens), 1)
    counts = dot(one_hot(across < down), one_hot(hit0 | hit1), 1, 0)
    dest0 = ids[:, 0:1].astype(f32) * capacity + jnp.sum(
        jnp.where(hit0, counts, 0.0), -1, keepdims=True
    )
    dest1 = ids[:, 1:2].astype(f32) * capacity + jnp.sum(
        jnp.where(hit1, counts, 0.0), -1, keepdims=True
    )
    fields = (dest0, dest1, picked0 / pick_total, picked1 / pick_total, pick_total)
    meta = jnp.zeros((tokens, LANES), f32)
    for index, field in enumerate(fields):
        meta = jnp.where(lane == index, field, meta)
    meta_ref[...] = meta
    dest_rows = slot_rows(idst_ref[...], capacity)
    dest_ref[...] = dest_rows
    first, second = dispatch_grid(dest_rows, slots, tokens)
    rows_ref[...] = dot(one_hot(first | second), normed.astype(bf16), 1, 0).astype(bf16)
    if last:
        total = None
        for index, flags in enumerate((first, second)):
            gate = meta[:, 2 + index : 3 + index]
            spread = jnp.zeros((tokens, LANES), f32)
            for term in range(3):
                piece = gate.astype(bf16).astype(f32)
                spread = jnp.where(lane == term, piece, spread)
                gate = gate - piece
            got = dot(one_hot(flags), spread.astype(bf16), 1, 0)
            total = got if total is None else total + got
        sent_ref[...] = total.astype(bf16)


def route(layer, experts, capacity, x, keep, recv, far, feature, ids, idst, last, after=()):
    tokens = x.shape[0]
    slots = experts * capacity
    outs = [
        shape((tokens, D), f32),
        shape((slots, D), bf16),
        shape((tokens, LANES), f32),
        shape((tokens, LANES), f32),
        shape((8, tokens), jnp.int32),
    ]
    args = [x, keep, recv, far, feature, ids, idst]
    if last:
        outs.append(shape((slots, LANES), bf16))

    def body(*refs):
        route_body(layer, experts, capacity, last, *refs)

    return whole_call(
        body, outs, args, flops=2 * slots * tokens * D, after=after, name="route"
    )


def combine_body(last, *refs):
    if last:
        middle_ref, back_ref, meta_ref, out_ref = refs
    else:
        middle_ref, back_ref, meta_ref, gain_ref, out_ref, normed_ref = refs
    meta = meta_ref[...]
    first, second = collect_grid(meta, back_ref.shape[0])
    x = (
        middle_ref[...]
        + meta[:, 2:3] * dot(one_hot(first), back_ref[...], 1, 0)
        + meta[:, 3:4] * dot(one_hot(second), back_ref[...], 1, 0)
    )
    out_ref[...] = x.astype(out_ref.dtype)
    if not last:
        normed_ref[...] = (x * rms_scale(x) * gain_ref[48:49, :]).astype(bf16)


def combine(middle, back, meta, gain=None):
    tokens = middle.shape[0]
    args = [middle, back, meta]
    outs = [shape((tokens, D), bf16 if gain is None else f32)]
    if gain is not None:
        args.append(gain)
        outs.append(shape((tokens, D), bf16))

    def body(*refs):
        combine_body(gain is None, *refs)

    return whole_call(
        body, outs, args, flops=4 * tokens * D * back.shape[0], name="combine"
    )


def expert_token_back_body(
    layer, back_ref, came_ref, g_ref, middle_ref, soft_ref, meta_ref, ids_ref, feature_ref,
    dmiddle_ref, dattn_ref, small_ref,
):
    top = 32 * layer
    gain_row = feature_ref[top + 17 : top + 18, :]
    meta = meta_ref[...]
    g = g_ref[...].astype(f32)
    slots = back_ref.shape[0]
    first, second = collect_grid(meta, slots)
    grad_gate0 = jnp.sum(g * dot(one_hot(first), back_ref[...], 1, 0), -1, keepdims=True)
    grad_gate1 = jnp.sum(g * dot(one_hot(second), back_ref[...], 1, 0), -1, keepdims=True)
    grad_normed = dot(one_hot(first | second), came_ref[...], 1, 0)
    gap = (grad_gate0 - grad_gate1) / meta[:, 4:5]
    ids = ids_ref[...]
    lane = lax.broadcasted_iota(jnp.int32, meta.shape, 1)
    grad_soft = jnp.where(lane == ids[:, 0:1] + top, meta[:, 3:4] * gap, 0.0) + jnp.where(
        lane == ids[:, 1:2] + top, -meta[:, 2:3] * gap, 0.0
    )
    soft = soft_ref[...]
    grad_logits = soft * (grad_soft - jnp.sum(soft * grad_soft, -1, keepdims=True))
    middle = middle_ref[...]
    normed = middle * rms_scale(middle) * gain_row
    grad_router = dot(grad_logits.T, normed, 1, 0, lax.Precision.HIGHEST)
    grad_normed = grad_normed + dot(
        grad_logits, feature_ref[...], 1, 0, lax.Precision.HIGHEST
    )
    grad_branch, grad_gain = norm_back(middle, gain_row, grad_normed)
    dmiddle = g + grad_branch
    dmiddle_ref[...] = dmiddle
    dattn_ref[...] = dmiddle.astype(bf16)
    small_ref[:16, :] = grad_router[top : top + 16, :]
    small_ref[16:24, :] = jnp.broadcast_to(grad_gain, (8, D))


def expert_token_back(layer, back, came, g, middle, soft, meta, ids, feature, after=()):
    tokens = middle.shape[0]

    def body(*refs):
        expert_token_back_body(layer, *refs)

    return whole_call(
        body,
        (shape((tokens, D), f32), shape((tokens, D), bf16), shape((24, D), f32)),
        [back, came, g, middle, soft, meta, ids, feature],
        after=after,
        flops=6 * tokens * D * back.shape[0],
        streamed=True,
        limit=32,
        name="expert_token_back",
    )


def attention_token_back_body(layer, *refs):
    if layer == 0:
        x_ref, dmiddle_ref, keep_ref, recv_ref, far_ref, feature_ref, out_ref = refs
    else:
        (x_ref, dmiddle_ref, keep_ref, recv_ref, far_ref, feature_ref, meta_ref, dest_ref,
         out_ref, sent_ref) = refs
    tokens = x_ref.shape[0]
    grad_normed = (
        keep_ref[:tokens, :] + recv_ref[:tokens, :].astype(f32) + far_ref[...].astype(f32)
    )
    gain_row = feature_ref[32 * layer + 16 : 32 * layer + 17, :]
    grad_branch, _ = norm_back(x_ref[...].astype(f32), gain_row, grad_normed)
    g = dmiddle_ref[...] + grad_branch
    out_ref[...] = g
    if layer > 0:
        sent_ref[...] = scatter_grads(g, meta_ref[...], dest_ref[...], sent_ref.shape[0])


def attention_token_back(
    layer, x, dmiddle, keep, recv, far, feature, meta=None, dest=None, slots=0, after=()
):
    tokens = x.shape[0]
    outs = [shape((tokens, D), f32)]
    args = [x, dmiddle, keep, recv, far, feature]
    if meta is not None:
        outs.append(shape((slots, D), bf16))
        args += [meta, dest]

    def body(*refs):
        attention_token_back_body(layer, *refs)

    return whole_call(
        body, outs, args, flops=4 * tokens * D * slots, after=after, name="attention_token_back"
    )


def gelu_parts(gate):
    inner = math.sqrt(2.0 / math.pi) * (gate + 0.044715 * gate * gate * gate)
    return jnp.tanh(inner)


def expert_forward_body(rows_ref, wg_ref, wu_ref, wo_ref, produced_ref, acts_ref, total_ref):
    step = pl.program_id(0)
    rows = rows_ref[...]
    gate = dot(rows, wg_ref[0, 0], 1, 0)
    up = dot(rows, wu_ref[0, 0], 1, 0)
    acts_ref[0] = gate.astype(bf16)
    acts_ref[1] = up.astype(bf16)
    hidden = (0.5 * gate * (1.0 + gelu_parts(gate)) * up).astype(bf16)
    out = dot(hidden, wo_ref[0, 0], 1, 1)

    @pl.when(step == 0)
    def _():
        total_ref[...] = out

    @pl.when(step > 0)
    def _():
        total_ref[...] += out

    @pl.when(step == FF_STEPS - 1)
    def _():
        produced_ref[...] = total_ref[...].astype(bf16)


def weight_specs(layer, tile):
    return [
        pl.BlockSpec((1, 1, D, tile), lambda s: (layer, 0, 0, s)),
        pl.BlockSpec((1, 1, D, tile), lambda s: (layer, 0, 0, FF // tile + s)),
        pl.BlockSpec((1, 1, D, tile), lambda s: (layer, 0, 0, s)),
    ]


def expert_forward(layer, rows, w_in, w_out, after=()):
    count = rows.shape[0]

    def body(*refs):
        expert_forward_body(*refs[:4], *refs[4 + len(after) :])

    return pl.pallas_call(
        body,
        grid=(FF_STEPS,),
        out_shape=(shape((count, D), bf16), pltpu.HBM((2, count, FF), bf16)),
        in_specs=[pl.BlockSpec((count, D), lambda s: (0, 0))]
        + weight_specs(layer, FF_TILE)
        + [pl.BlockSpec(memory_space=pltpu.HBM)] * len(after),
        out_specs=(
            pl.BlockSpec((count, D), lambda s: (0, 0)),
            pl.BlockSpec((2, count, FF_TILE), lambda s: (0, 0, s)),
        ),
        scratch_shapes=[pltpu.VMEM((count, D), f32)],
        compiler_params=pltpu.CompilerParams(vmem_limit_bytes=28 * MIB),
        cost_estimate=pl.CostEstimate(
            flops=6 * count * D * FF, bytes_accessed=6 * D * FF, transcendentals=count * FF
        ),
        name="expert_forward",
    )(
        rows,
        far_away(w_in),
        far_away(w_in),
        far_away(w_out),
        *[far_away(a) for a in after],
    )


def expert_backward_body(
    grad_ref, acts_ref, wg_ref, wu_ref, wo_ref, drows_ref, grads_ref, total_ref
):
    step = pl.program_id(0)
    grad_hidden = dot(grad_ref[...], wo_ref[0, 0], 1, 0)
    gate = acts_ref[0].astype(f32)
    up = acts_ref[1].astype(f32)
    curve = gelu_parts(gate)
    value = 0.5 * gate * (1.0 + curve)
    slope = 0.5 * (1.0 + curve) + 0.5 * gate * (1.0 - curve * curve) * math.sqrt(
        2.0 / math.pi
    ) * (1.0 + 3.0 * 0.044715 * gate * gate)
    grad_gate = (grad_hidden * up * slope).astype(bf16)
    grad_up = (grad_hidden * value).astype(bf16)
    grads_ref[0] = grad_gate
    grads_ref[1] = grad_up
    grads_ref[2] = (value * up).astype(bf16)
    out = dot(grad_gate, wg_ref[0, 0], 1, 1) + dot(grad_up, wu_ref[0, 0], 1, 1)

    @pl.when(step == 0)
    def _():
        total_ref[...] = out

    @pl.when(step > 0)
    def _():
        total_ref[...] += out

    @pl.when(step == BACK_STEPS - 1)
    def _():
        drows_ref[...] = total_ref[...].astype(bf16)


def expert_backward(layer, grad, acts, w_in, w_out, after=()):
    count = grad.shape[0]

    def body(*refs):
        expert_backward_body(*refs[:5], *refs[5 + len(after) :])

    return pl.pallas_call(
        body,
        grid=(BACK_STEPS,),
        out_shape=(shape((count, D), bf16), pltpu.HBM((3, count, FF), bf16)),
        in_specs=[
            pl.BlockSpec((count, D), lambda s: (0, 0)),
            pl.BlockSpec((2, count, BACK_TILE), lambda s: (0, 0, s)),
        ]
        + weight_specs(layer, BACK_TILE)
        + [pl.BlockSpec(memory_space=pltpu.HBM)] * len(after),
        out_specs=(
            pl.BlockSpec((count, D), lambda s: (0, 0)),
            pl.BlockSpec((3, count, BACK_TILE), lambda s: (0, 0, s)),
        ),
        scratch_shapes=[pltpu.VMEM((count, D), f32)],
        compiler_params=pltpu.CompilerParams(vmem_limit_bytes=56 * MIB),
        cost_estimate=pl.CostEstimate(
            flops=6 * count * D * FF, bytes_accessed=6 * D * FF, transcendentals=count * FF
        ),
        name="expert_backward",
    )(
        grad,
        far_away(acts),
        far_away(w_in),
        far_away(w_in),
        far_away(w_out),
        *[far_away(a) for a in after],
    )


def expert_grads_body(shares, rows_ref, grad_ref, parts_ref, out_ref, rows_t, grad_t):
    @pl.when(pl.program_id(0) == 0)
    def _():
        rows_t[...] = rows_ref[...].T
        grad_t[...] = grad_ref[...].T

    tall = D // shares
    for which in range(3):
        left = rows_t if which < 2 else grad_t
        got = dot(left[...], parts_ref[which], 1, 0).astype(bf16)
        for share in range(shares):
            out_ref[share, which] = got[share * tall : (share + 1) * tall, :]


def expert_grads(shares, rows, grad, parts, after=()):
    count = rows.shape[0]
    tall = D // shares

    def body(*refs):
        expert_grads_body(shares, *refs[:3], *refs[3 + len(after) :])

    return pl.pallas_call(
        body,
        grid=(FF_STEPS,),
        out_shape=pltpu.HBM((shares, 3, tall, FF), bf16),
        in_specs=[
            pl.BlockSpec((count, D), lambda s: (0, 0)),
            pl.BlockSpec((count, D), lambda s: (0, 0)),
            pl.BlockSpec((3, count, FF_TILE), lambda s: (0, 0, s)),
        ]
        + [pl.BlockSpec(memory_space=pltpu.HBM)] * len(after),
        out_specs=pl.BlockSpec((shares, 3, tall, FF_TILE), lambda s: (0, 0, 0, s)),
        scratch_shapes=[pltpu.VMEM((D, count), bf16), pltpu.VMEM((D, count), bf16)],
        compiler_params=pltpu.CompilerParams(vmem_limit_bytes=28 * MIB),
        cost_estimate=pl.CostEstimate(
            flops=6 * count * D * FF, bytes_accessed=6 * D * FF, transcendentals=0
        ),
        name="expert_grads",
    )(rows, grad, far_away(parts), *[far_away(a) for a in after])


def place_expert_grads(layer, summed, before=None, after=()):
    tall = summed.shape[1]
    outs = (
        pltpu.HBM((LAYERS, 1, tall, 2 * FF), f32),
        pltpu.HBM((LAYERS, 1, tall, FF), f32),
    )
    held = [] if before is None else list(before)

    def body(part_ref, out_part_ref, *refs):
        in_ref, out_ref = refs[-2:]
        in_ref[0, 0] = part_ref[0].astype(f32)
        out_ref[0, 0] = out_part_ref[0].astype(f32)

    return pl.pallas_call(
        body,
        grid=(2,),
        out_shape=outs,
        in_specs=[
            pl.BlockSpec((1, tall, FF), lambda s: (s, 0, 0)),
            pl.BlockSpec((1, tall, FF), lambda s: (2, 0, 0)),
        ]
        + [pl.BlockSpec(memory_space=pl.ANY)] * (len(held) + len(after)),
        out_specs=(
            pl.BlockSpec((1, 1, tall, FF), lambda s: (layer, 0, 0, s)),
            pl.BlockSpec((1, 1, tall, FF), lambda s: (layer, 0, 0, 0)),
        ),
        input_output_aliases={2: 0, 3: 1} if held else {},
        compiler_params=pltpu.CompilerParams(vmem_limit_bytes=32 * MIB),
        name="place_expert_grads",
    )(far_away(summed), far_away(summed), *[far_away(h) for h in [*held, *after]])


TWIN = [(i, i ^ 1) for i in range(GROUP)]
ACROSS = [(i, i ^ 2) for i in range(GROUP)]
FLIP = [(0, 1), (1, 0)]


def share_pieces(piece):
    across = lax.ppermute(piece, "context", ACROSS)
    twin = lax.ppermute(piece, "context", TWIN)
    return [piece, twin, across, lax.ppermute(across, "context", TWIN)]


def sum_pieces(keep, send):
    rows = keep.shape[0] // 2
    recv = lax.ppermute(send, "context", TWIN)
    other = (keep[rows:] + recv[rows:].astype(f32)).astype(bf16)
    return keep, recv, lax.ppermute(other, "context", ACROSS)


def sum_zone(zone):
    return jnp.sum(zone.astype(f32), 0)


def dense_sum(
    experts, pairs, share, table_share, place, grad_w_in, grad_w_out, small, gain_a, by_distance,
    hits,
):
    by_bucket = jnp.dot(hits, by_distance[:OWN].T, precision=lax.Precision.HIGHEST)
    buckets = jnp.where(
        jnp.arange(GROUP)[None, None, :] == place[0], by_bucket[:, :, None], 0.0
    ).reshape(experts, GROUP, pairs, 1, table_share)
    features = jnp.concatenate([small[:16], gain_a[:1], small[16:17]], 0).T
    features = features.reshape(experts, GROUP, pairs, share, 18)
    flat = jnp.zeros((experts, GROUP, pairs, share, LANES), f32)
    flat = flat.at[..., :18].set(features).at[..., :1, 64 : 64 + table_share].set(buckets)
    pack = jnp.concatenate(
        [grad_w_in.reshape(experts, GROUP, pairs, share, PACKED), flat.astype(bf16)], -1
    ).transpose(0, 2, 1, 3, 4)
    pack = pack.reshape(experts * pairs, GROUP * share, PACKED + LANES)
    mine = lax.psum_scatter(pack, ("experts", "dp"), scatter_dimension=0, tiled=False)
    inner = lax.all_to_all(
        mine.reshape(GROUP, share, PACKED + LANES), "context", split_axis=0, concat_axis=0
    ).astype(f32)
    g_in = inner[..., :PACKED].reshape(GROUP, share, 3, OWN, HEAD_DIM)
    g_in = g_in.transpose(1, 2, 3, 0, 4).reshape(share, 3 * D)
    placed_rows = jnp.where(
        jnp.arange(GROUP)[None, :, None, None] == place[0],
        grad_w_out.reshape(OWN, 1, HEAD_DIM, D),
        jnp.zeros((), bf16),
    ).reshape(D, D)
    g_out = lax.psum_scatter(placed_rows, ALL, scatter_dimension=0, tiled=True).astype(f32)
    return g_in, g_out, jnp.sum(inner[..., PACKED:], 0)


def exchange(rows):
    return lax.all_to_all(rows, "experts", split_axis=0, concat_axis=0, tiled=True)


def on_device(
    tokens, doc_starts, expert_ids, attn_in, attn_out, router, gains, rel_table,
    expert_in, expert_out, out_grad,
):
    experts = lax.axis_size("experts")
    pairs = lax.axis_size("dp")
    share = attn_in.shape[1]
    table_share = rel_table.shape[1]
    direct = share * pairs == HEAD_DIM and experts * GROUP == HEADS and pairs == 2
    place = jnp.stack(
        [lax.axis_index("context"), lax.axis_index("dp"), lax.axis_index("experts")]
    ).astype(jnp.int32)
    start_tokens = tokens[0]
    ids = expert_ids[0]
    idst = ids.T
    rows = start_tokens.shape[0]
    capacity = (10 * rows + 4 * experts - 1) // (4 * experts)
    slots = experts * capacity
    grad_in = out_grad[0]
    hits = jnp.asarray(bucket_hits())

    packets = prepare(direct, attn_in, attn_out, router, gains, rel_table)

    def spread(packet):
        return lax.all_to_all(packet, "context", split_axis=0, concat_axis=0)

    def gather(part):
        return lax.all_gather(part, ("experts", "dp"), axis=0, tiled=False).reshape(
            experts, pairs, *part.shape
        )

    if direct:
        packet = spread(packets[0])
        top = PACKED + LANES

        def together(columns, rows_out):
            part = jnp.concatenate([columns, rows_out], -1)
            return lax.all_gather(part, ("experts", "dp"), axis=0, tiled=False)

        first = together(packet[..., :top], packets[1])
        w_in0, w_out0, feature, bias = unpack(place, hits, experts, pairs, 0, first)
        second = together(packet[..., top:], packets[2])
        w_in1, w_out1 = unpack(place, hits, experts, pairs, 1, second)
        w_in, w_out = [w_in0, w_in1], [w_out0, w_out1]
    else:
        w_in, w_out = [], []
        for layer in range(LAYERS):
            at = layer * (PACKED + LANES)
            part = spread(packets[0])[..., at : at + PACKED + LANES]
            got = gather(part).transpose(0, 2, 1, 3, 4)
            w_in.append(got[..., :PACKED].reshape(D, PACKED))
            if layer == 0:
                small_all = got[..., PACKED : PACKED + LANES]
            full = lax.all_gather(attn_out[layer], ALL, axis=0, tiled=True)
            mine = lax.dynamic_index_in_dim(
                full.reshape(OWN, GROUP, HEAD_DIM, D), place[0], 1, keepdims=False
            )
            w_out.append(mine.reshape(OWN_COLS, GROUP, D // GROUP).transpose(1, 0, 2))
        feature = small_all.reshape(D, LANES).astype(f32).T
        bias_rows = []
        for layer in range(LAYERS):
            at = 64 + 32 * layer
            table = small_all[:, :, :, 0, at : at + table_share].reshape(BUCKETS, OWN, GROUP)
            table = lax.dynamic_index_in_dim(table, place[0], 2, keepdims=False).astype(f32)
            row = jnp.dot((table - table[-1:]).T, hits, precision=lax.Precision.HIGHEST)
            bias_rows.append(jnp.pad(row, ((0, 8 - OWN), (0, 0))))
        bias = jnp.stack(bias_rows)
    places = jnp.arange(GROUP * rows, dtype=jnp.int32)
    starts = doc_starts[0]
    low = jnp.max(
        jnp.where(starts[:, None] <= places[None, :], starts[:, None], 0), 0, keepdims=True
    )

    pieces = share_pieces(start_tokens)
    x = start_tokens
    kept = []
    arrived_grad = exchange(send_grads(experts, capacity, idst, grad_in, [feature]))
    for layer in range(LAYERS):
        packed, log_total, mixed, keep, send, *normed_all = attention_forward(
            layer, place, pieces, w_in[layer], feature, bias, low, w_out[layer]
        )
        normed_rows = normed_all if layer == 0 else pieces
        keep, recv, far = sum_pieces(keep, send)
        last = layer == LAYERS - 1
        routed = route(
            layer, experts, capacity, x, keep, recv, far, feature, ids, idst, last,
            after=[arrived_grad] if layer == 0 else [],
        )
        middle, sent_rows, soft, meta, dest = routed[:5]
        arrived = exchange(sent_rows)
        if last:
            gates = exchange(routed[5])
        produced, acts = expert_forward(
            layer, arrived, expert_in, expert_out
        )
        back = exchange(produced)
        if last:
            arrived_grad = apply_gates(arrived_grad, gates)
        kept.append(
            (x, normed_rows, packed, log_total, mixed, middle, soft, meta, dest, arrived, acts, back)
        )
        if last:
            (result,) = combine(middle, back, meta)
        else:
            x, normed = combine(middle, back, meta, feature)
            pieces = share_pieces(normed)

    g = grad_in
    inner, outer, expert_totals = [], [], []
    other = None
    placed_grads = None
    for layer in range(LAYERS - 1, -1, -1):
        (x, normed_rows, packed, log_total, mixed, middle, soft, meta, dest, arrived, acts,
         back) = kept[layer]
        drows, parts = expert_backward(layer, arrived_grad, acts, expert_in, expert_out)
        came = exchange(drows)
        early = [] if other is None else [other]
        weight_grads = expert_grads(
            GROUP * pairs, arrived, arrived_grad, parts, after=[back] + early
        )
        weight_grads = hold(weight_grads, [came])
        total = lax.psum_scatter(
            weight_grads, ("context", "dp"), scatter_dimension=0, tiled=False
        )
        dmiddle, dattn, small_b = expert_token_back(
            layer, back, came, g, middle, soft, meta, ids, feature, after=[weight_grads]
        )
        zones = []
        if direct and other is not None:
            ours = hold(keep_dense, [dattn]) + other.astype(f32)
            zones = [exchange(ours.astype(bf16))]
        expert_totals.append(total)
        grad_pieces = share_pieces(dattn)
        grad_packed, keep, send, by_distance, gain_a = attention_backward(
            layer, place, grad_pieces, w_in[layer], feature, bias, low, w_out[layer], packed,
            log_total, normed_rows,
        )
        keep, recv, far = sum_pieces(keep, send)
        if layer > 0:
            below = kept[layer - 1]
            g, sent = attention_token_back(
                layer, x, dmiddle, keep, recv, far, feature, below[7], below[8], slots
            )
            arrived_grad = exchange(sent)
        else:
            placed_grads = place_expert_grads(layer + 1, expert_totals[0])
            (g,) = attention_token_back(
                layer, x, dmiddle, keep, recv, far, feature, after=[placed_grads[0]]
            )
        if direct:
            keep_dense, send_dense, *rest = dense_pack(
                experts, pairs, share, place, normed_rows, grad_pieces, grad_packed, mixed,
                small_b, gain_a, by_distance, hits, split=layer == 0, after=zones,
            )
            other = lax.ppermute(send_dense, "dp", FLIP)
            if layer == 0:
                (zone,) = zones
                total = sum_zone(zone)
                flats = [total[:, : PACKED + LANES].astype(bf16)]
                outer.append(total[:, PACKED + LANES :])
                rest = sum_zone(exchange(rest[0]))
                theirs = lax.ppermute(rest[1].astype(bf16), "dp", FLIP)
                rest = rest[0] + theirs.astype(f32)
                ours = hold(keep_dense, [g, result, placed_grads[0]]) + other.astype(f32)
                total = sum_zone(exchange(ours.astype(bf16)))
                flats.insert(0, jnp.concatenate([total, rest[:, :LANES]], -1).astype(bf16))
                outer.append(rest[:, LANES:])
                flat = jnp.stack([flat.reshape(GROUP, share, -1) for flat in flats], 1)
                inner = spread(flat)
        else:
            grad_w_in, grad_w_out = dense_grads(normed_rows, grad_pieces, grad_packed, mixed)
            inner.append(
                dense_sum(
                    experts, pairs, share, table_share, place, grad_w_in, grad_w_out, small_b,
                    gain_a, by_distance, hits,
                )
            )
    expert_grads_all = place_expert_grads(0, expert_totals[1], placed_grads)
    if direct:
        grad_attn_in, grad_attn_out, small_grad = finish_dense(
            share, inner, outer[::-1]
        )
    else:
        grad_attn_in, grad_attn_out, small_grad = (
            jnp.stack([entry[k] for entry in inner[::-1]]) for k in range(3)
        )
    return (
        result[None],
        g[None],
        grad_attn_in,
        grad_attn_out,
        small_grad[..., :experts],
        small_grad[..., 16:18],
        small_grad[:, 0, 64 : 64 + table_share],
        *expert_grads_all,
    )


def solution(mesh):
    return jax.shard_map(
        on_device,
        mesh=mesh,
        in_specs=(
            P(("experts", "dp"), "context", None),
            P(("experts", "dp"), None),
            P(("experts", "dp"), "context", None),
            P(None, ("experts", "context", "dp"), None),
            P(None, ("experts", "context", "dp"), None),
            P(None, ("experts", "context", "dp"), None),
            P(None, ("experts", "context", "dp"), None),
            P(None, ("experts", "context", "dp")),
            P(None, "experts", None, None),
            P(None, "experts", None, None),
            P(("experts", "dp"), "context", None),
        ),
        out_specs=(
            P(("experts", "dp"), "context", None),
            P(("experts", "dp"), "context", None),
            P(None, ("experts", "context", "dp"), None),
            P(None, ("experts", "context", "dp"), None),
            P(None, ("experts", "context", "dp"), None),
            P(None, ("experts", "context", "dp"), None),
            P(None, ("experts", "context", "dp")),
            P(None, "experts", ("context", "dp"), None),
            P(None, "experts", ("context", "dp"), None),
        ),
        check_vma=False,
    )
```

```python
import math

import jax
import jax.numpy as jnp
import numpy as np
from jax import lax
from jax.experimental import pallas as pl
from jax.experimental.pallas import tpu as pltpu
from jax.sharding import PartitionSpec as P

D = 1024
HEADS = 16
HEAD_DIM = 64
FF = 2816
BUCKETS = 32
MAX_DISTANCE = 128
LAYERS = 2
EPSILON = 1e-06
NEGATIVE = -1e30
SCORE_SCALE = 0.125
ALL = ("experts", "context", "dp")
GROUP = 4
OWN = HEADS // GROUP
OWN_COLS = OWN * HEAD_DIM
PACKED = 3 * OWN_COLS
LANES = 128
REACH = 512
FF_TILE = 256
FF_STEPS = FF // FF_TILE
WIDE_TILE = FF // 2
EARLY_COLS = 512
ROWS_HINT = 320
MIB = 1 << 20

bf16 = jnp.bfloat16
f32 = jnp.float32


def bucket_bounds(bucket_count, far_reach):
    half_count = bucket_count // 2
    bounds = list(range(1, half_count + 1))
    for section_index in range(1, half_count):
        bounds.append(
            int(math.ceil(half_count * (far_reach / half_count) ** (section_index / half_count)))
        )
    return np.array(bounds, np.int32)


def bucket_hits():
    distance = np.arange(REACH)
    bucket = (distance[:, None] >= bucket_bounds(BUCKETS, MAX_DISTANCE)).sum(-1)
    return (np.arange(BUCKETS)[:, None] == bucket[None, :]).astype(np.float32)


def dot(a, b, ca, cb, precision=None):
    return lax.dot_general(
        a, b, (((ca,), (cb,)), ((), ())), precision=precision, preferred_element_type=f32
    )


def whole_call(
    body, out_shape, args, *, flops=0, limit=16, scratch=(), smem=0, name=None, after=(),
    streamed=False,
):
    specs = [pl.BlockSpec(memory_space=pltpu.SMEM)] * smem + [
        pl.BlockSpec(memory_space=pltpu.VMEM)
    ] * (len(args) - smem)
    outs = tuple(out_shape)
    moved = sum(a.size * a.dtype.itemsize for a in list(args) + list(outs))
    specs += [pl.BlockSpec(memory_space=pltpu.HBM)] * len(after)
    used = len(args)
    args = list(args) + [far_away(a) for a in after]

    def ordered(*refs):
        body(*refs[:used], *refs[used + len(after) :])

    if streamed:
        args = args[:smem] + [far_away(a) for a in args[smem:]]

        def full(a):
            return pl.BlockSpec(a.shape, lambda i: (0,) * len(a.shape))

        return pl.pallas_call(
            ordered,
            grid=(1,),
            out_shape=outs,
            in_specs=specs[:smem] + [full(a) for a in args[smem:used]] + specs[used:],
            out_specs=tuple(full(o) for o in outs),
            scratch_shapes=list(scratch),
            compiler_params=pltpu.CompilerParams(vmem_limit_bytes=limit * MIB),
            cost_estimate=pl.CostEstimate(
                flops=int(flops), bytes_accessed=int(moved), transcendentals=0
            ),
            name=name,
        )(*args)
    return pl.pallas_call(
        ordered,
        out_shape=outs,
        in_specs=specs,
        out_specs=tuple(pl.BlockSpec(memory_space=pltpu.VMEM) for _ in outs),
        scratch_shapes=list(scratch),
        compiler_params=pltpu.CompilerParams(vmem_limit_bytes=limit * MIB),
        cost_estimate=pl.CostEstimate(
            flops=int(flops), bytes_accessed=int(moved), transcendentals=0
        ),
        name=name,
    )(*args)


def far_away(x):
    return pltpu.with_memory_space_constraint(x, pltpu.HBM)


def hold(x, after):
    def body(*refs):
        pass

    return pl.pallas_call(
        body,
        out_shape=pltpu.HBM(x.shape, x.dtype),
        in_specs=[pl.BlockSpec(memory_space=pltpu.HBM)] * (1 + len(after)),
        out_specs=pl.BlockSpec(memory_space=pltpu.HBM),
        input_output_aliases={0: 0},
        compiler_params=pltpu.CompilerParams(vmem_limit_bytes=MIB),
        cost_estimate=pl.CostEstimate(flops=0, bytes_accessed=0, transcendentals=0),
        name="hold",
    )(far_away(x), *[far_away(a) for a in after])


def shape(dims, dtype):
    return jax.ShapeDtypeStruct(dims, dtype)


def rms_scale(inputs):
    return lax.rsqrt(jnp.mean(inputs * inputs, -1, keepdims=True) + EPSILON)


def norm_back(inputs, gain_row, upstream):
    inverse = rms_scale(inputs)
    scaled = upstream * gain_row
    inner_mean = jnp.mean(inputs * scaled, -1, keepdims=True)
    grad_inputs = inverse * scaled - inputs * (inverse * inverse * inverse) * inner_mean
    grad_gain = jnp.sum(upstream * inputs * inverse, 0, keepdims=True)
    return grad_inputs, grad_gain


def placed(count, offset):
    index = lax.broadcasted_iota(jnp.int32, (count, LANES), 0)
    lane = lax.broadcasted_iota(jnp.int32, (count, LANES), 1)
    return one_hot(lane == index + offset)


def prepare_body(direct, in_ref, out_ref, router_ref, gains_ref, table_ref, *packets):
    share = in_ref.shape[1]
    for layer in range(LAYERS):
        for which in range(3):
            for head in range(OWN):
                for c in range(GROUP):
                    source = which * D + (head * GROUP + c) * HEAD_DIM
                    target = which * OWN_COLS + head * HEAD_DIM
                    target += layer * (PACKED + LANES)
                    packets[0][c, :, target : target + HEAD_DIM] = in_ref[
                        layer, :, source : source + HEAD_DIM
                    ]
        if direct:
            width = D // GROUP
            for q in range(GROUP):
                packets[1 + layer][q] = out_ref[layer, :, q * width : (q + 1) * width]
    small = jnp.zeros((share, LANES), f32)
    row = lax.broadcasted_iota(jnp.int32, (share, LANES), 0)
    for layer in range(LAYERS):
        top = 32 * layer
        small = small + dot(router_ref[layer], placed(router_ref.shape[2], top), 1, 0)
        small = small + dot(gains_ref[layer], placed(2, top + 16), 1, 0)
        bucket = dot(table_ref[layer : layer + 1, :], placed(table_ref.shape[1], top + 64), 1, 0)
        small = small + jnp.where(row == 0, bucket, 0.0)
    for c in range(GROUP):
        packets[0][c, :, PACKED : PACKED + LANES] = small.astype(bf16)


def prepare(direct, attn_in, attn_out, router, gains, rel_table):
    share = attn_in.shape[1]
    outs = [shape((GROUP, share, 2 * PACKED + LANES), bf16)]
    if direct:
        outs += [shape((GROUP, share, D // GROUP), bf16)] * LAYERS

    def body(*refs):
        prepare_body(direct, *refs)

    return whole_call(
        body, outs, [attn_in, attn_out, router, gains, rel_table], streamed=True, name="prepare"
    )


def unpack(place, hits, experts, pairs, layer, got):
    share = got.shape[-2]
    width = D // GROUP
    first = layer == 0

    def body(place_ref, hits_ref, got_ref, w_in_ref, w_out_ref, *rest):
        for index in range(experts * pairs):
            e, d = index // pairs, index % pairs
            for c in range(GROUP):
                owner = (e * GROUP + c) * pairs + d
                at = owner * share
                w_in_ref[at : at + share, :] = got_ref[index, c, :, :PACKED]
                w_out_ref[c, index * share : (index + 1) * share, :] = got_ref[
                    index, c, :, got_ref.shape[-1] - width :
                ]
                if first:
                    flags = got_ref[index, c, :, PACKED : PACKED + LANES].astype(f32)
                    rest[2][at : at + share, :] = flags
                    rest[3][owner : owner + 1, :] = flags[:1, :]
        if not first:
            return
        feature_ref, bias_ref, flat_ref, bucket_ref = rest
        feature_ref[...] = flat_ref[...].T
        head = lax.broadcasted_iota(jnp.int32, (8, LANES), 0)
        lane = lax.broadcasted_iota(jnp.int32, (8, LANES), 1)
        for other in range(LAYERS):
            mine = jnp.where(
                (lane == 64 + 32 * other + head * GROUP + place_ref[0]) & (head < OWN), 1.0, 0.0
            )
            table = dot(mine, bucket_ref[...], 1, 1, lax.Precision.HIGHEST)
            bias_ref[other] = dot(
                table - table[:, BUCKETS - 1 :], hits_ref[...], 1, 0, lax.Precision.HIGHEST
            )

    outs = [shape((D, PACKED), bf16), shape((GROUP, OWN_COLS, D // GROUP), bf16)]
    scratch = []
    if first:
        outs += [shape((LANES, D), f32), shape((LAYERS, 8, REACH), f32)]
        scratch = [pltpu.VMEM((D, LANES), f32), pltpu.VMEM((BUCKETS, LANES), f32)]
    return whole_call(
        body, outs, [place, hits, got], smem=1, scratch=scratch, name="unpack"
    )


def near_bias(bias_ref, layer, head, rows):
    row = bias_ref[layer, head : head + 1, :]
    return pltpu.roll(jnp.broadcast_to(row, (rows, REACH)), 0, 1, stride=1, stride_axis=0)


def masked_scores(keys, queries, near, low, key_block, query_block, rows):
    scores = dot(keys, queries, 1, 1)
    key_place = lax.broadcasted_iota(jnp.int32, (rows, rows), 0)
    seen = key_place >= low - key_block * rows
    if key_block == query_block:
        scores = scores + near[:, :rows]
        seen = seen & (key_place <= lax.broadcasted_iota(jnp.int32, (rows, rows), 1))
    elif key_block == query_block - 1:
        scores = scores + near[:, rows:]
    return jnp.where(seen, scores, NEGATIVE)


def attention_forward_body(
    layer, place_ref, n0, n1, n2, n3, w_ref, feature_ref, bias_ref, low_ref, wo_ref,
    packed_ref, log_ref, mixed_ref, keep_ref, send_ref, *normed_ref,
):
    me = place_ref[0]
    rows = n0.shape[0]
    for r, piece in enumerate((n0, n1, n2, n3)):
        normed = piece[...]
        if layer == 0:
            wide = normed.astype(f32)
            normed = (wide * rms_scale(wide) * feature_ref[16:17, :]).astype(bf16)
            normed_ref[0][r * rows : (r + 1) * rows, :] = normed
        packed_ref[r * rows : (r + 1) * rows, :] = dot(normed, w_ref[...], 1, 0).astype(bf16)
    lane = lax.broadcasted_iota(jnp.int32, (rows, LANES), 1)
    starts = [pl.multiple_of((b ^ me) * rows, rows) for b in range(GROUP)]
    for pair in range(OWN // 2):
        at = pair * LANES

        def part(b, which):
            column = which * OWN_COLS + at
            return packed_ref[pl.ds(starts[b], rows), column : column + LANES]

        sides = [(lane // HEAD_DIM) == side for side in range(2)]
        nears = [near_bias(bias_ref, layer, pair * 2 + side, rows) for side in range(2)]
        for qb in range(GROUP):
            low = low_ref[:, qb * rows : (qb + 1) * rows]
            queries = part(qb, 0) * SCORE_SCALE
            total = None
            for side in range(2):
                mine = jnp.where(sides[side], queries, 0).astype(bf16)
                tiles = [
                    masked_scores(part(kb, 1), mine, nears[side], low, kb, qb, rows)
                    for kb in range(qb + 1)
                ]
                peak = jnp.max(tiles[0], 0, keepdims=True)
                for tile in tiles[1:]:
                    peak = jnp.maximum(peak, jnp.max(tile, 0, keepdims=True))
                weight_sum = jnp.zeros((1, rows), f32)
                out = jnp.zeros((LANES, rows), f32)
                for kb, tile in enumerate(tiles):
                    power = jnp.exp(tile - peak)
                    weight_sum = weight_sum + jnp.sum(power, 0, keepdims=True)
                    values = jnp.where(sides[side], part(kb, 2), 0).astype(bf16)
                    out = out + dot(values, power.astype(bf16), 0, 0)
                out = out / weight_sum
                total = out if total is None else total + out
                head = pair * 2 + side
                log_ref[head : head + 1, qb * rows : (qb + 1) * rows] = peak + jnp.log(weight_sum)
            mixed_ref[pl.ds(starts[qb], rows), at : at + LANES] = total.T.astype(bf16)
    width = wo_ref.shape[2]
    for r, (target, offset) in enumerate(
        ((keep_ref, 0), (send_ref, 0), (keep_ref, rows), (send_ref, rows))
    ):
        mixed = mixed_ref[r * rows : (r + 1) * rows, :]
        for q in range(wo_ref.shape[0]):
            target[offset : offset + rows, q * width : (q + 1) * width] = dot(
                mixed, wo_ref[q], 1, 0
            ).astype(target.dtype)


def attention_forward(layer, place, pieces, w_in, feature, bias, low, w_out):
    rows = pieces[0].shape[0]
    total = GROUP * rows
    outs = [
        shape((total, PACKED), bf16),
        shape((8, total), f32),
        shape((total, OWN_COLS), bf16),
        shape((2 * rows, D), f32),
        shape((2 * rows, D), bf16),
    ]
    if layer == 0:
        outs.append(shape((total, D), bf16))

    def body(*refs):
        attention_forward_body(layer, *refs)

    return whole_call(
        body,
        outs,
        [place, *pieces, w_in, feature, bias, low, w_out],
        smem=1,
        flops=2 * total * D * (PACKED + OWN_COLS) + 2 * total * total * OWN_COLS * 2,
        limit=24,
        name="attention_forward",
    )


def attention_backward_body(
    layer, place_ref, d0, d1, d2, d3, w_ref, feature_ref, bias_ref, low_ref, wo_ref, packed_ref,
    log_ref, *refs,
):
    normed_refs = refs[:-8]
    (grad_packed_ref, keep_ref, send_ref, table_ref, gain_ref, grad_mixed_ref, dk_ref,
     dv_ref) = refs[-8:]
    me = place_ref[0]
    rows = d0.shape[0]
    width = wo_ref.shape[2]
    for r, piece in enumerate((d0, d1, d2, d3)):
        got = jnp.zeros((rows, OWN_COLS), f32)
        for q in range(wo_ref.shape[0]):
            got = got + dot(piece[:, q * width : (q + 1) * width], wo_ref[q], 1, 1)
        grad_mixed_ref[r * rows : (r + 1) * rows, :] = got.astype(bf16)
    lane = lax.broadcasted_iota(jnp.int32, (rows, LANES), 1)
    starts = [pl.multiple_of((b ^ me) * rows, rows) for b in range(GROUP)]
    table_ref[...] = jnp.zeros(table_ref.shape, f32)
    for pair in range(OWN // 2):
        at = pair * LANES

        def part(b, which):
            column = which * OWN_COLS + at
            return packed_ref[pl.ds(starts[b], rows), column : column + LANES]

        sides = [(lane // HEAD_DIM) == side for side in range(2)]
        nears = [near_bias(bias_ref, layer, pair * 2 + side, rows) for side in range(2)]
        diag = [jnp.zeros((rows, rows), f32) for _ in range(2)]
        before = [jnp.zeros((rows, rows), f32) for _ in range(2)]
        far = [jnp.zeros((1, rows), f32) for _ in range(2)]
        dk_ref[...] = jnp.zeros(dk_ref.shape, f32)
        dv_ref[...] = jnp.zeros(dv_ref.shape, f32)
        for qb in range(GROUP):
            low = low_ref[:, qb * rows : (qb + 1) * rows]
            queries = part(qb, 0) * SCORE_SCALE
            upstream = grad_mixed_ref[pl.ds(starts[qb], rows), at : at + LANES]
            grad_queries = jnp.zeros((LANES, rows), f32)
            for side in range(2):
                head = pair * 2 + side
                mine = jnp.where(sides[side], queries, 0).astype(bf16)
                above = jnp.where(sides[side], upstream, 0).astype(bf16)
                log_total = log_ref[head : head + 1, qb * rows : (qb + 1) * rows]
                probs, grads = [], []
                row_dot = jnp.zeros((1, rows), f32)
                for kb in range(qb + 1):
                    scores = masked_scores(part(kb, 1), mine, nears[side], low, kb, qb, rows)
                    prob = jnp.exp(scores - log_total)
                    grad = dot(part(kb, 2), above, 1, 1)
                    row_dot = row_dot + jnp.sum(prob * grad, 0, keepdims=True)
                    probs.append(prob)
                    grads.append(grad)
                for kb in range(qb + 1):
                    grad_score = probs[kb] * (grads[kb] - row_dot)
                    if kb == qb:
                        diag[side] = diag[side] + grad_score
                    elif kb == qb - 1:
                        before[side] = before[side] + grad_score
                    else:
                        far[side] = far[side] + jnp.sum(grad_score, 0, keepdims=True)
                    grad_low = grad_score.astype(bf16)
                    keys = jnp.where(sides[side], part(kb, 1), 0).astype(bf16)
                    grad_queries = grad_queries + dot(keys, grad_low, 0, 0)
                    span = slice(kb * rows, (kb + 1) * rows)
                    dk_ref[span, :] += dot(grad_low, mine, 1, 0)
                    dv_ref[span, :] += dot(probs[kb].astype(bf16), above, 1, 0)
            grad_packed_ref[pl.ds(starts[qb], rows), at : at + LANES] = (
                grad_queries.T * SCORE_SCALE
            ).astype(bf16)
        for kb in range(GROUP):
            span = slice(kb * rows, (kb + 1) * rows)
            for which, source in ((1, dk_ref), (2, dv_ref)):
                column = which * OWN_COLS + at
                grad_packed_ref[pl.ds(starts[kb], rows), column : column + LANES] = source[
                    span, :
                ].astype(bf16)
        distance = lax.broadcasted_iota(jnp.int32, (1, REACH), 1)
        for side in range(2):
            head = pair * 2 + side
            skewed = jnp.concatenate([diag[side], before[side]], 1)
            row_index = lax.broadcasted_iota(jnp.int32, (rows, REACH), 0)
            step = 1
            while step < rows:
                skewed = jnp.where(
                    (row_index & step) != 0, pltpu.roll(skewed, REACH - step, 1), skewed
                )
                step *= 2
            by_distance = jnp.sum(skewed, 0, keepdims=True)
            far_sum = jnp.sum(far[side], 1, keepdims=True)
            table_ref[head : head + 1, :] = by_distance + jnp.where(
                distance == REACH - 1, far_sum, 0.0
            )
    for r, (target, offset) in enumerate(
        ((keep_ref, 0), (send_ref, 0), (keep_ref, rows), (send_ref, rows))
    ):
        grad_normed = dot(grad_packed_ref[r * rows : (r + 1) * rows, :], w_ref[...], 1, 1)
        target[offset : offset + rows, :] = grad_normed.astype(target.dtype)
        part_gain = jnp.sum(grad_normed * block_of(normed_refs, r, rows).astype(f32), 0, keepdims=True)
        gain_sum = part_gain if r == 0 else gain_sum + part_gain
    gain_row = feature_ref[32 * layer + 16 : 32 * layer + 17, :]
    gain_ref[...] = jnp.broadcast_to(gain_sum / gain_row, gain_ref.shape)


def block_of(refs, r, rows):
    return refs[r][...] if len(refs) > 1 else refs[0][r * rows : (r + 1) * rows, :]


def attention_backward(
    layer, place, pieces, w_in, feature, bias, low, w_out, packed, log_total, normed, after=()
):
    rows = pieces[0].shape[0]
    total = GROUP * rows

    def body(*refs):
        attention_backward_body(layer, *refs)

    return whole_call(
        body,
        (
            shape((total, PACKED), bf16),
            shape((2 * rows, D), f32),
            shape((2 * rows, D), bf16),
            shape((8, REACH), f32),
            shape((8, D), f32),
        ),
        [place, *pieces, w_in, feature, bias, low, w_out, packed, log_total, *normed],
        smem=1,
        after=after,
        scratch=[
            pltpu.VMEM((total, OWN_COLS), bf16),
            pltpu.VMEM((total, LANES), f32),
            pltpu.VMEM((total, LANES), f32),
        ],
        flops=2 * total * D * (PACKED + OWN_COLS) + 2 * total * total * OWN_COLS * 5,
        limit=24,
        name="attention_backward",
    )


def dense_products(normed, upstream, grad_packed_ref, mixed_ref):
    rows = upstream[0].shape[0]
    total_in = None
    total_out = None
    for r in range(GROUP):
        span = slice(r * rows, (r + 1) * rows)
        one = dot(block_of(normed, r, rows), grad_packed_ref[span, :], 0, 0)
        two = dot(mixed_ref[span, :], upstream[r][...], 0, 0)
        total_in = one if total_in is None else total_in + one
        total_out = two if total_out is None else total_out + two
    return total_in, total_out


def dense_grads(normed, upstream, grad_packed, mixed):
    rows = upstream[0].shape[0]
    count = len(normed)

    def body(*refs):
        total_in, total_out = dense_products(
            refs[:count], refs[count : count + GROUP], refs[-4], refs[-3]
        )
        refs[-2][...] = total_in.astype(bf16)
        refs[-1][...] = total_out.astype(bf16)

    return whole_call(
        body,
        (shape((D, PACKED), bf16), shape((OWN_COLS, D), bf16)),
        [*normed, *upstream, grad_packed, mixed],
        flops=2 * GROUP * rows * D * (PACKED + OWN_COLS),
        name="dense_grads",
    )


def dense_pack(experts, pairs, share, place, normed, upstream, grad_packed, mixed, small, gain_a,
               by_distance, hits, split, after=()):
    rows = upstream[0].shape[0]
    count = len(normed)
    width = D // GROUP
    cut = EARLY_COLS if split else PACKED
    rest = PACKED - cut + LANES + width
    total = cut if split else PACKED + rest

    def body(place_ref, *refs):
        grad_packed_ref, mixed_ref, small_ref, gain_ref, distance_ref, hits_ref = refs[
            count + GROUP : count + GROUP + 6
        ]
        outs = refs[count + GROUP + 6 : -3]
        in_ref, out_ref, flat_ref = refs[-3:]
        total_in, total_out = dense_products(
            refs[:count], refs[count : count + GROUP], grad_packed_ref, mixed_ref
        )
        in_ref[...] = total_in
        out_ref[...] = total_out
        row = lax.broadcasted_iota(jnp.int32, (8, D), 0)
        gains = jnp.where(
            row == 0, gain_ref[...], jnp.where(row == 1, small_ref[16:24, :], 0.0)
        )
        features = jnp.concatenate(
            [small_ref[:16, :], gains, jnp.zeros((LANES - 24, D), f32)], 0
        )
        flat_ref[...] = features.T
        by_bucket = dot(hits_ref[...], distance_ref[...], 1, 1, lax.Precision.HIGHEST)
        head = lax.broadcasted_iota(jnp.int32, (8, LANES), 0)
        lane = lax.broadcasted_iota(jnp.int32, (8, LANES), 1)
        mine = jnp.where((lane == 64 + head * GROUP + place_ref[0]) & (head < OWN), 1.0, 0.0)
        buckets = dot(by_bucket, mine, 1, 0, lax.Precision.HIGHEST)
        for index in range(BUCKETS):
            at = index * share
            flat_ref[at : at + 1, :] = flat_ref[at : at + 1, :] + buckets[index : index + 1, :]
        for side, d in enumerate((place_ref[1], 1 - place_ref[1])):
            for e in range(experts):
                for c in range(GROUP):
                    at = ((e * GROUP + c) * pairs + d) * share
                    span = pl.ds(pl.multiple_of(at, share), share)
                    to = slice(c * share, (c + 1) * share)
                    target = outs[side]
                    target[e, to, :cut] = in_ref[span, :cut].astype(target.dtype)
                    out_span = pl.ds(pl.multiple_of((e * pairs + d) * share, share), share)
                    outer = out_ref[out_span, c * width : (c + 1) * width]
                    if split:
                        more = PACKED - cut
                        outs[2][e, side, to, :more] = in_ref[span, cut:].astype(bf16)
                        outs[2][e, side, to, more : more + LANES] = flat_ref[span, :].astype(bf16)
                        outs[2][e, side, to, more + LANES :] = outer.astype(bf16)
                    else:
                        target[e, to, PACKED : PACKED + LANES] = flat_ref[span, :].astype(
                            target.dtype
                        )
                        target[e, to, PACKED + LANES :] = outer.astype(target.dtype)

    outs = [
        shape((experts, GROUP * share, total), f32),
        shape((experts, GROUP * share, total), bf16),
    ]
    if split:
        outs.append(shape((experts, pairs, GROUP * share, rest), bf16))
    return whole_call(
        body,
        outs,
        [place, *normed, *upstream, grad_packed, mixed, small, gain_a, by_distance, hits],
        smem=1,
        scratch=[
            pltpu.VMEM((D, PACKED), f32),
            pltpu.VMEM((OWN_COLS, D), f32),
            pltpu.VMEM((D, LANES), f32),
        ],
        flops=2 * GROUP * rows * D * (PACKED + OWN_COLS),
        after=after,
        streamed=True,
        limit=32,
        name="dense_pack",
    )


def finish_dense(share, inner, outer):
    width = D // GROUP

    def body(*refs):
        in_ref, out_ref, small_ref = refs[1 + LAYERS :]
        for layer in range(LAYERS):
            got, rows_out = refs[0], refs[1 + layer]
            for c in range(GROUP):
                for which in range(3):
                    for head in range(OWN):
                        source = which * OWN_COLS + head * HEAD_DIM
                        target = which * D + (head * GROUP + c) * HEAD_DIM
                        in_ref[layer, :, target : target + HEAD_DIM] = got[
                            c, layer, :, source : source + HEAD_DIM
                        ].astype(f32)
                out_ref[layer, :, c * width : (c + 1) * width] = rows_out[
                    c * share : (c + 1) * share, :
                ]
            total = got[0, layer, :, PACKED:].astype(f32)
            for c in range(1, GROUP):
                total = total + got[c, layer, :, PACKED:].astype(f32)
            small_ref[layer] = total

    return whole_call(
        body,
        (
            shape((LAYERS, share, 3 * D), f32),
            shape((LAYERS, share, D), f32),
            shape((LAYERS, share, LANES), f32),
        ),
        [inner, *outer],
        name="finish_dense",
    )


def stacked(refs):
    return refs[0][...] if len(refs) == 1 else jnp.concatenate([ref[...] for ref in refs], 0)


def store_blocks(refs, rows):
    count = rows.shape[0] // len(refs)
    for index, ref in enumerate(refs):
        ref[...] = rows[index * count : (index + 1) * count, :].astype(ref.dtype)


def block_shapes(blocks, slots, width=D):
    return [shape((slots // blocks, width), bf16)] * blocks


def dispatch_grid(dest_rows, slots, tokens):
    place = lax.broadcasted_iota(jnp.int32, (slots, tokens), 0)
    first = place == dest_rows[0:1, :]
    second = place == dest_rows[1:2, :]
    return first, second


def one_hot(flags):
    return jnp.where(flags, 1.0, 0.0).astype(bf16)


def collect_grid(meta, slots):
    tokens = meta.shape[0]
    place = lax.broadcasted_iota(jnp.int32, (tokens, slots), 1)
    first = place == meta[:, 0:1].astype(jnp.int32)
    second = place == meta[:, 1:2].astype(jnp.int32)
    return first, second


def scatter_grads(upstream, meta, dest_rows, slots):
    tokens = upstream.shape[0]
    first, second = dispatch_grid(dest_rows, slots, tokens)
    return (
        dot(one_hot(first), (meta[:, 2:3] * upstream).astype(bf16), 1, 0)
        + dot(one_hot(second), (meta[:, 3:4] * upstream).astype(bf16), 1, 0)
    ).astype(bf16)


def slot_rows(idst, capacity, own):
    tokens = idst.shape[1]
    down = lax.broadcasted_iota(jnp.int32, (tokens, tokens), 0)
    across = lax.broadcasted_iota(jnp.int32, (tokens, tokens), 1)
    sub = lax.broadcasted_iota(jnp.int32, (16, tokens), 0)
    row0 = sub == idst[0:1, :]
    row1 = sub == idst[1:2, :]
    counts = dot(one_hot(row0 | row1), one_hot(down < across), 1, 0)
    found = []
    for index, row in enumerate((row0, row1)):
        slot = jnp.sum(jnp.where(row, counts, 0.0), 0, keepdims=True).astype(jnp.int32)
        found.append((idst[index : index + 1, :] ^ own) * capacity + slot)
    return jnp.where(lax.broadcasted_iota(jnp.int32, (8, tokens), 0) == 0, found[0], found[1])


def send_grads(experts, capacity, idst, grad, after):
    tokens = grad.shape[0]
    slots = experts * capacity

    def body(idst_ref, grad_ref, out_ref):
        first, second = dispatch_grid(slot_rows(idst_ref[...], capacity, 0), slots, tokens)
        out_ref[...] = dot(one_hot(first | second), grad_ref[...], 1, 0).astype(bf16)

    (out,) = whole_call(
        body, [shape((slots, D), bf16)], [idst, grad], after=after, name="send_grads"
    )
    return out


def apply_gates(experts, blocks, place, rows, gates):
    slots = gates.shape[0]
    capacity = slots // experts
    if blocks == 1:
        order = jnp.arange(experts) ^ place[2]
        rows = rows.reshape(experts, capacity, D)[order].reshape(slots, D)
        gates = gates.reshape(experts, capacity, LANES)[order].reshape(slots, LANES)

    def body(place_ref, rows_ref, gates_ref, *outs):
        for index, out_ref in enumerate(outs):
            span = pl.ds(0, slots)
            if blocks > 1:
                source = pl.multiple_of((index ^ place_ref[2]) * capacity, capacity)
                span = pl.ds(source, capacity)
            out_ref[...] = (gates_ref[span, 0:1] * rows_ref[span, :].astype(f32)).astype(bf16)

    return whole_call(
        body, block_shapes(blocks, slots), [place, rows, gates], smem=1, streamed=True,
        name="apply_gates",
    )


def route_body(layer, experts, capacity, last, blocks, place_ref, *refs):
    top = 32 * layer
    own = place_ref[2]
    x_ref, keep_ref, recv_ref, far_ref, feature_ref, ids_ref, idst_ref = refs[:7]
    middle_ref, soft_ref, meta_ref, dest_ref = refs[7:11]
    rows_refs = refs[11 : 11 + blocks]
    tokens = x_ref.shape[0]
    slots = experts * capacity
    middle = (
        x_ref[...].astype(f32)
        + keep_ref[:tokens, :]
        + recv_ref[:tokens, :].astype(f32)
        + far_ref[...].astype(f32)
    )
    middle_ref[...] = middle
    normed = middle * rms_scale(middle) * feature_ref[top + 17 : top + 18, :]
    lane = lax.broadcasted_iota(jnp.int32, (tokens, LANES), 1)
    logits = dot(normed, feature_ref[...], 1, 1, lax.Precision.HIGHEST)
    logits = jnp.where((lane >= top) & (lane < top + experts), logits, NEGATIVE)
    power = jnp.exp(logits - jnp.max(logits, -1, keepdims=True))
    soft = power / jnp.sum(power, -1, keepdims=True)
    soft_ref[...] = soft
    ids = ids_ref[...]
    hit0 = lane == ids[:, 0:1] + top
    hit1 = lane == ids[:, 1:2] + top
    picked0 = jnp.sum(jnp.where(hit0, soft, 0.0), -1, keepdims=True)
    picked1 = jnp.sum(jnp.where(hit1, soft, 0.0), -1, keepdims=True)
    pick_total = picked0 + picked1
    down = lax.broadcasted_iota(jnp.int32, (tokens, tokens), 0)
    across = lax.broadcasted_iota(jnp.int32, (tokens, tokens), 1)
    counts = dot(one_hot(across < down), one_hot(hit0 | hit1), 1, 0)
    dest0 = (ids[:, 0:1] ^ own).astype(f32) * capacity + jnp.sum(
        jnp.where(hit0, counts, 0.0), -1, keepdims=True
    )
    dest1 = (ids[:, 1:2] ^ own).astype(f32) * capacity + jnp.sum(
        jnp.where(hit1, counts, 0.0), -1, keepdims=True
    )
    fields = (dest0, dest1, picked0 / pick_total, picked1 / pick_total, pick_total)
    meta = jnp.zeros((tokens, LANES), f32)
    for index, field in enumerate(fields):
        meta = jnp.where(lane == index, field, meta)
    meta_ref[...] = meta
    dest_rows = slot_rows(idst_ref[...], capacity, own)
    dest_ref[...] = dest_rows
    first, second = dispatch_grid(dest_rows, slots, tokens)
    store_blocks(rows_refs, dot(one_hot(first | second), normed.astype(bf16), 1, 0))
    if last:
        total = None
        place = lax.broadcasted_iota(jnp.int32, (slots, tokens), 0)
        for index in range(2):
            slot = dest_rows[index : index + 1, :] - (idst_ref[index : index + 1, :] ^ own) * capacity
            flags = place == slot + idst_ref[index : index + 1, :] * capacity
            gate = meta[:, 2 + index : 3 + index]
            spread = jnp.zeros((tokens, LANES), f32)
            for term in range(3):
                piece = gate.astype(bf16).astype(f32)
                spread = jnp.where(lane == term, piece, spread)
                gate = gate - piece
            got = dot(one_hot(flags), spread.astype(bf16), 1, 0)
            total = got if total is None else total + got
        refs[-1][...] = jnp.broadcast_to(jnp.sum(total, -1, keepdims=True), total.shape)


def route(
    layer, experts, capacity, blocks, place, x, keep, recv, far, feature, ids, idst, last, after=()
):
    tokens = x.shape[0]
    slots = experts * capacity
    outs = [
        shape((tokens, D), f32),
        shape((tokens, LANES), f32),
        shape((tokens, LANES), f32),
        shape((8, tokens), jnp.int32),
    ] + block_shapes(blocks, slots)
    if last:
        outs.append(shape((slots, LANES), f32))

    def body(*refs):
        route_body(layer, experts, capacity, last, blocks, *refs)

    return whole_call(
        body, outs, [place, x, keep, recv, far, feature, ids, idst], smem=1,
        flops=2 * slots * tokens * D, after=after, name="route",
    )


def combine(middle, back, meta, feature=None):
    tokens = middle.shape[0]
    count = len(back)
    last = feature is None
    args = [middle, meta, *back]
    outs = [shape((tokens, D), bf16 if last else f32)]
    if not last:
        args.append(feature)
        outs.append(shape((tokens, D), bf16))

    def body(middle_ref, meta_ref, *refs):
        meta = meta_ref[...]
        rows = stacked(refs[:count])
        first, second = collect_grid(meta, rows.shape[0])
        x = (
            middle_ref[...]
            + meta[:, 2:3] * dot(one_hot(first), rows, 1, 0)
            + meta[:, 3:4] * dot(one_hot(second), rows, 1, 0)
        )
        if last:
            refs[-1][...] = x.astype(bf16)
        else:
            refs[-2][...] = x
            refs[-1][...] = (x * rms_scale(x) * refs[count][48:49, :]).astype(bf16)

    return whole_call(
        body, outs, args, flops=4 * tokens * D * count * back[0].shape[0], name="combine"
    )


def expert_token_back_body(
    layer, back_refs, came_refs, g_ref, middle_ref, soft_ref, meta_ref, ids_ref, feature_ref,
    dmiddle_ref, dattn_ref, small_ref,
):
    back, came = stacked(back_refs), stacked(came_refs)
    top = 32 * layer
    gain_row = feature_ref[top + 17 : top + 18, :]
    meta = meta_ref[...]
    g = g_ref[...].astype(f32)
    slots = back.shape[0]
    first, second = collect_grid(meta, slots)
    grad_gate0 = jnp.sum(g * dot(one_hot(first), back, 1, 0), -1, keepdims=True)
    grad_gate1 = jnp.sum(g * dot(one_hot(second), back, 1, 0), -1, keepdims=True)
    grad_normed = dot(one_hot(first | second), came, 1, 0)
    gap = (grad_gate0 - grad_gate1) / meta[:, 4:5]
    ids = ids_ref[...]
    lane = lax.broadcasted_iota(jnp.int32, meta.shape, 1)
    grad_soft = jnp.where(lane == ids[:, 0:1] + top, meta[:, 3:4] * gap, 0.0) + jnp.where(
        lane == ids[:, 1:2] + top, -meta[:, 2:3] * gap, 0.0
    )
    soft = soft_ref[...]
    grad_logits = soft * (grad_soft - jnp.sum(soft * grad_soft, -1, keepdims=True))
    middle = middle_ref[...]
    normed = middle * rms_scale(middle) * gain_row
    grad_router = dot(grad_logits.T, normed, 1, 0, lax.Precision.HIGHEST)
    grad_normed = grad_normed + dot(
        grad_logits, feature_ref[...], 1, 0, lax.Precision.HIGHEST
    )
    grad_branch, grad_gain = norm_back(middle, gain_row, grad_normed)
    dmiddle = g + grad_branch
    dmiddle_ref[...] = dmiddle
    dattn_ref[...] = dmiddle.astype(bf16)
    small_ref[:16, :] = grad_router[top : top + 16, :]
    small_ref[16:24, :] = jnp.broadcast_to(grad_gain, (8, D))


def expert_token_back(layer, back, came, g, middle, soft, meta, ids, feature, after=()):
    tokens = middle.shape[0]

    def body(*refs):
        count = len(back)
        expert_token_back_body(layer, refs[:count], refs[count : 2 * count], *refs[2 * count :])

    return whole_call(
        body,
        (shape((tokens, D), f32), shape((tokens, D), bf16), shape((24, D), f32)),
        [*back, *came, g, middle, soft, meta, ids, feature],
        after=after,
        flops=6 * tokens * D * len(back) * back[0].shape[0],
        streamed=True,
        limit=32,
        name="expert_token_back",
    )


def attention_token_back_body(layer, *refs):
    if layer == 0:
        x_ref, dmiddle_ref, keep_ref, recv_ref, far_ref, feature_ref, out_ref = refs
    else:
        (x_ref, dmiddle_ref, keep_ref, recv_ref, far_ref, feature_ref, meta_ref, dest_ref,
         out_ref, *sent_refs) = refs
    tokens = x_ref.shape[0]
    grad_normed = (
        keep_ref[:tokens, :] + recv_ref[:tokens, :].astype(f32) + far_ref[...].astype(f32)
    )
    gain_row = feature_ref[32 * layer + 16 : 32 * layer + 17, :]
    grad_branch, _ = norm_back(x_ref[...].astype(f32), gain_row, grad_normed)
    g = dmiddle_ref[...] + grad_branch
    out_ref[...] = g
    if layer > 0:
        slots = len(sent_refs) * sent_refs[0].shape[0]
        store_blocks(sent_refs, scatter_grads(g, meta_ref[...], dest_ref[...], slots))


def attention_token_back(
    layer, x, dmiddle, keep, recv, far, feature, meta=None, dest=None, blocks=1, slots=0, after=()
):
    tokens = x.shape[0]
    outs = [shape((tokens, D), f32)]
    args = [x, dmiddle, keep, recv, far, feature]
    if meta is not None:
        outs += block_shapes(blocks, slots)
        args += [meta, dest]

    def body(*refs):
        attention_token_back_body(layer, *refs)

    return whole_call(
        body, outs, args, flops=4 * tokens * D * slots, after=after, name="attention_token_back"
    )


def gelu_parts(gate):
    inner = math.sqrt(2.0 / math.pi) * (gate + 0.044715 * gate * gate * gate)
    return jnp.tanh(inner)


def weight_specs(layer, tile):
    return [
        pl.BlockSpec((1, 1, D, tile), lambda s: (layer, 0, 0, s)),
        pl.BlockSpec((1, 1, D, tile), lambda s: (layer, 0, 0, FF // tile + s)),
        pl.BlockSpec((1, 1, D, tile), lambda s: (layer, 0, 0, s)),
    ]


def block_specs(blocks):
    return [pl.BlockSpec(b.shape, lambda s: (0, 0)) for b in blocks]


def expert_call(body, steps, outs, out_specs, args, in_specs, scratch, limit, after, name):
    used = len(args)

    def ordered(*refs):
        body(*refs[:used], *refs[used + len(after) :])

    count = ROWS_HINT
    return pl.pallas_call(
        ordered,
        grid=(steps,),
        out_shape=tuple(outs),
        in_specs=list(in_specs) + [pl.BlockSpec(memory_space=pltpu.HBM)] * len(after),
        out_specs=tuple(out_specs),
        scratch_shapes=list(scratch),
        compiler_params=pltpu.CompilerParams(vmem_limit_bytes=limit * MIB),
        cost_estimate=pl.CostEstimate(
            flops=6 * count * D * FF, bytes_accessed=6 * D * FF, transcendentals=count * FF
        ),
        name=name,
    )(*args, *[far_away(a) for a in after])


def expert_forward(layer, blocks, w_in, w_out, after=()):
    number = len(blocks)
    count = number * blocks[0].shape[0]
    steps = FF // WIDE_TILE

    def body(*refs):
        wg_ref, wu_ref, wo_ref = refs[number : number + 3]
        produced_refs = refs[number + 3 : 2 * number + 3]
        acts_ref, rows_ref, total_ref = refs[2 * number + 3 :]
        step = pl.program_id(0)

        @pl.when(step == 0)
        def _():
            rows_ref[...] = stacked(refs[:number])

        rows = rows_ref[...]
        gate = dot(rows, wg_ref[0, 0], 1, 0)
        up = dot(rows, wu_ref[0, 0], 1, 0)
        acts_ref[0] = gate.astype(bf16)
        acts_ref[1] = up.astype(bf16)
        hidden = (0.5 * gate * (1.0 + gelu_parts(gate)) * up).astype(bf16)
        out = dot(hidden, wo_ref[0, 0], 1, 1)

        @pl.when(step == 0)
        def _():
            total_ref[...] = out

        @pl.when(step == steps - 1)
        def _():
            store_blocks(produced_refs, total_ref[...] + out)

    *produced, acts = expert_call(
        body,
        steps,
        [shape(b.shape, bf16) for b in blocks] + [pltpu.HBM((2, count, FF), bf16)],
        block_specs(blocks) + [pl.BlockSpec((2, count, WIDE_TILE), lambda s: (0, 0, s))],
        [*blocks, far_away(w_in), far_away(w_in), far_away(w_out)],
        block_specs(blocks) + weight_specs(layer, WIDE_TILE),
        [pltpu.VMEM((count, D), bf16), pltpu.VMEM((count, D), f32)],
        56,
        after,
        "expert_forward",
    )
    return produced, acts


def expert_backward(layer, blocks, out_blocks, acts, w_in, w_out, after=()):
    number = len(blocks)
    count = number * blocks[0].shape[0]
    steps = FF // WIDE_TILE
    outs = block_shapes(out_blocks, count)

    def body(*refs):
        acts_refs = refs[number : number + len(acts)]
        wg_ref, wu_ref, wo_ref, *rest = refs[number + len(acts) :]
        drows_refs = rest[:out_blocks]
        parts_ref, grad_ref, total_ref = rest[out_blocks:]
        step = pl.program_id(0)

        @pl.when(step == 0)
        def _():
            grad_ref[...] = stacked(refs[:number])

        grad_hidden = dot(grad_ref[...], wo_ref[0, 0], 1, 0)
        gate = jnp.concatenate([ref[0] for ref in acts_refs], 0).astype(f32)
        up = jnp.concatenate([ref[1] for ref in acts_refs], 0).astype(f32)
        curve = gelu_parts(gate)
        value = 0.5 * gate * (1.0 + curve)
        slope = 0.5 * (1.0 + curve) + 0.5 * gate * (1.0 - curve * curve) * math.sqrt(
            2.0 / math.pi
        ) * (1.0 + 3.0 * 0.044715 * gate * gate)
        grad_gate = (grad_hidden * up * slope).astype(bf16)
        grad_up = (grad_hidden * value).astype(bf16)
        parts_ref[0] = grad_gate
        parts_ref[1] = grad_up
        parts_ref[2] = (value * up).astype(bf16)
        out = dot(grad_gate, wg_ref[0, 0], 1, 1) + dot(grad_up, wu_ref[0, 0], 1, 1)

        @pl.when(step == 0)
        def _():
            total_ref[...] = out

        @pl.when(step == steps - 1)
        def _():
            store_blocks(drows_refs, total_ref[...] + out)

    *drows, parts = expert_call(
        body,
        steps,
        outs + [pltpu.HBM((3, count, FF), bf16)],
        block_specs(outs) + [pl.BlockSpec((3, count, WIDE_TILE), lambda s: (0, 0, s))],
        [*blocks, *[far_away(a) for a in acts], far_away(w_in), far_away(w_in), far_away(w_out)],
        block_specs(blocks)
        + [pl.BlockSpec((2, a.shape[1], WIDE_TILE), lambda s: (0, 0, s)) for a in acts]
        + weight_specs(layer, WIDE_TILE),
        [pltpu.VMEM((count, D), bf16), pltpu.VMEM((count, D), f32)],
        58,
        after,
        "expert_backward",
    )
    return drows, parts


def expert_grads(shares, rows, grads, parts, after=()):
    count = len(rows) * rows[0].shape[0]
    tall = D // shares
    first = len(rows)
    second = first + len(grads)
    third = second + len(parts)

    def body(*refs):
        out_ref, rows_t, grad_t = refs[third:]

        @pl.when(pl.program_id(0) == 0)
        def _():
            rows_t[...] = stacked(refs[:first]).T
            grad_t[...] = stacked(refs[first:second]).T

        for which in range(3):
            left = rows_t if which < 2 else grad_t
            right = [ref[which] for ref in refs[second:third]]
            right = right[0] if len(right) == 1 else jnp.concatenate(right, 0)
            got = dot(left[...], right, 1, 0).astype(bf16)
            for share in range(shares):
                out_ref[share, which] = got[share * tall : (share + 1) * tall, :]

    (out,) = expert_call(
        body,
        FF_STEPS,
        [pltpu.HBM((shares, 3, tall, FF), bf16)],
        [pl.BlockSpec((shares, 3, tall, FF_TILE), lambda s: (0, 0, 0, s))],
        [*rows, *grads, *[far_away(p) for p in parts]],
        block_specs(rows)
        + block_specs(grads)
        + [pl.BlockSpec((3, p.shape[1], FF_TILE), lambda s: (0, 0, s)) for p in parts],
        [pltpu.VMEM((D, count), bf16), pltpu.VMEM((D, count), bf16)],
        32,
        after,
        "expert_grads",
    )
    return out


def place_expert_grads(layer, summed, before=None, after=()):
    tall = summed.shape[1]
    outs = (
        pltpu.HBM((LAYERS, 1, tall, 2 * FF), f32),
        pltpu.HBM((LAYERS, 1, tall, FF), f32),
    )
    held = [] if before is None else list(before)

    def body(part_ref, out_part_ref, *refs):
        in_ref, out_ref = refs[-2:]
        in_ref[0, 0] = part_ref[0].astype(f32)
        out_ref[0, 0] = out_part_ref[0].astype(f32)

    return pl.pallas_call(
        body,
        grid=(2,),
        out_shape=outs,
        in_specs=[
            pl.BlockSpec((1, tall, FF), lambda s: (s, 0, 0)),
            pl.BlockSpec((1, tall, FF), lambda s: (2, 0, 0)),
        ]
        + [pl.BlockSpec(memory_space=pl.ANY)] * (len(held) + len(after)),
        out_specs=(
            pl.BlockSpec((1, 1, tall, FF), lambda s: (layer, 0, 0, s)),
            pl.BlockSpec((1, 1, tall, FF), lambda s: (layer, 0, 0, 0)),
        ),
        input_output_aliases={2: 0, 3: 1} if held else {},
        compiler_params=pltpu.CompilerParams(vmem_limit_bytes=32 * MIB),
        name="place_expert_grads",
    )(far_away(summed), far_away(summed), *[far_away(h) for h in [*held, *after]])


TWIN = [(i, i ^ 1) for i in range(GROUP)]
ACROSS = [(i, i ^ 2) for i in range(GROUP)]
FLIP = [(0, 1), (1, 0)]


def share_pieces(piece):
    across = lax.ppermute(piece, "context", ACROSS)
    twin = lax.ppermute(piece, "context", TWIN)
    return [piece, twin, across, lax.ppermute(across, "context", TWIN)]


def sum_pieces(keep, send):
    rows = keep.shape[0] // 2
    recv = lax.ppermute(send, "context", TWIN)
    other = (keep[rows:] + recv[rows:].astype(f32)).astype(bf16)
    return keep, recv, lax.ppermute(other, "context", ACROSS)


def sum_zone(zone):
    return jnp.sum(zone.astype(f32), 0)


def dense_sum(
    experts, pairs, share, table_share, place, grad_w_in, grad_w_out, small, gain_a, by_distance,
    hits,
):
    by_bucket = jnp.dot(hits, by_distance[:OWN].T, precision=lax.Precision.HIGHEST)
    buckets = jnp.where(
        jnp.arange(GROUP)[None, None, :] == place[0], by_bucket[:, :, None], 0.0
    ).reshape(experts, GROUP, pairs, 1, table_share)
    features = jnp.concatenate([small[:16], gain_a[:1], small[16:17]], 0).T
    features = features.reshape(experts, GROUP, pairs, share, 18)
    flat = jnp.zeros((experts, GROUP, pairs, share, LANES), f32)
    flat = flat.at[..., :18].set(features).at[..., :1, 64 : 64 + table_share].set(buckets)
    pack = jnp.concatenate(
        [grad_w_in.reshape(experts, GROUP, pairs, share, PACKED), flat.astype(bf16)], -1
    ).transpose(0, 2, 1, 3, 4)
    pack = pack.reshape(experts * pairs, GROUP * share, PACKED + LANES)
    mine = lax.psum_scatter(pack, ("experts", "dp"), scatter_dimension=0, tiled=False)
    inner = lax.all_to_all(
        mine.reshape(GROUP, share, PACKED + LANES), "context", split_axis=0, concat_axis=0
    ).astype(f32)
    g_in = inner[..., :PACKED].reshape(GROUP, share, 3, OWN, HEAD_DIM)
    g_in = g_in.transpose(1, 2, 3, 0, 4).reshape(share, 3 * D)
    placed_rows = jnp.where(
        jnp.arange(GROUP)[None, :, None, None] == place[0],
        grad_w_out.reshape(OWN, 1, HEAD_DIM, D),
        jnp.zeros((), bf16),
    ).reshape(D, D)
    g_out = lax.psum_scatter(placed_rows, ALL, scatter_dimension=0, tiled=True).astype(f32)
    return g_in, g_out, jnp.sum(inner[..., PACKED:], 0)


def exchange(rows):
    return lax.all_to_all(rows, "experts", split_axis=0, concat_axis=0, tiled=True)


def swap(blocks, experts):
    split = blocks if len(blocks) > 1 else jnp.split(blocks[0], experts)
    moved = [
        part if k == 0 else lax.ppermute(part, "experts", [(i, i ^ k) for i in range(experts)])
        for k, part in enumerate(split)
    ]
    return moved if len(blocks) > 1 else [jnp.concatenate(moved)]


def on_device(
    tokens, doc_starts, expert_ids, attn_in, attn_out, router, gains, rel_table,
    expert_in, expert_out, out_grad,
):
    experts = lax.axis_size("experts")
    pairs = lax.axis_size("dp")
    share = attn_in.shape[1]
    table_share = rel_table.shape[1]
    direct = share * pairs == HEAD_DIM and experts * GROUP == HEADS and pairs == 2
    place = jnp.stack(
        [lax.axis_index("context"), lax.axis_index("dp"), lax.axis_index("experts")]
    ).astype(jnp.int32)
    start_tokens = tokens[0]
    ids = expert_ids[0]
    idst = ids.T
    rows = start_tokens.shape[0]
    capacity = (10 * rows + 4 * experts - 1) // (4 * experts)
    slots = experts * capacity
    blocks = experts if experts == 4 and capacity % 16 == 0 else 1
    chunks = [(0, 1), (2,), (3,)] if blocks == 4 else [(0,)]
    grad_in = out_grad[0]
    hits = jnp.asarray(bucket_hits())

    packets = prepare(direct, attn_in, attn_out, router, gains, rel_table)

    def spread(packet):
        return lax.all_to_all(packet, "context", split_axis=0, concat_axis=0)

    def gather(part):
        return lax.all_gather(part, ("experts", "dp"), axis=0, tiled=False).reshape(
            experts, pairs, *part.shape
        )

    if direct:
        packet = spread(packets[0])
        top = PACKED + LANES

        def together(columns, rows_out):
            part = jnp.concatenate([columns, rows_out], -1)
            return lax.all_gather(part, ("experts", "dp"), axis=0, tiled=False)

        first = together(packet[..., :top], packets[1])
        w_in0, w_out0, feature, bias = unpack(place, hits, experts, pairs, 0, first)
        second = [together(packet[..., top:], packets[2])]
        w_in1, w_out1 = unpack(place, hits, experts, pairs, 1, second[0])
        w_in, w_out = [w_in0, w_in1], [w_out0, w_out1]
    else:
        second = []
        w_in, w_out = [], []
        for layer in range(LAYERS):
            at = layer * (PACKED + LANES)
            part = spread(packets[0])[..., at : at + PACKED + LANES]
            got = gather(part).transpose(0, 2, 1, 3, 4)
            w_in.append(got[..., :PACKED].reshape(D, PACKED))
            if layer == 0:
                small_all = got[..., PACKED : PACKED + LANES]
            full = lax.all_gather(attn_out[layer], ALL, axis=0, tiled=True)
            mine = lax.dynamic_index_in_dim(
                full.reshape(OWN, GROUP, HEAD_DIM, D), place[0], 1, keepdims=False
            )
            w_out.append(mine.reshape(OWN_COLS, GROUP, D // GROUP).transpose(1, 0, 2))
        feature = small_all.reshape(D, LANES).astype(f32).T
        bias_rows = []
        for layer in range(LAYERS):
            at = 64 + 32 * layer
            table = small_all[:, :, :, 0, at : at + table_share].reshape(BUCKETS, OWN, GROUP)
            table = lax.dynamic_index_in_dim(table, place[0], 2, keepdims=False).astype(f32)
            row = jnp.dot((table - table[-1:]).T, hits, precision=lax.Precision.HIGHEST)
            bias_rows.append(jnp.pad(row, ((0, 8 - OWN), (0, 0))))
        bias = jnp.stack(bias_rows)
    places = jnp.arange(GROUP * rows, dtype=jnp.int32)
    starts = doc_starts[0]
    low = jnp.max(
        jnp.where(starts[:, None] <= places[None, :], starts[:, None], 0), 0, keepdims=True
    )

    pieces = share_pieces(start_tokens)
    x = start_tokens
    kept = []
    for layer in range(LAYERS):
        packed, log_total, mixed, keep, send, *normed_all = attention_forward(
            layer, place, pieces, w_in[layer], feature, bias, low, w_out[layer]
        )
        normed_rows = normed_all if layer == 0 else pieces
        keep, recv, far = sum_pieces(keep, send)
        last = layer == LAYERS - 1
        middle, soft, meta, dest, *sent = route(
            layer, experts, capacity, blocks, place, x, keep, recv, far, feature, ids, idst, last,
            after=[arrived_grad] if last else [],
        )
        arrived = swap(sent[:blocks], experts)
        if last:
            gates = exchange(sent[blocks])
        produced, acts, drows, parts = [], [], [], []
        order = second if layer == 0 else []
        for chunk in chunks:
            done, kept_acts = expert_forward(
                layer, [arrived[k] for k in chunk], expert_in, expert_out, after=order
            )
            produced += done
            acts.append(kept_acts)
            order = done[:1]
            if last:
                if not drows:
                    arrived_grad = apply_gates(experts, blocks, place, arrived_grad, gates)
                done, some = expert_backward(
                    layer, [arrived_grad[k] for k in chunk], len(chunk), acts[-1:], expert_in,
                    expert_out,
                )
                drows += done
                parts.append(some)
                order = done[:1]
        back = swap(produced, experts)
        kept.append(
            (x, normed_rows, packed, log_total, mixed, middle, soft, meta, dest, arrived, acts, back)
        )
        if last:
            (result,) = combine(middle, back, meta)
        else:
            x, normed = combine(middle, back, meta, feature)
            ungated = send_grads(experts, capacity, idst, grad_in, [x])
            arrived_grad = exchange(ungated)
            pieces = share_pieces(hold(normed, [ungated]))

    g = grad_in
    inner, outer, expert_totals = [], [], []
    other = None
    placed_grads = None
    for layer in range(LAYERS - 1, -1, -1):
        (x, normed_rows, packed, log_total, mixed, middle, soft, meta, dest, arrived, acts,
         back) = kept[layer]
        if layer < LAYERS - 1:
            drows, parts = [], []
            for index, chunk in enumerate(chunks):
                done, some = expert_backward(
                    layer, [arrived_grad[k] for k in chunk], len(chunk), acts[index : index + 1],
                    expert_in, expert_out, after=drows[-1:],
                )
                drows += done
                parts.append(some)
        came = swap(drows, experts)
        early = [] if other is None else [other]
        weight_grads = expert_grads(
            GROUP * pairs, arrived, arrived_grad, parts, after=(back if layer else []) + early
        )
        weight_grads = hold(weight_grads, came)
        total = lax.psum_scatter(
            weight_grads, ("context", "dp"), scatter_dimension=0, tiled=False
        )
        dmiddle, dattn, small_b = expert_token_back(
            layer, back, came, g, middle, soft, meta, ids, feature, after=[weight_grads]
        )
        zones = []
        if direct and other is not None:
            ours = hold(keep_dense, [dattn]) + other.astype(f32)
            zones = [exchange(ours.astype(bf16))]
        expert_totals.append(total)
        grad_pieces = share_pieces(dattn)
        grad_packed, keep, send, by_distance, gain_a = attention_backward(
            layer, place, grad_pieces, w_in[layer], feature, bias, low, w_out[layer], packed,
            log_total, normed_rows,
        )
        keep, recv, far = sum_pieces(keep, send)
        if layer > 0:
            below = kept[layer - 1]
            g, *sent = attention_token_back(
                layer, x, dmiddle, keep, recv, far, feature, below[7], below[8], blocks, slots
            )
            arrived_grad = swap(sent, experts)
        else:
            placed_grads = place_expert_grads(layer + 1, expert_totals[0])
            (g,) = attention_token_back(
                layer, x, dmiddle, keep, recv, far, feature, after=[placed_grads[0]]
            )
        if direct:
            keep_dense, send_dense, *rest = dense_pack(
                experts, pairs, share, place, normed_rows, grad_pieces, grad_packed, mixed,
                small_b, gain_a, by_distance, hits, split=layer == 0, after=zones,
            )
            other = lax.ppermute(send_dense, "dp", FLIP)
            if layer == 0:
                (zone,) = zones
                total = sum_zone(zone)
                flats = [total[:, : PACKED + LANES].astype(bf16)]
                outer.append(total[:, PACKED + LANES :])
                rest = sum_zone(exchange(rest[0]))
                theirs = lax.ppermute(rest[1].astype(bf16), "dp", FLIP)
                rest = rest[0] + theirs.astype(f32)
                ours = hold(keep_dense, [g, result, placed_grads[0]]) + other.astype(f32)
                total = sum_zone(exchange(ours.astype(bf16)))
                more = PACKED + LANES - EARLY_COLS
                flats.insert(0, jnp.concatenate([total, rest[:, :more]], -1).astype(bf16))
                outer.append(rest[:, more:])
                flat = jnp.stack([flat.reshape(GROUP, share, -1) for flat in flats], 1)
                inner = spread(flat)
        else:
            grad_w_in, grad_w_out = dense_grads(normed_rows, grad_pieces, grad_packed, mixed)
            inner.append(
                dense_sum(
                    experts, pairs, share, table_share, place, grad_w_in, grad_w_out, small_b,
                    gain_a, by_distance, hits,
                )
            )
    expert_grads_all = place_expert_grads(0, expert_totals[1], placed_grads)
    if direct:
        grad_attn_in, grad_attn_out, small_grad = finish_dense(
            share, inner, outer[::-1]
        )
    else:
        grad_attn_in, grad_attn_out, small_grad = (
            jnp.stack([entry[k] for entry in inner[::-1]]) for k in range(3)
        )
    return (
        result[None],
        g[None],
        grad_attn_in,
        grad_attn_out,
        small_grad[..., :experts],
        small_grad[..., 16:18],
        small_grad[:, 0, 64 : 64 + table_share],
        *expert_grads_all,
    )


def solution(mesh):
    return jax.shard_map(
        on_device,
        mesh=mesh,
        in_specs=(
            P(("experts", "dp"), "context", None),
            P(("experts", "dp"), None),
            P(("experts", "dp"), "context", None),
            P(None, ("experts", "context", "dp"), None),
            P(None, ("experts", "context", "dp"), None),
            P(None, ("experts", "context", "dp"), None),
            P(None, ("experts", "context", "dp"), None),
            P(None, ("experts", "context", "dp")),
            P(None, "experts", None, None),
            P(None, "experts", None, None),
            P(("experts", "dp"), "context", None),
        ),
        out_specs=(
            P(("experts", "dp"), "context", None),
            P(("experts", "dp"), "context", None),
            P(None, ("experts", "context", "dp"), None),
            P(None, ("experts", "context", "dp"), None),
            P(None, ("experts", "context", "dp"), None),
            P(None, ("experts", "context", "dp"), None),
            P(None, ("experts", "context", "dp")),
            P(None, "experts", ("context", "dp"), None),
            P(None, "experts", ("context", "dp"), None),
        ),
        check_vma=False,
    )
```

```python
import math

import jax
import jax.numpy as jnp
import numpy as np
from jax import lax
from jax.experimental import pallas as pl
from jax.experimental.pallas import tpu as pltpu
from jax.sharding import PartitionSpec as P

D = 1024
HEADS = 16
HEAD_DIM = 64
FF = 2816
BUCKETS = 32
MAX_DISTANCE = 128
LAYERS = 2
EPSILON = 1e-06
NEGATIVE = -1e30
SCORE_SCALE = 0.125
ALL = ("experts", "context", "dp")
GROUP = 4
OWN = HEADS // GROUP
OWN_COLS = OWN * HEAD_DIM
PACKED = 3 * OWN_COLS
LANES = 128
REACH = 512
FF_TILE = 256
FF_STEPS = FF // FF_TILE
WIDE_TILE = FF // 2
EARLY_COLS = 512
ROWS_HINT = 320
MIB = 1 << 20

bf16 = jnp.bfloat16
f32 = jnp.float32


def bucket_bounds(bucket_count, far_reach):
    half_count = bucket_count // 2
    bounds = list(range(1, half_count + 1))
    for section_index in range(1, half_count):
        bounds.append(
            int(math.ceil(half_count * (far_reach / half_count) ** (section_index / half_count)))
        )
    return np.array(bounds, np.int32)


def bucket_hits():
    distance = np.arange(REACH)
    bucket = (distance[:, None] >= bucket_bounds(BUCKETS, MAX_DISTANCE)).sum(-1)
    return (np.arange(BUCKETS)[:, None] == bucket[None, :]).astype(np.float32)


def dot(a, b, ca, cb, precision=None):
    return lax.dot_general(
        a, b, (((ca,), (cb,)), ((), ())), precision=precision, preferred_element_type=f32
    )


def whole_call(
    body, out_shape, args, *, flops=0, limit=16, scratch=(), smem=0, name=None, after=(),
    streamed=False,
):
    specs = [pl.BlockSpec(memory_space=pltpu.SMEM)] * smem + [
        pl.BlockSpec(memory_space=pltpu.VMEM)
    ] * (len(args) - smem)
    outs = tuple(out_shape)
    moved = sum(a.size * a.dtype.itemsize for a in list(args) + list(outs))
    specs += [pl.BlockSpec(memory_space=pltpu.HBM)] * len(after)
    used = len(args)
    args = list(args) + [far_away(a) for a in after]

    def ordered(*refs):
        body(*refs[:used], *refs[used + len(after) :])

    if streamed:
        args = args[:smem] + [far_away(a) for a in args[smem:]]

        def full(a):
            return pl.BlockSpec(a.shape, lambda i: (0,) * len(a.shape))

        return pl.pallas_call(
            ordered,
            grid=(1,),
            out_shape=outs,
            in_specs=specs[:smem] + [full(a) for a in args[smem:used]] + specs[used:],
            out_specs=tuple(full(o) for o in outs),
            scratch_shapes=list(scratch),
            compiler_params=pltpu.CompilerParams(vmem_limit_bytes=limit * MIB),
            cost_estimate=pl.CostEstimate(
                flops=int(flops), bytes_accessed=int(moved), transcendentals=0
            ),
            name=name,
        )(*args)
    return pl.pallas_call(
        ordered,
        out_shape=outs,
        in_specs=specs,
        out_specs=tuple(pl.BlockSpec(memory_space=pltpu.VMEM) for _ in outs),
        scratch_shapes=list(scratch),
        compiler_params=pltpu.CompilerParams(vmem_limit_bytes=limit * MIB),
        cost_estimate=pl.CostEstimate(
            flops=int(flops), bytes_accessed=int(moved), transcendentals=0
        ),
        name=name,
    )(*args)


def far_away(x):
    return pltpu.with_memory_space_constraint(x, pltpu.HBM)


def hold(x, after):
    def body(*refs):
        pass

    return pl.pallas_call(
        body,
        out_shape=pltpu.HBM(x.shape, x.dtype),
        in_specs=[pl.BlockSpec(memory_space=pltpu.HBM)] * (1 + len(after)),
        out_specs=pl.BlockSpec(memory_space=pltpu.HBM),
        input_output_aliases={0: 0},
        compiler_params=pltpu.CompilerParams(vmem_limit_bytes=MIB),
        cost_estimate=pl.CostEstimate(flops=0, bytes_accessed=0, transcendentals=0),
        name="hold",
    )(far_away(x), *[far_away(a) for a in after])


def shape(dims, dtype):
    return jax.ShapeDtypeStruct(dims, dtype)


def rms_scale(inputs):
    return lax.rsqrt(jnp.mean(inputs * inputs, -1, keepdims=True) + EPSILON)


def norm_back(inputs, gain_row, upstream):
    inverse = rms_scale(inputs)
    scaled = upstream * gain_row
    inner_mean = jnp.mean(inputs * scaled, -1, keepdims=True)
    grad_inputs = inverse * scaled - inputs * (inverse * inverse * inverse) * inner_mean
    grad_gain = jnp.sum(upstream * inputs * inverse, 0, keepdims=True)
    return grad_inputs, grad_gain


def placed(count, offset):
    index = lax.broadcasted_iota(jnp.int32, (count, LANES), 0)
    lane = lax.broadcasted_iota(jnp.int32, (count, LANES), 1)
    return one_hot(lane == index + offset)


def prepare_body(direct, in_ref, out_ref, router_ref, gains_ref, table_ref, *packets):
    share = in_ref.shape[1]
    for layer in range(LAYERS):
        for which in range(3):
            for head in range(OWN):
                for c in range(GROUP):
                    source = which * D + (head * GROUP + c) * HEAD_DIM
                    target = which * OWN_COLS + head * HEAD_DIM
                    target += layer * (PACKED + LANES)
                    packets[0][c, :, target : target + HEAD_DIM] = in_ref[
                        layer, :, source : source + HEAD_DIM
                    ]
        if direct:
            width = D // GROUP
            for q in range(GROUP):
                packets[1 + layer][q] = out_ref[layer, :, q * width : (q + 1) * width]
    small = jnp.zeros((share, LANES), f32)
    row = lax.broadcasted_iota(jnp.int32, (share, LANES), 0)
    for layer in range(LAYERS):
        top = 32 * layer
        small = small + dot(router_ref[layer], placed(router_ref.shape[2], top), 1, 0)
        small = small + dot(gains_ref[layer], placed(2, top + 16), 1, 0)
        bucket = dot(table_ref[layer : layer + 1, :], placed(table_ref.shape[1], top + 64), 1, 0)
        small = small + jnp.where(row == 0, bucket, 0.0)
    for c in range(GROUP):
        packets[0][c, :, PACKED : PACKED + LANES] = small.astype(bf16)


def prepare(direct, attn_in, attn_out, router, gains, rel_table):
    share = attn_in.shape[1]
    outs = [shape((GROUP, share, 2 * PACKED + LANES), bf16)]
    if direct:
        outs += [shape((GROUP, share, D // GROUP), bf16)] * LAYERS

    def body(*refs):
        prepare_body(direct, *refs)

    return whole_call(
        body, outs, [attn_in, attn_out, router, gains, rel_table], streamed=True, name="prepare"
    )


def unpack(place, hits, experts, pairs, layer, got):
    share = got.shape[-2]
    width = D // GROUP
    first = layer == 0

    def body(place_ref, hits_ref, got_ref, w_in_ref, w_out_ref, *rest):
        for index in range(experts * pairs):
            e, d = index // pairs, index % pairs
            for c in range(GROUP):
                owner = (e * GROUP + c) * pairs + d
                at = owner * share
                w_in_ref[at : at + share, :] = got_ref[index, c, :, :PACKED]
                w_out_ref[c, index * share : (index + 1) * share, :] = got_ref[
                    index, c, :, got_ref.shape[-1] - width :
                ]
                if first:
                    flags = got_ref[index, c, :, PACKED : PACKED + LANES].astype(f32)
                    rest[2][at : at + share, :] = flags
                    rest[3][owner : owner + 1, :] = flags[:1, :]
        if not first:
            return
        feature_ref, bias_ref, flat_ref, bucket_ref = rest
        feature_ref[...] = flat_ref[...].T
        head = lax.broadcasted_iota(jnp.int32, (8, LANES), 0)
        lane = lax.broadcasted_iota(jnp.int32, (8, LANES), 1)
        for other in range(LAYERS):
            mine = jnp.where(
                (lane == 64 + 32 * other + head * GROUP + place_ref[0]) & (head < OWN), 1.0, 0.0
            )
            table = dot(mine, bucket_ref[...], 1, 1, lax.Precision.HIGHEST)
            bias_ref[other] = dot(
                table - table[:, BUCKETS - 1 :], hits_ref[...], 1, 0, lax.Precision.HIGHEST
            )

    outs = [shape((D, PACKED), bf16), shape((GROUP, OWN_COLS, D // GROUP), bf16)]
    scratch = []
    if first:
        outs += [shape((LANES, D), f32), shape((LAYERS, 8, REACH), f32)]
        scratch = [pltpu.VMEM((D, LANES), f32), pltpu.VMEM((BUCKETS, LANES), f32)]
    return whole_call(
        body, outs, [place, hits, got], smem=1, scratch=scratch, name="unpack"
    )


def near_bias(bias_ref, layer, head, rows):
    row = bias_ref[layer, head : head + 1, :]
    return pltpu.roll(jnp.broadcast_to(row, (rows, REACH)), 0, 1, stride=1, stride_axis=0)


def masked_scores(keys, queries, near, low, key_block, query_block, rows):
    scores = dot(keys, queries, 1, 1)
    key_place = lax.broadcasted_iota(jnp.int32, (rows, rows), 0)
    seen = key_place >= low - key_block * rows
    if key_block == query_block:
        scores = scores + near[:, :rows]
        seen = seen & (key_place <= lax.broadcasted_iota(jnp.int32, (rows, rows), 1))
    elif key_block == query_block - 1:
        scores = scores + near[:, rows:]
    return jnp.where(seen, scores, NEGATIVE)


def attention_forward_body(
    layer, place_ref, n0, n1, n2, n3, w_ref, feature_ref, bias_ref, low_ref, wo_ref,
    packed_ref, log_ref, mixed_ref, keep_ref, send_ref, *normed_ref,
):
    me = place_ref[0]
    rows = n0.shape[0]
    for r, piece in enumerate((n0, n1, n2, n3)):
        normed = piece[...]
        if layer == 0:
            wide = normed.astype(f32)
            normed = (wide * rms_scale(wide) * feature_ref[16:17, :]).astype(bf16)
            normed_ref[0][r * rows : (r + 1) * rows, :] = normed
        packed_ref[r * rows : (r + 1) * rows, :] = dot(normed, w_ref[...], 1, 0).astype(bf16)
    lane = lax.broadcasted_iota(jnp.int32, (rows, LANES), 1)
    starts = [pl.multiple_of((b ^ me) * rows, rows) for b in range(GROUP)]
    for pair in range(OWN // 2):
        at = pair * LANES

        def part(b, which):
            column = which * OWN_COLS + at
            return packed_ref[pl.ds(starts[b], rows), column : column + LANES]

        sides = [(lane // HEAD_DIM) == side for side in range(2)]
        nears = [near_bias(bias_ref, layer, pair * 2 + side, rows) for side in range(2)]
        for qb in range(GROUP):
            low = low_ref[:, qb * rows : (qb + 1) * rows]
            queries = part(qb, 0) * SCORE_SCALE
            total = None
            for side in range(2):
                mine = jnp.where(sides[side], queries, 0).astype(bf16)
                tiles = [
                    masked_scores(part(kb, 1), mine, nears[side], low, kb, qb, rows)
                    for kb in range(qb + 1)
                ]
                peak = jnp.max(tiles[0], 0, keepdims=True)
                for tile in tiles[1:]:
                    peak = jnp.maximum(peak, jnp.max(tile, 0, keepdims=True))
                weight_sum = jnp.zeros((1, rows), f32)
                out = jnp.zeros((LANES, rows), f32)
                for kb, tile in enumerate(tiles):
                    power = jnp.exp(tile - peak)
                    weight_sum = weight_sum + jnp.sum(power, 0, keepdims=True)
                    values = jnp.where(sides[side], part(kb, 2), 0).astype(bf16)
                    out = out + dot(values, power.astype(bf16), 0, 0)
                out = out / weight_sum
                total = out if total is None else total + out
                head = pair * 2 + side
                log_ref[head : head + 1, qb * rows : (qb + 1) * rows] = peak + jnp.log(weight_sum)
            mixed_ref[pl.ds(starts[qb], rows), at : at + LANES] = total.T.astype(bf16)
    width = wo_ref.shape[2]
    for r, (target, offset) in enumerate(
        ((keep_ref, 0), (send_ref, 0), (keep_ref, rows), (send_ref, rows))
    ):
        mixed = mixed_ref[r * rows : (r + 1) * rows, :]
        for q in range(wo_ref.shape[0]):
            target[offset : offset + rows, q * width : (q + 1) * width] = dot(
                mixed, wo_ref[q], 1, 0
            ).astype(target.dtype)


def attention_forward(layer, place, pieces, w_in, feature, bias, low, w_out):
    rows = pieces[0].shape[0]
    total = GROUP * rows
    outs = [
        shape((total, PACKED), bf16),
        shape((8, total), f32),
        shape((total, OWN_COLS), bf16),
        shape((2 * rows, D), f32),
        shape((2 * rows, D), bf16),
    ]
    if layer == 0:
        outs.append(shape((total, D), bf16))

    def body(*refs):
        attention_forward_body(layer, *refs)

    return whole_call(
        body,
        outs,
        [place, *pieces, w_in, feature, bias, low, w_out],
        smem=1,
        flops=2 * total * D * (PACKED + OWN_COLS) + 2 * total * total * OWN_COLS * 2,
        limit=24,
        name="attention_forward",
    )


def attention_backward_body(
    layer, place_ref, d0, d1, d2, d3, w_ref, feature_ref, bias_ref, low_ref, wo_ref, packed_ref,
    log_ref, *refs,
):
    normed_refs = refs[:-8]
    (grad_packed_ref, keep_ref, send_ref, table_ref, gain_ref, grad_mixed_ref, dk_ref,
     dv_ref) = refs[-8:]
    me = place_ref[0]
    rows = d0.shape[0]
    width = wo_ref.shape[2]
    for r, piece in enumerate((d0, d1, d2, d3)):
        got = jnp.zeros((rows, OWN_COLS), f32)
        for q in range(wo_ref.shape[0]):
            got = got + dot(piece[:, q * width : (q + 1) * width], wo_ref[q], 1, 1)
        grad_mixed_ref[r * rows : (r + 1) * rows, :] = got.astype(bf16)
    lane = lax.broadcasted_iota(jnp.int32, (rows, LANES), 1)
    starts = [pl.multiple_of((b ^ me) * rows, rows) for b in range(GROUP)]
    table_ref[...] = jnp.zeros(table_ref.shape, f32)
    for pair in range(OWN // 2):
        at = pair * LANES

        def part(b, which):
            column = which * OWN_COLS + at
            return packed_ref[pl.ds(starts[b], rows), column : column + LANES]

        sides = [(lane // HEAD_DIM) == side for side in range(2)]
        nears = [near_bias(bias_ref, layer, pair * 2 + side, rows) for side in range(2)]
        diag = [jnp.zeros((rows, rows), f32) for _ in range(2)]
        before = [jnp.zeros((rows, rows), f32) for _ in range(2)]
        far = [jnp.zeros((1, rows), f32) for _ in range(2)]
        dk_ref[...] = jnp.zeros(dk_ref.shape, f32)
        dv_ref[...] = jnp.zeros(dv_ref.shape, f32)
        for qb in range(GROUP):
            low = low_ref[:, qb * rows : (qb + 1) * rows]
            queries = part(qb, 0) * SCORE_SCALE
            upstream = grad_mixed_ref[pl.ds(starts[qb], rows), at : at + LANES]
            grad_queries = jnp.zeros((LANES, rows), f32)
            for side in range(2):
                head = pair * 2 + side
                mine = jnp.where(sides[side], queries, 0).astype(bf16)
                above = jnp.where(sides[side], upstream, 0).astype(bf16)
                log_total = log_ref[head : head + 1, qb * rows : (qb + 1) * rows]
                probs, grads = [], []
                row_dot = jnp.zeros((1, rows), f32)
                for kb in range(qb + 1):
                    scores = masked_scores(part(kb, 1), mine, nears[side], low, kb, qb, rows)
                    prob = jnp.exp(scores - log_total)
                    grad = dot(part(kb, 2), above, 1, 1)
                    row_dot = row_dot + jnp.sum(prob * grad, 0, keepdims=True)
                    probs.append(prob)
                    grads.append(grad)
                for kb in range(qb + 1):
                    grad_score = probs[kb] * (grads[kb] - row_dot)
                    if kb == qb:
                        diag[side] = diag[side] + grad_score
                    elif kb == qb - 1:
                        before[side] = before[side] + grad_score
                    else:
                        far[side] = far[side] + jnp.sum(grad_score, 0, keepdims=True)
                    grad_low = grad_score.astype(bf16)
                    keys = jnp.where(sides[side], part(kb, 1), 0).astype(bf16)
                    grad_queries = grad_queries + dot(keys, grad_low, 0, 0)
                    span = slice(kb * rows, (kb + 1) * rows)
                    dk_ref[span, :] += dot(grad_low, mine, 1, 0)
                    dv_ref[span, :] += dot(probs[kb].astype(bf16), above, 1, 0)
            grad_packed_ref[pl.ds(starts[qb], rows), at : at + LANES] = (
                grad_queries.T * SCORE_SCALE
            ).astype(bf16)
        for kb in range(GROUP):
            span = slice(kb * rows, (kb + 1) * rows)
            for which, source in ((1, dk_ref), (2, dv_ref)):
                column = which * OWN_COLS + at
                grad_packed_ref[pl.ds(starts[kb], rows), column : column + LANES] = source[
                    span, :
                ].astype(bf16)
        distance = lax.broadcasted_iota(jnp.int32, (1, REACH), 1)
        for side in range(2):
            head = pair * 2 + side
            skewed = jnp.concatenate([diag[side], before[side]], 1)
            row_index = lax.broadcasted_iota(jnp.int32, (rows, REACH), 0)
            step = 1
            while step < rows:
                skewed = jnp.where(
                    (row_index & step) != 0, pltpu.roll(skewed, REACH - step, 1), skewed
                )
                step *= 2
            by_distance = jnp.sum(skewed, 0, keepdims=True)
            far_sum = jnp.sum(far[side], 1, keepdims=True)
            table_ref[head : head + 1, :] = by_distance + jnp.where(
                distance == REACH - 1, far_sum, 0.0
            )
    for r, (target, offset) in enumerate(
        ((keep_ref, 0), (send_ref, 0), (keep_ref, rows), (send_ref, rows))
    ):
        grad_normed = dot(grad_packed_ref[r * rows : (r + 1) * rows, :], w_ref[...], 1, 1)
        target[offset : offset + rows, :] = grad_normed.astype(target.dtype)
        part_gain = jnp.sum(grad_normed * block_of(normed_refs, r, rows).astype(f32), 0, keepdims=True)
        gain_sum = part_gain if r == 0 else gain_sum + part_gain
    gain_row = feature_ref[32 * layer + 16 : 32 * layer + 17, :]
    gain_ref[...] = jnp.broadcast_to(gain_sum / gain_row, gain_ref.shape)


def block_of(refs, r, rows):
    return refs[r][...] if len(refs) > 1 else refs[0][r * rows : (r + 1) * rows, :]


def attention_backward(
    layer, place, pieces, w_in, feature, bias, low, w_out, packed, log_total, normed, after=()
):
    rows = pieces[0].shape[0]
    total = GROUP * rows

    def body(*refs):
        attention_backward_body(layer, *refs)

    return whole_call(
        body,
        (
            shape((total, PACKED), bf16),
            shape((2 * rows, D), f32),
            shape((2 * rows, D), bf16),
            shape((8, REACH), f32),
            shape((8, D), f32),
        ),
        [place, *pieces, w_in, feature, bias, low, w_out, packed, log_total, *normed],
        smem=1,
        after=after,
        scratch=[
            pltpu.VMEM((total, OWN_COLS), bf16),
            pltpu.VMEM((total, LANES), f32),
            pltpu.VMEM((total, LANES), f32),
        ],
        flops=2 * total * D * (PACKED + OWN_COLS) + 2 * total * total * OWN_COLS * 5,
        limit=24,
        name="attention_backward",
    )


def dense_products(normed, upstream, grad_packed_ref, mixed_ref):
    rows = upstream[0].shape[0]
    total_in = None
    total_out = None
    for r in range(GROUP):
        span = slice(r * rows, (r + 1) * rows)
        one = dot(block_of(normed, r, rows), grad_packed_ref[span, :], 0, 0)
        two = dot(mixed_ref[span, :], upstream[r][...], 0, 0)
        total_in = one if total_in is None else total_in + one
        total_out = two if total_out is None else total_out + two
    return total_in, total_out


def dense_grads(normed, upstream, grad_packed, mixed):
    rows = upstream[0].shape[0]
    count = len(normed)

    def body(*refs):
        total_in, total_out = dense_products(
            refs[:count], refs[count : count + GROUP], refs[-4], refs[-3]
        )
        refs[-2][...] = total_in.astype(bf16)
        refs[-1][...] = total_out.astype(bf16)

    return whole_call(
        body,
        (shape((D, PACKED), bf16), shape((OWN_COLS, D), bf16)),
        [*normed, *upstream, grad_packed, mixed],
        flops=2 * GROUP * rows * D * (PACKED + OWN_COLS),
        name="dense_grads",
    )


def dense_pack(experts, pairs, share, place, normed, upstream, grad_packed, mixed, small, gain_a,
               by_distance, hits, split, after=()):
    rows = upstream[0].shape[0]
    count = len(normed)
    width = D // GROUP
    cut = EARLY_COLS if split else PACKED
    rest = PACKED - cut + LANES + width
    total = cut if split else PACKED + rest

    def body(place_ref, *refs):
        grad_packed_ref, mixed_ref, small_ref, gain_ref, distance_ref, hits_ref = refs[
            count + GROUP : count + GROUP + 6
        ]
        outs = refs[count + GROUP + 6 : -3]
        in_ref, out_ref, flat_ref = refs[-3:]
        total_in, total_out = dense_products(
            refs[:count], refs[count : count + GROUP], grad_packed_ref, mixed_ref
        )
        in_ref[...] = total_in
        out_ref[...] = total_out
        row = lax.broadcasted_iota(jnp.int32, (8, D), 0)
        gains = jnp.where(
            row == 0, gain_ref[...], jnp.where(row == 1, small_ref[16:24, :], 0.0)
        )
        features = jnp.concatenate(
            [small_ref[:16, :], gains, jnp.zeros((LANES - 24, D), f32)], 0
        )
        flat_ref[...] = features.T
        by_bucket = dot(hits_ref[...], distance_ref[...], 1, 1, lax.Precision.HIGHEST)
        head = lax.broadcasted_iota(jnp.int32, (8, LANES), 0)
        lane = lax.broadcasted_iota(jnp.int32, (8, LANES), 1)
        mine = jnp.where((lane == 64 + head * GROUP + place_ref[0]) & (head < OWN), 1.0, 0.0)
        buckets = dot(by_bucket, mine, 1, 0, lax.Precision.HIGHEST)
        for index in range(BUCKETS):
            at = index * share
            flat_ref[at : at + 1, :] = flat_ref[at : at + 1, :] + buckets[index : index + 1, :]
        for side, d in enumerate((place_ref[1], 1 - place_ref[1])):
            for e in range(experts):
                for c in range(GROUP):
                    at = ((e * GROUP + c) * pairs + d) * share
                    span = pl.ds(pl.multiple_of(at, share), share)
                    to = slice(c * share, (c + 1) * share)
                    target = outs[side]
                    target[e, to, :cut] = in_ref[span, :cut].astype(target.dtype)
                    out_span = pl.ds(pl.multiple_of((e * pairs + d) * share, share), share)
                    outer = out_ref[out_span, c * width : (c + 1) * width]
                    if split:
                        more = PACKED - cut
                        outs[2][e, side, to, :more] = in_ref[span, cut:].astype(bf16)
                        outs[2][e, side, to, more : more + LANES] = flat_ref[span, :].astype(bf16)
                        outs[2][e, side, to, more + LANES :] = outer.astype(bf16)
                    else:
                        target[e, to, PACKED : PACKED + LANES] = flat_ref[span, :].astype(
                            target.dtype
                        )
                        target[e, to, PACKED + LANES :] = outer.astype(target.dtype)

    outs = [
        shape((experts, GROUP * share, total), f32),
        shape((experts, GROUP * share, total), bf16),
    ]
    if split:
        outs.append(shape((experts, pairs, GROUP * share, rest), bf16))
    return whole_call(
        body,
        outs,
        [place, *normed, *upstream, grad_packed, mixed, small, gain_a, by_distance, hits],
        smem=1,
        scratch=[
            pltpu.VMEM((D, PACKED), f32),
            pltpu.VMEM((OWN_COLS, D), f32),
            pltpu.VMEM((D, LANES), f32),
        ],
        flops=2 * GROUP * rows * D * (PACKED + OWN_COLS),
        after=after,
        streamed=True,
        limit=32,
        name="dense_pack",
    )


def finish_dense(share, inner, outer):
    width = D // GROUP

    def body(*refs):
        in_ref, out_ref, small_ref = refs[1 + LAYERS :]
        for layer in range(LAYERS):
            got, rows_out = refs[0], refs[1 + layer]
            for c in range(GROUP):
                for which in range(3):
                    for head in range(OWN):
                        source = which * OWN_COLS + head * HEAD_DIM
                        target = which * D + (head * GROUP + c) * HEAD_DIM
                        in_ref[layer, :, target : target + HEAD_DIM] = got[
                            c, layer, :, source : source + HEAD_DIM
                        ].astype(f32)
                out_ref[layer, :, c * width : (c + 1) * width] = rows_out[
                    c * share : (c + 1) * share, :
                ]
            total = got[0, layer, :, PACKED:].astype(f32)
            for c in range(1, GROUP):
                total = total + got[c, layer, :, PACKED:].astype(f32)
            small_ref[layer] = total

    return whole_call(
        body,
        (
            shape((LAYERS, share, 3 * D), f32),
            shape((LAYERS, share, D), f32),
            shape((LAYERS, share, LANES), f32),
        ),
        [inner, *outer],
        name="finish_dense",
    )


def stacked(refs):
    return refs[0][...] if len(refs) == 1 else jnp.concatenate([ref[...] for ref in refs], 0)


def store_blocks(refs, rows):
    count = rows.shape[0] // len(refs)
    for index, ref in enumerate(refs):
        ref[...] = rows[index * count : (index + 1) * count, :].astype(ref.dtype)


def block_shapes(blocks, slots, width=D):
    return [shape((slots // blocks, width), bf16)] * blocks


def dispatch_grid(dest_rows, slots, tokens):
    place = lax.broadcasted_iota(jnp.int32, (slots, tokens), 0)
    first = place == dest_rows[0:1, :]
    second = place == dest_rows[1:2, :]
    return first, second


def one_hot(flags):
    return jnp.where(flags, 1.0, 0.0).astype(bf16)


def collect_grid(meta, slots):
    tokens = meta.shape[0]
    place = lax.broadcasted_iota(jnp.int32, (tokens, slots), 1)
    first = place == meta[:, 0:1].astype(jnp.int32)
    second = place == meta[:, 1:2].astype(jnp.int32)
    return first, second


def scatter_grads(upstream, meta, dest_rows, slots):
    tokens = upstream.shape[0]
    first, second = dispatch_grid(dest_rows, slots, tokens)
    return (
        dot(one_hot(first), (meta[:, 2:3] * upstream).astype(bf16), 1, 0)
        + dot(one_hot(second), (meta[:, 3:4] * upstream).astype(bf16), 1, 0)
    ).astype(bf16)


def slot_rows(idst, capacity, own):
    tokens = idst.shape[1]
    down = lax.broadcasted_iota(jnp.int32, (tokens, tokens), 0)
    across = lax.broadcasted_iota(jnp.int32, (tokens, tokens), 1)
    sub = lax.broadcasted_iota(jnp.int32, (16, tokens), 0)
    row0 = sub == idst[0:1, :]
    row1 = sub == idst[1:2, :]
    counts = dot(one_hot(row0 | row1), one_hot(down < across), 1, 0)
    found = []
    for index, row in enumerate((row0, row1)):
        slot = jnp.sum(jnp.where(row, counts, 0.0), 0, keepdims=True).astype(jnp.int32)
        found.append((idst[index : index + 1, :] ^ own) * capacity + slot)
    return jnp.where(lax.broadcasted_iota(jnp.int32, (8, tokens), 0) == 0, found[0], found[1])


def send_grads(experts, capacity, idst, grad, after):
    tokens = grad.shape[0]
    slots = experts * capacity

    def body(idst_ref, grad_ref, out_ref):
        first, second = dispatch_grid(slot_rows(idst_ref[...], capacity, 0), slots, tokens)
        out_ref[...] = dot(one_hot(first | second), grad_ref[...], 1, 0).astype(bf16)

    (out,) = whole_call(
        body, [shape((slots, D), bf16)], [idst, grad], after=after, name="send_grads"
    )
    return out


def apply_gates(experts, blocks, place, rows, gates):
    slots = gates.shape[0]
    capacity = slots // experts
    if blocks == 1:
        order = jnp.arange(experts) ^ place[2]
        rows = rows.reshape(experts, capacity, D)[order].reshape(slots, D)
        gates = gates.reshape(experts, capacity, LANES)[order].reshape(slots, LANES)

    def body(place_ref, rows_ref, gates_ref, *outs):
        for index, out_ref in enumerate(outs):
            span = pl.ds(0, slots)
            if blocks > 1:
                source = pl.multiple_of((index ^ place_ref[2]) * capacity, capacity)
                span = pl.ds(source, capacity)
            out_ref[...] = (gates_ref[span, 0:1] * rows_ref[span, :].astype(f32)).astype(bf16)

    return whole_call(
        body, block_shapes(blocks, slots), [place, rows, gates], smem=1, streamed=True,
        name="apply_gates",
    )


def route_body(layer, experts, capacity, last, blocks, place_ref, *refs):
    top = 32 * layer
    own = place_ref[2]
    x_ref, keep_ref, recv_ref, far_ref, feature_ref, ids_ref, idst_ref = refs[:7]
    middle_ref, soft_ref, meta_ref, dest_ref = refs[7:11]
    rows_refs = refs[11 : 11 + blocks]
    tokens = x_ref.shape[0]
    slots = experts * capacity
    middle = (
        x_ref[...].astype(f32)
        + keep_ref[:tokens, :]
        + recv_ref[:tokens, :].astype(f32)
        + far_ref[...].astype(f32)
    )
    middle_ref[...] = middle
    normed = middle * rms_scale(middle) * feature_ref[top + 17 : top + 18, :]
    lane = lax.broadcasted_iota(jnp.int32, (tokens, LANES), 1)
    logits = dot(normed, feature_ref[...], 1, 1, lax.Precision.HIGHEST)
    logits = jnp.where((lane >= top) & (lane < top + experts), logits, NEGATIVE)
    power = jnp.exp(logits - jnp.max(logits, -1, keepdims=True))
    soft = power / jnp.sum(power, -1, keepdims=True)
    soft_ref[...] = soft
    ids = ids_ref[...]
    hit0 = lane == ids[:, 0:1] + top
    hit1 = lane == ids[:, 1:2] + top
    picked0 = jnp.sum(jnp.where(hit0, soft, 0.0), -1, keepdims=True)
    picked1 = jnp.sum(jnp.where(hit1, soft, 0.0), -1, keepdims=True)
    pick_total = picked0 + picked1
    down = lax.broadcasted_iota(jnp.int32, (tokens, tokens), 0)
    across = lax.broadcasted_iota(jnp.int32, (tokens, tokens), 1)
    counts = dot(one_hot(across < down), one_hot(hit0 | hit1), 1, 0)
    dest0 = (ids[:, 0:1] ^ own).astype(f32) * capacity + jnp.sum(
        jnp.where(hit0, counts, 0.0), -1, keepdims=True
    )
    dest1 = (ids[:, 1:2] ^ own).astype(f32) * capacity + jnp.sum(
        jnp.where(hit1, counts, 0.0), -1, keepdims=True
    )
    fields = (dest0, dest1, picked0 / pick_total, picked1 / pick_total, pick_total)
    meta = jnp.zeros((tokens, LANES), f32)
    for index, field in enumerate(fields):
        meta = jnp.where(lane == index, field, meta)
    meta_ref[...] = meta
    dest_rows = slot_rows(idst_ref[...], capacity, own)
    dest_ref[...] = dest_rows
    first, second = dispatch_grid(dest_rows, slots, tokens)
    store_blocks(rows_refs, dot(one_hot(first | second), normed.astype(bf16), 1, 0))
    if last:
        total = None
        place = lax.broadcasted_iota(jnp.int32, (slots, tokens), 0)
        for index in range(2):
            slot = dest_rows[index : index + 1, :] - (idst_ref[index : index + 1, :] ^ own) * capacity
            flags = place == slot + idst_ref[index : index + 1, :] * capacity
            gate = meta[:, 2 + index : 3 + index]
            spread = jnp.zeros((tokens, LANES), f32)
            for term in range(3):
                piece = gate.astype(bf16).astype(f32)
                spread = jnp.where(lane == term, piece, spread)
                gate = gate - piece
            got = dot(one_hot(flags), spread.astype(bf16), 1, 0)
            total = got if total is None else total + got
        refs[-1][...] = jnp.broadcast_to(jnp.sum(total, -1, keepdims=True), total.shape)


def route(
    layer, experts, capacity, blocks, place, x, keep, recv, far, feature, ids, idst, last, after=()
):
    tokens = x.shape[0]
    slots = experts * capacity
    outs = [
        shape((tokens, D), f32),
        shape((tokens, LANES), f32),
        shape((tokens, LANES), f32),
        shape((8, tokens), jnp.int32),
    ] + block_shapes(blocks, slots)
    if last:
        outs.append(shape((slots, LANES), f32))

    def body(*refs):
        route_body(layer, experts, capacity, last, blocks, *refs)

    return whole_call(
        body, outs, [place, x, keep, recv, far, feature, ids, idst], smem=1,
        flops=2 * slots * tokens * D, after=after, name="route",
    )


def combine(middle, back, meta, feature=None):
    tokens = middle.shape[0]
    count = len(back)
    last = feature is None
    args = [middle, meta, *back]
    outs = [shape((tokens, D), bf16 if last else f32)]
    if not last:
        args.append(feature)
        outs.append(shape((tokens, D), bf16))

    def body(middle_ref, meta_ref, *refs):
        meta = meta_ref[...]
        rows = stacked(refs[:count])
        first, second = collect_grid(meta, rows.shape[0])
        x = (
            middle_ref[...]
            + meta[:, 2:3] * dot(one_hot(first), rows, 1, 0)
            + meta[:, 3:4] * dot(one_hot(second), rows, 1, 0)
        )
        if last:
            refs[-1][...] = x.astype(bf16)
        else:
            refs[-2][...] = x
            refs[-1][...] = (x * rms_scale(x) * refs[count][48:49, :]).astype(bf16)

    return whole_call(
        body, outs, args, flops=4 * tokens * D * count * back[0].shape[0], name="combine"
    )


def expert_token_back_body(
    layer, back_refs, came_refs, g_ref, middle_ref, soft_ref, meta_ref, ids_ref, feature_ref,
    dmiddle_ref, dattn_ref, small_ref,
):
    back, came = stacked(back_refs), stacked(came_refs)
    top = 32 * layer
    gain_row = feature_ref[top + 17 : top + 18, :]
    meta = meta_ref[...]
    g = g_ref[...].astype(f32)
    slots = back.shape[0]
    first, second = collect_grid(meta, slots)
    grad_gate0 = jnp.sum(g * dot(one_hot(first), back, 1, 0), -1, keepdims=True)
    grad_gate1 = jnp.sum(g * dot(one_hot(second), back, 1, 0), -1, keepdims=True)
    grad_normed = dot(one_hot(first | second), came, 1, 0)
    gap = (grad_gate0 - grad_gate1) / meta[:, 4:5]
    ids = ids_ref[...]
    lane = lax.broadcasted_iota(jnp.int32, meta.shape, 1)
    grad_soft = jnp.where(lane == ids[:, 0:1] + top, meta[:, 3:4] * gap, 0.0) + jnp.where(
        lane == ids[:, 1:2] + top, -meta[:, 2:3] * gap, 0.0
    )
    soft = soft_ref[...]
    grad_logits = soft * (grad_soft - jnp.sum(soft * grad_soft, -1, keepdims=True))
    middle = middle_ref[...]
    normed = middle * rms_scale(middle) * gain_row
    grad_router = dot(grad_logits.T, normed, 1, 0, lax.Precision.HIGHEST)
    grad_normed = grad_normed + dot(
        grad_logits, feature_ref[...], 1, 0, lax.Precision.HIGHEST
    )
    grad_branch, grad_gain = norm_back(middle, gain_row, grad_normed)
    dmiddle = g + grad_branch
    dmiddle_ref[...] = dmiddle
    dattn_ref[...] = dmiddle.astype(bf16)
    small_ref[:16, :] = grad_router[top : top + 16, :]
    small_ref[16:24, :] = jnp.broadcast_to(grad_gain, (8, D))


def expert_token_back(layer, back, came, g, middle, soft, meta, ids, feature, after=()):
    tokens = middle.shape[0]

    def body(*refs):
        count = len(back)
        expert_token_back_body(layer, refs[:count], refs[count : 2 * count], *refs[2 * count :])

    return whole_call(
        body,
        (shape((tokens, D), f32), shape((tokens, D), bf16), shape((24, D), f32)),
        [*back, *came, g, middle, soft, meta, ids, feature],
        after=after,
        flops=6 * tokens * D * len(back) * back[0].shape[0],
        streamed=True,
        limit=32,
        name="expert_token_back",
    )


def attention_token_back_body(layer, *refs):
    if layer == 0:
        x_ref, dmiddle_ref, keep_ref, recv_ref, far_ref, feature_ref, out_ref = refs
    else:
        (x_ref, dmiddle_ref, keep_ref, recv_ref, far_ref, feature_ref, meta_ref, dest_ref,
         out_ref, *sent_refs) = refs
    tokens = x_ref.shape[0]
    grad_normed = (
        keep_ref[:tokens, :] + recv_ref[:tokens, :].astype(f32) + far_ref[...].astype(f32)
    )
    gain_row = feature_ref[32 * layer + 16 : 32 * layer + 17, :]
    grad_branch, _ = norm_back(x_ref[...].astype(f32), gain_row, grad_normed)
    g = dmiddle_ref[...] + grad_branch
    out_ref[...] = g
    if layer > 0:
        slots = len(sent_refs) * sent_refs[0].shape[0]
        store_blocks(sent_refs, scatter_grads(g, meta_ref[...], dest_ref[...], slots))


def attention_token_back(
    layer, x, dmiddle, keep, recv, far, feature, meta=None, dest=None, blocks=1, slots=0, after=()
):
    tokens = x.shape[0]
    outs = [shape((tokens, D), f32)]
    args = [x, dmiddle, keep, recv, far, feature]
    if meta is not None:
        outs += block_shapes(blocks, slots)
        args += [meta, dest]

    def body(*refs):
        attention_token_back_body(layer, *refs)

    return whole_call(
        body, outs, args, flops=4 * tokens * D * slots, after=after, name="attention_token_back"
    )


def gelu_parts(gate):
    inner = math.sqrt(2.0 / math.pi) * (gate + 0.044715 * gate * gate * gate)
    return jnp.tanh(inner)


def weight_specs(layer, tile):
    return [
        pl.BlockSpec((1, 1, D, tile), lambda s: (layer, 0, 0, s)),
        pl.BlockSpec((1, 1, D, tile), lambda s: (layer, 0, 0, FF // tile + s)),
        pl.BlockSpec((1, 1, D, tile), lambda s: (layer, 0, 0, s)),
    ]


def block_specs(blocks):
    return [pl.BlockSpec(b.shape, lambda s: (0, 0)) for b in blocks]


def expert_call(body, steps, outs, out_specs, args, in_specs, scratch, limit, after, name):
    used = len(args)

    def ordered(*refs):
        body(*refs[:used], *refs[used + len(after) :])

    count = ROWS_HINT
    return pl.pallas_call(
        ordered,
        grid=(steps,),
        out_shape=tuple(outs),
        in_specs=list(in_specs) + [pl.BlockSpec(memory_space=pltpu.HBM)] * len(after),
        out_specs=tuple(out_specs),
        scratch_shapes=list(scratch),
        compiler_params=pltpu.CompilerParams(vmem_limit_bytes=limit * MIB),
        cost_estimate=pl.CostEstimate(
            flops=6 * count * D * FF, bytes_accessed=6 * D * FF, transcendentals=count * FF
        ),
        name=name,
    )(*args, *[far_away(a) for a in after])


def expert_forward(layer, blocks, w_in, w_out, after=()):
    number = len(blocks)
    count = number * blocks[0].shape[0]
    steps = FF // WIDE_TILE

    def body(*refs):
        wg_ref, wu_ref, wo_ref = refs[number : number + 3]
        produced_refs = refs[number + 3 : 2 * number + 3]
        acts_ref, rows_ref, total_ref = refs[2 * number + 3 :]
        step = pl.program_id(0)

        @pl.when(step == 0)
        def _():
            rows_ref[...] = stacked(refs[:number])

        rows = rows_ref[...]
        gate = dot(rows, wg_ref[0, 0], 1, 0)
        up = dot(rows, wu_ref[0, 0], 1, 0)
        acts_ref[0] = gate.astype(bf16)
        acts_ref[1] = up.astype(bf16)
        hidden = (0.5 * gate * (1.0 + gelu_parts(gate)) * up).astype(bf16)
        out = dot(hidden, wo_ref[0, 0], 1, 1)

        @pl.when(step == 0)
        def _():
            total_ref[...] = out

        @pl.when(step == steps - 1)
        def _():
            store_blocks(produced_refs, total_ref[...] + out)

    *produced, acts = expert_call(
        body,
        steps,
        [shape(b.shape, bf16) for b in blocks] + [pltpu.HBM((2, count, FF), bf16)],
        block_specs(blocks) + [pl.BlockSpec((2, count, WIDE_TILE), lambda s: (0, 0, s))],
        [*blocks, far_away(w_in), far_away(w_in), far_away(w_out)],
        block_specs(blocks) + weight_specs(layer, WIDE_TILE),
        [pltpu.VMEM((count, D), bf16), pltpu.VMEM((count, D), f32)],
        56,
        after,
        "expert_forward",
    )
    return produced, acts


def expert_backward(layer, blocks, out_blocks, acts, w_in, w_out, after=()):
    number = len(blocks)
    count = number * blocks[0].shape[0]
    steps = FF // WIDE_TILE
    outs = block_shapes(out_blocks, count)

    def body(*refs):
        acts_refs = refs[number : number + len(acts)]
        wg_ref, wu_ref, wo_ref, *rest = refs[number + len(acts) :]
        drows_refs = rest[:out_blocks]
        parts_ref, grad_ref, total_ref = rest[out_blocks:]
        step = pl.program_id(0)

        @pl.when(step == 0)
        def _():
            grad_ref[...] = stacked(refs[:number])

        grad_hidden = dot(grad_ref[...], wo_ref[0, 0], 1, 0)
        gate = jnp.concatenate([ref[0] for ref in acts_refs], 0).astype(f32)
        up = jnp.concatenate([ref[1] for ref in acts_refs], 0).astype(f32)
        curve = gelu_parts(gate)
        value = 0.5 * gate * (1.0 + curve)
        slope = 0.5 * (1.0 + curve) + 0.5 * gate * (1.0 - curve * curve) * math.sqrt(
            2.0 / math.pi
        ) * (1.0 + 3.0 * 0.044715 * gate * gate)
        grad_gate = (grad_hidden * up * slope).astype(bf16)
        grad_up = (grad_hidden * value).astype(bf16)
        parts_ref[0] = grad_gate
        parts_ref[1] = grad_up
        parts_ref[2] = (value * up).astype(bf16)
        out = dot(grad_gate, wg_ref[0, 0], 1, 1) + dot(grad_up, wu_ref[0, 0], 1, 1)

        @pl.when(step == 0)
        def _():
            total_ref[...] = out

        @pl.when(step == steps - 1)
        def _():
            store_blocks(drows_refs, total_ref[...] + out)

    *drows, parts = expert_call(
        body,
        steps,
        outs + [pltpu.HBM((3, count, FF), bf16)],
        block_specs(outs) + [pl.BlockSpec((3, count, WIDE_TILE), lambda s: (0, 0, s))],
        [*blocks, *[far_away(a) for a in acts], far_away(w_in), far_away(w_in), far_away(w_out)],
        block_specs(blocks)
        + [pl.BlockSpec((2, a.shape[1], WIDE_TILE), lambda s: (0, 0, s)) for a in acts]
        + weight_specs(layer, WIDE_TILE),
        [pltpu.VMEM((count, D), bf16), pltpu.VMEM((count, D), f32)],
        58,
        after,
        "expert_backward",
    )
    return drows, parts


def expert_grads(shares, rows, grads, parts, after=()):
    count = len(rows) * rows[0].shape[0]
    tall = D // shares
    first = len(rows)
    second = first + len(grads)
    third = second + len(parts)

    def body(*refs):
        out_ref, rows_t, grad_t = refs[third:]

        @pl.when(pl.program_id(0) == 0)
        def _():
            rows_t[...] = stacked(refs[:first]).T
            grad_t[...] = stacked(refs[first:second]).T

        for which in range(3):
            left = rows_t if which < 2 else grad_t
            right = [ref[which] for ref in refs[second:third]]
            right = right[0] if len(right) == 1 else jnp.concatenate(right, 0)
            got = dot(left[...], right, 1, 0).astype(bf16)
            for share in range(shares):
                out_ref[share, which] = got[share * tall : (share + 1) * tall, :]

    (out,) = expert_call(
        body,
        FF_STEPS,
        [pltpu.HBM((shares, 3, tall, FF), bf16)],
        [pl.BlockSpec((shares, 3, tall, FF_TILE), lambda s: (0, 0, 0, s))],
        [*rows, *grads, *[far_away(p) for p in parts]],
        block_specs(rows)
        + block_specs(grads)
        + [pl.BlockSpec((3, p.shape[1], FF_TILE), lambda s: (0, 0, s)) for p in parts],
        [pltpu.VMEM((D, count), bf16), pltpu.VMEM((D, count), bf16)],
        32,
        after,
        "expert_grads",
    )
    return out


def place_expert_grads(layer, summed, before=None, after=()):
    tall = summed.shape[1]
    outs = (
        pltpu.HBM((LAYERS, 1, tall, 2 * FF), f32),
        pltpu.HBM((LAYERS, 1, tall, FF), f32),
    )
    held = [] if before is None else list(before)

    def body(part_ref, out_part_ref, *refs):
        in_ref, out_ref = refs[-2:]
        in_ref[0, 0] = part_ref[0].astype(f32)
        out_ref[0, 0] = out_part_ref[0].astype(f32)

    return pl.pallas_call(
        body,
        grid=(2,),
        out_shape=outs,
        in_specs=[
            pl.BlockSpec((1, tall, FF), lambda s: (s, 0, 0)),
            pl.BlockSpec((1, tall, FF), lambda s: (2, 0, 0)),
        ]
        + [pl.BlockSpec(memory_space=pl.ANY)] * (len(held) + len(after)),
        out_specs=(
            pl.BlockSpec((1, 1, tall, FF), lambda s: (layer, 0, 0, s)),
            pl.BlockSpec((1, 1, tall, FF), lambda s: (layer, 0, 0, 0)),
        ),
        input_output_aliases={2: 0, 3: 1} if held else {},
        compiler_params=pltpu.CompilerParams(vmem_limit_bytes=32 * MIB),
        name="place_expert_grads",
    )(far_away(summed), far_away(summed), *[far_away(h) for h in [*held, *after]])


TWIN = [(i, i ^ 1) for i in range(GROUP)]
ACROSS = [(i, i ^ 2) for i in range(GROUP)]
FLIP = [(0, 1), (1, 0)]


def share_pieces(piece):
    across = lax.ppermute(piece, "context", ACROSS)
    twin = lax.ppermute(piece, "context", TWIN)
    return [piece, twin, across, lax.ppermute(across, "context", TWIN)]


def sum_pieces(keep, send):
    rows = keep.shape[0] // 2
    recv = lax.ppermute(send, "context", TWIN)
    other = (keep[rows:] + recv[rows:].astype(f32)).astype(bf16)
    return keep, recv, lax.ppermute(other, "context", ACROSS)


def sum_zone(zone):
    return jnp.sum(zone.astype(f32), 0)


def dense_sum(
    experts, pairs, share, table_share, place, grad_w_in, grad_w_out, small, gain_a, by_distance,
    hits,
):
    by_bucket = jnp.dot(hits, by_distance[:OWN].T, precision=lax.Precision.HIGHEST)
    buckets = jnp.where(
        jnp.arange(GROUP)[None, None, :] == place[0], by_bucket[:, :, None], 0.0
    ).reshape(experts, GROUP, pairs, 1, table_share)
    features = jnp.concatenate([small[:16], gain_a[:1], small[16:17]], 0).T
    features = features.reshape(experts, GROUP, pairs, share, 18)
    flat = jnp.zeros((experts, GROUP, pairs, share, LANES), f32)
    flat = flat.at[..., :18].set(features).at[..., :1, 64 : 64 + table_share].set(buckets)
    pack = jnp.concatenate(
        [grad_w_in.reshape(experts, GROUP, pairs, share, PACKED), flat.astype(bf16)], -1
    ).transpose(0, 2, 1, 3, 4)
    pack = pack.reshape(experts * pairs, GROUP * share, PACKED + LANES)
    mine = lax.psum_scatter(pack, ("experts", "dp"), scatter_dimension=0, tiled=False)
    inner = lax.all_to_all(
        mine.reshape(GROUP, share, PACKED + LANES), "context", split_axis=0, concat_axis=0
    ).astype(f32)
    g_in = inner[..., :PACKED].reshape(GROUP, share, 3, OWN, HEAD_DIM)
    g_in = g_in.transpose(1, 2, 3, 0, 4).reshape(share, 3 * D)
    placed_rows = jnp.where(
        jnp.arange(GROUP)[None, :, None, None] == place[0],
        grad_w_out.reshape(OWN, 1, HEAD_DIM, D),
        jnp.zeros((), bf16),
    ).reshape(D, D)
    g_out = lax.psum_scatter(placed_rows, ALL, scatter_dimension=0, tiled=True).astype(f32)
    return g_in, g_out, jnp.sum(inner[..., PACKED:], 0)


def exchange(rows):
    return lax.all_to_all(rows, "experts", split_axis=0, concat_axis=0, tiled=True)


def swap(blocks, experts):
    split = blocks if len(blocks) > 1 else jnp.split(blocks[0], experts)
    moved = [
        part if k == 0 else lax.ppermute(part, "experts", [(i, i ^ k) for i in range(experts)])
        for k, part in enumerate(split)
    ]
    return moved if len(blocks) > 1 else [jnp.concatenate(moved)]


def on_device(
    tokens, doc_starts, expert_ids, attn_in, attn_out, router, gains, rel_table,
    expert_in, expert_out, out_grad,
):
    experts = lax.axis_size("experts")
    pairs = lax.axis_size("dp")
    share = attn_in.shape[1]
    table_share = rel_table.shape[1]
    direct = share * pairs == HEAD_DIM and experts * GROUP == HEADS and pairs == 2
    place = jnp.stack(
        [lax.axis_index("context"), lax.axis_index("dp"), lax.axis_index("experts")]
    ).astype(jnp.int32)
    start_tokens = tokens[0]
    ids = expert_ids[0]
    idst = ids.T
    rows = start_tokens.shape[0]
    capacity = (10 * rows + 4 * experts - 1) // (4 * experts)
    slots = experts * capacity
    blocks = experts if experts == 4 and capacity % 16 == 0 else 1
    fine = [(0, 1), (2,), (3,)] if blocks == 4 else [(0,)]
    coarse = [(0, 1), (2, 3)] if blocks == 4 else [(0,)]
    grad_in = out_grad[0]
    hits = jnp.asarray(bucket_hits())

    packets = prepare(direct, attn_in, attn_out, router, gains, rel_table)

    def spread(packet):
        return lax.all_to_all(packet, "context", split_axis=0, concat_axis=0)

    def gather(part):
        return lax.all_gather(part, ("experts", "dp"), axis=0, tiled=False).reshape(
            experts, pairs, *part.shape
        )

    if direct:
        packet = spread(packets[0])
        top = PACKED + LANES

        def together(columns, rows_out):
            part = jnp.concatenate([columns, rows_out], -1)
            return lax.all_gather(part, ("experts", "dp"), axis=0, tiled=False)

        first = together(packet[..., :top], packets[1])
        w_in0, w_out0, feature, bias = unpack(place, hits, experts, pairs, 0, first)
        second = [together(packet[..., top:], packets[2])]
        w_in1, w_out1 = unpack(place, hits, experts, pairs, 1, second[0])
        w_in, w_out = [w_in0, w_in1], [w_out0, w_out1]
    else:
        second = []
        w_in, w_out = [], []
        for layer in range(LAYERS):
            at = layer * (PACKED + LANES)
            part = spread(packets[0])[..., at : at + PACKED + LANES]
            got = gather(part).transpose(0, 2, 1, 3, 4)
            w_in.append(got[..., :PACKED].reshape(D, PACKED))
            if layer == 0:
                small_all = got[..., PACKED : PACKED + LANES]
            full = lax.all_gather(attn_out[layer], ALL, axis=0, tiled=True)
            mine = lax.dynamic_index_in_dim(
                full.reshape(OWN, GROUP, HEAD_DIM, D), place[0], 1, keepdims=False
            )
            w_out.append(mine.reshape(OWN_COLS, GROUP, D // GROUP).transpose(1, 0, 2))
        feature = small_all.reshape(D, LANES).astype(f32).T
        bias_rows = []
        for layer in range(LAYERS):
            at = 64 + 32 * layer
            table = small_all[:, :, :, 0, at : at + table_share].reshape(BUCKETS, OWN, GROUP)
            table = lax.dynamic_index_in_dim(table, place[0], 2, keepdims=False).astype(f32)
            row = jnp.dot((table - table[-1:]).T, hits, precision=lax.Precision.HIGHEST)
            bias_rows.append(jnp.pad(row, ((0, 8 - OWN), (0, 0))))
        bias = jnp.stack(bias_rows)
    places = jnp.arange(GROUP * rows, dtype=jnp.int32)
    starts = doc_starts[0]
    low = jnp.max(
        jnp.where(starts[:, None] <= places[None, :], starts[:, None], 0), 0, keepdims=True
    )

    pieces = share_pieces(start_tokens)
    x = start_tokens
    kept = []
    for layer in range(LAYERS):
        packed, log_total, mixed, keep, send, *normed_all = attention_forward(
            layer, place, pieces, w_in[layer], feature, bias, low, w_out[layer]
        )
        normed_rows = normed_all if layer == 0 else pieces
        last = layer == LAYERS - 1
        if last:
            send = hold(send, [arrived_grad])
        keep, recv, far = sum_pieces(keep, send)
        middle, soft, meta, dest, *sent = route(
            layer, experts, capacity, blocks, place, x, keep, recv, far, feature, ids, idst, last,
        )
        arrived = swap(sent[:blocks], experts)
        if last:
            gates = exchange(sent[blocks])
        produced, acts, drows, parts = [], [], [], []
        order = second if layer == 0 else []
        for chunk in coarse if last else fine:
            done, kept_acts = expert_forward(
                layer, [arrived[k] for k in chunk], expert_in, expert_out, after=order
            )
            produced += done
            acts.append(kept_acts)
            order = done[:1]
            if last:
                if not drows:
                    arrived_grad = apply_gates(experts, blocks, place, arrived_grad, gates)
                done, some = expert_backward(
                    layer, [arrived_grad[k] for k in chunk], len(chunk), acts[-1:], expert_in,
                    expert_out,
                )
                drows += done
                parts.append(some)
                order = done[:1]
        back = swap(produced, experts)
        kept.append(
            (x, normed_rows, packed, log_total, mixed, middle, soft, meta, dest, arrived, acts, back)
        )
        if last:
            (result,) = combine(middle, back, meta)
        else:
            x, normed = combine(middle, back, meta, feature)
            ungated = send_grads(experts, capacity, idst, grad_in, [x])
            arrived_grad = exchange(ungated)
            pieces = share_pieces(hold(normed, [ungated]))

    g = grad_in
    inner, outer, expert_totals = [], [], []
    other = None
    placed_grads = None
    for layer in range(LAYERS - 1, -1, -1):
        (x, normed_rows, packed, log_total, mixed, middle, soft, meta, dest, arrived, acts,
         back) = kept[layer]
        if layer < LAYERS - 1:
            drows, parts = [], []
            for index, chunk in enumerate(coarse):
                some_acts = acts[:1] if index == 0 else acts[1:]
                done, some = expert_backward(
                    layer, [arrived_grad[k] for k in chunk], len(chunk), some_acts, expert_in,
                    expert_out, after=drows[-1:],
                )
                drows += done
                parts.append(some)
        came = swap(drows, experts)
        early = [] if other is None else [other]
        weight_grads = expert_grads(
            GROUP * pairs, arrived, arrived_grad, parts, after=(back if layer else []) + early
        )
        weight_grads = hold(weight_grads, came)
        total = lax.psum_scatter(
            weight_grads, ("context", "dp"), scatter_dimension=0, tiled=False
        )
        dmiddle, dattn, small_b = expert_token_back(
            layer, back, came, g, middle, soft, meta, ids, feature, after=[weight_grads]
        )
        zones = []
        if direct and other is not None:
            ours = hold(keep_dense, [dattn]) + other.astype(f32)
            zones = [exchange(ours.astype(bf16))]
        expert_totals.append(total)
        grad_pieces = share_pieces(dattn)
        grad_packed, keep, send, by_distance, gain_a = attention_backward(
            layer, place, grad_pieces, w_in[layer], feature, bias, low, w_out[layer], packed,
            log_total, normed_rows,
        )
        keep, recv, far = sum_pieces(keep, send)
        if layer > 0:
            below = kept[layer - 1]
            g, *sent = attention_token_back(
                layer, x, dmiddle, keep, recv, far, feature, below[7], below[8], blocks, slots
            )
            arrived_grad = swap(sent, experts)
        else:
            placed_grads = place_expert_grads(layer + 1, expert_totals[0])
            (g,) = attention_token_back(
                layer, x, dmiddle, keep, recv, far, feature, after=[placed_grads[0]]
            )
        if direct:
            keep_dense, send_dense, *rest = dense_pack(
                experts, pairs, share, place, normed_rows, grad_pieces, grad_packed, mixed,
                small_b, gain_a, by_distance, hits, split=layer == 0, after=zones,
            )
            other = lax.ppermute(send_dense, "dp", FLIP)
            if layer == 0:
                (zone,) = zones
                total = sum_zone(zone)
                flats = [total[:, : PACKED + LANES].astype(bf16)]
                outer.append(total[:, PACKED + LANES :])
                rest = sum_zone(exchange(rest[0]))
                theirs = lax.ppermute(rest[1].astype(bf16), "dp", FLIP)
                rest = rest[0] + theirs.astype(f32)
                ours = hold(keep_dense, [g, result, placed_grads[0]]) + other.astype(f32)
                total = sum_zone(exchange(ours.astype(bf16)))
                more = PACKED + LANES - EARLY_COLS
                flats.insert(0, jnp.concatenate([total, rest[:, :more]], -1).astype(bf16))
                outer.append(rest[:, more:])
                flat = jnp.stack([flat.reshape(GROUP, share, -1) for flat in flats], 1)
                inner = spread(flat)
        else:
            grad_w_in, grad_w_out = dense_grads(normed_rows, grad_pieces, grad_packed, mixed)
            inner.append(
                dense_sum(
                    experts, pairs, share, table_share, place, grad_w_in, grad_w_out, small_b,
                    gain_a, by_distance, hits,
                )
            )
    expert_grads_all = place_expert_grads(0, expert_totals[1], placed_grads)
    if direct:
        grad_attn_in, grad_attn_out, small_grad = finish_dense(
            share, inner, outer[::-1]
        )
    else:
        grad_attn_in, grad_attn_out, small_grad = (
            jnp.stack([entry[k] for entry in inner[::-1]]) for k in range(3)
        )
    return (
        result[None],
        g[None],
        grad_attn_in,
        grad_attn_out,
        small_grad[..., :experts],
        small_grad[..., 16:18],
        small_grad[:, 0, 64 : 64 + table_share],
        *expert_grads_all,
    )


def solution(mesh):
    return jax.shard_map(
        on_device,
        mesh=mesh,
        in_specs=(
            P(("experts", "dp"), "context", None),
            P(("experts", "dp"), None),
            P(("experts", "dp"), "context", None),
            P(None, ("experts", "context", "dp"), None),
            P(None, ("experts", "context", "dp"), None),
            P(None, ("experts", "context", "dp"), None),
            P(None, ("experts", "context", "dp"), None),
            P(None, ("experts", "context", "dp")),
            P(None, "experts", None, None),
            P(None, "experts", None, None),
            P(("experts", "dp"), "context", None),
        ),
        out_specs=(
            P(("experts", "dp"), "context", None),
            P(("experts", "dp"), "context", None),
            P(None, ("experts", "context", "dp"), None),
            P(None, ("experts", "context", "dp"), None),
            P(None, ("experts", "context", "dp"), None),
            P(None, ("experts", "context", "dp"), None),
            P(None, ("experts", "context", "dp")),
            P(None, "experts", ("context", "dp"), None),
            P(None, "experts", ("context", "dp"), None),
        ),
        check_vma=False,
    )
```

```python
import math

import jax
import jax.numpy as jnp
import numpy as np
from jax import lax
from jax.experimental import pallas as pl
from jax.experimental.pallas import tpu as pltpu
from jax.sharding import PartitionSpec as P

D = 1024
HEADS = 16
HEAD_DIM = 64
FF = 2816
BUCKETS = 32
MAX_DISTANCE = 128
LAYERS = 2
EPSILON = 1e-06
NEGATIVE = -1e30
SCORE_SCALE = 0.125
ALL = ("experts", "context", "dp")
GROUP = 4
OWN = HEADS // GROUP
OWN_COLS = OWN * HEAD_DIM
PACKED = 3 * OWN_COLS
LANES = 128
REACH = 512
FF_TILE = 256
FF_STEPS = FF // FF_TILE
WIDE_TILE = FF // 2
EARLY_COLS = 512
ROWS_HINT = 320
MIB = 1 << 20

bf16 = jnp.bfloat16
f32 = jnp.float32


def bucket_bounds(bucket_count, far_reach):
    half_count = bucket_count // 2
    bounds = list(range(1, half_count + 1))
    for section_index in range(1, half_count):
        bounds.append(
            int(math.ceil(half_count * (far_reach / half_count) ** (section_index / half_count)))
        )
    return np.array(bounds, np.int32)


def bucket_hits():
    distance = np.arange(REACH)
    bucket = (distance[:, None] >= bucket_bounds(BUCKETS, MAX_DISTANCE)).sum(-1)
    return (np.arange(BUCKETS)[:, None] == bucket[None, :]).astype(np.float32)


def dot(a, b, ca, cb, precision=None):
    return lax.dot_general(
        a, b, (((ca,), (cb,)), ((), ())), precision=precision, preferred_element_type=f32
    )


def whole_call(
    body, out_shape, args, *, flops=0, limit=16, scratch=(), smem=0, name=None, after=(),
    streamed=False,
):
    specs = [pl.BlockSpec(memory_space=pltpu.SMEM)] * smem + [
        pl.BlockSpec(memory_space=pltpu.VMEM)
    ] * (len(args) - smem)
    outs = tuple(out_shape)
    moved = sum(a.size * a.dtype.itemsize for a in list(args) + list(outs))
    specs += [pl.BlockSpec(memory_space=pltpu.HBM)] * len(after)
    used = len(args)
    args = list(args) + [far_away(a) for a in after]

    def ordered(*refs):
        body(*refs[:used], *refs[used + len(after) :])

    if streamed:
        args = args[:smem] + [far_away(a) for a in args[smem:]]

        def full(a):
            return pl.BlockSpec(a.shape, lambda i: (0,) * len(a.shape))

        return pl.pallas_call(
            ordered,
            grid=(1,),
            out_shape=outs,
            in_specs=specs[:smem] + [full(a) for a in args[smem:used]] + specs[used:],
            out_specs=tuple(full(o) for o in outs),
            scratch_shapes=list(scratch),
            compiler_params=pltpu.CompilerParams(vmem_limit_bytes=limit * MIB),
            cost_estimate=pl.CostEstimate(
                flops=int(flops), bytes_accessed=int(moved), transcendentals=0
            ),
            name=name,
        )(*args)
    return pl.pallas_call(
        ordered,
        out_shape=outs,
        in_specs=specs,
        out_specs=tuple(pl.BlockSpec(memory_space=pltpu.VMEM) for _ in outs),
        scratch_shapes=list(scratch),
        compiler_params=pltpu.CompilerParams(vmem_limit_bytes=limit * MIB),
        cost_estimate=pl.CostEstimate(
            flops=int(flops), bytes_accessed=int(moved), transcendentals=0
        ),
        name=name,
    )(*args)


def far_away(x):
    return pltpu.with_memory_space_constraint(x, pltpu.HBM)


def hold(x, after):
    def body(*refs):
        pass

    return pl.pallas_call(
        body,
        out_shape=pltpu.HBM(x.shape, x.dtype),
        in_specs=[pl.BlockSpec(memory_space=pltpu.HBM)] * (1 + len(after)),
        out_specs=pl.BlockSpec(memory_space=pltpu.HBM),
        input_output_aliases={0: 0},
        compiler_params=pltpu.CompilerParams(vmem_limit_bytes=MIB),
        cost_estimate=pl.CostEstimate(flops=0, bytes_accessed=0, transcendentals=0),
        name="hold",
    )(far_away(x), *[far_away(a) for a in after])


def shape(dims, dtype):
    return jax.ShapeDtypeStruct(dims, dtype)


def rms_scale(inputs):
    return lax.rsqrt(jnp.mean(inputs * inputs, -1, keepdims=True) + EPSILON)


def norm_back(inputs, gain_row, upstream):
    inverse = rms_scale(inputs)
    scaled = upstream * gain_row
    inner_mean = jnp.mean(inputs * scaled, -1, keepdims=True)
    grad_inputs = inverse * scaled - inputs * (inverse * inverse * inverse) * inner_mean
    grad_gain = jnp.sum(upstream * inputs * inverse, 0, keepdims=True)
    return grad_inputs, grad_gain


def placed(count, offset):
    index = lax.broadcasted_iota(jnp.int32, (count, LANES), 0)
    lane = lax.broadcasted_iota(jnp.int32, (count, LANES), 1)
    return one_hot(lane == index + offset)


def prepare_body(direct, in_ref, out_ref, router_ref, gains_ref, table_ref, *packets):
    share = in_ref.shape[1]
    for layer in range(LAYERS):
        for which in range(3):
            for head in range(OWN):
                for c in range(GROUP):
                    source = which * D + (head * GROUP + c) * HEAD_DIM
                    target = which * OWN_COLS + head * HEAD_DIM
                    target += layer * (PACKED + LANES)
                    packets[0][c, :, target : target + HEAD_DIM] = in_ref[
                        layer, :, source : source + HEAD_DIM
                    ]
        if direct:
            width = D // GROUP
            for q in range(GROUP):
                packets[1 + layer][q] = out_ref[layer, :, q * width : (q + 1) * width]
    small = jnp.zeros((share, LANES), f32)
    row = lax.broadcasted_iota(jnp.int32, (share, LANES), 0)
    for layer in range(LAYERS):
        top = 32 * layer
        small = small + dot(router_ref[layer], placed(router_ref.shape[1], top), 0, 0)
        small = small + dot(gains_ref[layer], placed(2, top + 16), 0, 0)
        bucket = dot(table_ref[layer : layer + 1, :], placed(table_ref.shape[1], top + 64), 1, 0)
        small = small + jnp.where(row == 0, bucket, 0.0)
    for c in range(GROUP):
        packets[0][c, :, PACKED : PACKED + LANES] = small.astype(bf16)


def prepare(direct, attn_in, attn_out, router, gains, rel_table):
    share = attn_in.shape[1]
    outs = [shape((GROUP, share, 2 * PACKED + LANES), bf16)]
    if direct:
        outs += [shape((GROUP, share, D // GROUP), bf16)] * LAYERS

    def body(*refs):
        prepare_body(direct, *refs)

    return whole_call(
        body, outs, [attn_in, attn_out, router, gains, rel_table], streamed=True, name="prepare"
    )


def unpack(place, hits, experts, pairs, layer, got):
    share = got.shape[-2]
    width = D // GROUP
    first = layer == 0

    def body(place_ref, hits_ref, got_ref, w_in_ref, w_out_ref, *rest):
        for index in range(experts * pairs):
            e, d = index // pairs, index % pairs
            for c in range(GROUP):
                owner = (e * GROUP + c) * pairs + d
                at = owner * share
                w_in_ref[at : at + share, :] = got_ref[index, c, :, :PACKED]
                w_out_ref[c, index * share : (index + 1) * share, :] = got_ref[
                    index, c, :, got_ref.shape[-1] - width :
                ]
                if first:
                    flags = got_ref[index, c, :, PACKED : PACKED + LANES].astype(f32)
                    rest[2][at : at + share, :] = flags
                    rest[3][owner : owner + 1, :] = flags[:1, :]
        if not first:
            return
        feature_ref, bias_ref, flat_ref, bucket_ref = rest
        feature_ref[...] = flat_ref[...].T
        head = lax.broadcasted_iota(jnp.int32, (8, LANES), 0)
        lane = lax.broadcasted_iota(jnp.int32, (8, LANES), 1)
        for other in range(LAYERS):
            mine = jnp.where(
                (lane == 64 + 32 * other + head * GROUP + place_ref[0]) & (head < OWN), 1.0, 0.0
            )
            table = dot(mine, bucket_ref[...], 1, 1, lax.Precision.HIGHEST)
            bias_ref[other] = dot(
                table - table[:, BUCKETS - 1 :], hits_ref[...], 1, 0, lax.Precision.HIGHEST
            )

    outs = [shape((D, PACKED), bf16), shape((GROUP, OWN_COLS, D // GROUP), bf16)]
    scratch = []
    if first:
        outs += [shape((LANES, D), f32), shape((LAYERS, 8, REACH), f32)]
        scratch = [pltpu.VMEM((D, LANES), f32), pltpu.VMEM((BUCKETS, LANES), f32)]
    return whole_call(
        body, outs, [place, hits, got], smem=1, scratch=scratch, name="unpack"
    )


def near_bias(bias_ref, layer, head, rows):
    row = bias_ref[layer, head : head + 1, :]
    return pltpu.roll(jnp.broadcast_to(row, (rows, REACH)), 0, 1, stride=1, stride_axis=0)


def masked_scores(keys, queries, near, low, key_block, query_block, rows):
    scores = dot(keys, queries, 1, 1)
    key_place = lax.broadcasted_iota(jnp.int32, (rows, rows), 0)
    seen = key_place >= low - key_block * rows
    if key_block == query_block:
        scores = scores + near[:, :rows]
        seen = seen & (key_place <= lax.broadcasted_iota(jnp.int32, (rows, rows), 1))
    elif key_block == query_block - 1:
        scores = scores + near[:, rows:]
    return jnp.where(seen, scores, NEGATIVE)


def attention_forward_body(
    layer, place_ref, n0, n1, n2, n3, w_ref, feature_ref, bias_ref, low_ref, wo_ref,
    packed_ref, log_ref, mixed_ref, keep_ref, send_ref, *normed_ref,
):
    me = place_ref[0]
    rows = n0.shape[0]
    for r, piece in enumerate((n0, n1, n2, n3)):
        normed = piece[...]
        if layer == 0:
            wide = normed.astype(f32)
            normed = (wide * rms_scale(wide) * feature_ref[16:17, :]).astype(bf16)
            normed_ref[0][r * rows : (r + 1) * rows, :] = normed
        packed_ref[r * rows : (r + 1) * rows, :] = dot(normed, w_ref[...], 1, 0).astype(bf16)
    lane = lax.broadcasted_iota(jnp.int32, (rows, LANES), 1)
    starts = [pl.multiple_of((b ^ me) * rows, rows) for b in range(GROUP)]
    for pair in range(OWN // 2):
        at = pair * LANES

        def part(b, which):
            column = which * OWN_COLS + at
            return packed_ref[pl.ds(starts[b], rows), column : column + LANES]

        sides = [(lane // HEAD_DIM) == side for side in range(2)]
        nears = [near_bias(bias_ref, layer, pair * 2 + side, rows) for side in range(2)]
        for qb in range(GROUP):
            low = low_ref[:, qb * rows : (qb + 1) * rows]
            queries = part(qb, 0) * SCORE_SCALE
            total = None
            for side in range(2):
                mine = jnp.where(sides[side], queries, 0).astype(bf16)
                tiles = [
                    masked_scores(part(kb, 1), mine, nears[side], low, kb, qb, rows)
                    for kb in range(qb + 1)
                ]
                peak = jnp.max(tiles[0], 0, keepdims=True)
                for tile in tiles[1:]:
                    peak = jnp.maximum(peak, jnp.max(tile, 0, keepdims=True))
                weight_sum = jnp.zeros((1, rows), f32)
                out = jnp.zeros((LANES, rows), f32)
                for kb, tile in enumerate(tiles):
                    power = jnp.exp(tile - peak)
                    weight_sum = weight_sum + jnp.sum(power, 0, keepdims=True)
                    values = jnp.where(sides[side], part(kb, 2), 0).astype(bf16)
                    out = out + dot(values, power.astype(bf16), 0, 0)
                out = out / weight_sum
                total = out if total is None else total + out
                head = pair * 2 + side
                log_ref[head : head + 1, qb * rows : (qb + 1) * rows] = peak + jnp.log(weight_sum)
            mixed_ref[pl.ds(starts[qb], rows), at : at + LANES] = total.T.astype(bf16)
    width = wo_ref.shape[2]
    for r, (target, offset) in enumerate(
        ((keep_ref, 0), (send_ref, 0), (keep_ref, rows), (send_ref, rows))
    ):
        mixed = mixed_ref[r * rows : (r + 1) * rows, :]
        for q in range(wo_ref.shape[0]):
            target[offset : offset + rows, q * width : (q + 1) * width] = dot(
                mixed, wo_ref[q], 1, 0
            ).astype(target.dtype)


def attention_forward(layer, place, pieces, w_in, feature, bias, low, w_out):
    rows = pieces[0].shape[0]
    total = GROUP * rows
    outs = [
        shape((total, PACKED), bf16),
        shape((8, total), f32),
        shape((total, OWN_COLS), bf16),
        shape((2 * rows, D), f32),
        shape((2 * rows, D), bf16),
    ]
    if layer == 0:
        outs.append(shape((total, D), bf16))

    def body(*refs):
        attention_forward_body(layer, *refs)

    return whole_call(
        body,
        outs,
        [place, *pieces, w_in, feature, bias, low, w_out],
        smem=1,
        flops=2 * total * D * (PACKED + OWN_COLS) + 2 * total * total * OWN_COLS * 2,
        limit=24,
        name="attention_forward",
    )


def attention_backward_body(
    layer, place_ref, d0, d1, d2, d3, w_ref, feature_ref, bias_ref, low_ref, wo_ref, packed_ref,
    log_ref, *refs,
):
    normed_refs = refs[:-8]
    (grad_packed_ref, keep_ref, send_ref, table_ref, gain_ref, grad_mixed_ref, dk_ref,
     dv_ref) = refs[-8:]
    me = place_ref[0]
    rows = d0.shape[0]
    width = wo_ref.shape[2]
    for r, piece in enumerate((d0, d1, d2, d3)):
        got = jnp.zeros((rows, OWN_COLS), f32)
        for q in range(wo_ref.shape[0]):
            got = got + dot(piece[:, q * width : (q + 1) * width], wo_ref[q], 1, 1)
        grad_mixed_ref[r * rows : (r + 1) * rows, :] = got.astype(bf16)
    lane = lax.broadcasted_iota(jnp.int32, (rows, LANES), 1)
    starts = [pl.multiple_of((b ^ me) * rows, rows) for b in range(GROUP)]
    table_ref[...] = jnp.zeros(table_ref.shape, f32)
    for pair in range(OWN // 2):
        at = pair * LANES

        def part(b, which):
            column = which * OWN_COLS + at
            return packed_ref[pl.ds(starts[b], rows), column : column + LANES]

        sides = [(lane // HEAD_DIM) == side for side in range(2)]
        nears = [near_bias(bias_ref, layer, pair * 2 + side, rows) for side in range(2)]
        diag = [jnp.zeros((rows, rows), f32) for _ in range(2)]
        before = [jnp.zeros((rows, rows), f32) for _ in range(2)]
        far = [jnp.zeros((1, rows), f32) for _ in range(2)]
        dk_ref[...] = jnp.zeros(dk_ref.shape, f32)
        dv_ref[...] = jnp.zeros(dv_ref.shape, f32)
        for qb in range(GROUP):
            low = low_ref[:, qb * rows : (qb + 1) * rows]
            queries = part(qb, 0) * SCORE_SCALE
            upstream = grad_mixed_ref[pl.ds(starts[qb], rows), at : at + LANES]
            grad_queries = jnp.zeros((LANES, rows), f32)
            for side in range(2):
                head = pair * 2 + side
                mine = jnp.where(sides[side], queries, 0).astype(bf16)
                above = jnp.where(sides[side], upstream, 0).astype(bf16)
                log_total = log_ref[head : head + 1, qb * rows : (qb + 1) * rows]
                probs, grads = [], []
                row_dot = jnp.zeros((1, rows), f32)
                for kb in range(qb + 1):
                    scores = masked_scores(part(kb, 1), mine, nears[side], low, kb, qb, rows)
                    prob = jnp.exp(scores - log_total)
                    grad = dot(part(kb, 2), above, 1, 1)
                    row_dot = row_dot + jnp.sum(prob * grad, 0, keepdims=True)
                    probs.append(prob)
                    grads.append(grad)
                for kb in range(qb + 1):
                    grad_score = probs[kb] * (grads[kb] - row_dot)
                    if kb == qb:
                        diag[side] = diag[side] + grad_score
                    elif kb == qb - 1:
                        before[side] = before[side] + grad_score
                    else:
                        far[side] = far[side] + jnp.sum(grad_score, 0, keepdims=True)
                    grad_low = grad_score.astype(bf16)
                    keys = jnp.where(sides[side], part(kb, 1), 0).astype(bf16)
                    grad_queries = grad_queries + dot(keys, grad_low, 0, 0)
                    span = slice(kb * rows, (kb + 1) * rows)
                    dk_ref[span, :] += dot(grad_low, mine, 1, 0)
                    dv_ref[span, :] += dot(probs[kb].astype(bf16), above, 1, 0)
            grad_packed_ref[pl.ds(starts[qb], rows), at : at + LANES] = (
                grad_queries.T * SCORE_SCALE
            ).astype(bf16)
        for kb in range(GROUP):
            span = slice(kb * rows, (kb + 1) * rows)
            for which, source in ((1, dk_ref), (2, dv_ref)):
                column = which * OWN_COLS + at
                grad_packed_ref[pl.ds(starts[kb], rows), column : column + LANES] = source[
                    span, :
                ].astype(bf16)
        distance = lax.broadcasted_iota(jnp.int32, (1, REACH), 1)
        for side in range(2):
            head = pair * 2 + side
            skewed = jnp.concatenate([diag[side], before[side]], 1)
            row_index = lax.broadcasted_iota(jnp.int32, (rows, REACH), 0)
            step = 1
            while step < rows:
                skewed = jnp.where(
                    (row_index & step) != 0, pltpu.roll(skewed, REACH - step, 1), skewed
                )
                step *= 2
            by_distance = jnp.sum(skewed, 0, keepdims=True)
            far_sum = jnp.sum(far[side], 1, keepdims=True)
            table_ref[head : head + 1, :] = by_distance + jnp.where(
                distance == REACH - 1, far_sum, 0.0
            )
    for r, (target, offset) in enumerate(
        ((keep_ref, 0), (send_ref, 0), (keep_ref, rows), (send_ref, rows))
    ):
        grad_normed = dot(grad_packed_ref[r * rows : (r + 1) * rows, :], w_ref[...], 1, 1)
        target[offset : offset + rows, :] = grad_normed.astype(target.dtype)
        part_gain = jnp.sum(grad_normed * block_of(normed_refs, r, rows).astype(f32), 0, keepdims=True)
        gain_sum = part_gain if r == 0 else gain_sum + part_gain
    gain_row = feature_ref[32 * layer + 16 : 32 * layer + 17, :]
    gain_ref[...] = jnp.broadcast_to(gain_sum / gain_row, gain_ref.shape)


def block_of(refs, r, rows):
    return refs[r][...] if len(refs) > 1 else refs[0][r * rows : (r + 1) * rows, :]


def attention_backward(
    layer, place, pieces, w_in, feature, bias, low, w_out, packed, log_total, normed, after=()
):
    rows = pieces[0].shape[0]
    total = GROUP * rows

    def body(*refs):
        attention_backward_body(layer, *refs)

    return whole_call(
        body,
        (
            shape((total, PACKED), bf16),
            shape((2 * rows, D), f32),
            shape((2 * rows, D), bf16),
            shape((8, REACH), f32),
            shape((8, D), f32),
        ),
        [place, *pieces, w_in, feature, bias, low, w_out, packed, log_total, *normed],
        smem=1,
        after=after,
        scratch=[
            pltpu.VMEM((total, OWN_COLS), bf16),
            pltpu.VMEM((total, LANES), f32),
            pltpu.VMEM((total, LANES), f32),
        ],
        flops=2 * total * D * (PACKED + OWN_COLS) + 2 * total * total * OWN_COLS * 5,
        limit=24,
        name="attention_backward",
    )


def dense_products(normed, upstream, grad_packed_ref, mixed_ref):
    rows = upstream[0].shape[0]
    total_in = None
    total_out = None
    for r in range(GROUP):
        span = slice(r * rows, (r + 1) * rows)
        one = dot(block_of(normed, r, rows), grad_packed_ref[span, :], 0, 0)
        two = dot(mixed_ref[span, :], upstream[r][...], 0, 0)
        total_in = one if total_in is None else total_in + one
        total_out = two if total_out is None else total_out + two
    return total_in, total_out


def dense_grads(normed, upstream, grad_packed, mixed):
    rows = upstream[0].shape[0]
    count = len(normed)

    def body(*refs):
        total_in, total_out = dense_products(
            refs[:count], refs[count : count + GROUP], refs[-4], refs[-3]
        )
        refs[-2][...] = total_in.astype(bf16)
        refs[-1][...] = total_out.astype(bf16)

    return whole_call(
        body,
        (shape((D, PACKED), bf16), shape((OWN_COLS, D), bf16)),
        [*normed, *upstream, grad_packed, mixed],
        flops=2 * GROUP * rows * D * (PACKED + OWN_COLS),
        name="dense_grads",
    )


def dense_pack(experts, pairs, share, place, normed, upstream, grad_packed, mixed, small, gain_a,
               by_distance, hits, split, after=()):
    rows = upstream[0].shape[0]
    count = len(normed)
    width = D // GROUP
    cut = EARLY_COLS if split else PACKED
    rest = PACKED - cut + LANES + width
    total = cut if split else PACKED + rest

    def body(place_ref, *refs):
        grad_packed_ref, mixed_ref, small_ref, gain_ref, distance_ref, hits_ref = refs[
            count + GROUP : count + GROUP + 6
        ]
        outs = refs[count + GROUP + 6 : -3]
        in_ref, out_ref, flat_ref = refs[-3:]
        total_in, total_out = dense_products(
            refs[:count], refs[count : count + GROUP], grad_packed_ref, mixed_ref
        )
        in_ref[...] = total_in
        out_ref[...] = total_out
        row = lax.broadcasted_iota(jnp.int32, (8, D), 0)
        gains = jnp.where(
            row == 0, gain_ref[...], jnp.where(row == 1, small_ref[16:24, :], 0.0)
        )
        features = jnp.concatenate(
            [small_ref[:16, :], gains, jnp.zeros((LANES - 24, D), f32)], 0
        )
        flat_ref[...] = features.T
        by_bucket = dot(hits_ref[...], distance_ref[...], 1, 1, lax.Precision.HIGHEST)
        head = lax.broadcasted_iota(jnp.int32, (8, LANES), 0)
        lane = lax.broadcasted_iota(jnp.int32, (8, LANES), 1)
        mine = jnp.where((lane == 64 + head * GROUP + place_ref[0]) & (head < OWN), 1.0, 0.0)
        buckets = dot(by_bucket, mine, 1, 0, lax.Precision.HIGHEST)
        for index in range(BUCKETS):
            at = index * share
            flat_ref[at : at + 1, :] = flat_ref[at : at + 1, :] + buckets[index : index + 1, :]
        for side, d in enumerate((place_ref[1], 1 - place_ref[1])):
            for e in range(experts):
                for c in range(GROUP):
                    at = ((e * GROUP + c) * pairs + d) * share
                    span = pl.ds(pl.multiple_of(at, share), share)
                    to = slice(c * share, (c + 1) * share)
                    target = outs[side]
                    target[e, to, :cut] = in_ref[span, :cut].astype(target.dtype)
                    out_span = pl.ds(pl.multiple_of((e * pairs + d) * share, share), share)
                    outer = out_ref[out_span, c * width : (c + 1) * width]
                    if split:
                        more = PACKED - cut
                        outs[2][e, side, to, :more] = in_ref[span, cut:].astype(bf16)
                        outs[2][e, side, to, more : more + LANES] = flat_ref[span, :].astype(bf16)
                        outs[2][e, side, to, more + LANES :] = outer.astype(bf16)
                    else:
                        target[e, to, PACKED : PACKED + LANES] = flat_ref[span, :].astype(
                            target.dtype
                        )
                        target[e, to, PACKED + LANES :] = outer.astype(target.dtype)

    outs = [
        shape((experts, GROUP * share, total), f32),
        shape((experts, GROUP * share, total), bf16),
    ]
    if split:
        outs.append(shape((experts, pairs, GROUP * share, rest), bf16))
    return whole_call(
        body,
        outs,
        [place, *normed, *upstream, grad_packed, mixed, small, gain_a, by_distance, hits],
        smem=1,
        scratch=[
            pltpu.VMEM((D, PACKED), f32),
            pltpu.VMEM((OWN_COLS, D), f32),
            pltpu.VMEM((D, LANES), f32),
        ],
        flops=2 * GROUP * rows * D * (PACKED + OWN_COLS),
        after=after,
        streamed=True,
        limit=32,
        name="dense_pack",
    )


def finish_dense(share, inner, outer):
    width = D // GROUP

    def body(*refs):
        in_ref, out_ref, small_ref = refs[1 + LAYERS :]
        for layer in range(LAYERS):
            got, rows_out = refs[0], refs[1 + layer]
            for c in range(GROUP):
                for which in range(3):
                    for head in range(OWN):
                        source = which * OWN_COLS + head * HEAD_DIM
                        target = which * D + (head * GROUP + c) * HEAD_DIM
                        in_ref[layer, :, target : target + HEAD_DIM] = got[
                            c, layer, :, source : source + HEAD_DIM
                        ].astype(f32)
                out_ref[layer, :, c * width : (c + 1) * width] = rows_out[
                    c * share : (c + 1) * share, :
                ]
            total = got[0, layer, :, PACKED:].astype(f32)
            for c in range(1, GROUP):
                total = total + got[c, layer, :, PACKED:].astype(f32)
            small_ref[layer] = total

    return whole_call(
        body,
        (
            shape((LAYERS, share, 3 * D), f32),
            shape((LAYERS, share, D), f32),
            shape((LAYERS, share, LANES), f32),
        ),
        [inner, *outer],
        name="finish_dense",
    )


def stacked(refs):
    return refs[0][...] if len(refs) == 1 else jnp.concatenate([ref[...] for ref in refs], 0)


def store_blocks(refs, rows):
    count = rows.shape[0] // len(refs)
    for index, ref in enumerate(refs):
        ref[...] = rows[index * count : (index + 1) * count, :].astype(ref.dtype)


def block_shapes(blocks, slots, width=D):
    return [shape((slots // blocks, width), bf16)] * blocks


def dispatch_grid(dest_rows, slots, tokens):
    place = lax.broadcasted_iota(jnp.int32, (slots, tokens), 0)
    first = place == dest_rows[0:1, :]
    second = place == dest_rows[1:2, :]
    return first, second


def one_hot(flags):
    return jnp.where(flags, 1.0, 0.0).astype(bf16)


def collect_grid(meta, slots):
    tokens = meta.shape[0]
    place = lax.broadcasted_iota(jnp.int32, (tokens, slots), 1)
    first = place == meta[:, 0:1].astype(jnp.int32)
    second = place == meta[:, 1:2].astype(jnp.int32)
    return first, second


def scatter_grads(upstream, meta, dest_rows, slots):
    tokens = upstream.shape[0]
    first, second = dispatch_grid(dest_rows, slots, tokens)
    return (
        dot(one_hot(first), (meta[:, 2:3] * upstream).astype(bf16), 1, 0)
        + dot(one_hot(second), (meta[:, 3:4] * upstream).astype(bf16), 1, 0)
    ).astype(bf16)


def slot_rows(idst, capacity, own):
    tokens = idst.shape[1]
    down = lax.broadcasted_iota(jnp.int32, (tokens, tokens), 0)
    across = lax.broadcasted_iota(jnp.int32, (tokens, tokens), 1)
    sub = lax.broadcasted_iota(jnp.int32, (16, tokens), 0)
    row0 = sub == idst[0:1, :]
    row1 = sub == idst[1:2, :]
    counts = dot(one_hot(row0 | row1), one_hot(down < across), 1, 0)
    found = []
    for index, row in enumerate((row0, row1)):
        slot = jnp.sum(jnp.where(row, counts, 0.0), 0, keepdims=True).astype(jnp.int32)
        found.append((idst[index : index + 1, :] ^ own) * capacity + slot)
    return jnp.where(lax.broadcasted_iota(jnp.int32, (8, tokens), 0) == 0, found[0], found[1])


def send_grads(experts, capacity, idst, grad, after):
    tokens = grad.shape[0]
    slots = experts * capacity

    def body(idst_ref, grad_ref, out_ref):
        first, second = dispatch_grid(slot_rows(idst_ref[...], capacity, 0), slots, tokens)
        out_ref[...] = dot(one_hot(first | second), grad_ref[...], 1, 0).astype(bf16)

    (out,) = whole_call(
        body, [shape((slots, D), bf16)], [idst, grad], after=after, name="send_grads"
    )
    return out


def apply_gates(experts, blocks, place, rows, gates):
    slots = gates.shape[0]
    capacity = slots // experts
    if blocks == 1:
        order = jnp.arange(experts) ^ place[2]
        rows = rows.reshape(experts, capacity, D)[order].reshape(slots, D)
        gates = gates.reshape(experts, capacity, LANES)[order].reshape(slots, LANES)

    def body(place_ref, rows_ref, gates_ref, *outs):
        for index, out_ref in enumerate(outs):
            span = pl.ds(0, slots)
            if blocks > 1:
                source = pl.multiple_of((index ^ place_ref[2]) * capacity, capacity)
                span = pl.ds(source, capacity)
            out_ref[...] = (gates_ref[span, 0:1] * rows_ref[span, :].astype(f32)).astype(bf16)

    return whole_call(
        body, block_shapes(blocks, slots), [place, rows, gates], smem=1, streamed=True,
        name="apply_gates",
    )


def route_body(layer, experts, capacity, last, blocks, place_ref, *refs):
    top = 32 * layer
    own = place_ref[2]
    x_ref, keep_ref, recv_ref, far_ref, feature_ref, ids_ref, idst_ref = refs[:7]
    middle_ref, soft_ref, meta_ref, dest_ref = refs[7:11]
    rows_refs = refs[11 : 11 + blocks]
    tokens = x_ref.shape[0]
    slots = experts * capacity
    middle = (
        x_ref[...].astype(f32)
        + keep_ref[:tokens, :]
        + recv_ref[:tokens, :].astype(f32)
        + far_ref[...].astype(f32)
    )
    middle_ref[...] = middle
    normed = middle * rms_scale(middle) * feature_ref[top + 17 : top + 18, :]
    lane = lax.broadcasted_iota(jnp.int32, (tokens, LANES), 1)
    logits = dot(normed, feature_ref[...], 1, 1, lax.Precision.HIGHEST)
    logits = jnp.where((lane >= top) & (lane < top + experts), logits, NEGATIVE)
    power = jnp.exp(logits - jnp.max(logits, -1, keepdims=True))
    soft = power / jnp.sum(power, -1, keepdims=True)
    soft_ref[...] = soft
    ids = ids_ref[...]
    hit0 = lane == ids[:, 0:1] + top
    hit1 = lane == ids[:, 1:2] + top
    picked0 = jnp.sum(jnp.where(hit0, soft, 0.0), -1, keepdims=True)
    picked1 = jnp.sum(jnp.where(hit1, soft, 0.0), -1, keepdims=True)
    pick_total = picked0 + picked1
    down = lax.broadcasted_iota(jnp.int32, (tokens, tokens), 0)
    across = lax.broadcasted_iota(jnp.int32, (tokens, tokens), 1)
    counts = dot(one_hot(across < down), one_hot(hit0 | hit1), 1, 0)
    dest0 = (ids[:, 0:1] ^ own).astype(f32) * capacity + jnp.sum(
        jnp.where(hit0, counts, 0.0), -1, keepdims=True
    )
    dest1 = (ids[:, 1:2] ^ own).astype(f32) * capacity + jnp.sum(
        jnp.where(hit1, counts, 0.0), -1, keepdims=True
    )
    fields = (dest0, dest1, picked0 / pick_total, picked1 / pick_total, pick_total)
    meta = jnp.zeros((tokens, LANES), f32)
    for index, field in enumerate(fields):
        meta = jnp.where(lane == index, field, meta)
    meta_ref[...] = meta
    dest_rows = slot_rows(idst_ref[...], capacity, own)
    dest_ref[...] = dest_rows
    first, second = dispatch_grid(dest_rows, slots, tokens)
    store_blocks(rows_refs, dot(one_hot(first | second), normed.astype(bf16), 1, 0))
    if last:
        total = None
        place = lax.broadcasted_iota(jnp.int32, (slots, tokens), 0)
        for index in range(2):
            slot = dest_rows[index : index + 1, :] - (idst_ref[index : index + 1, :] ^ own) * capacity
            flags = place == slot + idst_ref[index : index + 1, :] * capacity
            gate = meta[:, 2 + index : 3 + index]
            spread = jnp.zeros((tokens, LANES), f32)
            for term in range(3):
                piece = gate.astype(bf16).astype(f32)
                spread = jnp.where(lane == term, piece, spread)
                gate = gate - piece
            got = dot(one_hot(flags), spread.astype(bf16), 1, 0)
            total = got if total is None else total + got
        refs[-1][...] = jnp.broadcast_to(jnp.sum(total, -1, keepdims=True), total.shape)


def route(
    layer, experts, capacity, blocks, place, x, keep, recv, far, feature, ids, idst, last, after=()
):
    tokens = x.shape[0]
    slots = experts * capacity
    outs = [
        shape((tokens, D), f32),
        shape((tokens, LANES), f32),
        shape((tokens, LANES), f32),
        shape((8, tokens), jnp.int32),
    ] + block_shapes(blocks, slots)
    if last:
        outs.append(shape((slots, LANES), f32))

    def body(*refs):
        route_body(layer, experts, capacity, last, blocks, *refs)

    return whole_call(
        body, outs, [place, x, keep, recv, far, feature, ids, idst], smem=1,
        flops=2 * slots * tokens * D, after=after, name="route",
    )


def combine(middle, back, meta, feature=None):
    tokens = middle.shape[0]
    count = len(back)
    last = feature is None
    args = [middle, meta, *back]
    outs = [shape((tokens, D), bf16 if last else f32)]
    if not last:
        args.append(feature)
        outs.append(shape((tokens, D), bf16))

    def body(middle_ref, meta_ref, *refs):
        meta = meta_ref[...]
        rows = stacked(refs[:count])
        first, second = collect_grid(meta, rows.shape[0])
        x = (
            middle_ref[...]
            + meta[:, 2:3] * dot(one_hot(first), rows, 1, 0)
            + meta[:, 3:4] * dot(one_hot(second), rows, 1, 0)
        )
        if last:
            refs[-1][...] = x.astype(bf16)
        else:
            refs[-2][...] = x
            refs[-1][...] = (x * rms_scale(x) * refs[count][48:49, :]).astype(bf16)

    return whole_call(
        body, outs, args, flops=4 * tokens * D * count * back[0].shape[0], name="combine"
    )


def expert_token_back_body(
    layer, back_refs, came_refs, g_ref, middle_ref, soft_ref, meta_ref, ids_ref, feature_ref,
    dmiddle_ref, dattn_ref, small_ref,
):
    back, came = stacked(back_refs), stacked(came_refs)
    top = 32 * layer
    gain_row = feature_ref[top + 17 : top + 18, :]
    meta = meta_ref[...]
    g = g_ref[...].astype(f32)
    slots = back.shape[0]
    first, second = collect_grid(meta, slots)
    grad_gate0 = jnp.sum(g * dot(one_hot(first), back, 1, 0), -1, keepdims=True)
    grad_gate1 = jnp.sum(g * dot(one_hot(second), back, 1, 0), -1, keepdims=True)
    grad_normed = dot(one_hot(first | second), came, 1, 0)
    gap = (grad_gate0 - grad_gate1) / meta[:, 4:5]
    ids = ids_ref[...]
    lane = lax.broadcasted_iota(jnp.int32, meta.shape, 1)
    grad_soft = jnp.where(lane == ids[:, 0:1] + top, meta[:, 3:4] * gap, 0.0) + jnp.where(
        lane == ids[:, 1:2] + top, -meta[:, 2:3] * gap, 0.0
    )
    soft = soft_ref[...]
    grad_logits = soft * (grad_soft - jnp.sum(soft * grad_soft, -1, keepdims=True))
    middle = middle_ref[...]
    normed = middle * rms_scale(middle) * gain_row
    grad_router = dot(grad_logits.T, normed, 1, 0, lax.Precision.HIGHEST)
    grad_normed = grad_normed + dot(
        grad_logits, feature_ref[...], 1, 0, lax.Precision.HIGHEST
    )
    grad_branch, grad_gain = norm_back(middle, gain_row, grad_normed)
    dmiddle = g + grad_branch
    dmiddle_ref[...] = dmiddle
    dattn_ref[...] = dmiddle.astype(bf16)
    small_ref[:16, :] = grad_router[top : top + 16, :]
    small_ref[16:24, :] = jnp.broadcast_to(grad_gain, (8, D))


def expert_token_back(layer, back, came, g, middle, soft, meta, ids, feature, after=()):
    tokens = middle.shape[0]

    def body(*refs):
        count = len(back)
        expert_token_back_body(layer, refs[:count], refs[count : 2 * count], *refs[2 * count :])

    return whole_call(
        body,
        (shape((tokens, D), f32), shape((tokens, D), bf16), shape((24, D), f32)),
        [*back, *came, g, middle, soft, meta, ids, feature],
        after=after,
        flops=6 * tokens * D * len(back) * back[0].shape[0],
        streamed=True,
        limit=32,
        name="expert_token_back",
    )


def attention_token_back_body(layer, *refs):
    if layer == 0:
        x_ref, dmiddle_ref, keep_ref, recv_ref, far_ref, feature_ref, out_ref = refs
    else:
        (x_ref, dmiddle_ref, keep_ref, recv_ref, far_ref, feature_ref, meta_ref, dest_ref,
         out_ref, *sent_refs) = refs
    tokens = x_ref.shape[0]
    grad_normed = (
        keep_ref[:tokens, :] + recv_ref[:tokens, :].astype(f32) + far_ref[...].astype(f32)
    )
    gain_row = feature_ref[32 * layer + 16 : 32 * layer + 17, :]
    grad_branch, _ = norm_back(x_ref[...].astype(f32), gain_row, grad_normed)
    g = dmiddle_ref[...] + grad_branch
    out_ref[...] = g
    if layer > 0:
        slots = len(sent_refs) * sent_refs[0].shape[0]
        store_blocks(sent_refs, scatter_grads(g, meta_ref[...], dest_ref[...], slots))


def attention_token_back(
    layer, x, dmiddle, keep, recv, far, feature, meta=None, dest=None, blocks=1, slots=0, after=()
):
    tokens = x.shape[0]
    outs = [shape((tokens, D), f32)]
    args = [x, dmiddle, keep, recv, far, feature]
    if meta is not None:
        outs += block_shapes(blocks, slots)
        args += [meta, dest]

    def body(*refs):
        attention_token_back_body(layer, *refs)

    return whole_call(
        body, outs, args, flops=4 * tokens * D * slots, after=after, name="attention_token_back"
    )


def gelu_parts(gate):
    inner = math.sqrt(2.0 / math.pi) * (gate + 0.044715 * gate * gate * gate)
    return jnp.tanh(inner)


def weight_specs(layer, tile):
    return [
        pl.BlockSpec((1, 1, D, tile), lambda s: (layer, 0, 0, s)),
        pl.BlockSpec((1, 1, D, tile), lambda s: (layer, 0, 0, FF // tile + s)),
        pl.BlockSpec((1, 1, D, tile), lambda s: (layer, 0, 0, s)),
    ]


def block_specs(blocks):
    return [pl.BlockSpec(b.shape, lambda s: (0, 0)) for b in blocks]


def expert_call(body, steps, outs, out_specs, args, in_specs, scratch, limit, after, name):
    used = len(args)

    def ordered(*refs):
        body(*refs[:used], *refs[used + len(after) :])

    count = ROWS_HINT
    return pl.pallas_call(
        ordered,
        grid=(steps,),
        out_shape=tuple(outs),
        in_specs=list(in_specs) + [pl.BlockSpec(memory_space=pltpu.HBM)] * len(after),
        out_specs=tuple(out_specs),
        scratch_shapes=list(scratch),
        compiler_params=pltpu.CompilerParams(vmem_limit_bytes=limit * MIB),
        cost_estimate=pl.CostEstimate(
            flops=6 * count * D * FF, bytes_accessed=6 * D * FF, transcendentals=count * FF
        ),
        name=name,
    )(*args, *[far_away(a) for a in after])


def expert_forward(layer, blocks, w_in, w_out, after=()):
    number = len(blocks)
    count = number * blocks[0].shape[0]
    steps = FF // WIDE_TILE

    def body(*refs):
        wg_ref, wu_ref, wo_ref = refs[number : number + 3]
        produced_refs = refs[number + 3 : 2 * number + 3]
        acts_ref, rows_ref, total_ref = refs[2 * number + 3 :]
        step = pl.program_id(0)

        @pl.when(step == 0)
        def _():
            rows_ref[...] = stacked(refs[:number])

        rows = rows_ref[...]
        gate = dot(rows, wg_ref[0, 0], 1, 0)
        up = dot(rows, wu_ref[0, 0], 1, 0)
        acts_ref[0] = gate.astype(bf16)
        acts_ref[1] = up.astype(bf16)
        hidden = (0.5 * gate * (1.0 + gelu_parts(gate)) * up).astype(bf16)
        out = dot(hidden, wo_ref[0, 0], 1, 1)

        @pl.when(step == 0)
        def _():
            total_ref[...] = out

        @pl.when(step == steps - 1)
        def _():
            store_blocks(produced_refs, total_ref[...] + out)

    *produced, acts = expert_call(
        body,
        steps,
        [shape(b.shape, bf16) for b in blocks] + [pltpu.HBM((2, count, FF), bf16)],
        block_specs(blocks) + [pl.BlockSpec((2, count, WIDE_TILE), lambda s: (0, 0, s))],
        [*blocks, far_away(w_in), far_away(w_in), far_away(w_out)],
        block_specs(blocks) + weight_specs(layer, WIDE_TILE),
        [pltpu.VMEM((count, D), bf16), pltpu.VMEM((count, D), f32)],
        56,
        after,
        "expert_forward",
    )
    return produced, acts


def expert_backward(layer, blocks, out_blocks, acts, w_in, w_out, after=()):
    number = len(blocks)
    count = number * blocks[0].shape[0]
    steps = FF // WIDE_TILE
    outs = block_shapes(out_blocks, count)

    def body(*refs):
        acts_refs = refs[number : number + len(acts)]
        wg_ref, wu_ref, wo_ref, *rest = refs[number + len(acts) :]
        drows_refs = rest[:out_blocks]
        parts_ref, grad_ref, total_ref = rest[out_blocks:]
        step = pl.program_id(0)

        @pl.when(step == 0)
        def _():
            grad_ref[...] = stacked(refs[:number])

        grad_hidden = dot(grad_ref[...], wo_ref[0, 0], 1, 0)
        gate = jnp.concatenate([ref[0] for ref in acts_refs], 0).astype(f32)
        up = jnp.concatenate([ref[1] for ref in acts_refs], 0).astype(f32)
        curve = gelu_parts(gate)
        value = 0.5 * gate * (1.0 + curve)
        slope = 0.5 * (1.0 + curve) + 0.5 * gate * (1.0 - curve * curve) * math.sqrt(
            2.0 / math.pi
        ) * (1.0 + 3.0 * 0.044715 * gate * gate)
        grad_gate = (grad_hidden * up * slope).astype(bf16)
        grad_up = (grad_hidden * value).astype(bf16)
        parts_ref[0] = grad_gate
        parts_ref[1] = grad_up
        parts_ref[2] = (value * up).astype(bf16)
        out = dot(grad_gate, wg_ref[0, 0], 1, 1) + dot(grad_up, wu_ref[0, 0], 1, 1)

        @pl.when(step == 0)
        def _():
            total_ref[...] = out

        @pl.when(step == steps - 1)
        def _():
            store_blocks(drows_refs, total_ref[...] + out)

    *drows, parts = expert_call(
        body,
        steps,
        outs + [pltpu.HBM((3, count, FF), bf16)],
        block_specs(outs) + [pl.BlockSpec((3, count, WIDE_TILE), lambda s: (0, 0, s))],
        [*blocks, *[far_away(a) for a in acts], far_away(w_in), far_away(w_in), far_away(w_out)],
        block_specs(blocks)
        + [pl.BlockSpec((2, a.shape[1], WIDE_TILE), lambda s: (0, 0, s)) for a in acts]
        + weight_specs(layer, WIDE_TILE),
        [pltpu.VMEM((count, D), bf16), pltpu.VMEM((count, D), f32)],
        58,
        after,
        "expert_backward",
    )
    return drows, parts


def expert_grads(shares, rows, grads, parts, after=()):
    count = len(rows) * rows[0].shape[0]
    tall = D // shares
    first = len(rows)
    second = first + len(grads)
    third = second + len(parts)

    def body(*refs):
        out_ref, rows_t, grad_t = refs[third:]

        @pl.when(pl.program_id(0) == 0)
        def _():
            rows_t[...] = stacked(refs[:first]).T
            grad_t[...] = stacked(refs[first:second]).T

        for which in range(3):
            left = rows_t if which < 2 else grad_t
            right = [ref[which] for ref in refs[second:third]]
            right = right[0] if len(right) == 1 else jnp.concatenate(right, 0)
            got = dot(left[...], right, 1, 0).astype(bf16)
            for share in range(shares):
                out_ref[share, which] = got[share * tall : (share + 1) * tall, :]

    (out,) = expert_call(
        body,
        FF_STEPS,
        [pltpu.HBM((shares, 3, tall, FF), bf16)],
        [pl.BlockSpec((shares, 3, tall, FF_TILE), lambda s: (0, 0, 0, s))],
        [*rows, *grads, *[far_away(p) for p in parts]],
        block_specs(rows)
        + block_specs(grads)
        + [pl.BlockSpec((3, p.shape[1], FF_TILE), lambda s: (0, 0, s)) for p in parts],
        [pltpu.VMEM((D, count), bf16), pltpu.VMEM((D, count), bf16)],
        32,
        after,
        "expert_grads",
    )
    return out


def place_expert_grads(layer, summed, before=None, after=()):
    tall = summed.shape[1]
    outs = (
        pltpu.HBM((LAYERS, 1, tall, 2 * FF), f32),
        pltpu.HBM((LAYERS, 1, tall, FF), f32),
    )
    held = [] if before is None else list(before)

    def body(part_ref, out_part_ref, *refs):
        in_ref, out_ref = refs[-2:]
        in_ref[0, 0] = part_ref[0].astype(f32)
        out_ref[0, 0] = out_part_ref[0].astype(f32)

    return pl.pallas_call(
        body,
        grid=(2,),
        out_shape=outs,
        in_specs=[
            pl.BlockSpec((1, tall, FF), lambda s: (s, 0, 0)),
            pl.BlockSpec((1, tall, FF), lambda s: (2, 0, 0)),
        ]
        + [pl.BlockSpec(memory_space=pl.ANY)] * (len(held) + len(after)),
        out_specs=(
            pl.BlockSpec((1, 1, tall, FF), lambda s: (layer, 0, 0, s)),
            pl.BlockSpec((1, 1, tall, FF), lambda s: (layer, 0, 0, 0)),
        ),
        input_output_aliases={2: 0, 3: 1} if held else {},
        compiler_params=pltpu.CompilerParams(vmem_limit_bytes=32 * MIB),
        name="place_expert_grads",
    )(far_away(summed), far_away(summed), *[far_away(h) for h in [*held, *after]])


TWIN = [(i, i ^ 1) for i in range(GROUP)]
ACROSS = [(i, i ^ 2) for i in range(GROUP)]
FLIP = [(0, 1), (1, 0)]


def share_pieces(piece):
    across = lax.ppermute(piece, "context", ACROSS)
    twin = lax.ppermute(piece, "context", TWIN)
    return [piece, twin, across, lax.ppermute(across, "context", TWIN)]


def sum_pieces(keep, send):
    rows = keep.shape[0] // 2
    recv = lax.ppermute(send, "context", TWIN)
    other = (keep[rows:] + recv[rows:].astype(f32)).astype(bf16)
    return keep, recv, lax.ppermute(other, "context", ACROSS)


def sum_zone(zone):
    return jnp.sum(zone.astype(f32), 0)


def dense_sum(
    experts, pairs, share, table_share, place, grad_w_in, grad_w_out, small, gain_a, by_distance,
    hits,
):
    by_bucket = jnp.dot(hits, by_distance[:OWN].T, precision=lax.Precision.HIGHEST)
    buckets = jnp.where(
        jnp.arange(GROUP)[None, None, :] == place[0], by_bucket[:, :, None], 0.0
    ).reshape(experts, GROUP, pairs, 1, table_share)
    features = jnp.concatenate([small[:16], gain_a[:1], small[16:17]], 0).T
    features = features.reshape(experts, GROUP, pairs, share, 18)
    flat = jnp.zeros((experts, GROUP, pairs, share, LANES), f32)
    flat = flat.at[..., :18].set(features).at[..., :1, 64 : 64 + table_share].set(buckets)
    pack = jnp.concatenate(
        [grad_w_in.reshape(experts, GROUP, pairs, share, PACKED), flat.astype(bf16)], -1
    ).transpose(0, 2, 1, 3, 4)
    pack = pack.reshape(experts * pairs, GROUP * share, PACKED + LANES)
    mine = lax.psum_scatter(pack, ("experts", "dp"), scatter_dimension=0, tiled=False)
    inner = lax.all_to_all(
        mine.reshape(GROUP, share, PACKED + LANES), "context", split_axis=0, concat_axis=0
    ).astype(f32)
    g_in = inner[..., :PACKED].reshape(GROUP, share, 3, OWN, HEAD_DIM)
    g_in = g_in.transpose(1, 2, 3, 0, 4).reshape(share, 3 * D)
    placed_rows = jnp.where(
        jnp.arange(GROUP)[None, :, None, None] == place[0],
        grad_w_out.reshape(OWN, 1, HEAD_DIM, D),
        jnp.zeros((), bf16),
    ).reshape(D, D)
    g_out = lax.psum_scatter(placed_rows, ALL, scatter_dimension=0, tiled=True).astype(f32)
    return g_in, g_out, jnp.sum(inner[..., PACKED:], 0)


def exchange(rows):
    return lax.all_to_all(rows, "experts", split_axis=0, concat_axis=0, tiled=True)


def swap(blocks, experts):
    split = blocks if len(blocks) > 1 else jnp.split(blocks[0], experts)
    moved = [
        part if k == 0 else lax.ppermute(part, "experts", [(i, i ^ k) for i in range(experts)])
        for k, part in enumerate(split)
    ]
    return moved if len(blocks) > 1 else [jnp.concatenate(moved)]


def on_device(
    tokens, doc_starts, expert_ids, attn_in, attn_out, router, gains, rel_table,
    expert_in, expert_out, out_grad,
):
    experts = lax.axis_size("experts")
    pairs = lax.axis_size("dp")
    share = attn_in.shape[1]
    table_share = rel_table.shape[1]
    direct = share * pairs == HEAD_DIM and experts * GROUP == HEADS and pairs == 2
    place = jnp.stack(
        [lax.axis_index("context"), lax.axis_index("dp"), lax.axis_index("experts")]
    ).astype(jnp.int32)
    start_tokens = tokens[0]
    ids = expert_ids[0]
    idst = ids.T
    rows = start_tokens.shape[0]
    capacity = (10 * rows + 4 * experts - 1) // (4 * experts)
    slots = experts * capacity
    blocks = experts if experts == 4 and capacity % 16 == 0 else 1
    fine = [(0, 1), (2,), (3,)] if blocks == 4 else [(0,)]
    coarse = [(0, 1), (2, 3)] if blocks == 4 else [(0,)]
    grad_in = out_grad[0]
    hits = jnp.asarray(bucket_hits())

    packets = prepare(
        direct, attn_in, attn_out, router.transpose(0, 2, 1), gains.transpose(0, 2, 1), rel_table
    )

    def spread(packet):
        return lax.all_to_all(packet, "context", split_axis=0, concat_axis=0)

    def gather(part):
        return lax.all_gather(part, ("experts", "dp"), axis=0, tiled=False).reshape(
            experts, pairs, *part.shape
        )

    if direct:
        packet = spread(packets[0])
        top = PACKED + LANES

        def together(columns, rows_out):
            part = jnp.concatenate([columns, rows_out], -1)
            return lax.all_gather(part, ("experts", "dp"), axis=0, tiled=False)

        first = together(packet[..., :top], packets[1])
        w_in0, w_out0, feature, bias = unpack(place, hits, experts, pairs, 0, first)
        second = [together(packet[..., top:], packets[2])]
        w_in1, w_out1 = unpack(place, hits, experts, pairs, 1, second[0])
        w_in, w_out = [w_in0, w_in1], [w_out0, w_out1]
    else:
        second = []
        w_in, w_out = [], []
        for layer in range(LAYERS):
            at = layer * (PACKED + LANES)
            part = spread(packets[0])[..., at : at + PACKED + LANES]
            got = gather(part).transpose(0, 2, 1, 3, 4)
            w_in.append(got[..., :PACKED].reshape(D, PACKED))
            if layer == 0:
                small_all = got[..., PACKED : PACKED + LANES]
            full = lax.all_gather(attn_out[layer], ALL, axis=0, tiled=True)
            mine = lax.dynamic_index_in_dim(
                full.reshape(OWN, GROUP, HEAD_DIM, D), place[0], 1, keepdims=False
            )
            w_out.append(mine.reshape(OWN_COLS, GROUP, D // GROUP).transpose(1, 0, 2))
        feature = small_all.reshape(D, LANES).astype(f32).T
        bias_rows = []
        for layer in range(LAYERS):
            at = 64 + 32 * layer
            table = small_all[:, :, :, 0, at : at + table_share].reshape(BUCKETS, OWN, GROUP)
            table = lax.dynamic_index_in_dim(table, place[0], 2, keepdims=False).astype(f32)
            row = jnp.dot((table - table[-1:]).T, hits, precision=lax.Precision.HIGHEST)
            bias_rows.append(jnp.pad(row, ((0, 8 - OWN), (0, 0))))
        bias = jnp.stack(bias_rows)
    places = jnp.arange(GROUP * rows, dtype=jnp.int32)
    starts = doc_starts[0]
    low = jnp.max(
        jnp.where(starts[:, None] <= places[None, :], starts[:, None], 0), 0, keepdims=True
    )

    pieces = share_pieces(start_tokens)
    x = start_tokens
    kept = []
    for layer in range(LAYERS):
        packed, log_total, mixed, keep, send, *normed_all = attention_forward(
            layer, place, pieces, w_in[layer], feature, bias, low, w_out[layer]
        )
        normed_rows = normed_all if layer == 0 else pieces
        last = layer == LAYERS - 1
        if last:
            send = hold(send, [arrived_grad])
        keep, recv, far = sum_pieces(keep, send)
        middle, soft, meta, dest, *sent = route(
            layer, experts, capacity, blocks, place, x, keep, recv, far, feature, ids, idst, last,
        )
        arrived = swap(sent[:blocks], experts)
        if last:
            gates = exchange(sent[blocks])
        produced, acts, drows, parts = [], [], [], []
        order = []
        for chunk in coarse if last else fine:
            done, kept_acts = expert_forward(
                layer, [arrived[k] for k in chunk], expert_in, expert_out, after=order
            )
            produced += done
            acts.append(kept_acts)
            order = done[:1] + (second if layer == 0 and len(acts) == 1 else [])
            if last:
                if not drows:
                    arrived_grad = apply_gates(experts, blocks, place, arrived_grad, gates)
                done, some = expert_backward(
                    layer, [arrived_grad[k] for k in chunk], len(chunk), acts[-1:], expert_in,
                    expert_out,
                )
                drows += done
                parts.append(some)
                order = done[:1]
        back = swap(produced, experts)
        kept.append(
            (x, normed_rows, packed, log_total, mixed, middle, soft, meta, dest, arrived, acts, back)
        )
        if last:
            (result,) = combine(middle, back, meta)
        else:
            x, normed = combine(middle, back, meta, feature)
            ungated = send_grads(experts, capacity, idst, grad_in, [x])
            arrived_grad = exchange(ungated)
            pieces = share_pieces(hold(normed, [ungated]))

    g = grad_in
    inner, outer, expert_totals = [], [], []
    other = None
    placed_grads = None
    for layer in range(LAYERS - 1, -1, -1):
        (x, normed_rows, packed, log_total, mixed, middle, soft, meta, dest, arrived, acts,
         back) = kept[layer]
        if layer < LAYERS - 1:
            drows, parts = [], []
            for index, chunk in enumerate(coarse):
                some_acts = acts[:1] if index == 0 else acts[1:]
                done, some = expert_backward(
                    layer, [arrived_grad[k] for k in chunk], len(chunk), some_acts, expert_in,
                    expert_out, after=drows[-1:],
                )
                drows += done
                parts.append(some)
        came = swap(drows, experts)
        early = [] if other is None else [other]
        weight_grads = expert_grads(
            GROUP * pairs, arrived, arrived_grad, parts, after=(back if layer else []) + early
        )
        weight_grads = hold(weight_grads, came)
        total = lax.psum_scatter(
            weight_grads, ("context", "dp"), scatter_dimension=0, tiled=False
        )
        dmiddle, dattn, small_b = expert_token_back(
            layer, back, came, g, middle, soft, meta, ids, feature, after=[weight_grads]
        )
        zones = []
        if direct and other is not None:
            ours = hold(keep_dense, [dattn]) + other.astype(f32)
            zones = [exchange(ours.astype(bf16))]
        expert_totals.append(total)
        grad_pieces = share_pieces(dattn)
        grad_packed, keep, send, by_distance, gain_a = attention_backward(
            layer, place, grad_pieces, w_in[layer], feature, bias, low, w_out[layer], packed,
            log_total, normed_rows,
        )
        keep, recv, far = sum_pieces(keep, send)
        if layer > 0:
            below = kept[layer - 1]
            g, *sent = attention_token_back(
                layer, x, dmiddle, keep, recv, far, feature, below[7], below[8], blocks, slots
            )
            arrived_grad = swap(sent, experts)
        else:
            placed_grads = place_expert_grads(layer + 1, expert_totals[0])
            (g,) = attention_token_back(
                layer, x, dmiddle, keep, recv, far, feature, after=[placed_grads[0]]
            )
        if direct:
            keep_dense, send_dense, *rest = dense_pack(
                experts, pairs, share, place, normed_rows, grad_pieces, grad_packed, mixed,
                small_b, gain_a, by_distance, hits, split=layer == 0, after=zones,
            )
            other = lax.ppermute(send_dense, "dp", FLIP)
            if layer == 0:
                (zone,) = zones
                total = sum_zone(zone)
                flats = [total[:, : PACKED + LANES].astype(bf16)]
                outer.append(total[:, PACKED + LANES :])
                rest = sum_zone(exchange(rest[0]))
                theirs = lax.ppermute(rest[1].astype(bf16), "dp", FLIP)
                rest = rest[0] + theirs.astype(f32)
                ours = hold(keep_dense, [g, result, placed_grads[0]]) + other.astype(f32)
                total = sum_zone(exchange(ours.astype(bf16)))
                more = PACKED + LANES - EARLY_COLS
                flats.insert(0, jnp.concatenate([total, rest[:, :more]], -1).astype(bf16))
                outer.append(rest[:, more:])
                flat = jnp.stack([flat.reshape(GROUP, share, -1) for flat in flats], 1)
                inner = spread(flat)
        else:
            grad_w_in, grad_w_out = dense_grads(normed_rows, grad_pieces, grad_packed, mixed)
            inner.append(
                dense_sum(
                    experts, pairs, share, table_share, place, grad_w_in, grad_w_out, small_b,
                    gain_a, by_distance, hits,
                )
            )
    expert_grads_all = place_expert_grads(0, expert_totals[1], placed_grads)
    if direct:
        grad_attn_in, grad_attn_out, small_grad = finish_dense(
            share, inner, outer[::-1]
        )
    else:
        grad_attn_in, grad_attn_out, small_grad = (
            jnp.stack([entry[k] for entry in inner[::-1]]) for k in range(3)
        )
    return (
        result[None],
        g[None],
        grad_attn_in,
        grad_attn_out,
        small_grad[..., :experts],
        small_grad[..., 16:18],
        small_grad[:, 0, 64 : 64 + table_share],
        *expert_grads_all,
    )


def solution(mesh):
    return jax.shard_map(
        on_device,
        mesh=mesh,
        in_specs=(
            P(("experts", "dp"), "context", None),
            P(("experts", "dp"), None),
            P(("experts", "dp"), "context", None),
            P(None, ("experts", "context", "dp"), None),
            P(None, ("experts", "context", "dp"), None),
            P(None, ("experts", "context", "dp"), None),
            P(None, ("experts", "context", "dp"), None),
            P(None, ("experts", "context", "dp")),
            P(None, "experts", None, None),
            P(None, "experts", None, None),
            P(("experts", "dp"), "context", None),
        ),
        out_specs=(
            P(("experts", "dp"), "context", None),
            P(("experts", "dp"), "context", None),
            P(None, ("experts", "context", "dp"), None),
            P(None, ("experts", "context", "dp"), None),
            P(None, ("experts", "context", "dp"), None),
            P(None, ("experts", "context", "dp"), None),
            P(None, ("experts", "context", "dp")),
            P(None, "experts", ("context", "dp"), None),
            P(None, "experts", ("context", "dp"), None),
        ),
        check_vma=False,
    )
```

```python
import math

import jax
import jax.numpy as jnp
import numpy as np
from jax import lax
from jax.experimental import pallas as pl
from jax.experimental.pallas import tpu as pltpu
from jax.sharding import PartitionSpec as P

D = 1024
HEADS = 16
HEAD_DIM = 64
FF = 2816
BUCKETS = 32
MAX_DISTANCE = 128
LAYERS = 2
EPSILON = 1e-06
NEGATIVE = -1e30
SCORE_SCALE = 0.125
ALL = ("experts", "context", "dp")
GROUP = 4
OWN = HEADS // GROUP
OWN_COLS = OWN * HEAD_DIM
PACKED = 3 * OWN_COLS
LANES = 128
REACH = 512
FF_TILE = 256
FF_STEPS = FF // FF_TILE
WIDE_TILE = FF // 2
EARLY_COLS = 512
ROWS_HINT = 320
MIB = 1 << 20

bf16 = jnp.bfloat16
f32 = jnp.float32


def bucket_bounds(bucket_count, far_reach):
    half_count = bucket_count // 2
    bounds = list(range(1, half_count + 1))
    for section_index in range(1, half_count):
        bounds.append(
            int(math.ceil(half_count * (far_reach / half_count) ** (section_index / half_count)))
        )
    return np.array(bounds, np.int32)


def bucket_hits():
    distance = np.arange(REACH)
    bucket = (distance[:, None] >= bucket_bounds(BUCKETS, MAX_DISTANCE)).sum(-1)
    return (np.arange(BUCKETS)[:, None] == bucket[None, :]).astype(np.float32)


def dot(a, b, ca, cb, precision=None):
    return lax.dot_general(
        a, b, (((ca,), (cb,)), ((), ())), precision=precision, preferred_element_type=f32
    )


def whole_call(
    body, out_shape, args, *, flops=0, limit=16, scratch=(), smem=0, name=None, after=(),
    streamed=False,
):
    specs = [pl.BlockSpec(memory_space=pltpu.SMEM)] * smem + [
        pl.BlockSpec(memory_space=pltpu.VMEM)
    ] * (len(args) - smem)
    outs = tuple(out_shape)
    moved = sum(a.size * a.dtype.itemsize for a in list(args) + list(outs))
    specs += [pl.BlockSpec(memory_space=pltpu.HBM)] * len(after)
    used = len(args)
    args = list(args) + [far_away(a) for a in after]

    def ordered(*refs):
        body(*refs[:used], *refs[used + len(after) :])

    if streamed:
        args = args[:smem] + [far_away(a) for a in args[smem:]]

        def full(a):
            return pl.BlockSpec(a.shape, lambda i: (0,) * len(a.shape))

        return pl.pallas_call(
            ordered,
            grid=(1,),
            out_shape=outs,
            in_specs=specs[:smem] + [full(a) for a in args[smem:used]] + specs[used:],
            out_specs=tuple(full(o) for o in outs),
            scratch_shapes=list(scratch),
            compiler_params=pltpu.CompilerParams(vmem_limit_bytes=limit * MIB),
            cost_estimate=pl.CostEstimate(
                flops=int(flops), bytes_accessed=int(moved), transcendentals=0
            ),
            name=name,
        )(*args)
    return pl.pallas_call(
        ordered,
        out_shape=outs,
        in_specs=specs,
        out_specs=tuple(pl.BlockSpec(memory_space=pltpu.VMEM) for _ in outs),
        scratch_shapes=list(scratch),
        compiler_params=pltpu.CompilerParams(vmem_limit_bytes=limit * MIB),
        cost_estimate=pl.CostEstimate(
            flops=int(flops), bytes_accessed=int(moved), transcendentals=0
        ),
        name=name,
    )(*args)


def far_away(x):
    return pltpu.with_memory_space_constraint(x, pltpu.HBM)


def hold(x, after):
    def body(*refs):
        pass

    return pl.pallas_call(
        body,
        out_shape=pltpu.HBM(x.shape, x.dtype),
        in_specs=[pl.BlockSpec(memory_space=pltpu.HBM)] * (1 + len(after)),
        out_specs=pl.BlockSpec(memory_space=pltpu.HBM),
        input_output_aliases={0: 0},
        compiler_params=pltpu.CompilerParams(vmem_limit_bytes=MIB),
        cost_estimate=pl.CostEstimate(flops=0, bytes_accessed=0, transcendentals=0),
        name="hold",
    )(far_away(x), *[far_away(a) for a in after])


def shape(dims, dtype):
    return jax.ShapeDtypeStruct(dims, dtype)


def rms_scale(inputs):
    return lax.rsqrt(jnp.mean(inputs * inputs, -1, keepdims=True) + EPSILON)


def norm_back(inputs, gain_row, upstream):
    inverse = rms_scale(inputs)
    scaled = upstream * gain_row
    inner_mean = jnp.mean(inputs * scaled, -1, keepdims=True)
    grad_inputs = inverse * scaled - inputs * (inverse * inverse * inverse) * inner_mean
    grad_gain = jnp.sum(upstream * inputs * inverse, 0, keepdims=True)
    return grad_inputs, grad_gain


def placed(count, offset):
    index = lax.broadcasted_iota(jnp.int32, (count, LANES), 0)
    lane = lax.broadcasted_iota(jnp.int32, (count, LANES), 1)
    return one_hot(lane == index + offset)


def prepare_body(direct, in_ref, out_ref, router_ref, gains_ref, table_ref, *packets):
    share = in_ref.shape[1]
    for layer in range(LAYERS):
        for which in range(3):
            for head in range(OWN):
                for c in range(GROUP):
                    source = which * D + (head * GROUP + c) * HEAD_DIM
                    target = which * OWN_COLS + head * HEAD_DIM
                    target += layer * (PACKED + LANES)
                    packets[0][c, :, target : target + HEAD_DIM] = in_ref[
                        layer, :, source : source + HEAD_DIM
                    ]
        if direct:
            width = D // GROUP
            for q in range(GROUP):
                packets[1 + layer][q] = out_ref[layer, :, q * width : (q + 1) * width]
    small = jnp.zeros((share, LANES), f32)
    row = lax.broadcasted_iota(jnp.int32, (share, LANES), 0)
    for layer in range(LAYERS):
        top = 32 * layer
        small = small + dot(router_ref[layer], placed(router_ref.shape[1], top), 0, 0)
        small = small + dot(gains_ref[layer], placed(2, top + 16), 0, 0)
        bucket = dot(table_ref[layer : layer + 1, :], placed(table_ref.shape[1], top + 64), 1, 0)
        small = small + jnp.where(row == 0, bucket, 0.0)
    for c in range(GROUP):
        packets[0][c, :, PACKED : PACKED + LANES] = small.astype(bf16)


def prepare(direct, attn_in, attn_out, router, gains, rel_table):
    share = attn_in.shape[1]
    outs = [shape((GROUP, share, 2 * PACKED + LANES), bf16)]
    if direct:
        outs += [shape((GROUP, share, D // GROUP), bf16)] * LAYERS

    def body(*refs):
        prepare_body(direct, *refs)

    return whole_call(
        body, outs, [attn_in, attn_out, router, gains, rel_table], streamed=True, name="prepare"
    )


def unpack(place, hits, experts, pairs, layer, got):
    share = got.shape[-2]
    width = D // GROUP
    first = layer == 0

    def body(place_ref, hits_ref, got_ref, w_in_ref, w_out_ref, *rest):
        for index in range(experts * pairs):
            e, d = index // pairs, index % pairs
            for c in range(GROUP):
                owner = (e * GROUP + c) * pairs + d
                at = owner * share
                w_in_ref[at : at + share, :] = got_ref[index, c, :, :PACKED]
                w_out_ref[c, index * share : (index + 1) * share, :] = got_ref[
                    index, c, :, got_ref.shape[-1] - width :
                ]
                if first:
                    flags = got_ref[index, c, :, PACKED : PACKED + LANES].astype(f32)
                    rest[2][at : at + share, :] = flags
                    rest[3][owner : owner + 1, :] = flags[:1, :]
        if not first:
            return
        feature_ref, bias_ref, flat_ref, bucket_ref = rest
        feature_ref[...] = flat_ref[...].T
        head = lax.broadcasted_iota(jnp.int32, (8, LANES), 0)
        lane = lax.broadcasted_iota(jnp.int32, (8, LANES), 1)
        for other in range(LAYERS):
            mine = jnp.where(
                (lane == 64 + 32 * other + head * GROUP + place_ref[0]) & (head < OWN), 1.0, 0.0
            )
            table = dot(mine, bucket_ref[...], 1, 1, lax.Precision.HIGHEST)
            bias_ref[other] = dot(
                table - table[:, BUCKETS - 1 :], hits_ref[...], 1, 0, lax.Precision.HIGHEST
            )

    outs = [shape((D, PACKED), bf16), shape((GROUP, OWN_COLS, D // GROUP), bf16)]
    scratch = []
    if first:
        outs += [shape((LANES, D), f32), shape((LAYERS, 8, REACH), f32)]
        scratch = [pltpu.VMEM((D, LANES), f32), pltpu.VMEM((BUCKETS, LANES), f32)]
    return whole_call(
        body, outs, [place, hits, got], smem=1, scratch=scratch, name="unpack"
    )


def near_bias(bias_ref, layer, head, rows):
    row = bias_ref[layer, head : head + 1, :]
    return pltpu.roll(jnp.broadcast_to(row, (rows, REACH)), 0, 1, stride=1, stride_axis=0)


def masked_scores(keys, queries, near, low, key_block, query_block, rows):
    scores = dot(keys, queries, 1, 1)
    key_place = lax.broadcasted_iota(jnp.int32, (rows, rows), 0)
    seen = key_place >= low - key_block * rows
    if key_block == query_block:
        scores = scores + near[:, :rows]
        seen = seen & (key_place <= lax.broadcasted_iota(jnp.int32, (rows, rows), 1))
    elif key_block == query_block - 1:
        scores = scores + near[:, rows:]
    return jnp.where(seen, scores, NEGATIVE)


def attention_forward_body(
    layer, place_ref, n0, n1, n2, n3, w_ref, feature_ref, bias_ref, low_ref, wo_ref,
    packed_ref, log_ref, mixed_ref, keep_ref, send_ref, *normed_ref,
):
    me = place_ref[0]
    rows = n0.shape[0]
    for r, piece in enumerate((n0, n1, n2, n3)):
        normed = piece[...]
        if layer == 0:
            wide = normed.astype(f32)
            normed = (wide * rms_scale(wide) * feature_ref[16:17, :]).astype(bf16)
            normed_ref[0][r * rows : (r + 1) * rows, :] = normed
        packed_ref[r * rows : (r + 1) * rows, :] = dot(normed, w_ref[...], 1, 0).astype(bf16)
    lane = lax.broadcasted_iota(jnp.int32, (rows, LANES), 1)
    starts = [pl.multiple_of((b ^ me) * rows, rows) for b in range(GROUP)]
    for pair in range(OWN // 2):
        at = pair * LANES

        def part(b, which):
            column = which * OWN_COLS + at
            return packed_ref[pl.ds(starts[b], rows), column : column + LANES]

        sides = [(lane // HEAD_DIM) == side for side in range(2)]
        nears = [near_bias(bias_ref, layer, pair * 2 + side, rows) for side in range(2)]
        for qb in range(GROUP):
            low = low_ref[:, qb * rows : (qb + 1) * rows]
            queries = part(qb, 0) * SCORE_SCALE
            total = None
            for side in range(2):
                mine = jnp.where(sides[side], queries, 0).astype(bf16)
                tiles = [
                    masked_scores(part(kb, 1), mine, nears[side], low, kb, qb, rows)
                    for kb in range(qb + 1)
                ]
                peak = jnp.max(tiles[0], 0, keepdims=True)
                for tile in tiles[1:]:
                    peak = jnp.maximum(peak, jnp.max(tile, 0, keepdims=True))
                weight_sum = jnp.zeros((1, rows), f32)
                out = jnp.zeros((LANES, rows), f32)
                for kb, tile in enumerate(tiles):
                    power = jnp.exp(tile - peak)
                    weight_sum = weight_sum + jnp.sum(power, 0, keepdims=True)
                    values = jnp.where(sides[side], part(kb, 2), 0).astype(bf16)
                    out = out + dot(values, power.astype(bf16), 0, 0)
                out = out / weight_sum
                total = out if total is None else total + out
                head = pair * 2 + side
                log_ref[head : head + 1, qb * rows : (qb + 1) * rows] = peak + jnp.log(weight_sum)
            mixed_ref[pl.ds(starts[qb], rows), at : at + LANES] = total.T.astype(bf16)
    width = wo_ref.shape[2]
    for r, (target, offset) in enumerate(
        ((keep_ref, 0), (send_ref, 0), (keep_ref, rows), (send_ref, rows))
    ):
        mixed = mixed_ref[r * rows : (r + 1) * rows, :]
        for q in range(wo_ref.shape[0]):
            target[offset : offset + rows, q * width : (q + 1) * width] = dot(
                mixed, wo_ref[q], 1, 0
            ).astype(target.dtype)


def attention_forward(layer, place, pieces, w_in, feature, bias, low, w_out):
    rows = pieces[0].shape[0]
    total = GROUP * rows
    outs = [
        shape((total, PACKED), bf16),
        shape((8, total), f32),
        shape((total, OWN_COLS), bf16),
        shape((2 * rows, D), f32),
        shape((2 * rows, D), bf16),
    ]
    if layer == 0:
        outs.append(shape((total, D), bf16))

    def body(*refs):
        attention_forward_body(layer, *refs)

    return whole_call(
        body,
        outs,
        [place, *pieces, w_in, feature, bias, low, w_out],
        smem=1,
        flops=2 * total * D * (PACKED + OWN_COLS) + 2 * total * total * OWN_COLS * 2,
        limit=24,
        name="attention_forward",
    )


def attention_backward_body(
    layer, place_ref, d0, d1, d2, d3, w_ref, feature_ref, bias_ref, low_ref, wo_ref, packed_ref,
    log_ref, *refs,
):
    normed_refs = refs[:-8]
    (grad_packed_ref, keep_ref, send_ref, table_ref, gain_ref, grad_mixed_ref, dk_ref,
     dv_ref) = refs[-8:]
    me = place_ref[0]
    rows = d0.shape[0]
    width = wo_ref.shape[2]
    for r, piece in enumerate((d0, d1, d2, d3)):
        got = jnp.zeros((rows, OWN_COLS), f32)
        for q in range(wo_ref.shape[0]):
            got = got + dot(piece[:, q * width : (q + 1) * width], wo_ref[q], 1, 1)
        grad_mixed_ref[r * rows : (r + 1) * rows, :] = got.astype(bf16)
    lane = lax.broadcasted_iota(jnp.int32, (rows, LANES), 1)
    starts = [pl.multiple_of((b ^ me) * rows, rows) for b in range(GROUP)]
    table_ref[...] = jnp.zeros(table_ref.shape, f32)
    for pair in range(OWN // 2):
        at = pair * LANES

        def part(b, which):
            column = which * OWN_COLS + at
            return packed_ref[pl.ds(starts[b], rows), column : column + LANES]

        sides = [(lane // HEAD_DIM) == side for side in range(2)]
        nears = [near_bias(bias_ref, layer, pair * 2 + side, rows) for side in range(2)]
        diag = [jnp.zeros((rows, rows), f32) for _ in range(2)]
        before = [jnp.zeros((rows, rows), f32) for _ in range(2)]
        far = [jnp.zeros((1, rows), f32) for _ in range(2)]
        dk_ref[...] = jnp.zeros(dk_ref.shape, f32)
        dv_ref[...] = jnp.zeros(dv_ref.shape, f32)
        for qb in range(GROUP):
            low = low_ref[:, qb * rows : (qb + 1) * rows]
            queries = part(qb, 0) * SCORE_SCALE
            upstream = grad_mixed_ref[pl.ds(starts[qb], rows), at : at + LANES]
            grad_queries = jnp.zeros((LANES, rows), f32)
            for side in range(2):
                head = pair * 2 + side
                mine = jnp.where(sides[side], queries, 0).astype(bf16)
                above = jnp.where(sides[side], upstream, 0).astype(bf16)
                log_total = log_ref[head : head + 1, qb * rows : (qb + 1) * rows]
                probs, grads = [], []
                row_dot = jnp.zeros((1, rows), f32)
                for kb in range(qb + 1):
                    scores = masked_scores(part(kb, 1), mine, nears[side], low, kb, qb, rows)
                    prob = jnp.exp(scores - log_total)
                    grad = dot(part(kb, 2), above, 1, 1)
                    row_dot = row_dot + jnp.sum(prob * grad, 0, keepdims=True)
                    probs.append(prob)
                    grads.append(grad)
                for kb in range(qb + 1):
                    grad_score = probs[kb] * (grads[kb] - row_dot)
                    if kb == qb:
                        diag[side] = diag[side] + grad_score
                    elif kb == qb - 1:
                        before[side] = before[side] + grad_score
                    else:
                        far[side] = far[side] + jnp.sum(grad_score, 0, keepdims=True)
                    grad_low = grad_score.astype(bf16)
                    keys = jnp.where(sides[side], part(kb, 1), 0).astype(bf16)
                    grad_queries = grad_queries + dot(keys, grad_low, 0, 0)
                    span = slice(kb * rows, (kb + 1) * rows)
                    dk_ref[span, :] += dot(grad_low, mine, 1, 0)
                    dv_ref[span, :] += dot(probs[kb].astype(bf16), above, 1, 0)
            grad_packed_ref[pl.ds(starts[qb], rows), at : at + LANES] = (
                grad_queries.T * SCORE_SCALE
            ).astype(bf16)
        for kb in range(GROUP):
            span = slice(kb * rows, (kb + 1) * rows)
            for which, source in ((1, dk_ref), (2, dv_ref)):
                column = which * OWN_COLS + at
                grad_packed_ref[pl.ds(starts[kb], rows), column : column + LANES] = source[
                    span, :
                ].astype(bf16)
        distance = lax.broadcasted_iota(jnp.int32, (1, REACH), 1)
        for side in range(2):
            head = pair * 2 + side
            skewed = jnp.concatenate([diag[side], before[side]], 1)
            row_index = lax.broadcasted_iota(jnp.int32, (rows, REACH), 0)
            step = 1
            while step < rows:
                skewed = jnp.where(
                    (row_index & step) != 0, pltpu.roll(skewed, REACH - step, 1), skewed
                )
                step *= 2
            by_distance = jnp.sum(skewed, 0, keepdims=True)
            far_sum = jnp.sum(far[side], 1, keepdims=True)
            table_ref[head : head + 1, :] = by_distance + jnp.where(
                distance == REACH - 1, far_sum, 0.0
            )
    for r, (target, offset) in enumerate(
        ((keep_ref, 0), (send_ref, 0), (keep_ref, rows), (send_ref, rows))
    ):
        grad_normed = dot(grad_packed_ref[r * rows : (r + 1) * rows, :], w_ref[...], 1, 1)
        target[offset : offset + rows, :] = grad_normed.astype(target.dtype)
        part_gain = jnp.sum(grad_normed * block_of(normed_refs, r, rows).astype(f32), 0, keepdims=True)
        gain_sum = part_gain if r == 0 else gain_sum + part_gain
    gain_row = feature_ref[32 * layer + 16 : 32 * layer + 17, :]
    gain_ref[...] = jnp.broadcast_to(gain_sum / gain_row, gain_ref.shape)


def block_of(refs, r, rows):
    return refs[r][...] if len(refs) > 1 else refs[0][r * rows : (r + 1) * rows, :]


def attention_backward(
    layer, place, pieces, w_in, feature, bias, low, w_out, packed, log_total, normed, after=()
):
    rows = pieces[0].shape[0]
    total = GROUP * rows

    def body(*refs):
        attention_backward_body(layer, *refs)

    return whole_call(
        body,
        (
            shape((total, PACKED), bf16),
            shape((2 * rows, D), f32),
            shape((2 * rows, D), bf16),
            shape((8, REACH), f32),
            shape((8, D), f32),
        ),
        [place, *pieces, w_in, feature, bias, low, w_out, packed, log_total, *normed],
        smem=1,
        after=after,
        scratch=[
            pltpu.VMEM((total, OWN_COLS), bf16),
            pltpu.VMEM((total, LANES), f32),
            pltpu.VMEM((total, LANES), f32),
        ],
        flops=2 * total * D * (PACKED + OWN_COLS) + 2 * total * total * OWN_COLS * 5,
        limit=24,
        name="attention_backward",
    )


def dense_products(normed, upstream, grad_packed_ref, mixed_ref):
    rows = upstream[0].shape[0]
    total_in = None
    total_out = None
    for r in range(GROUP):
        span = slice(r * rows, (r + 1) * rows)
        one = dot(block_of(normed, r, rows), grad_packed_ref[span, :], 0, 0)
        two = dot(mixed_ref[span, :], upstream[r][...], 0, 0)
        total_in = one if total_in is None else total_in + one
        total_out = two if total_out is None else total_out + two
    return total_in, total_out


def dense_grads(normed, upstream, grad_packed, mixed):
    rows = upstream[0].shape[0]
    count = len(normed)

    def body(*refs):
        total_in, total_out = dense_products(
            refs[:count], refs[count : count + GROUP], refs[-4], refs[-3]
        )
        refs[-2][...] = total_in.astype(bf16)
        refs[-1][...] = total_out.astype(bf16)

    return whole_call(
        body,
        (shape((D, PACKED), bf16), shape((OWN_COLS, D), bf16)),
        [*normed, *upstream, grad_packed, mixed],
        flops=2 * GROUP * rows * D * (PACKED + OWN_COLS),
        name="dense_grads",
    )


def dense_pack(experts, pairs, share, place, normed, upstream, grad_packed, mixed, small, gain_a,
               by_distance, hits, split, after=()):
    rows = upstream[0].shape[0]
    count = len(normed)
    width = D // GROUP
    cut = EARLY_COLS if split else PACKED
    rest = PACKED - cut + LANES + width
    total = cut if split else PACKED + rest

    def body(place_ref, *refs):
        grad_packed_ref, mixed_ref, small_ref, gain_ref, distance_ref, hits_ref = refs[
            count + GROUP : count + GROUP + 6
        ]
        outs = refs[count + GROUP + 6 : -3]
        in_ref, out_ref, flat_ref = refs[-3:]
        total_in, total_out = dense_products(
            refs[:count], refs[count : count + GROUP], grad_packed_ref, mixed_ref
        )
        in_ref[...] = total_in
        out_ref[...] = total_out
        row = lax.broadcasted_iota(jnp.int32, (8, D), 0)
        gains = jnp.where(
            row == 0, gain_ref[...], jnp.where(row == 1, small_ref[16:24, :], 0.0)
        )
        features = jnp.concatenate(
            [small_ref[:16, :], gains, jnp.zeros((LANES - 24, D), f32)], 0
        )
        flat_ref[...] = features.T
        by_bucket = dot(hits_ref[...], distance_ref[...], 1, 1, lax.Precision.HIGHEST)
        head = lax.broadcasted_iota(jnp.int32, (8, LANES), 0)
        lane = lax.broadcasted_iota(jnp.int32, (8, LANES), 1)
        mine = jnp.where((lane == 64 + head * GROUP + place_ref[0]) & (head < OWN), 1.0, 0.0)
        buckets = dot(by_bucket, mine, 1, 0, lax.Precision.HIGHEST)
        for index in range(BUCKETS):
            at = index * share
            flat_ref[at : at + 1, :] = flat_ref[at : at + 1, :] + buckets[index : index + 1, :]
        for side, d in enumerate((place_ref[1], 1 - place_ref[1])):
            for e in range(experts):
                for c in range(GROUP):
                    at = ((e * GROUP + c) * pairs + d) * share
                    span = pl.ds(pl.multiple_of(at, share), share)
                    to = slice(c * share, (c + 1) * share)
                    target = outs[side]
                    target[e, to, :cut] = in_ref[span, :cut].astype(target.dtype)
                    out_span = pl.ds(pl.multiple_of((e * pairs + d) * share, share), share)
                    outer = out_ref[out_span, c * width : (c + 1) * width]
                    if split:
                        more = PACKED - cut
                        outs[2][e, side, to, :more] = in_ref[span, cut:].astype(bf16)
                        outs[2][e, side, to, more : more + LANES] = flat_ref[span, :].astype(bf16)
                        outs[2][e, side, to, more + LANES :] = outer.astype(bf16)
                    else:
                        target[e, to, PACKED : PACKED + LANES] = flat_ref[span, :].astype(
                            target.dtype
                        )
                        target[e, to, PACKED + LANES :] = outer.astype(target.dtype)

    outs = [
        shape((experts, GROUP * share, total), f32),
        shape((experts, GROUP * share, total), bf16),
    ]
    if split:
        outs.append(shape((experts, pairs, GROUP * share, rest), bf16))
    return whole_call(
        body,
        outs,
        [place, *normed, *upstream, grad_packed, mixed, small, gain_a, by_distance, hits],
        smem=1,
        scratch=[
            pltpu.VMEM((D, PACKED), f32),
            pltpu.VMEM((OWN_COLS, D), f32),
            pltpu.VMEM((D, LANES), f32),
        ],
        flops=2 * GROUP * rows * D * (PACKED + OWN_COLS),
        after=after,
        streamed=True,
        limit=32,
        name="dense_pack",
    )


def finish_dense(share, inner, outer):
    width = D // GROUP

    def body(*refs):
        in_ref, out_ref, small_ref = refs[1 + LAYERS :]
        for layer in range(LAYERS):
            got, rows_out = refs[0], refs[1 + layer]
            for c in range(GROUP):
                for which in range(3):
                    for head in range(OWN):
                        source = which * OWN_COLS + head * HEAD_DIM
                        target = which * D + (head * GROUP + c) * HEAD_DIM
                        in_ref[layer, :, target : target + HEAD_DIM] = got[
                            c, layer, :, source : source + HEAD_DIM
                        ].astype(f32)
                out_ref[layer, :, c * width : (c + 1) * width] = rows_out[
                    c * share : (c + 1) * share, :
                ]
            total = got[0, layer, :, PACKED:].astype(f32)
            for c in range(1, GROUP):
                total = total + got[c, layer, :, PACKED:].astype(f32)
            small_ref[layer] = total

    return whole_call(
        body,
        (
            shape((LAYERS, share, 3 * D), f32),
            shape((LAYERS, share, D), f32),
            shape((LAYERS, share, LANES), f32),
        ),
        [inner, *outer],
        name="finish_dense",
    )


def stacked(refs):
    return refs[0][...] if len(refs) == 1 else jnp.concatenate([ref[...] for ref in refs], 0)


def store_blocks(refs, rows):
    count = rows.shape[0] // len(refs)
    for index, ref in enumerate(refs):
        ref[...] = rows[index * count : (index + 1) * count, :].astype(ref.dtype)


def block_shapes(blocks, slots, width=D):
    return [shape((slots // blocks, width), bf16)] * blocks


def dispatch_grid(dest_rows, slots, tokens):
    place = lax.broadcasted_iota(jnp.int32, (slots, tokens), 0)
    first = place == dest_rows[0:1, :]
    second = place == dest_rows[1:2, :]
    return first, second


def one_hot(flags):
    return jnp.where(flags, 1.0, 0.0).astype(bf16)


def collect_grid(meta, slots):
    tokens = meta.shape[0]
    place = lax.broadcasted_iota(jnp.int32, (tokens, slots), 1)
    first = place == meta[:, 0:1].astype(jnp.int32)
    second = place == meta[:, 1:2].astype(jnp.int32)
    return first, second


def scatter_grads(upstream, meta, dest_rows, slots):
    tokens = upstream.shape[0]
    first, second = dispatch_grid(dest_rows, slots, tokens)
    return (
        dot(one_hot(first), (meta[:, 2:3] * upstream).astype(bf16), 1, 0)
        + dot(one_hot(second), (meta[:, 3:4] * upstream).astype(bf16), 1, 0)
    ).astype(bf16)


def slot_rows(idst, capacity, own):
    tokens = idst.shape[1]
    down = lax.broadcasted_iota(jnp.int32, (tokens, tokens), 0)
    across = lax.broadcasted_iota(jnp.int32, (tokens, tokens), 1)
    sub = lax.broadcasted_iota(jnp.int32, (16, tokens), 0)
    row0 = sub == idst[0:1, :]
    row1 = sub == idst[1:2, :]
    counts = dot(one_hot(row0 | row1), one_hot(down < across), 1, 0)
    found = []
    for index, row in enumerate((row0, row1)):
        slot = jnp.sum(jnp.where(row, counts, 0.0), 0, keepdims=True).astype(jnp.int32)
        found.append((idst[index : index + 1, :] ^ own) * capacity + slot)
    return jnp.where(lax.broadcasted_iota(jnp.int32, (8, tokens), 0) == 0, found[0], found[1])


def send_grads(experts, capacity, idst, grad, after):
    tokens = grad.shape[0]
    slots = experts * capacity

    def body(idst_ref, grad_ref, out_ref):
        first, second = dispatch_grid(slot_rows(idst_ref[...], capacity, 0), slots, tokens)
        out_ref[...] = dot(one_hot(first | second), grad_ref[...], 1, 0).astype(bf16)

    (out,) = whole_call(
        body, [shape((slots, D), bf16)], [idst, grad], after=after, name="send_grads"
    )
    return out


def apply_gates(experts, blocks, place, rows, gates):
    slots = gates.shape[0]
    capacity = slots // experts
    if blocks == 1:
        order = jnp.arange(experts) ^ place[2]
        rows = rows.reshape(experts, capacity, D)[order].reshape(slots, D)
        gates = gates.reshape(experts, capacity, LANES)[order].reshape(slots, LANES)

    def body(place_ref, rows_ref, gates_ref, *outs):
        for index, out_ref in enumerate(outs):
            span = pl.ds(0, slots)
            if blocks > 1:
                source = pl.multiple_of((index ^ place_ref[2]) * capacity, capacity)
                span = pl.ds(source, capacity)
            out_ref[...] = (gates_ref[span, 0:1] * rows_ref[span, :].astype(f32)).astype(bf16)

    return whole_call(
        body, block_shapes(blocks, slots), [place, rows, gates], smem=1, streamed=True,
        name="apply_gates",
    )


def route_body(layer, experts, capacity, last, blocks, place_ref, *refs):
    top = 32 * layer
    own = place_ref[2]
    x_ref, keep_ref, recv_ref, far_ref, feature_ref, ids_ref, idst_ref = refs[:7]
    middle_ref, soft_ref, meta_ref, dest_ref = refs[7:11]
    rows_refs = refs[11 : 11 + blocks]
    tokens = x_ref.shape[0]
    slots = experts * capacity
    middle = (
        x_ref[...].astype(f32)
        + keep_ref[:tokens, :]
        + recv_ref[:tokens, :].astype(f32)
        + far_ref[...].astype(f32)
    )
    middle_ref[...] = middle
    normed = middle * rms_scale(middle) * feature_ref[top + 17 : top + 18, :]
    lane = lax.broadcasted_iota(jnp.int32, (tokens, LANES), 1)
    logits = dot(normed, feature_ref[...], 1, 1, lax.Precision.HIGHEST)
    logits = jnp.where((lane >= top) & (lane < top + experts), logits, NEGATIVE)
    power = jnp.exp(logits - jnp.max(logits, -1, keepdims=True))
    soft = power / jnp.sum(power, -1, keepdims=True)
    soft_ref[...] = soft
    ids = ids_ref[...]
    hit0 = lane == ids[:, 0:1] + top
    hit1 = lane == ids[:, 1:2] + top
    picked0 = jnp.sum(jnp.where(hit0, soft, 0.0), -1, keepdims=True)
    picked1 = jnp.sum(jnp.where(hit1, soft, 0.0), -1, keepdims=True)
    pick_total = picked0 + picked1
    down = lax.broadcasted_iota(jnp.int32, (tokens, tokens), 0)
    across = lax.broadcasted_iota(jnp.int32, (tokens, tokens), 1)
    counts = dot(one_hot(across < down), one_hot(hit0 | hit1), 1, 0)
    dest0 = (ids[:, 0:1] ^ own).astype(f32) * capacity + jnp.sum(
        jnp.where(hit0, counts, 0.0), -1, keepdims=True
    )
    dest1 = (ids[:, 1:2] ^ own).astype(f32) * capacity + jnp.sum(
        jnp.where(hit1, counts, 0.0), -1, keepdims=True
    )
    fields = (dest0, dest1, picked0 / pick_total, picked1 / pick_total, pick_total)
    meta = jnp.zeros((tokens, LANES), f32)
    for index, field in enumerate(fields):
        meta = jnp.where(lane == index, field, meta)
    meta_ref[...] = meta
    dest_rows = slot_rows(idst_ref[...], capacity, own)
    dest_ref[...] = dest_rows
    first, second = dispatch_grid(dest_rows, slots, tokens)
    store_blocks(rows_refs, dot(one_hot(first | second), normed.astype(bf16), 1, 0))
    if last:
        total = None
        place = lax.broadcasted_iota(jnp.int32, (slots, tokens), 0)
        for index in range(2):
            slot = dest_rows[index : index + 1, :] - (idst_ref[index : index + 1, :] ^ own) * capacity
            flags = place == slot + idst_ref[index : index + 1, :] * capacity
            gate = meta[:, 2 + index : 3 + index]
            spread = jnp.zeros((tokens, LANES), f32)
            for term in range(3):
                piece = gate.astype(bf16).astype(f32)
                spread = jnp.where(lane == term, piece, spread)
                gate = gate - piece
            got = dot(one_hot(flags), spread.astype(bf16), 1, 0)
            total = got if total is None else total + got
        refs[-1][...] = jnp.broadcast_to(jnp.sum(total, -1, keepdims=True), total.shape)


def route(
    layer, experts, capacity, blocks, place, x, keep, recv, far, feature, ids, idst, last, after=()
):
    tokens = x.shape[0]
    slots = experts * capacity
    outs = [
        shape((tokens, D), f32),
        shape((tokens, LANES), f32),
        shape((tokens, LANES), f32),
        shape((8, tokens), jnp.int32),
    ] + block_shapes(blocks, slots)
    if last:
        outs.append(shape((slots, LANES), f32))

    def body(*refs):
        route_body(layer, experts, capacity, last, blocks, *refs)

    return whole_call(
        body, outs, [place, x, keep, recv, far, feature, ids, idst], smem=1,
        flops=2 * slots * tokens * D, after=after, name="route",
    )


def combine(middle, back, meta, feature=None):
    tokens = middle.shape[0]
    count = len(back)
    last = feature is None
    args = [middle, meta, *back]
    outs = [shape((tokens, D), bf16 if last else f32)]
    if not last:
        args.append(feature)
        outs.append(shape((tokens, D), bf16))

    def body(middle_ref, meta_ref, *refs):
        meta = meta_ref[...]
        rows = stacked(refs[:count])
        first, second = collect_grid(meta, rows.shape[0])
        x = (
            middle_ref[...]
            + meta[:, 2:3] * dot(one_hot(first), rows, 1, 0)
            + meta[:, 3:4] * dot(one_hot(second), rows, 1, 0)
        )
        if last:
            refs[-1][...] = x.astype(bf16)
        else:
            refs[-2][...] = x
            refs[-1][...] = (x * rms_scale(x) * refs[count][48:49, :]).astype(bf16)

    return whole_call(
        body, outs, args, flops=4 * tokens * D * count * back[0].shape[0], name="combine"
    )


def expert_token_back_body(
    layer, back_refs, came_refs, g_ref, middle_ref, soft_ref, meta_ref, ids_ref, feature_ref,
    dmiddle_ref, dattn_ref, small_ref,
):
    back, came = stacked(back_refs), stacked(came_refs)
    top = 32 * layer
    gain_row = feature_ref[top + 17 : top + 18, :]
    meta = meta_ref[...]
    g = g_ref[...].astype(f32)
    slots = back.shape[0]
    first, second = collect_grid(meta, slots)
    grad_gate0 = jnp.sum(g * dot(one_hot(first), back, 1, 0), -1, keepdims=True)
    grad_gate1 = jnp.sum(g * dot(one_hot(second), back, 1, 0), -1, keepdims=True)
    grad_normed = dot(one_hot(first | second), came, 1, 0)
    gap = (grad_gate0 - grad_gate1) / meta[:, 4:5]
    ids = ids_ref[...]
    lane = lax.broadcasted_iota(jnp.int32, meta.shape, 1)
    grad_soft = jnp.where(lane == ids[:, 0:1] + top, meta[:, 3:4] * gap, 0.0) + jnp.where(
        lane == ids[:, 1:2] + top, -meta[:, 2:3] * gap, 0.0
    )
    soft = soft_ref[...]
    grad_logits = soft * (grad_soft - jnp.sum(soft * grad_soft, -1, keepdims=True))
    middle = middle_ref[...]
    normed = middle * rms_scale(middle) * gain_row
    grad_router = dot(grad_logits.T, normed, 1, 0, lax.Precision.HIGHEST)
    grad_normed = grad_normed + dot(
        grad_logits, feature_ref[...], 1, 0, lax.Precision.HIGHEST
    )
    grad_branch, grad_gain = norm_back(middle, gain_row, grad_normed)
    dmiddle = g + grad_branch
    dmiddle_ref[...] = dmiddle
    dattn_ref[...] = dmiddle.astype(bf16)
    small_ref[:16, :] = grad_router[top : top + 16, :]
    small_ref[16:24, :] = jnp.broadcast_to(grad_gain, (8, D))


def expert_token_back(layer, back, came, g, middle, soft, meta, ids, feature, after=()):
    tokens = middle.shape[0]

    def body(*refs):
        count = len(back)
        expert_token_back_body(layer, refs[:count], refs[count : 2 * count], *refs[2 * count :])

    return whole_call(
        body,
        (shape((tokens, D), f32), shape((tokens, D), bf16), shape((24, D), f32)),
        [*back, *came, g, middle, soft, meta, ids, feature],
        after=after,
        flops=6 * tokens * D * len(back) * back[0].shape[0],
        streamed=True,
        limit=32,
        name="expert_token_back",
    )


def attention_token_back_body(layer, *refs):
    if layer == 0:
        x_ref, dmiddle_ref, keep_ref, recv_ref, far_ref, feature_ref, out_ref = refs
    else:
        (x_ref, dmiddle_ref, keep_ref, recv_ref, far_ref, feature_ref, meta_ref, dest_ref,
         out_ref, *sent_refs) = refs
    tokens = x_ref.shape[0]
    grad_normed = (
        keep_ref[:tokens, :] + recv_ref[:tokens, :].astype(f32) + far_ref[...].astype(f32)
    )
    gain_row = feature_ref[32 * layer + 16 : 32 * layer + 17, :]
    grad_branch, _ = norm_back(x_ref[...].astype(f32), gain_row, grad_normed)
    g = dmiddle_ref[...] + grad_branch
    out_ref[...] = g
    if layer > 0:
        slots = len(sent_refs) * sent_refs[0].shape[0]
        store_blocks(sent_refs, scatter_grads(g, meta_ref[...], dest_ref[...], slots))


def attention_token_back(
    layer, x, dmiddle, keep, recv, far, feature, meta=None, dest=None, blocks=1, slots=0, after=()
):
    tokens = x.shape[0]
    outs = [shape((tokens, D), f32)]
    args = [x, dmiddle, keep, recv, far, feature]
    if meta is not None:
        outs += block_shapes(blocks, slots)
        args += [meta, dest]

    def body(*refs):
        attention_token_back_body(layer, *refs)

    return whole_call(
        body, outs, args, flops=4 * tokens * D * slots, after=after, name="attention_token_back"
    )


def gelu_parts(gate):
    inner = math.sqrt(2.0 / math.pi) * (gate + 0.044715 * gate * gate * gate)
    return jnp.tanh(inner)


def weight_specs(layer, tile):
    return [
        pl.BlockSpec((1, 1, D, tile), lambda s: (layer, 0, 0, s)),
        pl.BlockSpec((1, 1, D, tile), lambda s: (layer, 0, 0, FF // tile + s)),
        pl.BlockSpec((1, 1, D, tile), lambda s: (layer, 0, 0, s)),
    ]


def block_specs(blocks):
    return [pl.BlockSpec(b.shape, lambda s: (0, 0)) for b in blocks]


def expert_call(body, steps, outs, out_specs, args, in_specs, scratch, limit, after, name):
    used = len(args)

    def ordered(*refs):
        body(*refs[:used], *refs[used + len(after) :])

    count = ROWS_HINT
    return pl.pallas_call(
        ordered,
        grid=(steps,),
        out_shape=tuple(outs),
        in_specs=list(in_specs) + [pl.BlockSpec(memory_space=pltpu.HBM)] * len(after),
        out_specs=tuple(out_specs),
        scratch_shapes=list(scratch),
        compiler_params=pltpu.CompilerParams(vmem_limit_bytes=limit * MIB),
        cost_estimate=pl.CostEstimate(
            flops=6 * count * D * FF, bytes_accessed=6 * D * FF, transcendentals=count * FF
        ),
        name=name,
    )(*args, *[far_away(a) for a in after])


def expert_forward(layer, blocks, w_in, w_out, after=()):
    number = len(blocks)
    count = number * blocks[0].shape[0]
    steps = FF // WIDE_TILE

    def body(*refs):
        wg_ref, wu_ref, wo_ref = refs[number : number + 3]
        produced_refs = refs[number + 3 : 2 * number + 3]
        acts_ref, rows_ref, total_ref = refs[2 * number + 3 :]
        step = pl.program_id(0)

        @pl.when(step == 0)
        def _():
            rows_ref[...] = stacked(refs[:number])

        rows = rows_ref[...]
        gate = dot(rows, wg_ref[0, 0], 1, 0)
        up = dot(rows, wu_ref[0, 0], 1, 0)
        acts_ref[0] = gate.astype(bf16)
        acts_ref[1] = up.astype(bf16)
        hidden = (0.5 * gate * (1.0 + gelu_parts(gate)) * up).astype(bf16)
        out = dot(hidden, wo_ref[0, 0], 1, 1)

        @pl.when(step == 0)
        def _():
            total_ref[...] = out

        @pl.when(step == steps - 1)
        def _():
            store_blocks(produced_refs, total_ref[...] + out)

    *produced, acts = expert_call(
        body,
        steps,
        [shape(b.shape, bf16) for b in blocks] + [pltpu.HBM((2, count, FF), bf16)],
        block_specs(blocks) + [pl.BlockSpec((2, count, WIDE_TILE), lambda s: (0, 0, s))],
        [*blocks, far_away(w_in), far_away(w_in), far_away(w_out)],
        block_specs(blocks) + weight_specs(layer, WIDE_TILE),
        [pltpu.VMEM((count, D), bf16), pltpu.VMEM((count, D), f32)],
        56,
        after,
        "expert_forward",
    )
    return produced, acts


def expert_backward(layer, blocks, out_blocks, acts, w_in, w_out, after=()):
    number = len(blocks)
    count = number * blocks[0].shape[0]
    steps = FF // WIDE_TILE
    outs = block_shapes(out_blocks, count)

    def body(*refs):
        acts_refs = refs[number : number + len(acts)]
        wg_ref, wu_ref, wo_ref, *rest = refs[number + len(acts) :]
        drows_refs = rest[:out_blocks]
        parts_ref, grad_ref, total_ref = rest[out_blocks:]
        step = pl.program_id(0)

        @pl.when(step == 0)
        def _():
            grad_ref[...] = stacked(refs[:number])

        grad_hidden = dot(grad_ref[...], wo_ref[0, 0], 1, 0)
        gate = jnp.concatenate([ref[0] for ref in acts_refs], 0).astype(f32)
        up = jnp.concatenate([ref[1] for ref in acts_refs], 0).astype(f32)
        curve = gelu_parts(gate)
        value = 0.5 * gate * (1.0 + curve)
        slope = 0.5 * (1.0 + curve) + 0.5 * gate * (1.0 - curve * curve) * math.sqrt(
            2.0 / math.pi
        ) * (1.0 + 3.0 * 0.044715 * gate * gate)
        grad_gate = (grad_hidden * up * slope).astype(bf16)
        grad_up = (grad_hidden * value).astype(bf16)
        parts_ref[0] = grad_gate
        parts_ref[1] = grad_up
        parts_ref[2] = (value * up).astype(bf16)
        out = dot(grad_gate, wg_ref[0, 0], 1, 1) + dot(grad_up, wu_ref[0, 0], 1, 1)

        @pl.when(step == 0)
        def _():
            total_ref[...] = out

        @pl.when(step == steps - 1)
        def _():
            store_blocks(drows_refs, total_ref[...] + out)

    *drows, parts = expert_call(
        body,
        steps,
        outs + [pltpu.HBM((3, count, FF), bf16)],
        block_specs(outs) + [pl.BlockSpec((3, count, WIDE_TILE), lambda s: (0, 0, s))],
        [*blocks, *[far_away(a) for a in acts], far_away(w_in), far_away(w_in), far_away(w_out)],
        block_specs(blocks)
        + [pl.BlockSpec((2, a.shape[1], WIDE_TILE), lambda s: (0, 0, s)) for a in acts]
        + weight_specs(layer, WIDE_TILE),
        [pltpu.VMEM((count, D), bf16), pltpu.VMEM((count, D), f32)],
        58,
        after,
        "expert_backward",
    )
    return drows, parts


def expert_grads(shares, rows, grads, parts, after=()):
    count = len(rows) * rows[0].shape[0]
    tall = D // shares
    first = len(rows)
    second = first + len(grads)
    third = second + len(parts)

    def body(*refs):
        out_ref, rows_t, grad_t = refs[third:]

        @pl.when(pl.program_id(0) == 0)
        def _():
            rows_t[...] = stacked(refs[:first]).T
            grad_t[...] = stacked(refs[first:second]).T

        for which in range(3):
            left = rows_t if which < 2 else grad_t
            right = [ref[which] for ref in refs[second:third]]
            right = right[0] if len(right) == 1 else jnp.concatenate(right, 0)
            got = dot(left[...], right, 1, 0).astype(bf16)
            for share in range(shares):
                out_ref[share, which] = got[share * tall : (share + 1) * tall, :]

    (out,) = expert_call(
        body,
        FF_STEPS,
        [pltpu.HBM((shares, 3, tall, FF), bf16)],
        [pl.BlockSpec((shares, 3, tall, FF_TILE), lambda s: (0, 0, 0, s))],
        [*rows, *grads, *[far_away(p) for p in parts]],
        block_specs(rows)
        + block_specs(grads)
        + [pl.BlockSpec((3, p.shape[1], FF_TILE), lambda s: (0, 0, s)) for p in parts],
        [pltpu.VMEM((D, count), bf16), pltpu.VMEM((D, count), bf16)],
        32,
        after,
        "expert_grads",
    )
    return out


def place_expert_grads(layer, summed, before=None, after=()):
    tall = summed.shape[1]
    outs = (
        pltpu.HBM((LAYERS, 1, tall, 2 * FF), f32),
        pltpu.HBM((LAYERS, 1, tall, FF), f32),
    )
    held = [] if before is None else list(before)

    def body(part_ref, out_part_ref, *refs):
        in_ref, out_ref = refs[-2:]
        in_ref[0, 0] = part_ref[0].astype(f32)
        out_ref[0, 0] = out_part_ref[0].astype(f32)

    return pl.pallas_call(
        body,
        grid=(2,),
        out_shape=outs,
        in_specs=[
            pl.BlockSpec((1, tall, FF), lambda s: (s, 0, 0)),
            pl.BlockSpec((1, tall, FF), lambda s: (2, 0, 0)),
        ]
        + [pl.BlockSpec(memory_space=pl.ANY)] * (len(held) + len(after)),
        out_specs=(
            pl.BlockSpec((1, 1, tall, FF), lambda s: (layer, 0, 0, s)),
            pl.BlockSpec((1, 1, tall, FF), lambda s: (layer, 0, 0, 0)),
        ),
        input_output_aliases={2: 0, 3: 1} if held else {},
        compiler_params=pltpu.CompilerParams(vmem_limit_bytes=32 * MIB),
        name="place_expert_grads",
    )(far_away(summed), far_away(summed), *[far_away(h) for h in [*held, *after]])


TWIN = [(i, i ^ 1) for i in range(GROUP)]
ACROSS = [(i, i ^ 2) for i in range(GROUP)]
FLIP = [(0, 1), (1, 0)]


def share_pieces(piece):
    across = lax.ppermute(piece, "context", ACROSS)
    twin = lax.ppermute(piece, "context", TWIN)
    return [piece, twin, across, lax.ppermute(across, "context", TWIN)]


def sum_pieces(keep, send, after=()):
    rows = keep.shape[0] // 2
    recv = lax.ppermute(send, "context", TWIN)
    other = (keep[rows:] + recv[rows:].astype(f32)).astype(bf16)
    if after:
        other = hold(other, after)
    return keep, recv, lax.ppermute(other, "context", ACROSS)


def sum_zone(zone):
    return jnp.sum(zone.astype(f32), 0)


def dense_sum(
    experts, pairs, share, table_share, place, grad_w_in, grad_w_out, small, gain_a, by_distance,
    hits,
):
    by_bucket = jnp.dot(hits, by_distance[:OWN].T, precision=lax.Precision.HIGHEST)
    buckets = jnp.where(
        jnp.arange(GROUP)[None, None, :] == place[0], by_bucket[:, :, None], 0.0
    ).reshape(experts, GROUP, pairs, 1, table_share)
    features = jnp.concatenate([small[:16], gain_a[:1], small[16:17]], 0).T
    features = features.reshape(experts, GROUP, pairs, share, 18)
    flat = jnp.zeros((experts, GROUP, pairs, share, LANES), f32)
    flat = flat.at[..., :18].set(features).at[..., :1, 64 : 64 + table_share].set(buckets)
    pack = jnp.concatenate(
        [grad_w_in.reshape(experts, GROUP, pairs, share, PACKED), flat.astype(bf16)], -1
    ).transpose(0, 2, 1, 3, 4)
    pack = pack.reshape(experts * pairs, GROUP * share, PACKED + LANES)
    mine = lax.psum_scatter(pack, ("experts", "dp"), scatter_dimension=0, tiled=False)
    inner = lax.all_to_all(
        mine.reshape(GROUP, share, PACKED + LANES), "context", split_axis=0, concat_axis=0
    ).astype(f32)
    g_in = inner[..., :PACKED].reshape(GROUP, share, 3, OWN, HEAD_DIM)
    g_in = g_in.transpose(1, 2, 3, 0, 4).reshape(share, 3 * D)
    placed_rows = jnp.where(
        jnp.arange(GROUP)[None, :, None, None] == place[0],
        grad_w_out.reshape(OWN, 1, HEAD_DIM, D),
        jnp.zeros((), bf16),
    ).reshape(D, D)
    g_out = lax.psum_scatter(placed_rows, ALL, scatter_dimension=0, tiled=True).astype(f32)
    return g_in, g_out, jnp.sum(inner[..., PACKED:], 0)


def exchange(rows):
    return lax.all_to_all(rows, "experts", split_axis=0, concat_axis=0, tiled=True)


def swap(blocks, experts):
    split = blocks if len(blocks) > 1 else jnp.split(blocks[0], experts)
    moved = [
        part if k == 0 else lax.ppermute(part, "experts", [(i, i ^ k) for i in range(experts)])
        for k, part in enumerate(split)
    ]
    return moved if len(blocks) > 1 else [jnp.concatenate(moved)]


def on_device(
    tokens, doc_starts, expert_ids, attn_in, attn_out, router, gains, rel_table,
    expert_in, expert_out, out_grad,
):
    experts = lax.axis_size("experts")
    pairs = lax.axis_size("dp")
    share = attn_in.shape[1]
    table_share = rel_table.shape[1]
    direct = share * pairs == HEAD_DIM and experts * GROUP == HEADS and pairs == 2
    place = jnp.stack(
        [lax.axis_index("context"), lax.axis_index("dp"), lax.axis_index("experts")]
    ).astype(jnp.int32)
    start_tokens = tokens[0]
    ids = expert_ids[0]
    idst = ids.T
    rows = start_tokens.shape[0]
    capacity = (10 * rows + 4 * experts - 1) // (4 * experts)
    slots = experts * capacity
    blocks = experts if experts == 4 and capacity % 16 == 0 else 1
    fine = [(0, 1), (2,), (3,)] if blocks == 4 else [(0,)]
    coarse = [(0, 1), (2, 3)] if blocks == 4 else [(0,)]
    grad_in = out_grad[0]
    hits = jnp.asarray(bucket_hits())

    packets = prepare(
        direct, attn_in, attn_out, router.transpose(0, 2, 1), gains.transpose(0, 2, 1), rel_table
    )

    def spread(packet):
        return lax.all_to_all(packet, "context", split_axis=0, concat_axis=0)

    def gather(part):
        return lax.all_gather(part, ("experts", "dp"), axis=0, tiled=False).reshape(
            experts, pairs, *part.shape
        )

    if direct:
        packet = spread(packets[0])
        top = PACKED + LANES

        def together(columns, rows_out):
            part = jnp.concatenate([columns, rows_out], -1)
            return lax.all_gather(part, ("experts", "dp"), axis=0, tiled=False)

        first = together(packet[..., :top], packets[1])
        w_in0, w_out0, feature, bias = unpack(place, hits, experts, pairs, 0, first)
        second = [together(packet[..., top:], packets[2])]
        w_in1, w_out1 = unpack(place, hits, experts, pairs, 1, second[0])
        w_in, w_out = [w_in0, w_in1], [w_out0, w_out1]
    else:
        second = []
        w_in, w_out = [], []
        for layer in range(LAYERS):
            at = layer * (PACKED + LANES)
            part = spread(packets[0])[..., at : at + PACKED + LANES]
            got = gather(part).transpose(0, 2, 1, 3, 4)
            w_in.append(got[..., :PACKED].reshape(D, PACKED))
            if layer == 0:
                small_all = got[..., PACKED : PACKED + LANES]
            full = lax.all_gather(attn_out[layer], ALL, axis=0, tiled=True)
            mine = lax.dynamic_index_in_dim(
                full.reshape(OWN, GROUP, HEAD_DIM, D), place[0], 1, keepdims=False
            )
            w_out.append(mine.reshape(OWN_COLS, GROUP, D // GROUP).transpose(1, 0, 2))
        feature = small_all.reshape(D, LANES).astype(f32).T
        bias_rows = []
        for layer in range(LAYERS):
            at = 64 + 32 * layer
            table = small_all[:, :, :, 0, at : at + table_share].reshape(BUCKETS, OWN, GROUP)
            table = lax.dynamic_index_in_dim(table, place[0], 2, keepdims=False).astype(f32)
            row = jnp.dot((table - table[-1:]).T, hits, precision=lax.Precision.HIGHEST)
            bias_rows.append(jnp.pad(row, ((0, 8 - OWN), (0, 0))))
        bias = jnp.stack(bias_rows)
    places = jnp.arange(GROUP * rows, dtype=jnp.int32)
    starts = doc_starts[0]
    low = jnp.max(
        jnp.where(starts[:, None] <= places[None, :], starts[:, None], 0), 0, keepdims=True
    )

    pieces = share_pieces(start_tokens)
    x = start_tokens
    kept = []
    for layer in range(LAYERS):
        packed, log_total, mixed, keep, send, *normed_all = attention_forward(
            layer, place, pieces, w_in[layer], feature, bias, low, w_out[layer]
        )
        normed_rows = normed_all if layer == 0 else pieces
        last = layer == LAYERS - 1
        keep, recv, far = sum_pieces(keep, send, [arrived_grad] if last else [])
        middle, soft, meta, dest, *sent = route(
            layer, experts, capacity, blocks, place, x, keep, recv, far, feature, ids, idst, last,
        )
        arrived = swap(sent[:blocks], experts)
        if last:
            gates = exchange(sent[blocks])
        produced, acts, drows, parts = [], [], [], []
        order = []
        for chunk in coarse if last else fine:
            done, kept_acts = expert_forward(
                layer, [arrived[k] for k in chunk], expert_in, expert_out, after=order
            )
            produced += done
            acts.append(kept_acts)
            order = done[:1] + (second if layer == 0 and len(acts) == 1 else [])
            if last:
                if not drows:
                    arrived_grad = apply_gates(experts, blocks, place, arrived_grad, gates)
                done, some = expert_backward(
                    layer, [arrived_grad[k] for k in chunk], len(chunk), acts[-1:], expert_in,
                    expert_out,
                )
                drows += done
                parts.append(some)
                order = done[:1]
        back = swap(produced, experts)
        kept.append(
            (x, normed_rows, packed, log_total, mixed, middle, soft, meta, dest, arrived, acts, back)
        )
        if last:
            (result,) = combine(middle, back, meta)
        else:
            x, normed = combine(middle, back, meta, feature)
            ungated = send_grads(experts, capacity, idst, grad_in, [x])
            arrived_grad = exchange(ungated)
            pieces = share_pieces(hold(normed, [ungated]))

    g = grad_in
    inner, outer, expert_totals = [], [], []
    other = None
    placed_grads = None
    for layer in range(LAYERS - 1, -1, -1):
        (x, normed_rows, packed, log_total, mixed, middle, soft, meta, dest, arrived, acts,
         back) = kept[layer]
        if layer < LAYERS - 1:
            drows, parts = [], []
            for index, chunk in enumerate(coarse):
                some_acts = acts[:1] if index == 0 else acts[1:]
                done, some = expert_backward(
                    layer, [arrived_grad[k] for k in chunk], len(chunk), some_acts, expert_in,
                    expert_out, after=drows[-1:],
                )
                drows += done
                parts.append(some)
        came = swap(drows, experts)
        early = [] if other is None else [other]
        weight_grads = expert_grads(
            GROUP * pairs, arrived, arrived_grad, parts, after=(back if layer else []) + early
        )
        weight_grads = hold(weight_grads, came)
        total = lax.psum_scatter(
            weight_grads, ("context", "dp"), scatter_dimension=0, tiled=False
        )
        dmiddle, dattn, small_b = expert_token_back(
            layer, back, came, g, middle, soft, meta, ids, feature, after=[weight_grads]
        )
        zones = []
        if direct and other is not None:
            ours = hold(keep_dense, [dattn]) + other.astype(f32)
            zones = [exchange(ours.astype(bf16))]
        expert_totals.append(total)
        grad_pieces = share_pieces(dattn)
        grad_packed, keep, send, by_distance, gain_a = attention_backward(
            layer, place, grad_pieces, w_in[layer], feature, bias, low, w_out[layer], packed,
            log_total, normed_rows,
        )
        keep, recv, far = sum_pieces(keep, send)
        if layer > 0:
            below = kept[layer - 1]
            g, *sent = attention_token_back(
                layer, x, dmiddle, keep, recv, far, feature, below[7], below[8], blocks, slots
            )
            arrived_grad = swap(sent, experts)
        else:
            placed_grads = place_expert_grads(layer + 1, expert_totals[0])
            (g,) = attention_token_back(
                layer, x, dmiddle, keep, recv, far, feature, after=[placed_grads[0]]
            )
        if direct:
            keep_dense, send_dense, *rest = dense_pack(
                experts, pairs, share, place, normed_rows, grad_pieces, grad_packed, mixed,
                small_b, gain_a, by_distance, hits, split=layer == 0, after=zones,
            )
            other = lax.ppermute(send_dense, "dp", FLIP)
            if layer == 0:
                (zone,) = zones
                total = sum_zone(zone)
                flats = [total[:, : PACKED + LANES].astype(bf16)]
                outer.append(total[:, PACKED + LANES :])
                rest = sum_zone(exchange(rest[0]))
                theirs = lax.ppermute(rest[1].astype(bf16), "dp", FLIP)
                rest = rest[0] + theirs.astype(f32)
                ours = hold(keep_dense, [g, result, placed_grads[0]]) + other.astype(f32)
                total = sum_zone(exchange(ours.astype(bf16)))
                more = PACKED + LANES - EARLY_COLS
                flats.insert(0, jnp.concatenate([total, rest[:, :more]], -1).astype(bf16))
                outer.append(rest[:, more:])
                flat = jnp.stack([flat.reshape(GROUP, share, -1) for flat in flats], 1)
                inner = spread(flat)
        else:
            grad_w_in, grad_w_out = dense_grads(normed_rows, grad_pieces, grad_packed, mixed)
            inner.append(
                dense_sum(
                    experts, pairs, share, table_share, place, grad_w_in, grad_w_out, small_b,
                    gain_a, by_distance, hits,
                )
            )
    expert_grads_all = place_expert_grads(0, expert_totals[1], placed_grads)
    if direct:
        grad_attn_in, grad_attn_out, small_grad = finish_dense(
            share, inner, outer[::-1]
        )
    else:
        grad_attn_in, grad_attn_out, small_grad = (
            jnp.stack([entry[k] for entry in inner[::-1]]) for k in range(3)
        )
    return (
        result[None],
        g[None],
        grad_attn_in,
        grad_attn_out,
        small_grad[..., :experts],
        small_grad[..., 16:18],
        small_grad[:, 0, 64 : 64 + table_share],
        *expert_grads_all,
    )


def solution(mesh):
    return jax.shard_map(
        on_device,
        mesh=mesh,
        in_specs=(
            P(("experts", "dp"), "context", None),
            P(("experts", "dp"), None),
            P(("experts", "dp"), "context", None),
            P(None, ("experts", "context", "dp"), None),
            P(None, ("experts", "context", "dp"), None),
            P(None, ("experts", "context", "dp"), None),
            P(None, ("experts", "context", "dp"), None),
            P(None, ("experts", "context", "dp")),
            P(None, "experts", None, None),
            P(None, "experts", None, None),
            P(("experts", "dp"), "context", None),
        ),
        out_specs=(
            P(("experts", "dp"), "context", None),
            P(("experts", "dp"), "context", None),
            P(None, ("experts", "context", "dp"), None),
            P(None, ("experts", "context", "dp"), None),
            P(None, ("experts", "context", "dp"), None),
            P(None, ("experts", "context", "dp"), None),
            P(None, ("experts", "context", "dp")),
            P(None, "experts", ("context", "dp"), None),
            P(None, "experts", ("context", "dp"), None),
        ),
        check_vma=False,
    )
```

```python
import math

import jax
import jax.numpy as jnp
import numpy as np
from jax import lax
from jax.experimental import pallas as pl
from jax.experimental.pallas import tpu as pltpu
from jax.sharding import PartitionSpec as P

D = 1024
HEADS = 16
HEAD_DIM = 64
FF = 2816
BUCKETS = 32
MAX_DISTANCE = 128
LAYERS = 2
EPSILON = 1e-06
NEGATIVE = -1e30
SCORE_SCALE = 0.125
ALL = ("experts", "context", "dp")
GROUP = 4
OWN = HEADS // GROUP
OWN_COLS = OWN * HEAD_DIM
PACKED = 3 * OWN_COLS
LANES = 128
REACH = 512
FF_TILE = 256
FF_STEPS = FF // FF_TILE
WIDE_TILE = FF // 2
EARLY_COLS = 512
ROWS_HINT = 320
MIB = 1 << 20

bf16 = jnp.bfloat16
f32 = jnp.float32


def bucket_bounds(bucket_count, far_reach):
    half_count = bucket_count // 2
    bounds = list(range(1, half_count + 1))
    for section_index in range(1, half_count):
        bounds.append(
            int(math.ceil(half_count * (far_reach / half_count) ** (section_index / half_count)))
        )
    return np.array(bounds, np.int32)


def bucket_hits():
    distance = np.arange(REACH)
    bucket = (distance[:, None] >= bucket_bounds(BUCKETS, MAX_DISTANCE)).sum(-1)
    return (np.arange(BUCKETS)[:, None] == bucket[None, :]).astype(np.float32)


def dot(a, b, ca, cb, precision=None):
    return lax.dot_general(
        a, b, (((ca,), (cb,)), ((), ())), precision=precision, preferred_element_type=f32
    )


def whole_call(
    body, out_shape, args, *, flops=0, limit=16, scratch=(), smem=0, name=None, after=(),
    streamed=False,
):
    specs = [pl.BlockSpec(memory_space=pltpu.SMEM)] * smem + [
        pl.BlockSpec(memory_space=pltpu.VMEM)
    ] * (len(args) - smem)
    outs = tuple(out_shape)
    moved = sum(a.size * a.dtype.itemsize for a in list(args) + list(outs))
    specs += [pl.BlockSpec(memory_space=pltpu.HBM)] * len(after)
    used = len(args)
    args = list(args) + [far_away(a) for a in after]

    def ordered(*refs):
        body(*refs[:used], *refs[used + len(after) :])

    if streamed:
        args = args[:smem] + [far_away(a) for a in args[smem:]]

        def full(a):
            return pl.BlockSpec(a.shape, lambda i: (0,) * len(a.shape))

        return pl.pallas_call(
            ordered,
            grid=(1,),
            out_shape=outs,
            in_specs=specs[:smem] + [full(a) for a in args[smem:used]] + specs[used:],
            out_specs=tuple(full(o) for o in outs),
            scratch_shapes=list(scratch),
            compiler_params=pltpu.CompilerParams(vmem_limit_bytes=limit * MIB),
            cost_estimate=pl.CostEstimate(
                flops=int(flops), bytes_accessed=int(moved), transcendentals=0
            ),
            name=name,
        )(*args)
    return pl.pallas_call(
        ordered,
        out_shape=outs,
        in_specs=specs,
        out_specs=tuple(pl.BlockSpec(memory_space=pltpu.VMEM) for _ in outs),
        scratch_shapes=list(scratch),
        compiler_params=pltpu.CompilerParams(vmem_limit_bytes=limit * MIB),
        cost_estimate=pl.CostEstimate(
            flops=int(flops), bytes_accessed=int(moved), transcendentals=0
        ),
        name=name,
    )(*args)


def far_away(x):
    return pltpu.with_memory_space_constraint(x, pltpu.HBM)


def hold(x, after):
    def body(*refs):
        pass

    return pl.pallas_call(
        body,
        out_shape=pltpu.HBM(x.shape, x.dtype),
        in_specs=[pl.BlockSpec(memory_space=pltpu.HBM)] * (1 + len(after)),
        out_specs=pl.BlockSpec(memory_space=pltpu.HBM),
        input_output_aliases={0: 0},
        compiler_params=pltpu.CompilerParams(vmem_limit_bytes=MIB),
        cost_estimate=pl.CostEstimate(flops=0, bytes_accessed=0, transcendentals=0),
        name="hold",
    )(far_away(x), *[far_away(a) for a in after])


def shape(dims, dtype):
    return jax.ShapeDtypeStruct(dims, dtype)


def rms_scale(inputs):
    return lax.rsqrt(jnp.mean(inputs * inputs, -1, keepdims=True) + EPSILON)


def norm_back(inputs, gain_row, upstream):
    inverse = rms_scale(inputs)
    scaled = upstream * gain_row
    inner_mean = jnp.mean(inputs * scaled, -1, keepdims=True)
    grad_inputs = inverse * scaled - inputs * (inverse * inverse * inverse) * inner_mean
    grad_gain = jnp.sum(upstream * inputs * inverse, 0, keepdims=True)
    return grad_inputs, grad_gain


def placed(count, offset):
    index = lax.broadcasted_iota(jnp.int32, (count, LANES), 0)
    lane = lax.broadcasted_iota(jnp.int32, (count, LANES), 1)
    return one_hot(lane == index + offset)


def prepare_body(direct, in_ref, out_ref, router_ref, gains_ref, table_ref, *packets):
    share = in_ref.shape[1]
    for layer in range(LAYERS):
        for which in range(3):
            for head in range(OWN):
                for c in range(GROUP):
                    source = which * D + (head * GROUP + c) * HEAD_DIM
                    target = which * OWN_COLS + head * HEAD_DIM
                    target += layer * (PACKED + LANES)
                    packets[0][c, :, target : target + HEAD_DIM] = in_ref[
                        layer, :, source : source + HEAD_DIM
                    ]
        if direct:
            width = D // GROUP
            for q in range(GROUP):
                packets[1 + layer][q] = out_ref[layer, :, q * width : (q + 1) * width]
    small = jnp.zeros((share, LANES), f32)
    row = lax.broadcasted_iota(jnp.int32, (share, LANES), 0)
    for layer in range(LAYERS):
        top = 32 * layer
        small = small + dot(router_ref[layer], placed(router_ref.shape[1], top), 0, 0)
        small = small + dot(gains_ref[layer], placed(2, top + 16), 0, 0)
        bucket = dot(table_ref[layer : layer + 1, :], placed(table_ref.shape[1], top + 64), 1, 0)
        small = small + jnp.where(row == 0, bucket, 0.0)
    for c in range(GROUP):
        packets[0][c, :, PACKED : PACKED + LANES] = small.astype(bf16)


def prepare(direct, attn_in, attn_out, router, gains, rel_table):
    share = attn_in.shape[1]
    outs = [shape((GROUP, share, 2 * PACKED + LANES), bf16)]
    if direct:
        outs += [shape((GROUP, share, D // GROUP), bf16)] * LAYERS

    def body(*refs):
        prepare_body(direct, *refs)

    return whole_call(
        body, outs, [attn_in, attn_out, router, gains, rel_table], streamed=True, name="prepare"
    )


def unpack(place, hits, experts, pairs, layer, got):
    share = got.shape[-2]
    width = D // GROUP
    first = layer == 0

    def body(place_ref, hits_ref, got_ref, w_in_ref, w_out_ref, *rest):
        for index in range(experts * pairs):
            e, d = index // pairs, index % pairs
            for c in range(GROUP):
                owner = (e * GROUP + c) * pairs + d
                at = owner * share
                w_in_ref[at : at + share, :] = got_ref[index, c, :, :PACKED]
                w_out_ref[c, index * share : (index + 1) * share, :] = got_ref[
                    index, c, :, got_ref.shape[-1] - width :
                ]
                if first:
                    flags = got_ref[index, c, :, PACKED : PACKED + LANES].astype(f32)
                    rest[2][at : at + share, :] = flags
                    rest[3][owner : owner + 1, :] = flags[:1, :]
        if not first:
            return
        feature_ref, bias_ref, flat_ref, bucket_ref = rest
        feature_ref[...] = flat_ref[...].T
        head = lax.broadcasted_iota(jnp.int32, (8, LANES), 0)
        lane = lax.broadcasted_iota(jnp.int32, (8, LANES), 1)
        for other in range(LAYERS):
            mine = jnp.where(
                (lane == 64 + 32 * other + head * GROUP + place_ref[0]) & (head < OWN), 1.0, 0.0
            )
            table = dot(mine, bucket_ref[...], 1, 1, lax.Precision.HIGHEST)
            bias_ref[other] = dot(
                table - table[:, BUCKETS - 1 :], hits_ref[...], 1, 0, lax.Precision.HIGHEST
            )

    outs = [shape((D, PACKED), bf16), shape((GROUP, OWN_COLS, D // GROUP), bf16)]
    scratch = []
    if first:
        outs += [shape((LANES, D), f32), shape((LAYERS, 8, REACH), f32)]
        scratch = [pltpu.VMEM((D, LANES), f32), pltpu.VMEM((BUCKETS, LANES), f32)]
    return whole_call(
        body, outs, [place, hits, got], smem=1, scratch=scratch, name="unpack"
    )


def near_bias(bias_ref, layer, head, rows):
    row = bias_ref[layer, head : head + 1, :]
    return pltpu.roll(jnp.broadcast_to(row, (rows, REACH)), 0, 1, stride=1, stride_axis=0)


def masked_scores(keys, queries, near, low, key_block, query_block, rows):
    scores = dot(keys, queries, 1, 1)
    key_place = lax.broadcasted_iota(jnp.int32, (rows, rows), 0)
    seen = key_place >= low - key_block * rows
    if key_block == query_block:
        scores = scores + near[:, :rows]
        seen = seen & (key_place <= lax.broadcasted_iota(jnp.int32, (rows, rows), 1))
    elif key_block == query_block - 1:
        scores = scores + near[:, rows:]
    return jnp.where(seen, scores, NEGATIVE)


def attention_forward_body(
    layer, place_ref, n0, n1, n2, n3, w_ref, feature_ref, bias_ref, low_ref, wo_ref,
    packed_ref, log_ref, mixed_ref, keep_ref, send_ref, *normed_ref,
):
    me = place_ref[0]
    rows = n0.shape[0]
    for r, piece in enumerate((n0, n1, n2, n3)):
        normed = piece[...]
        if layer == 0:
            wide = normed.astype(f32)
            normed = (wide * rms_scale(wide) * feature_ref[16:17, :]).astype(bf16)
            normed_ref[0][r * rows : (r + 1) * rows, :] = normed
        packed_ref[r * rows : (r + 1) * rows, :] = dot(normed, w_ref[...], 1, 0).astype(bf16)
    lane = lax.broadcasted_iota(jnp.int32, (rows, LANES), 1)
    starts = [pl.multiple_of((b ^ me) * rows, rows) for b in range(GROUP)]
    for pair in range(OWN // 2):
        at = pair * LANES

        def part(b, which):
            column = which * OWN_COLS + at
            return packed_ref[pl.ds(starts[b], rows), column : column + LANES]

        sides = [(lane // HEAD_DIM) == side for side in range(2)]
        nears = [near_bias(bias_ref, layer, pair * 2 + side, rows) for side in range(2)]
        for qb in range(GROUP):
            low = low_ref[:, qb * rows : (qb + 1) * rows]
            queries = part(qb, 0) * SCORE_SCALE
            total = None
            for side in range(2):
                mine = jnp.where(sides[side], queries, 0).astype(bf16)
                tiles = [
                    masked_scores(part(kb, 1), mine, nears[side], low, kb, qb, rows)
                    for kb in range(qb + 1)
                ]
                peak = jnp.max(tiles[0], 0, keepdims=True)
                for tile in tiles[1:]:
                    peak = jnp.maximum(peak, jnp.max(tile, 0, keepdims=True))
                weight_sum = jnp.zeros((1, rows), f32)
                out = jnp.zeros((LANES, rows), f32)
                for kb, tile in enumerate(tiles):
                    power = jnp.exp(tile - peak)
                    weight_sum = weight_sum + jnp.sum(power, 0, keepdims=True)
                    values = jnp.where(sides[side], part(kb, 2), 0).astype(bf16)
                    out = out + dot(values, power.astype(bf16), 0, 0)
                out = out / weight_sum
                total = out if total is None else total + out
                head = pair * 2 + side
                log_ref[head : head + 1, qb * rows : (qb + 1) * rows] = peak + jnp.log(weight_sum)
            mixed_ref[pl.ds(starts[qb], rows), at : at + LANES] = total.T.astype(bf16)
    width = wo_ref.shape[2]
    for r, (target, offset) in enumerate(
        ((keep_ref, 0), (send_ref, 0), (keep_ref, rows), (send_ref, rows))
    ):
        mixed = mixed_ref[r * rows : (r + 1) * rows, :]
        for q in range(wo_ref.shape[0]):
            target[offset : offset + rows, q * width : (q + 1) * width] = dot(
                mixed, wo_ref[q], 1, 0
            ).astype(target.dtype)


def attention_forward(layer, place, pieces, w_in, feature, bias, low, w_out):
    rows = pieces[0].shape[0]
    total = GROUP * rows
    outs = [
        shape((total, PACKED), bf16),
        shape((8, total), f32),
        shape((total, OWN_COLS), bf16),
        shape((2 * rows, D), f32),
        shape((2 * rows, D), bf16),
    ]
    if layer == 0:
        outs.append(shape((total, D), bf16))

    def body(*refs):
        attention_forward_body(layer, *refs)

    return whole_call(
        body,
        outs,
        [place, *pieces, w_in, feature, bias, low, w_out],
        smem=1,
        flops=2 * total * D * (PACKED + OWN_COLS) + 2 * total * total * OWN_COLS * 2,
        limit=24,
        name="attention_forward",
    )


def attention_backward_body(
    layer, place_ref, d0, d1, d2, d3, w_ref, feature_ref, bias_ref, low_ref, wo_ref, packed_ref,
    log_ref, *refs,
):
    normed_refs = refs[:-8]
    (grad_packed_ref, keep_ref, send_ref, table_ref, gain_ref, grad_mixed_ref, dk_ref,
     dv_ref) = refs[-8:]
    me = place_ref[0]
    rows = d0.shape[0]
    width = wo_ref.shape[2]
    for r, piece in enumerate((d0, d1, d2, d3)):
        got = jnp.zeros((rows, OWN_COLS), f32)
        for q in range(wo_ref.shape[0]):
            got = got + dot(piece[:, q * width : (q + 1) * width], wo_ref[q], 1, 1)
        grad_mixed_ref[r * rows : (r + 1) * rows, :] = got.astype(bf16)
    lane = lax.broadcasted_iota(jnp.int32, (rows, LANES), 1)
    starts = [pl.multiple_of((b ^ me) * rows, rows) for b in range(GROUP)]
    table_ref[...] = jnp.zeros(table_ref.shape, f32)
    for pair in range(OWN // 2):
        at = pair * LANES

        def part(b, which):
            column = which * OWN_COLS + at
            return packed_ref[pl.ds(starts[b], rows), column : column + LANES]

        sides = [(lane // HEAD_DIM) == side for side in range(2)]
        nears = [near_bias(bias_ref, layer, pair * 2 + side, rows) for side in range(2)]
        diag = [jnp.zeros((rows, rows), f32) for _ in range(2)]
        before = [jnp.zeros((rows, rows), f32) for _ in range(2)]
        far = [jnp.zeros((1, rows), f32) for _ in range(2)]
        dk_ref[...] = jnp.zeros(dk_ref.shape, f32)
        dv_ref[...] = jnp.zeros(dv_ref.shape, f32)
        for qb in range(GROUP):
            low = low_ref[:, qb * rows : (qb + 1) * rows]
            queries = part(qb, 0) * SCORE_SCALE
            upstream = grad_mixed_ref[pl.ds(starts[qb], rows), at : at + LANES]
            grad_queries = jnp.zeros((LANES, rows), f32)
            for side in range(2):
                head = pair * 2 + side
                mine = jnp.where(sides[side], queries, 0).astype(bf16)
                above = jnp.where(sides[side], upstream, 0).astype(bf16)
                log_total = log_ref[head : head + 1, qb * rows : (qb + 1) * rows]
                probs, grads = [], []
                row_dot = jnp.zeros((1, rows), f32)
                for kb in range(qb + 1):
                    scores = masked_scores(part(kb, 1), mine, nears[side], low, kb, qb, rows)
                    prob = jnp.exp(scores - log_total)
                    grad = dot(part(kb, 2), above, 1, 1)
                    row_dot = row_dot + jnp.sum(prob * grad, 0, keepdims=True)
                    probs.append(prob)
                    grads.append(grad)
                for kb in range(qb + 1):
                    grad_score = probs[kb] * (grads[kb] - row_dot)
                    if kb == qb:
                        diag[side] = diag[side] + grad_score
                    elif kb == qb - 1:
                        before[side] = before[side] + grad_score
                    else:
                        far[side] = far[side] + jnp.sum(grad_score, 0, keepdims=True)
                    grad_low = grad_score.astype(bf16)
                    keys = jnp.where(sides[side], part(kb, 1), 0).astype(bf16)
                    grad_queries = grad_queries + dot(keys, grad_low, 0, 0)
                    span = slice(kb * rows, (kb + 1) * rows)
                    dk_ref[span, :] += dot(grad_low, mine, 1, 0)
                    dv_ref[span, :] += dot(probs[kb].astype(bf16), above, 1, 0)
            grad_packed_ref[pl.ds(starts[qb], rows), at : at + LANES] = (
                grad_queries.T * SCORE_SCALE
            ).astype(bf16)
        for kb in range(GROUP):
            span = slice(kb * rows, (kb + 1) * rows)
            for which, source in ((1, dk_ref), (2, dv_ref)):
                column = which * OWN_COLS + at
                grad_packed_ref[pl.ds(starts[kb], rows), column : column + LANES] = source[
                    span, :
                ].astype(bf16)
        distance = lax.broadcasted_iota(jnp.int32, (1, REACH), 1)
        for side in range(2):
            head = pair * 2 + side
            skewed = jnp.concatenate([diag[side], before[side]], 1)
            row_index = lax.broadcasted_iota(jnp.int32, (rows, REACH), 0)
            step = 1
            while step < rows:
                skewed = jnp.where(
                    (row_index & step) != 0, pltpu.roll(skewed, REACH - step, 1), skewed
                )
                step *= 2
            by_distance = jnp.sum(skewed, 0, keepdims=True)
            far_sum = jnp.sum(far[side], 1, keepdims=True)
            table_ref[head : head + 1, :] = by_distance + jnp.where(
                distance == REACH - 1, far_sum, 0.0
            )
    for r, (target, offset) in enumerate(
        ((keep_ref, 0), (send_ref, 0), (keep_ref, rows), (send_ref, rows))
    ):
        grad_normed = dot(grad_packed_ref[r * rows : (r + 1) * rows, :], w_ref[...], 1, 1)
        target[offset : offset + rows, :] = grad_normed.astype(target.dtype)
        part_gain = jnp.sum(grad_normed * block_of(normed_refs, r, rows).astype(f32), 0, keepdims=True)
        gain_sum = part_gain if r == 0 else gain_sum + part_gain
    gain_row = feature_ref[32 * layer + 16 : 32 * layer + 17, :]
    gain_ref[...] = jnp.broadcast_to(gain_sum / gain_row, gain_ref.shape)


def block_of(refs, r, rows):
    return refs[r][...] if len(refs) > 1 else refs[0][r * rows : (r + 1) * rows, :]


def attention_backward(
    layer, place, pieces, w_in, feature, bias, low, w_out, packed, log_total, normed, after=()
):
    rows = pieces[0].shape[0]
    total = GROUP * rows

    def body(*refs):
        attention_backward_body(layer, *refs)

    return whole_call(
        body,
        (
            shape((total, PACKED), bf16),
            shape((2 * rows, D), f32),
            shape((2 * rows, D), bf16),
            shape((8, REACH), f32),
            shape((8, D), f32),
        ),
        [place, *pieces, w_in, feature, bias, low, w_out, packed, log_total, *normed],
        smem=1,
        after=after,
        scratch=[
            pltpu.VMEM((total, OWN_COLS), bf16),
            pltpu.VMEM((total, LANES), f32),
            pltpu.VMEM((total, LANES), f32),
        ],
        flops=2 * total * D * (PACKED + OWN_COLS) + 2 * total * total * OWN_COLS * 5,
        limit=24,
        name="attention_backward",
    )


def dense_products(normed, upstream, grad_packed_ref, mixed_ref):
    rows = upstream[0].shape[0]
    total_in = None
    total_out = None
    for r in range(GROUP):
        span = slice(r * rows, (r + 1) * rows)
        one = dot(block_of(normed, r, rows), grad_packed_ref[span, :], 0, 0)
        two = dot(mixed_ref[span, :], upstream[r][...], 0, 0)
        total_in = one if total_in is None else total_in + one
        total_out = two if total_out is None else total_out + two
    return total_in, total_out


def dense_grads(normed, upstream, grad_packed, mixed):
    rows = upstream[0].shape[0]
    count = len(normed)

    def body(*refs):
        total_in, total_out = dense_products(
            refs[:count], refs[count : count + GROUP], refs[-4], refs[-3]
        )
        refs[-2][...] = total_in.astype(bf16)
        refs[-1][...] = total_out.astype(bf16)

    return whole_call(
        body,
        (shape((D, PACKED), bf16), shape((OWN_COLS, D), bf16)),
        [*normed, *upstream, grad_packed, mixed],
        flops=2 * GROUP * rows * D * (PACKED + OWN_COLS),
        name="dense_grads",
    )


def dense_pack(experts, pairs, share, place, normed, upstream, grad_packed, mixed, small, gain_a,
               by_distance, hits, split, after=()):
    rows = upstream[0].shape[0]
    count = len(normed)
    width = D // GROUP
    cut = EARLY_COLS if split else PACKED
    rest = PACKED - cut + LANES + width
    total = cut if split else PACKED + rest

    def body(place_ref, *refs):
        grad_packed_ref, mixed_ref, small_ref, gain_ref, distance_ref, hits_ref = refs[
            count + GROUP : count + GROUP + 6
        ]
        outs = refs[count + GROUP + 6 : -3]
        in_ref, out_ref, flat_ref = refs[-3:]
        total_in, total_out = dense_products(
            refs[:count], refs[count : count + GROUP], grad_packed_ref, mixed_ref
        )
        in_ref[...] = total_in
        out_ref[...] = total_out
        row = lax.broadcasted_iota(jnp.int32, (8, D), 0)
        gains = jnp.where(
            row == 0, gain_ref[...], jnp.where(row == 1, small_ref[16:24, :], 0.0)
        )
        features = jnp.concatenate(
            [small_ref[:16, :], gains, jnp.zeros((LANES - 24, D), f32)], 0
        )
        flat_ref[...] = features.T
        by_bucket = dot(hits_ref[...], distance_ref[...], 1, 1, lax.Precision.HIGHEST)
        head = lax.broadcasted_iota(jnp.int32, (8, LANES), 0)
        lane = lax.broadcasted_iota(jnp.int32, (8, LANES), 1)
        mine = jnp.where((lane == 64 + head * GROUP + place_ref[0]) & (head < OWN), 1.0, 0.0)
        buckets = dot(by_bucket, mine, 1, 0, lax.Precision.HIGHEST)
        for index in range(BUCKETS):
            at = index * share
            flat_ref[at : at + 1, :] = flat_ref[at : at + 1, :] + buckets[index : index + 1, :]
        for side, d in enumerate((place_ref[1], 1 - place_ref[1])):
            for e in range(experts):
                for c in range(GROUP):
                    at = ((e * GROUP + c) * pairs + d) * share
                    span = pl.ds(pl.multiple_of(at, share), share)
                    to = slice(c * share, (c + 1) * share)
                    target = outs[side]
                    target[e, to, :cut] = in_ref[span, :cut].astype(target.dtype)
                    out_span = pl.ds(pl.multiple_of((e * pairs + d) * share, share), share)
                    outer = out_ref[out_span, c * width : (c + 1) * width]
                    if split:
                        more = PACKED - cut
                        outs[2][e, side, to, :more] = in_ref[span, cut:].astype(bf16)
                        outs[2][e, side, to, more : more + LANES] = flat_ref[span, :].astype(bf16)
                        outs[2][e, side, to, more + LANES :] = outer.astype(bf16)
                    else:
                        target[e, to, PACKED : PACKED + LANES] = flat_ref[span, :].astype(
                            target.dtype
                        )
                        target[e, to, PACKED + LANES :] = outer.astype(target.dtype)

    outs = [
        shape((experts, GROUP * share, total), f32),
        shape((experts, GROUP * share, total), bf16),
    ]
    if split:
        outs.append(shape((experts, pairs, GROUP * share, rest), bf16))
    return whole_call(
        body,
        outs,
        [place, *normed, *upstream, grad_packed, mixed, small, gain_a, by_distance, hits],
        smem=1,
        scratch=[
            pltpu.VMEM((D, PACKED), f32),
            pltpu.VMEM((OWN_COLS, D), f32),
            pltpu.VMEM((D, LANES), f32),
        ],
        flops=2 * GROUP * rows * D * (PACKED + OWN_COLS),
        after=after,
        streamed=True,
        limit=32,
        name="dense_pack",
    )


def finish_dense(share, inner, outer):
    width = D // GROUP

    def body(*refs):
        in_ref, out_ref, small_ref = refs[1 + LAYERS :]
        for layer in range(LAYERS):
            got, rows_out = refs[0], refs[1 + layer]
            for c in range(GROUP):
                for which in range(3):
                    for head in range(OWN):
                        source = which * OWN_COLS + head * HEAD_DIM
                        target = which * D + (head * GROUP + c) * HEAD_DIM
                        in_ref[layer, :, target : target + HEAD_DIM] = got[
                            c, layer, :, source : source + HEAD_DIM
                        ].astype(f32)
                out_ref[layer, :, c * width : (c + 1) * width] = rows_out[
                    c * share : (c + 1) * share, :
                ]
            total = got[0, layer, :, PACKED:].astype(f32)
            for c in range(1, GROUP):
                total = total + got[c, layer, :, PACKED:].astype(f32)
            small_ref[layer] = total

    return whole_call(
        body,
        (
            shape((LAYERS, share, 3 * D), f32),
            shape((LAYERS, share, D), f32),
            shape((LAYERS, share, LANES), f32),
        ),
        [inner, *outer],
        name="finish_dense",
    )


def stacked(refs):
    return refs[0][...] if len(refs) == 1 else jnp.concatenate([ref[...] for ref in refs], 0)


def store_blocks(refs, rows):
    count = rows.shape[0] // len(refs)
    for index, ref in enumerate(refs):
        ref[...] = rows[index * count : (index + 1) * count, :].astype(ref.dtype)


def block_shapes(blocks, slots, width=D):
    return [shape((slots // blocks, width), bf16)] * blocks


def dispatch_grid(dest_rows, slots, tokens):
    place = lax.broadcasted_iota(jnp.int32, (slots, tokens), 0)
    first = place == dest_rows[0:1, :]
    second = place == dest_rows[1:2, :]
    return first, second


def one_hot(flags):
    return jnp.where(flags, 1.0, 0.0).astype(bf16)


def collect_grid(meta, slots):
    tokens = meta.shape[0]
    place = lax.broadcasted_iota(jnp.int32, (tokens, slots), 1)
    first = place == meta[:, 0:1].astype(jnp.int32)
    second = place == meta[:, 1:2].astype(jnp.int32)
    return first, second


def scatter_grads(upstream, meta, dest_rows, slots):
    tokens = upstream.shape[0]
    first, second = dispatch_grid(dest_rows, slots, tokens)
    return (
        dot(one_hot(first), (meta[:, 2:3] * upstream).astype(bf16), 1, 0)
        + dot(one_hot(second), (meta[:, 3:4] * upstream).astype(bf16), 1, 0)
    ).astype(bf16)


def slot_rows(idst, capacity, own):
    tokens = idst.shape[1]
    down = lax.broadcasted_iota(jnp.int32, (tokens, tokens), 0)
    across = lax.broadcasted_iota(jnp.int32, (tokens, tokens), 1)
    sub = lax.broadcasted_iota(jnp.int32, (16, tokens), 0)
    row0 = sub == idst[0:1, :]
    row1 = sub == idst[1:2, :]
    counts = dot(one_hot(row0 | row1), one_hot(down < across), 1, 0)
    found = []
    for index, row in enumerate((row0, row1)):
        slot = jnp.sum(jnp.where(row, counts, 0.0), 0, keepdims=True).astype(jnp.int32)
        found.append((idst[index : index + 1, :] ^ own) * capacity + slot)
    return jnp.where(lax.broadcasted_iota(jnp.int32, (8, tokens), 0) == 0, found[0], found[1])


def send_grads(experts, capacity, idst, grad, after):
    tokens = grad.shape[0]
    slots = experts * capacity

    def body(idst_ref, grad_ref, out_ref):
        first, second = dispatch_grid(slot_rows(idst_ref[...], capacity, 0), slots, tokens)
        out_ref[...] = dot(one_hot(first | second), grad_ref[...], 1, 0).astype(bf16)

    (out,) = whole_call(
        body, [shape((slots, D), bf16)], [idst, grad], after=after, name="send_grads"
    )
    return out


def apply_gates(experts, blocks, place, rows, gates):
    slots = gates.shape[0]
    capacity = slots // experts
    if blocks == 1:
        order = jnp.arange(experts) ^ place[2]
        rows = rows.reshape(experts, capacity, D)[order].reshape(slots, D)
        gates = gates.reshape(experts, capacity, LANES)[order].reshape(slots, LANES)

    def body(place_ref, rows_ref, gates_ref, *outs):
        for index, out_ref in enumerate(outs):
            span = pl.ds(0, slots)
            if blocks > 1:
                source = pl.multiple_of((index ^ place_ref[2]) * capacity, capacity)
                span = pl.ds(source, capacity)
            out_ref[...] = (gates_ref[span, 0:1] * rows_ref[span, :].astype(f32)).astype(bf16)

    return whole_call(
        body, block_shapes(blocks, slots), [place, rows, gates], smem=1, streamed=True,
        name="apply_gates",
    )


def route_body(layer, experts, capacity, last, blocks, place_ref, *refs):
    top = 32 * layer
    own = place_ref[2]
    x_ref, keep_ref, recv_ref, far_ref, feature_ref, ids_ref, idst_ref = refs[:7]
    middle_ref, soft_ref, meta_ref, dest_ref = refs[7:11]
    rows_refs = refs[11 : 11 + blocks]
    tokens = x_ref.shape[0]
    slots = experts * capacity
    middle = (
        x_ref[...].astype(f32)
        + keep_ref[:tokens, :]
        + recv_ref[:tokens, :].astype(f32)
        + far_ref[...].astype(f32)
    )
    middle_ref[...] = middle
    normed = middle * rms_scale(middle) * feature_ref[top + 17 : top + 18, :]
    lane = lax.broadcasted_iota(jnp.int32, (tokens, LANES), 1)
    logits = dot(normed, feature_ref[...], 1, 1, lax.Precision.HIGHEST)
    logits = jnp.where((lane >= top) & (lane < top + experts), logits, NEGATIVE)
    power = jnp.exp(logits - jnp.max(logits, -1, keepdims=True))
    soft = power / jnp.sum(power, -1, keepdims=True)
    soft_ref[...] = soft
    ids = ids_ref[...]
    hit0 = lane == ids[:, 0:1] + top
    hit1 = lane == ids[:, 1:2] + top
    picked0 = jnp.sum(jnp.where(hit0, soft, 0.0), -1, keepdims=True)
    picked1 = jnp.sum(jnp.where(hit1, soft, 0.0), -1, keepdims=True)
    pick_total = picked0 + picked1
    down = lax.broadcasted_iota(jnp.int32, (tokens, tokens), 0)
    across = lax.broadcasted_iota(jnp.int32, (tokens, tokens), 1)
    counts = dot(one_hot(across < down), one_hot(hit0 | hit1), 1, 0)
    dest0 = (ids[:, 0:1] ^ own).astype(f32) * capacity + jnp.sum(
        jnp.where(hit0, counts, 0.0), -1, keepdims=True
    )
    dest1 = (ids[:, 1:2] ^ own).astype(f32) * capacity + jnp.sum(
        jnp.where(hit1, counts, 0.0), -1, keepdims=True
    )
    fields = (dest0, dest1, picked0 / pick_total, picked1 / pick_total, pick_total)
    meta = jnp.zeros((tokens, LANES), f32)
    for index, field in enumerate(fields):
        meta = jnp.where(lane == index, field, meta)
    meta_ref[...] = meta
    dest_rows = slot_rows(idst_ref[...], capacity, own)
    dest_ref[...] = dest_rows
    first, second = dispatch_grid(dest_rows, slots, tokens)
    store_blocks(rows_refs, dot(one_hot(first | second), normed.astype(bf16), 1, 0))
    if last:
        total = None
        place = lax.broadcasted_iota(jnp.int32, (slots, tokens), 0)
        for index in range(2):
            slot = dest_rows[index : index + 1, :] - (idst_ref[index : index + 1, :] ^ own) * capacity
            flags = place == slot + idst_ref[index : index + 1, :] * capacity
            gate = meta[:, 2 + index : 3 + index]
            spread = jnp.zeros((tokens, LANES), f32)
            for term in range(3):
                piece = gate.astype(bf16).astype(f32)
                spread = jnp.where(lane == term, piece, spread)
                gate = gate - piece
            got = dot(one_hot(flags), spread.astype(bf16), 1, 0)
            total = got if total is None else total + got
        refs[-1][...] = jnp.broadcast_to(jnp.sum(total, -1, keepdims=True), total.shape)


def route(
    layer, experts, capacity, blocks, place, x, keep, recv, far, feature, ids, idst, last, after=()
):
    tokens = x.shape[0]
    slots = experts * capacity
    outs = [
        shape((tokens, D), f32),
        shape((tokens, LANES), f32),
        shape((tokens, LANES), f32),
        shape((8, tokens), jnp.int32),
    ] + block_shapes(blocks, slots)
    if last:
        outs.append(shape((slots, LANES), f32))

    def body(*refs):
        route_body(layer, experts, capacity, last, blocks, *refs)

    return whole_call(
        body, outs, [place, x, keep, recv, far, feature, ids, idst], smem=1,
        flops=2 * slots * tokens * D, after=after, name="route",
    )


def combine(middle, back, meta, feature=None):
    tokens = middle.shape[0]
    count = len(back)
    last = feature is None
    args = [middle, meta, *back]
    outs = [shape((tokens, D), bf16 if last else f32)]
    if not last:
        args.append(feature)
        outs.append(shape((tokens, D), bf16))

    def body(middle_ref, meta_ref, *refs):
        meta = meta_ref[...]
        rows = stacked(refs[:count])
        first, second = collect_grid(meta, rows.shape[0])
        x = (
            middle_ref[...]
            + meta[:, 2:3] * dot(one_hot(first), rows, 1, 0)
            + meta[:, 3:4] * dot(one_hot(second), rows, 1, 0)
        )
        if last:
            refs[-1][...] = x.astype(bf16)
        else:
            refs[-2][...] = x
            refs[-1][...] = (x * rms_scale(x) * refs[count][48:49, :]).astype(bf16)

    return whole_call(
        body, outs, args, flops=4 * tokens * D * count * back[0].shape[0], name="combine"
    )


def expert_token_back_body(
    layer, back_refs, came_refs, g_ref, middle_ref, soft_ref, meta_ref, ids_ref, feature_ref,
    dmiddle_ref, dattn_ref, small_ref,
):
    back, came = stacked(back_refs), stacked(came_refs)
    top = 32 * layer
    gain_row = feature_ref[top + 17 : top + 18, :]
    meta = meta_ref[...]
    g = g_ref[...].astype(f32)
    slots = back.shape[0]
    first, second = collect_grid(meta, slots)
    grad_gate0 = jnp.sum(g * dot(one_hot(first), back, 1, 0), -1, keepdims=True)
    grad_gate1 = jnp.sum(g * dot(one_hot(second), back, 1, 0), -1, keepdims=True)
    grad_normed = dot(one_hot(first | second), came, 1, 0)
    gap = (grad_gate0 - grad_gate1) / meta[:, 4:5]
    ids = ids_ref[...]
    lane = lax.broadcasted_iota(jnp.int32, meta.shape, 1)
    grad_soft = jnp.where(lane == ids[:, 0:1] + top, meta[:, 3:4] * gap, 0.0) + jnp.where(
        lane == ids[:, 1:2] + top, -meta[:, 2:3] * gap, 0.0
    )
    soft = soft_ref[...]
    grad_logits = soft * (grad_soft - jnp.sum(soft * grad_soft, -1, keepdims=True))
    middle = middle_ref[...]
    normed = middle * rms_scale(middle) * gain_row
    grad_router = dot(grad_logits.T, normed, 1, 0, lax.Precision.HIGHEST)
    grad_normed = grad_normed + dot(
        grad_logits, feature_ref[...], 1, 0, lax.Precision.HIGHEST
    )
    grad_branch, grad_gain = norm_back(middle, gain_row, grad_normed)
    dmiddle = g + grad_branch
    dmiddle_ref[...] = dmiddle
    dattn_ref[...] = dmiddle.astype(bf16)
    small_ref[:16, :] = grad_router[top : top + 16, :]
    small_ref[16:24, :] = jnp.broadcast_to(grad_gain, (8, D))


def expert_token_back(layer, back, came, g, middle, soft, meta, ids, feature, after=()):
    tokens = middle.shape[0]

    def body(*refs):
        count = len(back)
        expert_token_back_body(layer, refs[:count], refs[count : 2 * count], *refs[2 * count :])

    return whole_call(
        body,
        (shape((tokens, D), f32), shape((tokens, D), bf16), shape((24, D), f32)),
        [*back, *came, g, middle, soft, meta, ids, feature],
        after=after,
        flops=6 * tokens * D * len(back) * back[0].shape[0],
        streamed=True,
        limit=32,
        name="expert_token_back",
    )


def attention_token_back_body(layer, *refs):
    if layer == 0:
        x_ref, dmiddle_ref, keep_ref, recv_ref, far_ref, feature_ref, out_ref = refs
    else:
        (x_ref, dmiddle_ref, keep_ref, recv_ref, far_ref, feature_ref, meta_ref, dest_ref,
         out_ref, *sent_refs) = refs
    tokens = x_ref.shape[0]
    grad_normed = (
        keep_ref[:tokens, :] + recv_ref[:tokens, :].astype(f32) + far_ref[...].astype(f32)
    )
    gain_row = feature_ref[32 * layer + 16 : 32 * layer + 17, :]
    grad_branch, _ = norm_back(x_ref[...].astype(f32), gain_row, grad_normed)
    g = dmiddle_ref[...] + grad_branch
    out_ref[...] = g
    if layer > 0:
        slots = len(sent_refs) * sent_refs[0].shape[0]
        store_blocks(sent_refs, scatter_grads(g, meta_ref[...], dest_ref[...], slots))


def attention_token_back(
    layer, x, dmiddle, keep, recv, far, feature, meta=None, dest=None, blocks=1, slots=0, after=()
):
    tokens = x.shape[0]
    outs = [shape((tokens, D), f32)]
    args = [x, dmiddle, keep, recv, far, feature]
    if meta is not None:
        outs += block_shapes(blocks, slots)
        args += [meta, dest]

    def body(*refs):
        attention_token_back_body(layer, *refs)

    return whole_call(
        body, outs, args, flops=4 * tokens * D * slots, after=after, name="attention_token_back"
    )


def gelu_parts(gate):
    inner = math.sqrt(2.0 / math.pi) * (gate + 0.044715 * gate * gate * gate)
    return jnp.tanh(inner)


def weight_specs(layer, tile):
    return [
        pl.BlockSpec((1, 1, D, tile), lambda s: (layer, 0, 0, s)),
        pl.BlockSpec((1, 1, D, tile), lambda s: (layer, 0, 0, FF // tile + s)),
        pl.BlockSpec((1, 1, D, tile), lambda s: (layer, 0, 0, s)),
    ]


def block_specs(blocks):
    return [pl.BlockSpec(b.shape, lambda s: (0, 0)) for b in blocks]


def expert_call(body, steps, outs, out_specs, args, in_specs, scratch, limit, after, name):
    used = len(args)

    def ordered(*refs):
        body(*refs[:used], *refs[used + len(after) :])

    count = ROWS_HINT
    return pl.pallas_call(
        ordered,
        grid=(steps,),
        out_shape=tuple(outs),
        in_specs=list(in_specs) + [pl.BlockSpec(memory_space=pltpu.HBM)] * len(after),
        out_specs=tuple(out_specs),
        scratch_shapes=list(scratch),
        compiler_params=pltpu.CompilerParams(vmem_limit_bytes=limit * MIB),
        cost_estimate=pl.CostEstimate(
            flops=6 * count * D * FF, bytes_accessed=6 * D * FF, transcendentals=count * FF
        ),
        name=name,
    )(*args, *[far_away(a) for a in after])


def expert_forward(layer, blocks, w_in, w_out, after=()):
    number = len(blocks)
    count = number * blocks[0].shape[0]
    steps = FF // WIDE_TILE

    def body(*refs):
        wg_ref, wu_ref, wo_ref = refs[number : number + 3]
        produced_refs = refs[number + 3 : 2 * number + 3]
        acts_ref, rows_ref, total_ref = refs[2 * number + 3 :]
        step = pl.program_id(0)

        @pl.when(step == 0)
        def _():
            rows_ref[...] = stacked(refs[:number])

        rows = rows_ref[...]
        gate = dot(rows, wg_ref[0, 0], 1, 0)
        up = dot(rows, wu_ref[0, 0], 1, 0)
        acts_ref[0] = gate.astype(bf16)
        acts_ref[1] = up.astype(bf16)
        hidden = (0.5 * gate * (1.0 + gelu_parts(gate)) * up).astype(bf16)
        out = dot(hidden, wo_ref[0, 0], 1, 1)

        @pl.when(step == 0)
        def _():
            total_ref[...] = out

        @pl.when(step == steps - 1)
        def _():
            store_blocks(produced_refs, total_ref[...] + out)

    *produced, acts = expert_call(
        body,
        steps,
        [shape(b.shape, bf16) for b in blocks] + [pltpu.HBM((2, count, FF), bf16)],
        block_specs(blocks) + [pl.BlockSpec((2, count, WIDE_TILE), lambda s: (0, 0, s))],
        [*blocks, far_away(w_in), far_away(w_in), far_away(w_out)],
        block_specs(blocks) + weight_specs(layer, WIDE_TILE),
        [pltpu.VMEM((count, D), bf16), pltpu.VMEM((count, D), f32)],
        56,
        after,
        "expert_forward",
    )
    return produced, acts


def expert_backward(layer, blocks, out_blocks, acts, w_in, w_out, after=()):
    number = len(blocks)
    count = number * blocks[0].shape[0]
    steps = FF // WIDE_TILE
    outs = block_shapes(out_blocks, count)

    def body(*refs):
        acts_refs = refs[number : number + len(acts)]
        wg_ref, wu_ref, wo_ref, *rest = refs[number + len(acts) :]
        drows_refs = rest[:out_blocks]
        parts_ref, grad_ref, total_ref = rest[out_blocks:]
        step = pl.program_id(0)

        @pl.when(step == 0)
        def _():
            grad_ref[...] = stacked(refs[:number])

        grad_hidden = dot(grad_ref[...], wo_ref[0, 0], 1, 0)
        gate = jnp.concatenate([ref[0] for ref in acts_refs], 0).astype(f32)
        up = jnp.concatenate([ref[1] for ref in acts_refs], 0).astype(f32)
        curve = gelu_parts(gate)
        value = 0.5 * gate * (1.0 + curve)
        slope = 0.5 * (1.0 + curve) + 0.5 * gate * (1.0 - curve * curve) * math.sqrt(
            2.0 / math.pi
        ) * (1.0 + 3.0 * 0.044715 * gate * gate)
        grad_gate = (grad_hidden * up * slope).astype(bf16)
        grad_up = (grad_hidden * value).astype(bf16)
        parts_ref[0] = grad_gate
        parts_ref[1] = grad_up
        parts_ref[2] = (value * up).astype(bf16)
        out = dot(grad_gate, wg_ref[0, 0], 1, 1) + dot(grad_up, wu_ref[0, 0], 1, 1)

        @pl.when(step == 0)
        def _():
            total_ref[...] = out

        @pl.when(step == steps - 1)
        def _():
            store_blocks(drows_refs, total_ref[...] + out)

    *drows, parts = expert_call(
        body,
        steps,
        outs + [pltpu.HBM((3, count, FF), bf16)],
        block_specs(outs) + [pl.BlockSpec((3, count, WIDE_TILE), lambda s: (0, 0, s))],
        [*blocks, *[far_away(a) for a in acts], far_away(w_in), far_away(w_in), far_away(w_out)],
        block_specs(blocks)
        + [pl.BlockSpec((2, a.shape[1], WIDE_TILE), lambda s: (0, 0, s)) for a in acts]
        + weight_specs(layer, WIDE_TILE),
        [pltpu.VMEM((count, D), bf16), pltpu.VMEM((count, D), f32)],
        58,
        after,
        "expert_backward",
    )
    return drows, parts


def expert_grads(shares, rows, grads, parts, after=()):
    count = len(rows) * rows[0].shape[0]
    tall = D // shares
    first = len(rows)
    second = first + len(grads)
    third = second + len(parts)

    def body(*refs):
        out_ref, rows_t, grad_t = refs[third:]

        @pl.when(pl.program_id(0) == 0)
        def _():
            rows_t[...] = stacked(refs[:first]).T
            grad_t[...] = stacked(refs[first:second]).T

        for which in range(3):
            left = rows_t if which < 2 else grad_t
            right = [ref[which] for ref in refs[second:third]]
            right = right[0] if len(right) == 1 else jnp.concatenate(right, 0)
            got = dot(left[...], right, 1, 0).astype(bf16)
            for share in range(shares):
                out_ref[share, which] = got[share * tall : (share + 1) * tall, :]

    (out,) = expert_call(
        body,
        FF_STEPS,
        [pltpu.HBM((shares, 3, tall, FF), bf16)],
        [pl.BlockSpec((shares, 3, tall, FF_TILE), lambda s: (0, 0, 0, s))],
        [*rows, *grads, *[far_away(p) for p in parts]],
        block_specs(rows)
        + block_specs(grads)
        + [pl.BlockSpec((3, p.shape[1], FF_TILE), lambda s: (0, 0, s)) for p in parts],
        [pltpu.VMEM((D, count), bf16), pltpu.VMEM((D, count), bf16)],
        32,
        after,
        "expert_grads",
    )
    return out


def place_expert_grads(layer, summed, before=None, after=()):
    tall = summed.shape[1]
    outs = (
        pltpu.HBM((LAYERS, 1, tall, 2 * FF), f32),
        pltpu.HBM((LAYERS, 1, tall, FF), f32),
    )
    held = [] if before is None else list(before)

    def body(part_ref, out_part_ref, *refs):
        in_ref, out_ref = refs[-2:]
        in_ref[0, 0] = part_ref[0].astype(f32)
        out_ref[0, 0] = out_part_ref[0].astype(f32)

    return pl.pallas_call(
        body,
        grid=(2,),
        out_shape=outs,
        in_specs=[
            pl.BlockSpec((1, tall, FF), lambda s: (s, 0, 0)),
            pl.BlockSpec((1, tall, FF), lambda s: (2, 0, 0)),
        ]
        + [pl.BlockSpec(memory_space=pl.ANY)] * (len(held) + len(after)),
        out_specs=(
            pl.BlockSpec((1, 1, tall, FF), lambda s: (layer, 0, 0, s)),
            pl.BlockSpec((1, 1, tall, FF), lambda s: (layer, 0, 0, 0)),
        ),
        input_output_aliases={2: 0, 3: 1} if held else {},
        compiler_params=pltpu.CompilerParams(vmem_limit_bytes=32 * MIB),
        name="place_expert_grads",
    )(far_away(summed), far_away(summed), *[far_away(h) for h in [*held, *after]])


TWIN = [(i, i ^ 1) for i in range(GROUP)]
ACROSS = [(i, i ^ 2) for i in range(GROUP)]
FLIP = [(0, 1), (1, 0)]


def share_pieces(piece):
    across = lax.ppermute(piece, "context", ACROSS)
    twin = lax.ppermute(piece, "context", TWIN)
    return [piece, twin, across, lax.ppermute(across, "context", TWIN)]


def sum_pieces(keep, send):
    rows = keep.shape[0] // 2
    recv = lax.ppermute(send, "context", TWIN)
    other = (keep[rows:] + recv[rows:].astype(f32)).astype(bf16)
    return keep, recv, lax.ppermute(other, "context", ACROSS)


def sum_zone(zone):
    return jnp.sum(zone.astype(f32), 0)


def dense_sum(
    experts, pairs, share, table_share, place, grad_w_in, grad_w_out, small, gain_a, by_distance,
    hits,
):
    by_bucket = jnp.dot(hits, by_distance[:OWN].T, precision=lax.Precision.HIGHEST)
    buckets = jnp.where(
        jnp.arange(GROUP)[None, None, :] == place[0], by_bucket[:, :, None], 0.0
    ).reshape(experts, GROUP, pairs, 1, table_share)
    features = jnp.concatenate([small[:16], gain_a[:1], small[16:17]], 0).T
    features = features.reshape(experts, GROUP, pairs, share, 18)
    flat = jnp.zeros((experts, GROUP, pairs, share, LANES), f32)
    flat = flat.at[..., :18].set(features).at[..., :1, 64 : 64 + table_share].set(buckets)
    pack = jnp.concatenate(
        [grad_w_in.reshape(experts, GROUP, pairs, share, PACKED), flat.astype(bf16)], -1
    ).transpose(0, 2, 1, 3, 4)
    pack = pack.reshape(experts * pairs, GROUP * share, PACKED + LANES)
    mine = lax.psum_scatter(pack, ("experts", "dp"), scatter_dimension=0, tiled=False)
    inner = lax.all_to_all(
        mine.reshape(GROUP, share, PACKED + LANES), "context", split_axis=0, concat_axis=0
    ).astype(f32)
    g_in = inner[..., :PACKED].reshape(GROUP, share, 3, OWN, HEAD_DIM)
    g_in = g_in.transpose(1, 2, 3, 0, 4).reshape(share, 3 * D)
    placed_rows = jnp.where(
        jnp.arange(GROUP)[None, :, None, None] == place[0],
        grad_w_out.reshape(OWN, 1, HEAD_DIM, D),
        jnp.zeros((), bf16),
    ).reshape(D, D)
    g_out = lax.psum_scatter(placed_rows, ALL, scatter_dimension=0, tiled=True).astype(f32)
    return g_in, g_out, jnp.sum(inner[..., PACKED:], 0)


def exchange(rows):
    return lax.all_to_all(rows, "experts", split_axis=0, concat_axis=0, tiled=True)


def swap(blocks, experts):
    split = blocks if len(blocks) > 1 else jnp.split(blocks[0], experts)
    moved = [
        part if k == 0 else lax.ppermute(part, "experts", [(i, i ^ k) for i in range(experts)])
        for k, part in enumerate(split)
    ]
    return moved if len(blocks) > 1 else [jnp.concatenate(moved)]


def on_device(
    tokens, doc_starts, expert_ids, attn_in, attn_out, router, gains, rel_table,
    expert_in, expert_out, out_grad,
):
    experts = lax.axis_size("experts")
    pairs = lax.axis_size("dp")
    share = attn_in.shape[1]
    table_share = rel_table.shape[1]
    direct = share * pairs == HEAD_DIM and experts * GROUP == HEADS and pairs == 2
    place = jnp.stack(
        [lax.axis_index("context"), lax.axis_index("dp"), lax.axis_index("experts")]
    ).astype(jnp.int32)
    start_tokens = tokens[0]
    ids = expert_ids[0]
    idst = ids.T
    rows = start_tokens.shape[0]
    capacity = (10 * rows + 4 * experts - 1) // (4 * experts)
    slots = experts * capacity
    blocks = experts if experts == 4 and capacity % 16 == 0 else 1
    fine = [(0, 1), (2,), (3,)] if blocks == 4 else [(0,)]
    coarse = [(0, 1), (2, 3)] if blocks == 4 else [(0,)]
    grad_in = out_grad[0]
    hits = jnp.asarray(bucket_hits())

    packets = prepare(
        direct, attn_in, attn_out, router.transpose(0, 2, 1), gains.transpose(0, 2, 1), rel_table
    )

    def spread(packet):
        return lax.all_to_all(packet, "context", split_axis=0, concat_axis=0)

    def gather(part):
        return lax.all_gather(part, ("experts", "dp"), axis=0, tiled=False).reshape(
            experts, pairs, *part.shape
        )

    if direct:
        packet = spread(packets[0])
        top = PACKED + LANES

        def together(columns, rows_out):
            part = jnp.concatenate([columns, rows_out], -1)
            return lax.all_gather(part, ("experts", "dp"), axis=0, tiled=False)

        first = together(packet[..., :top], packets[1])
        w_in0, w_out0, feature, bias = unpack(place, hits, experts, pairs, 0, first)
        second = [together(packet[..., top:], packets[2])]
        w_in1, w_out1 = unpack(place, hits, experts, pairs, 1, second[0])
        w_in, w_out = [w_in0, w_in1], [w_out0, w_out1]
    else:
        second = []
        w_in, w_out = [], []
        for layer in range(LAYERS):
            at = layer * (PACKED + LANES)
            part = spread(packets[0])[..., at : at + PACKED + LANES]
            got = gather(part).transpose(0, 2, 1, 3, 4)
            w_in.append(got[..., :PACKED].reshape(D, PACKED))
            if layer == 0:
                small_all = got[..., PACKED : PACKED + LANES]
            full = lax.all_gather(attn_out[layer], ALL, axis=0, tiled=True)
            mine = lax.dynamic_index_in_dim(
                full.reshape(OWN, GROUP, HEAD_DIM, D), place[0], 1, keepdims=False
            )
            w_out.append(mine.reshape(OWN_COLS, GROUP, D // GROUP).transpose(1, 0, 2))
        feature = small_all.reshape(D, LANES).astype(f32).T
        bias_rows = []
        for layer in range(LAYERS):
            at = 64 + 32 * layer
            table = small_all[:, :, :, 0, at : at + table_share].reshape(BUCKETS, OWN, GROUP)
            table = lax.dynamic_index_in_dim(table, place[0], 2, keepdims=False).astype(f32)
            row = jnp.dot((table - table[-1:]).T, hits, precision=lax.Precision.HIGHEST)
            bias_rows.append(jnp.pad(row, ((0, 8 - OWN), (0, 0))))
        bias = jnp.stack(bias_rows)
    places = jnp.arange(GROUP * rows, dtype=jnp.int32)
    starts = doc_starts[0]
    low = jnp.max(
        jnp.where(starts[:, None] <= places[None, :], starts[:, None], 0), 0, keepdims=True
    )

    pieces = share_pieces(start_tokens)
    x = start_tokens
    kept = []
    for layer in range(LAYERS):
        packed, log_total, mixed, keep, send, *normed_all = attention_forward(
            layer, place, pieces, w_in[layer], feature, bias, low, w_out[layer]
        )
        normed_rows = normed_all if layer == 0 else pieces
        last = layer == LAYERS - 1
        if last:
            send = hold(send, [arrived_grad])
        keep, recv, far = sum_pieces(keep, send)
        middle, soft, meta, dest, *sent = route(
            layer, experts, capacity, blocks, place, x, keep, recv, far, feature, ids, idst, last,
        )
        arrived = swap(sent[:blocks], experts)
        if last:
            gates = exchange(sent[blocks])
        produced, acts, drows, parts = [], [], [], []
        order = []
        for chunk in coarse if last else fine:
            done, kept_acts = expert_forward(
                layer, [arrived[k] for k in chunk], expert_in, expert_out, after=order
            )
            produced += done
            acts.append(kept_acts)
            order = done[:1] + (second if layer == 0 and len(acts) == 1 else [])
            if last:
                if not drows:
                    arrived_grad = apply_gates(experts, blocks, place, arrived_grad, gates)
                done, some = expert_backward(
                    layer, [arrived_grad[k] for k in chunk], len(chunk), acts[-1:], expert_in,
                    expert_out,
                )
                drows += done
                parts.append(some)
                order = done[:1]
        back = swap(produced, experts)
        kept.append(
            (x, normed_rows, packed, log_total, mixed, middle, soft, meta, dest, arrived, acts, back)
        )
        if last:
            (result,) = combine(middle, back, meta)
        else:
            x, normed = combine(middle, back, meta, feature)
            ungated = send_grads(experts, capacity, idst, grad_in, [x])
            arrived_grad = exchange(ungated)
            pieces = share_pieces(hold(normed, [ungated]))

    g = grad_in
    inner, outer, expert_totals = [], [], []
    other = None
    placed_grads = None
    for layer in range(LAYERS - 1, -1, -1):
        (x, normed_rows, packed, log_total, mixed, middle, soft, meta, dest, arrived, acts,
         back) = kept[layer]
        if layer < LAYERS - 1:
            drows, parts = [], []
            for index, chunk in enumerate(coarse):
                some_acts = acts[:1] if index == 0 else acts[1:]
                done, some = expert_backward(
                    layer, [arrived_grad[k] for k in chunk], len(chunk), some_acts, expert_in,
                    expert_out, after=drows[-1:],
                )
                drows += done
                parts.append(some)
        came = swap(drows, experts)
        early = [] if other is None else [other]
        weight_grads = expert_grads(
            GROUP * pairs, arrived, arrived_grad, parts, after=early
        )
        weight_grads = hold(weight_grads, came)
        total = lax.psum_scatter(
            weight_grads, ("context", "dp"), scatter_dimension=0, tiled=False
        )
        dmiddle, dattn, small_b = expert_token_back(
            layer, back, came, g, middle, soft, meta, ids, feature, after=[weight_grads]
        )
        zones = []
        if direct and other is not None:
            ours = hold(keep_dense, [dattn]) + other.astype(f32)
            zones = [exchange(ours.astype(bf16))]
        expert_totals.append(total)
        grad_pieces = share_pieces(dattn)
        grad_packed, keep, send, by_distance, gain_a = attention_backward(
            layer, place, grad_pieces, w_in[layer], feature, bias, low, w_out[layer], packed,
            log_total, normed_rows,
        )
        keep, recv, far = sum_pieces(keep, send)
        if layer > 0:
            below = kept[layer - 1]
            g, *sent = attention_token_back(
                layer, x, dmiddle, keep, recv, far, feature, below[7], below[8], blocks, slots
            )
            arrived_grad = swap(sent, experts)
        else:
            placed_grads = place_expert_grads(layer + 1, expert_totals[0])
            (g,) = attention_token_back(
                layer, x, dmiddle, keep, recv, far, feature, after=[placed_grads[0]]
            )
        if direct:
            keep_dense, send_dense, *rest = dense_pack(
                experts, pairs, share, place, normed_rows, grad_pieces, grad_packed, mixed,
                small_b, gain_a, by_distance, hits, split=layer == 0, after=zones,
            )
            other = lax.ppermute(send_dense, "dp", FLIP)
            if layer == 0:
                (zone,) = zones
                total = sum_zone(zone)
                flats = [total[:, : PACKED + LANES].astype(bf16)]
                outer.append(total[:, PACKED + LANES :])
                rest = sum_zone(exchange(rest[0]))
                theirs = lax.ppermute(rest[1].astype(bf16), "dp", FLIP)
                rest = rest[0] + theirs.astype(f32)
                ours = hold(keep_dense, [g, result, placed_grads[0]]) + other.astype(f32)
                total = sum_zone(exchange(ours.astype(bf16)))
                more = PACKED + LANES - EARLY_COLS
                flats.insert(0, jnp.concatenate([total, rest[:, :more]], -1).astype(bf16))
                outer.append(rest[:, more:])
                flat = jnp.stack([flat.reshape(GROUP, share, -1) for flat in flats], 1)
                inner = spread(flat)
        else:
            grad_w_in, grad_w_out = dense_grads(normed_rows, grad_pieces, grad_packed, mixed)
            inner.append(
                dense_sum(
                    experts, pairs, share, table_share, place, grad_w_in, grad_w_out, small_b,
                    gain_a, by_distance, hits,
                )
            )
    expert_grads_all = place_expert_grads(0, expert_totals[1], placed_grads)
    if direct:
        grad_attn_in, grad_attn_out, small_grad = finish_dense(
            share, inner, outer[::-1]
        )
    else:
        grad_attn_in, grad_attn_out, small_grad = (
            jnp.stack([entry[k] for entry in inner[::-1]]) for k in range(3)
        )
    return (
        result[None],
        g[None],
        grad_attn_in,
        grad_attn_out,
        small_grad[..., :experts],
        small_grad[..., 16:18],
        small_grad[:, 0, 64 : 64 + table_share],
        *expert_grads_all,
    )


def solution(mesh):
    return jax.shard_map(
        on_device,
        mesh=mesh,
        in_specs=(
            P(("experts", "dp"), "context", None),
            P(("experts", "dp"), None),
            P(("experts", "dp"), "context", None),
            P(None, ("experts", "context", "dp"), None),
            P(None, ("experts", "context", "dp"), None),
            P(None, ("experts", "context", "dp"), None),
            P(None, ("experts", "context", "dp"), None),
            P(None, ("experts", "context", "dp")),
            P(None, "experts", None, None),
            P(None, "experts", None, None),
            P(("experts", "dp"), "context", None),
        ),
        out_specs=(
            P(("experts", "dp"), "context", None),
            P(("experts", "dp"), "context", None),
            P(None, ("experts", "context", "dp"), None),
            P(None, ("experts", "context", "dp"), None),
            P(None, ("experts", "context", "dp"), None),
            P(None, ("experts", "context", "dp"), None),
            P(None, ("experts", "context", "dp")),
            P(None, "experts", ("context", "dp"), None),
            P(None, "experts", ("context", "dp"), None),
        ),
        check_vma=False,
    )
```
